32 devices in a mesh: groups: 2 (over y), gx: 4 (over z), gy: 2 (over x), gz: 2 (over core).
Axes of the slice: x: 2, y: 2, z: 4, core: 2. Of those that a mesh axis runs over, the one named last changes fastest.
Arguments:
- coarse_fields: float32 [6, 96, 24, 256], P(None, ('groups', 'gx'), 'gy', 'gz'), parts along dimension 1, may hold values from -6 to 6
- permittivity: float32 [96, 24, 256], P(('groups', 'gx'), 'gy', 'gz'), parts along dimension 0, may hold values from 1 to 4.4
- fine_fields: float32 [8, 2, 8, 6, 4096], P(('groups', 'gx'), 'gy', 'gz'), parts along dimension 0, may hold values from -6 to 6
- fine_permittivity: float32 [8, 2, 8, 4096], P(('groups', 'gx'), 'gy', 'gz'), parts along dimension 0, may hold values from 1 to 4.4
- patch_corner: int32 [8, 2, 4, 3], P(('groups', 'gx'), 'gy', 'gz'), parts along dimension 0, may hold values from 1 to 119, as said below
- patch_owner: int32 [8, 4, 2], P(('groups', 'gx')), parts along dimension 0, may hold values from 0 to 3, as said below
Outputs:
- coarse_out: float32 [6, 96, 24, 256], P(None, ('groups', 'gx'), 'gy', 'gz'), parts along dimension 1
- fine_out: float32 [8, 2, 8, 6, 4096], P(('groups', 'gx'), 'gy', 'gz'), parts along dimension 0
The draws below stay inside these ranges and needn't reach their ends.
There are 2 independent parts, one for each index of `groups`. The reference program is written for one: setup_inputs(seed, part) draws one part's arguments, and reference() takes and returns one part's arrays. A program takes and returns all parts, laid end to end along the dimension named above; each array names one. Nothing has to cross between parts.
Inputs may be any that keep to these rules, and one draw needn't show every extreme that they name: `patch_corner`: coordinates x in 1 to 3, y in 1 to 3, and z of patch q of a device in q * 64 + 1 to (q + 1) * 64 - 9; a region with a rim of one cell lies inside its device's block, and two regions never meet. A device's 2 patches have different owners, so each slot of a device holds at most one patch; in every gx slab some device owns a patch of every device of the slab; a slot holds a patch only where patch_owner names that device for a patch of the slot's rank.
All inputs are finite; a program needn't handle non-finite values.
Results may differ from the reference program's by a relative error of at most 0.0003.
Values sent between devices are 32-bit elements; how exact they have to be, the bound alone decides.
No kernel may reach another device: no remote copies, remote signals or barrier semaphores. Data moves between devices by JAX's collectives and lax.ppermute only.
A program may use at most 128 MiB of HBM per device.

```python
import math
import jax
import jax.numpy as jnp
from jax import lax

CX = 12
CY = 12
CZ = 128
PF = 16
PAR = 2
STEPS = 1
PC = 8
FC = 4096
GROUP = 4
NX = 48
NY = 24
NZ = 256
N_GX = 4
N_GY = 2
N_GZ = 2


def draw_patch_corner(key, part):
    key = jax.random.fold_in(key, 11)
    first, second, third = jax.random.split(key, 3)
    shape = (N_GX, N_GY, N_GZ * PAR)
    corner_x = jax.random.randint(first, shape, 1, CX - PC)
    corner_y = jax.random.randint(second, shape, 1, CY - PC)
    span = CZ // PAR
    which = jnp.arange(N_GZ * PAR, dtype=jnp.int32) % PAR
    corner_z = which[None, None, :] * span + jax.random.randint(third, shape, 1, span - PC)
    return jnp.stack([corner_x, corner_y, corner_z], axis=-1).astype(jnp.int32)


def draw_patch_owner(key, part):
    key = jax.random.fold_in(key, 12)
    first, second, third = jax.random.split(key, 3)
    group = N_GY * N_GZ
    busiest = jax.random.randint(first, (N_GX, 1), 0, group)
    shared = jnp.broadcast_to(busiest, (N_GX, group))
    offset = jax.random.randint(second, (N_GX, group), 1, group)
    other = (shared + offset) % group
    flip = jax.random.randint(third, (N_GX, group), 0, 2)
    lead = jnp.where(flip == 1, other, shared)
    trail = jnp.where(flip == 1, shared, other)
    return jnp.stack([lead, trail], axis=-1).astype(jnp.int32)


def block_scale(key, extent, pieces, low, top_value):
    factor_of, own = 1.0, jax.random.fold_in(key, 6)
    for position, blocks in pieces:
        heights = jnp.exp(jax.random.uniform(jax.random.fold_in(own, position), (blocks,), jnp.float32, low / len(pieces), top_value / len(pieces)))
        factor_of = factor_of * jnp.repeat(heights, extent[position] // blocks).reshape([-1 if axis == position else 1 for axis in range(len(extent))])
    return factor_of


def normal_values(key, extent, scale, reach, shards=(), kind=jnp.bfloat16):
    gain = block_scale(key, extent, shards, -0.22, 0.18) if shards else 1.0
    drawn = jax.random.normal(key, extent, jnp.float32) * scale * gain
    return jnp.minimum(jnp.maximum(drawn, -reach), reach).astype(kind)


def setup_inputs(seed: int = 0, part: int = 0) -> dict:
    key_list = jax.random.split(jax.random.key(seed), 7)
    own_keys = jax.random.split(jax.random.fold_in(key_list[6], part), 7)
    coarse_fields = normal_values(own_keys[0], (6, NX, NY, NZ), 1.0, 6.0, ((1, 4), (2, 2), (3, 2)), jnp.float32)
    permittivity = jnp.clip(jnp.exp(math.log(4.4) - 1.4816046 * jax.random.uniform(own_keys[1], (NX, NY, NZ), jnp.float32) ** block_scale(own_keys[1], (NX, NY, NZ), ((0, 4), (1, 2), (2, 2)), -0.2, 0.2)), 1.0, 4.4)
    fine_fields = normal_values(own_keys[2], (N_GX, N_GY, N_GZ * GROUP, 6, FC), 1.0, 6.0, ((0, 4), (1, 2), (2, 2)), jnp.float32)
    fine_permittivity = jnp.clip(jnp.exp(math.log(4.4) - 1.4816046 * jax.random.uniform(own_keys[3], (N_GX, N_GY, N_GZ * GROUP, FC), jnp.float32) ** block_scale(own_keys[3], (N_GX, N_GY, N_GZ * GROUP, FC), ((0, 4), (1, 2), (2, 2)), -0.2, 0.2)), 1.0, 4.4)
    patch_corner = draw_patch_corner(jax.random.fold_in(jax.random.fold_in(key_list[6], part), 71), part)
    patch_owner = draw_patch_owner(jax.random.fold_in(jax.random.fold_in(key_list[6], part), 71), part)
    return {"coarse_fields": coarse_fields, "permittivity": permittivity, "fine_fields": fine_fields, "fine_permittivity": fine_permittivity, "patch_corner": patch_corner, "patch_owner": patch_owner}


def forward(field, axis):
    size = [m - 1 for m in field.shape]
    start = [0, 0, 0]
    start[axis] = 1
    upper = lax.slice(field, start, [s + z for s, z in zip(start, size)])
    lower = lax.slice(field, [0, 0, 0], size)
    return upper - lower


def backward(field, axis):
    size = [m - 1 for m in field.shape]
    start = [1, 1, 1]
    upper = lax.slice(field, start, [s + z for s, z in zip(start, size)])
    begin = [1, 1, 1]
    begin[axis] = 0
    lower = lax.slice(field, begin, [s + z for s, z in zip(begin, size)])
    return upper - lower


def leap(padded, perm):
    e_pad = padded[:3]
    h_pad = padded[3:]
    curl_e = jnp.stack([
        forward(e_pad[2], 1) - forward(e_pad[1], 2),
        forward(e_pad[0], 2) - forward(e_pad[2], 0),
        forward(e_pad[1], 0) - forward(e_pad[0], 1)])
    h_ext = h_pad[:, :-1, :-1, :-1] - 0.5 * curl_e
    curl_h = jnp.stack([
        backward(h_ext[2], 1) - backward(h_ext[1], 2),
        backward(h_ext[0], 2) - backward(h_ext[2], 0),
        backward(h_ext[1], 0) - backward(h_ext[0], 1)])
    e_new = e_pad[:, 1:-1, 1:-1, 1:-1] + (0.5 / perm) * curl_h
    return jnp.concatenate([e_new, h_ext[:, 1:, 1:, 1:]], axis=0)


def ghost(region_now, state):
    grown = jnp.repeat(jnp.repeat(jnp.repeat(region_now, 2, axis=1), 2, axis=2), 2, axis=3)
    grown = grown[:, 1:PF + 3, 1:PF + 3, 1:PF + 3]
    return lax.dynamic_update_slice(grown, state, (0, 1, 1, 1))


def advance(region_old, region_new, state, patch_perm):
    for sub in range(2):
        region_now = region_old + (0.5 * sub) * (region_new - region_old)
        state = leap(ghost(region_now, state), patch_perm)
    return state


def average(state):
    return state.reshape(6, PC, 2, PC, 2, PC, 2).mean(axis=(2, 4, 6))


def region(field, corner):
    start = (jnp.int32(0), corner[0] - 1, corner[1] - 1, corner[2] - 1)
    return lax.dynamic_slice(field, start, (6, PC + 2, PC + 2, PC + 2))


def place(field, item):
    corner, values = item
    start = (jnp.int32(0), corner[0], corner[1], corner[2])
    return lax.dynamic_update_slice(field, values, start), None


def reference(coarse_fields, permittivity, fine_fields, fine_permittivity, patch_corner, patch_owner):
    group = N_GY * N_GZ
    fine = fine_fields.reshape(N_GX, group, group, 6, FC)
    fine_perm = fine_permittivity.reshape(N_GX, group, group, FC)
    corner = patch_corner.reshape(N_GX, group, PAR, 3).astype(jnp.int32)
    rank = jnp.arange(group, dtype=jnp.int32)
    slab = jnp.arange(N_GX, dtype=jnp.int32)
    base = jnp.stack([
        jnp.broadcast_to(slab[:, None] * CX, (N_GX, group)),
        jnp.broadcast_to((rank // N_GZ)[None, :] * CY, (N_GX, group)),
        jnp.broadcast_to((rank % N_GZ)[None, :] * CZ, (N_GX, group))], axis=-1).astype(jnp.int32)
    corners = (corner + base[:, :, None, :]).reshape(-1, 3).astype(jnp.int32)
    slab_index = jnp.broadcast_to(slab[:, None, None], (N_GX, group, PAR))
    rank_index = jnp.broadcast_to(rank[None, :, None], (N_GX, group, PAR))
    owner = patch_owner.astype(jnp.int32)
    states = fine[slab_index, owner, rank_index].reshape(-1, 6, PF, PF, PF)
    perms = fine_perm[slab_index, owner, rank_index].reshape(-1, PF, PF, PF)
    coarse = coarse_fields
    for step in range(STEPS):
        padded = jnp.pad(coarse, ((0, 0), (1, 1), (1, 1), (1, 1)))
        new = leap(padded, permittivity)
        old_regions = jax.vmap(lambda c: region(coarse, c))(corners)
        new_regions = jax.vmap(lambda c: region(new, c))(corners)
        states = jax.vmap(advance)(old_regions, new_regions, states, perms)
        means = jax.vmap(average)(states)
        new, unused = lax.scan(place, new, (corners, means))
        coarse = new
    fine = fine.at[slab_index, owner, rank_index].set(states.reshape(N_GX, group, PAR, 6, FC))
    return coarse, fine.reshape(fine_fields.shape)
```

```python
import functools
import jax
import jax.numpy as jnp
import numpy as np
from jax import lax
from jax.experimental import pallas as pl
from jax.experimental.pallas import tpu as pltpu
from jax.sharding import PartitionSpec as P

PF = 16
PAR = 2
HALF = PF // 2
RIM = HALF + 2
PLANES = 9
LINE = PF + 2
LANES = 128
WIDE = 384
BATCH = 4
ROWS_BOX = PLANES * 8
ROWS_REGION = 64
EDGE_ROWS = 40
X_COMPS = (0, 1, 2, 4, 5)
Y_COMPS = (0, 1, 2, 3, 5)
VMEM_BYTES = 48 * 1024 * 1024
F32 = jnp.float32
BF16 = jnp.bfloat16


def grow_table():
    table = np.zeros((PF * PF, WIDE), np.float32)
    for y in range(PF):
        for z in range(PF):
            table[y * PF + z, (y + 1) * LINE + z + 1] = 1.0
    return table


def ghost_table():
    table = np.zeros((LANES, WIDE), np.float32)
    for y in range(LINE):
        for z in range(LINE):
            table[((y + 1) // 2) * RIM + (z + 1) // 2, y * LINE + z] = 1.0
    return table


def mean_table():
    table = np.zeros((2, WIDE, LANES), np.float32)
    for odd in range(2):
        for y in range(PF):
            for z in range(PF):
                lane = odd * HALF * HALF + (y // 2) * HALF + z // 2
                table[odd, (y + 1) * LINE + z + 1, lane] = 0.125
    return table.reshape(2 * WIDE, LANES)


def move(rows, table):
    high = rows.astype(BF16)
    low = (rows - high.astype(F32)).astype(BF16)
    out = jnp.dot(high, table, preferred_element_type=F32)
    return out + jnp.dot(low, table, preferred_element_type=F32)


def lane_iota(shape):
    return lax.broadcasted_iota(jnp.int32, shape, len(shape) - 1)


def whole(memory_space=pltpu.VMEM):
    return pl.BlockSpec(memory_space=memory_space)


def call(kernel, outs, in_specs, scratch=(), flops=1_000_000, size=1_000_000, **extra):
    return pl.pallas_call(
        kernel,
        out_shape=outs,
        in_specs=in_specs,
        out_specs=jax.tree.map(lambda _: whole(), outs),
        scratch_shapes=list(scratch),
        compiler_params=pltpu.CompilerParams(vmem_limit_bytes=VMEM_BYTES),
        cost_estimate=pl.CostEstimate(flops=flops, bytes_accessed=size, transcendentals=0),
        **extra,
    )


def swap_pairs(count, first):
    pairs = []
    for i in range(first, count - 1, 2):
        pairs += [(i, i + 1), (i + 1, i)]
    return pairs


def faces_kernel(block, x_even, x_odd, y_even, y_odd):
    deep, tall = block.shape[1], block.shape[2]
    gx_odd = lax.rem(lax.axis_index("gx"), 2)
    gy_odd = lax.rem(lax.axis_index("gy"), 2)
    for k, c in enumerate(X_COMPS):
        x_even[k] = block[c, (1 - gx_odd) * (deep - 1)]
        x_odd[k] = block[c, gx_odd * (deep - 1)]
    for k, c in enumerate(Y_COMPS):
        for x in range(deep):
            first = block[c, x, 0:1, :]
            last = block[c, x, tall - 1 : tall, :]
            y_even[k, x : x + 1, :] = jnp.where(gy_odd == 0, last, first)
            if y_odd is not None:
                y_odd[k, x : x + 1, :] = jnp.where(gy_odd == 0, first, last)


def leap_kernel(two_y, *refs):
    if two_y:
        block, beside, perm, corner, x_even, x_odd, y_even, y_odd, new, packed, pad, side, mag, rate, fresh = refs
    else:
        block, beside, perm, corner, x_even, x_odd, y_even, new, packed, pad, side, mag, rate, fresh = refs
        y_odd = None
    deep, tall = block.shape[1], block.shape[2]
    full = deep + 2
    gx_odd = lax.rem(lax.axis_index("gx"), 2)
    gy_odd = lax.rem(lax.axis_index("gy"), 2)
    gz = lax.axis_index("gz")
    pad[...] = jnp.zeros_like(pad)
    side[...] = jnp.zeros_like(side)
    rate[...] = jnp.ones_like(rate)
    lane = lane_iota((tall, LANES))
    keep = ((lane == 0) & (gz == 0)) | ((lane == LANES - 1) & (gz == 1))

    def at(c, x):
        return (c * full + x) * 16

    for x in range(deep):
        rate[pl.ds(x * 16 + 1, tall), :] = perm[x]
    for c in range(6):
        for x in range(deep):
            pad[pl.ds(at(c, x + 1) + 1, tall), :] = block[c, x]
            side[pl.ds(at(c, x + 1) + 1, tall), :] = jnp.where(keep, beside[c, x], 0.0)
    for k, c in enumerate(X_COMPS):
        even, odd = x_even[k], x_odd[k]
        pad[pl.ds(at(c, 0) + 1, tall), :] = jnp.where(gx_odd == 0, odd, even)
        if c in (1, 2):
            pad[pl.ds(at(c, full - 1) + 1, tall), :] = jnp.where(gx_odd == 0, even, odd)
    for k, c in enumerate(Y_COMPS):
        for x in range(deep):
            even = y_even[k, x : x + 1, :]
            odd = jnp.zeros_like(even) if y_odd is None else y_odd[k, x : x + 1, :]
            pad[pl.ds(at(c, x + 1), 1), :] = jnp.where(gy_odd == 0, odd, even)
            if c in (0, 2):
                pad[pl.ds(at(c, x + 1) + tall + 1, 1), :] = jnp.where(gy_odd == 0, even, odd)

    def up_y(a):
        return pltpu.roll(a, 15, 0)

    def up_z(a):
        return pltpu.roll(a, 2 * LANES - 1, 1)

    def down_y(a):
        return pltpu.roll(a, 1, 0)

    def down_z(a):
        return pltpu.roll(a, 1, 1)

    def plane(c, x):
        rows = pl.ds(at(c, x), 16)
        return jnp.concatenate([pad[rows, :], side[rows, :]], axis=1)

    def field(c, x):
        return mag[pl.ds((c * (full - 1) + x) * 16, 16), :]

    for x in range(full - 1):
        e0, e1, e2 = plane(0, x), plane(1, x), plane(2, x)
        h0 = plane(3, x) - 0.5 * ((up_y(e2) - e2) - (up_z(e1) - e1))
        h1 = plane(4, x) - 0.5 * ((up_z(e0) - e0) - (plane(2, x + 1) - e2))
        h2 = plane(5, x) - 0.5 * ((plane(1, x + 1) - e1) - (up_y(e0) - e0))
        for c, value in enumerate((h0, h1, h2)):
            mag[pl.ds((c * (full - 1) + x) * 16, 16), :] = value
    for x in range(deep):
        h0, h1, h2 = field(0, x + 1), field(1, x + 1), field(2, x + 1)
        coef = 0.5 / rate[pl.ds(x * 16, 16), :]
        c0 = ((h2 - down_y(h2)) - (h1 - down_z(h1)))[:, 0:LANES]
        c1 = ((h0 - down_z(h0)) - (h2 - field(2, x)))[:, 0:LANES]
        c2 = ((h1 - field(1, x)) - (h0 - down_y(h0)))[:, 0:LANES]
        for c, curl in enumerate((c0, c1, c2)):
            fresh[pl.ds((c * deep + x) * 16, 16), :] = plane(c, x + 1)[:, 0:LANES] + coef * curl
            fresh[pl.ds(((c + 3) * deep + x) * 16, 16), :] = (h0, h1, h2)[c][:, 0:LANES]
    for c in range(6):
        for x in range(deep):
            new[c, x] = fresh[pl.ds((c * deep + x) * 16 + 1, tall), :]
    region_lane = lane_iota((RIM, LANES))
    for q in range(PAR):
        cx, cy, cz = corner[0, 0, q, 0], corner[0, 0, q, 1], corner[0, 0, q, 2]
        for t in range(2):
            base = (q * 2 + t) * ROWS_REGION
            for c in range(6):
                total = jnp.zeros((RIM, LANES), F32)
                for j in range(RIM):
                    if t == 0:
                        rows = pad[pl.ds((c * full + cx) * 16 + cy + j, RIM, stride=16), :]
                    else:
                        rows = fresh[pl.ds((c * deep + cx - 1) * 16 + cy + j, RIM, stride=16), :]
                    shift = lax.rem(j * RIM - (cz - 1) + 2 * LANES, LANES)
                    rows = pltpu.roll(rows, shift, 1)
                    inside = (region_lane >= j * RIM) & (region_lane < (j + 1) * RIM)
                    total = jnp.where(inside, rows, total)
                packed[pl.ds(base + c * RIM, RIM), :] = total
            packed[pl.ds(base + 6 * RIM, ROWS_REGION - 6 * RIM), :] = jnp.zeros((ROWS_REGION - 6 * RIM, LANES), F32)
    base = PAR * 2 * ROWS_REGION
    half = lane_iota((16, LANES)) < LANES // 2
    packed[pl.ds(base, 16), :] = jnp.where(half, plane(0, 0)[:, 0:LANES], plane(2, full - 1)[:, 0:LANES])
    low = jnp.where(gy_odd == 0, jnp.zeros_like(y_even[1]) if y_odd is None else y_odd[1], y_even[1])
    high = jnp.where(gy_odd == 0, y_even[2], jnp.zeros_like(y_even[2]) if y_odd is None else y_odd[2])
    packed[pl.ds(base + 16, 16), :] = jnp.zeros((16, LANES), F32)
    packed[pl.ds(base + 16, deep), :] = jnp.where(lane_iota((deep, LANES)) < LANES // 2, low, high)
    packed[pl.ds(base + 32, 8), :] = jnp.zeros((8, LANES), F32)
    packed[pl.ds(base + 32, 1), :] = pad[pl.ds(at(1, full - 1) + tall, 1), :]
    packed[pl.ds(base + 33, 1), :] = pad[pl.ds(at(0, 0) + 1, 1), :]


def put(ref, g, c, m, value):
    for v in range(WIDE // LANES):
        ref[g, c * 3 + v, m * 8 : (m + 1) * 8, :] = value[:, v * LANES : (v + 1) * LANES]


def get(ref, g, c, m):
    return jnp.concatenate([ref[g, c * 3 + v, m * 8 : (m + 1) * 8, :] for v in range(WIDE // LANES)], axis=1)


def load_kernel(fine, perm, table, box, rate, lhs, wide, coefs):
    groups = fine.shape[2] // BATCH
    for g in range(groups):
        for s in range(BATCH):
            for x in range(PF):
                row = (s * PF + x) * 8
                lhs[row : row + 6, :] = fine[0, 0, g * BATCH + s, :, x * PF * PF : (x + 1) * PF * PF]
                lhs[row + 6 : row + 8, :] = jnp.zeros((2, PF * PF), F32)
        grown = move(lhs[...], table[...])
        for v in range(WIDE // LANES):
            wide[v] = grown[:, v * LANES : (v + 1) * LANES]
        zero = jnp.zeros((8, WIDE), F32)
        for c in range(6):
            put(box, g, c, 0, zero)
            put(box, g, c, PLANES - 1, zero)
            for s in range(BATCH):
                for xh in range(2):
                    source = pl.ds((s * PF + xh * 8) * 8 + c, 8, stride=8)
                    for v in range(WIDE // LANES):
                        target = pl.ds((1 - xh) * 8 + xh * BATCH + s, 8, stride=8)
                        box[g, c * 3 + v, target, :] = wide[v, source, :]
        coefs[...] = jnp.zeros_like(coefs)
        for x in range(PF):
            row = (x % 8 + (1 if x < 8 else 0)) * 8 + (0 if x < 8 else BATCH)
            cells = perm[0, 0, g * BATCH : (g + 1) * BATCH, x * PF * PF : (x + 1) * PF * PF]
            coefs[row : row + BATCH, :] = 0.5 / cells
        rate[g] = move(coefs[...], table[...])


def fine_kernel(regions, box, rate, owners, ghosts, means, out, small, lhs, now, mag, halves):
    groups = box.shape[0]
    rank = lax.axis_index("gy") * lax.axis_size("gz") + lax.axis_index("gz")
    flat = lane_iota((8, WIDE))
    yy = lax.shift_right_logical(flat * 3641, 16)
    zz = flat - yy * LINE
    inner = (yy >= 1) & (yy <= PF) & (zz >= 1) & (zz <= PF)
    upper = lax.broadcasted_iota(jnp.int32, (8, WIDE), 0) >= BATCH

    def inner_of(m):
        if m == 0:
            return inner & upper
        if m == PLANES - 1:
            return inner & jnp.logical_not(upper)
        return inner

    def up_y(a):
        return pltpu.roll(a, WIDE - LINE, 1)

    def up_z(a):
        return pltpu.roll(a, WIDE - 1, 1)

    def down_y(a):
        return pltpu.roll(a, LINE, 1)

    def down_z(a):
        return pltpu.roll(a, 1, 1)

    def rows_of(m):
        return pl.ds(m * 8, 8)

    for g in range(groups):
        for sub in range(2):
            for s in range(BATCH):
                r = g * BATCH + s
                q = jnp.where(owners[0, r, 0] == rank, 0, 1)
                for c in range(6):
                    old = regions[r, pl.ds(q * 2 * ROWS_REGION + c * RIM, RIM), :]
                    if sub == 1:
                        fresh = regions[r, pl.ds((q * 2 + 1) * ROWS_REGION + c * RIM, RIM), :]
                        old = old + 0.5 * (fresh - old)
                    row = c * ROWS_BOX + s
                    lhs[pl.ds(row, 5, stride=16), :] = old[0:5]
                    lhs[pl.ds(row + 8, 4, stride=16), :] = old[1:5]
                    lhs[pl.ds(row + BATCH, 5, stride=16), :] = old[5:10]
                    lhs[pl.ds(row + BATCH + 8, 4, stride=16), :] = old[5:9]
            source = box if sub == 0 else out
            for c in range(6):
                ghost = move(lhs[pl.ds(c * ROWS_BOX, ROWS_BOX), :], ghosts[...])
                for m in range(PLANES):
                    now[c, rows_of(m), :] = jnp.where(
                        inner_of(m), get(source, g, c, m), ghost[m * 8 : (m + 1) * 8]
                    )

            def next_x(c, m):
                if m == PLANES - 1:
                    return pltpu.roll(now[c, rows_of(0), :], BATCH, 0)
                return now[c, rows_of(m + 1), :]

            def last_x(c, m):
                if m == 0:
                    return pltpu.roll(mag[c, rows_of(PLANES - 1), :], BATCH, 0)
                return mag[c, rows_of(m - 1), :]

            for m in range(PLANES):
                e0, e1, e2 = (now[c, rows_of(m), :] for c in range(3))
                h0, h1, h2 = (now[c, rows_of(m), :] for c in range(3, 6))
                mag[0, rows_of(m), :] = h0 - 0.5 * ((up_y(e2) - e2) - (up_z(e1) - e1))
                mag[1, rows_of(m), :] = h1 - 0.5 * ((up_z(e0) - e0) - (next_x(2, m) - e2))
                mag[2, rows_of(m), :] = h2 - 0.5 * ((next_x(1, m) - e1) - (up_y(e0) - e0))
            for m in range(PLANES):
                h0, h1, h2 = (mag[c, rows_of(m), :] for c in range(3))
                coef = rate[g, rows_of(m), :]
                e0, e1, e2 = (now[c, rows_of(m), :] for c in range(3))
                put(out, g, 0, m, e0 + coef * ((h2 - down_y(h2)) - (h1 - down_z(h1))))
                put(out, g, 1, m, e1 + coef * ((h0 - down_z(h0)) - (h2 - last_x(2, m))))
                put(out, g, 2, m, e2 + coef * ((h1 - last_x(1, m)) - (h0 - down_y(h0))))
                for c, value in enumerate((h0, h1, h2)):
                    put(out, g, c + 3, m, value)
        for c in range(6):
            for k in range(4):
                other = jnp.where(upper, get(out, g, c, 2 * k), get(out, g, c, 2 * k + 2))
                pair = get(out, g, c, 2 * k + 1) + other
                halves[pl.ds((c * 2 + k // 2) * 8, 8), (k % 2) * WIDE : (k % 2 + 1) * WIDE] = pair
        small[pl.ds(g * 96, 96), :] = move(halves[...], means[...])


def store_kernel(box, fine, owners, table, out, cells):
    groups = box.shape[0]
    rank = lax.axis_index("gy") * lax.axis_size("gz") + lax.axis_index("gz")
    for g in range(groups):
        for c in range(6):
            rows = jnp.concatenate([box[g, c * 3 + v] for v in range(WIDE // LANES)], axis=1)
            flat = move(rows, table[...])
            for v in range(PF * PF // LANES):
                cells[v, pl.ds(c * ROWS_BOX, ROWS_BOX), :] = flat[:, v * LANES : (v + 1) * LANES]
        for s in range(BATCH):
            slot = g * BATCH + s
            live = (owners[0, slot, 0] == rank) | (owners[0, slot, 1] == rank)
            for x in range(PF):
                row = (x % 8 + (1 if x < 8 else 0)) * 8 + (0 if x < 8 else BATCH) + s
                for v in range(PF * PF // LANES):
                    cut = slice(x * PF * PF + v * LANES, x * PF * PF + (v + 1) * LANES)
                    value = cells[v, pl.ds(row, 6, stride=ROWS_BOX), :]
                    out[0, 0, slot, :, cut] = jnp.where(live, value, fine[0, 0, slot, :, cut])


def fix_kernel(new, perm, edges, out):
    deep, tall = new.shape[1], new.shape[2]
    ranks_y, gy, gz = lax.axis_size("gy"), lax.axis_index("gy"), lax.axis_index("gz")
    rank = gy * 2 + gz
    base = PAR * 2 * ROWS_REGION
    out[...] = new[...]

    def add(c, x, rows, amount):
        out[c, x, rows, :] = out[c, x, rows, :] + 0.25 / perm[x, rows, :] * amount

    lower = edges[jnp.maximum(rank - 2, gz), pl.ds(base + 32, 1), :]
    higher = edges[jnp.minimum(rank + 2, (ranks_y - 1) * 2 + gz), pl.ds(base + 33, 1), :]
    add(0, deep - 1, slice(0, 1), jnp.where(gy > 0, lower, 0.0))
    add(1, 0, slice(tall - 1, tall), jnp.where(gy < ranks_y - 1, higher, 0.0))
    side = gy * 2 + 1 - gz
    lane = lane_iota((tall, LANES))
    tile = edges[side, pl.ds(base + 1, tall), :]
    add(0, deep - 1, slice(0, tall), jnp.where((lane == 0) & (gz == 1), pltpu.roll(tile, 1, 1), 0.0))
    add(2, 0, slice(0, tall), jnp.where((lane == LANES - 1) & (gz == 0), pltpu.roll(tile, LANES - 1, 1), 0.0))
    lane = lane_iota((deep, LANES))
    tile = edges[side, pl.ds(base + 16, deep), :]
    first = jnp.where((lane == LANES - 1) & (gz == 0), pltpu.roll(tile, LANES - 1, 1), 0.0)
    last = jnp.where((lane == 0) & (gz == 1), pltpu.roll(tile, 1, 1), 0.0)
    for x in range(deep):
        add(2, x, slice(0, 1), first[x : x + 1])
        add(1, x, slice(tall - 1, tall), last[x : x + 1])


def place_kernel(new, means, corner, owners, out, spread):
    stretch = means.shape[1]
    rank = lax.axis_index("gy") * lax.axis_size("gz") + lax.axis_index("gz")
    out[...] = new[...]
    lane = lane_iota((HALF, LANES))
    for q in range(PAR):
        cx, cy, cz = corner[0, 0, q, 0], corner[0, 0, q, 1], corner[0, 0, q, 2]
        owner = owners[0, rank, q]
        start = (rank // BATCH) * 96 + lax.rem(rank, BATCH)
        for xh in range(2):
            rows = means[owner, pl.ds(start + xh * BATCH, 12, stride=8), :]
            for odd in range(2):
                for y in range(HALF):
                    shift = lax.rem(cz - y * HALF - odd * HALF * HALF + 2 * LANES, LANES)
                    spread[pl.ds((xh * 2 + odd) * 96 + y, 12, stride=8), :] = pltpu.roll(rows, shift, 1)
        inside = (lane >= cz) & (lane < cz + HALF)
        for c in range(6):
            for x in range(HALF):
                xh, k = x // 4, x % 4
                tile = spread[pl.ds((xh * 2 + k % 2) * 96 + (c * 2 + k // 2) * 8, 8), :]
                spot = out[c, cx + x, pl.ds(cy, HALF), :]
                out[c, cx + x, pl.ds(cy, HALF), :] = jnp.where(inside, tile, spot)


def local(coarse_fields, permittivity, fine_fields, fine_permittivity, patch_corner, patch_owner):
    deep, tall, cols = coarse_fields.shape[1:]
    slots = fine_fields.shape[2]
    groups = slots // BATCH
    count_x, count_y = lax.axis_size("gx"), lax.axis_size("gy")
    two_y = count_y > 2
    smem = whole(pltpu.SMEM)
    vmem = whole()
    shape = jax.ShapeDtypeStruct
    grow = grow_table()

    beside = lax.ppermute(coarse_fields, "gz", swap_pairs(2, 0))
    x_face = shape((5, tall, cols), F32)
    y_face = shape((5, deep, cols), F32)
    if two_y:
        body = faces_kernel
    else:
        body = functools.partial(faces_kernel, y_odd=None)
    faces = call(body, [x_face, x_face, y_face] + [y_face] * two_y, [vmem])(coarse_fields)
    got = [
        lax.ppermute(faces[0], "gx", swap_pairs(count_x, 0)),
        lax.ppermute(faces[1], "gx", swap_pairs(count_x, 1)),
        lax.ppermute(faces[2], "gy", swap_pairs(count_y, 0)),
    ]
    if two_y:
        got.append(lax.ppermute(faces[3], "gy", swap_pairs(count_y, 1)))

    box, rate = call(
        load_kernel,
        [shape((groups, 18, ROWS_BOX, LANES), F32), shape((groups, ROWS_BOX, WIDE), F32)],
        [vmem] * 3,
        [pltpu.VMEM((512, PF * PF), F32), pltpu.VMEM((3, 512, LANES), F32), pltpu.VMEM((ROWS_BOX, PF * PF), F32)],
        size=4_000_000,
    )(fine_fields, fine_permittivity, jnp.asarray(grow, BF16))

    full = deep + 2
    payload = PAR * 2 * ROWS_REGION + EDGE_ROWS
    new, packed = call(
        functools.partial(leap_kernel, two_y),
        [shape(coarse_fields.shape, F32), shape((payload, LANES), F32)],
        [vmem] * 3 + [smem] + [vmem] * len(got),
        [
            pltpu.VMEM((6 * full * 16, LANES), F32),
            pltpu.VMEM((6 * full * 16, LANES), F32),
            pltpu.VMEM((3 * (full - 1) * 16, 2 * LANES), F32),
            pltpu.VMEM((deep * 16, LANES), F32),
            pltpu.VMEM((6 * deep * 16, LANES), F32),
        ],
    )(coarse_fields, beside, permittivity, patch_corner, *got)
    regions = lax.all_gather(packed, ("gy", "gz"))

    box, small = call(
        fine_kernel,
        [shape((groups, 18, ROWS_BOX, LANES), F32), shape((groups * 96, LANES), F32)],
        [vmem] * 3 + [smem] + [vmem] * 2,
        [
            pltpu.VMEM((6 * ROWS_BOX, LANES), F32),
            pltpu.VMEM((6, ROWS_BOX, WIDE), F32),
            pltpu.VMEM((3, ROWS_BOX, WIDE), F32),
            pltpu.VMEM((96, 2 * WIDE), F32),
        ],
    )(regions, box, rate, patch_owner, jnp.asarray(ghost_table(), BF16), jnp.asarray(mean_table(), BF16))
    means = lax.all_gather(small, ("gy", "gz"))

    fine = call(
        store_kernel,
        shape(fine_fields.shape, F32),
        [vmem, vmem, smem, vmem],
        [pltpu.VMEM((2, 6 * ROWS_BOX, LANES), F32)],
        size=4_000_000,
    )(box, fine_fields, patch_owner, jnp.asarray(grow.T, BF16))
    new = call(fix_kernel, shape(coarse_fields.shape, F32), [vmem] * 3)(new, permittivity, regions)
    coarse = call(
        place_kernel,
        shape(coarse_fields.shape, F32),
        [vmem, vmem, smem, smem],
        [pltpu.VMEM((4 * 96, LANES), F32)],
    )(new, means, patch_corner, patch_owner)
    return coarse, fine


def solution(mesh):
    in_specs = (
        P(None, ("groups", "gx"), "gy", "gz"),
        P(("groups", "gx"), "gy", "gz"),
        P(("groups", "gx"), "gy", "gz", None, None),
        P(("groups", "gx"), "gy", "gz", None),
        P(("groups", "gx"), "gy", "gz", None),
        P(("groups", "gx"), None, None),
    )
    out_specs = (P(None, ("groups", "gx"), "gy", "gz"), P(("groups", "gx"), "gy", "gz", None, None))
    return jax.shard_map(local, mesh=mesh, in_specs=in_specs, out_specs=out_specs, check_vma=False)
```

```python
import functools
import jax
import jax.numpy as jnp
import numpy as np
from jax import lax
from jax.experimental import pallas as pl
from jax.experimental.pallas import tpu as pltpu
from jax.sharding import PartitionSpec as P

PF = 16
PAR = 2
HALF = PF // 2
RIM = HALF + 2
PLANES = 9
LINE = PF + 2
LANES = 128
WIDE = 384
BATCH = 4
ROWS_BOX = PLANES * 8
ROWS_REGION = 60
ROWS_PATCH = 128
ROWS_BESIDE = 160
X_COMPS = (0, 1, 2, 4, 5)
Y_COMPS = (0, 1, 2, 3, 5)
VMEM_BYTES = 48 * 1024 * 1024
F32 = jnp.float32
BF16 = jnp.bfloat16


def grow_table():
    table = np.zeros((PF * PF, WIDE), np.float32)
    for y in range(PF):
        for z in range(PF):
            table[y * PF + z, (y + 1) * LINE + z + 1] = 1.0
    return table


def ghost_table():
    table = np.zeros((LANES, WIDE), np.float32)
    for y in range(LINE):
        for z in range(LINE):
            table[((y + 1) // 2) * RIM + (z + 1) // 2, y * LINE + z] = 1.0
    return table


def mean_table():
    table = np.zeros((2, WIDE, LANES), np.float32)
    for odd in range(2):
        for y in range(PF):
            for z in range(PF):
                lane = odd * HALF * HALF + (y // 2) * HALF + z // 2
                table[odd, (y + 1) * LINE + z + 1, lane] = 0.125
    return table.reshape(2 * WIDE, LANES)


def move(rows, table):
    high = rows.astype(BF16)
    low = (rows - high.astype(F32)).astype(BF16)
    out = jnp.dot(high, table, preferred_element_type=F32)
    return out + jnp.dot(low, table, preferred_element_type=F32)


def lane_iota(shape):
    return lax.broadcasted_iota(jnp.int32, shape, len(shape) - 1)


def whole(memory_space=pltpu.VMEM):
    return pl.BlockSpec(memory_space=memory_space)


def call(kernel, outs, in_specs, scratch=(), flops=1_000_000, size=1_000_000, out_specs=None, **extra):
    return pl.pallas_call(
        kernel,
        out_shape=outs,
        in_specs=in_specs,
        out_specs=jax.tree.map(lambda _: whole(), outs) if out_specs is None else out_specs,
        scratch_shapes=list(scratch),
        compiler_params=pltpu.CompilerParams(vmem_limit_bytes=VMEM_BYTES),
        cost_estimate=pl.CostEstimate(flops=flops, bytes_accessed=size, transcendentals=0),
        **extra,
    )


def swap_pairs(count, first):
    pairs = []
    for i in range(first, count - 1, 2):
        pairs += [(i, i + 1), (i + 1, i)]
    return pairs


def faces_kernel(two_y, block, *refs):
    outs, sems = refs[:-1], refs[-1]
    deep, tall = block.shape[1], block.shape[2]
    gx_odd = lax.rem(lax.axis_index("gx"), 2)
    gy_odd = lax.rem(lax.axis_index("gy"), 2)
    copies = []
    for n, place in enumerate(((1 - gx_odd) * (deep - 1), gx_odd * (deep - 1))):
        for low, high, k in ((0, 3, 0), (4, 6, 3)):
            source = block.at[low:high, place]
            copies.append((source, outs[n].at[k : k + high - low]))
    for n, place in enumerate(((1 - gy_odd) * (tall - 1), gy_odd * (tall - 1))[: 1 + two_y]):
        for low, high, k in ((0, 4, 0), (5, 6, 4)):
            source = block.at[low:high, :, place]
            copies.append((source, outs[2 + n].at[k : k + high - low]))
    copies = [pltpu.make_async_copy(a, b, sems.at[i]) for i, (a, b) in enumerate(copies)]
    for copy in copies:
        copy.start()
    for copy in copies:
        copy.wait()


def leap_kernel(two_y, ranks, *refs):
    block, beside, perm, corner, owners, x_even, x_odd, y_even = refs[:8]
    y_odd = refs[8] if two_y else None
    refs = refs[8 + two_y :]
    new, sends = refs[0], refs[1 : 1 + ranks]
    pad, side, mag, rate, fresh, packed = refs[1 + ranks :]
    deep, tall = block.shape[1], block.shape[2]
    full = deep + 2
    gx_odd = lax.rem(lax.axis_index("gx"), 2)
    gy_odd = lax.rem(lax.axis_index("gy"), 2)
    gz = lax.axis_index("gz")
    pad[...] = jnp.zeros_like(pad)
    side[...] = jnp.zeros_like(side)
    rate[...] = jnp.ones_like(rate)
    lane = lane_iota((tall, LANES))
    keep = ((lane == 0) & (gz == 0)) | ((lane == LANES - 1) & (gz == 1))

    def at(c, x):
        return (c * full + x) * 16

    for x in range(deep):
        rate[pl.ds(x * 16 + 1, tall), :] = perm[x]
    for c in range(6):
        for x in range(deep):
            pad[pl.ds(at(c, x + 1) + 1, tall), :] = block[c, x]
            side[pl.ds(at(c, x + 1) + 1, tall), :] = jnp.where(keep, beside[c, x], 0.0)
    for k, c in enumerate(X_COMPS):
        even, odd = x_even[k], x_odd[k]
        pad[pl.ds(at(c, 0) + 1, tall), :] = jnp.where(gx_odd == 0, odd, even)
        if c in (1, 2):
            pad[pl.ds(at(c, full - 1) + 1, tall), :] = jnp.where(gx_odd == 0, even, odd)
    for k, c in enumerate(Y_COMPS):
        for x in range(deep):
            even = y_even[k, x : x + 1, :]
            odd = jnp.zeros_like(even) if y_odd is None else y_odd[k, x : x + 1, :]
            pad[pl.ds(at(c, x + 1), 1), :] = jnp.where(gy_odd == 0, odd, even)
            if c in (0, 2):
                pad[pl.ds(at(c, x + 1) + tall + 1, 1), :] = jnp.where(gy_odd == 0, even, odd)

    def up_y(a):
        return pltpu.roll(a, 15, 0)

    def up_z(a):
        return pltpu.roll(a, 2 * LANES - 1, 1)

    def down_y(a):
        return pltpu.roll(a, 1, 0)

    def down_z(a):
        return pltpu.roll(a, 1, 1)

    def plane(c, x):
        rows = pl.ds(at(c, x), 16)
        return jnp.concatenate([pad[rows, :], side[rows, :]], axis=1)

    def field(c, x):
        return mag[pl.ds((c * (full - 1) + x) * 16, 16), :]

    for x in range(full - 1):
        e0, e1, e2 = plane(0, x), plane(1, x), plane(2, x)
        h0 = plane(3, x) - 0.5 * ((up_y(e2) - e2) - (up_z(e1) - e1))
        h1 = plane(4, x) - 0.5 * ((up_z(e0) - e0) - (plane(2, x + 1) - e2))
        h2 = plane(5, x) - 0.5 * ((plane(1, x + 1) - e1) - (up_y(e0) - e0))
        for c, value in enumerate((h0, h1, h2)):
            mag[pl.ds((c * (full - 1) + x) * 16, 16), :] = value
    for x in range(deep):
        h0, h1, h2 = field(0, x + 1), field(1, x + 1), field(2, x + 1)
        coef = 0.5 / rate[pl.ds(x * 16, 16), :]
        c0 = ((h2 - down_y(h2)) - (h1 - down_z(h1)))[:, 0:LANES]
        c1 = ((h0 - down_z(h0)) - (h2 - field(2, x)))[:, 0:LANES]
        c2 = ((h1 - field(1, x)) - (h0 - down_y(h0)))[:, 0:LANES]
        for c, curl in enumerate((c0, c1, c2)):
            fresh[pl.ds((c * deep + x) * 16, 16), :] = plane(c, x + 1)[:, 0:LANES] + coef * curl
            fresh[pl.ds(((c + 3) * deep + x) * 16, 16), :] = (h0, h1, h2)[c][:, 0:LANES]
    for c in range(6):
        for x in range(deep):
            new[c, x] = fresh[pl.ds((c * deep + x) * 16 + 1, tall), :]
    region_lane = lane_iota((RIM, LANES))
    for q in range(PAR):
        cx, cy, cz = corner[0, 0, q, 0], corner[0, 0, q, 1], corner[0, 0, q, 2]
        for t in range(2):
            base = t * ROWS_REGION
            for c in range(6):
                total = jnp.zeros((RIM, LANES), F32)
                for j in range(RIM):
                    if t == 0:
                        rows = pad[pl.ds((c * full + cx) * 16 + cy + j, RIM, stride=16), :]
                    else:
                        rows = fresh[pl.ds((c * deep + cx - 1) * 16 + cy + j, RIM, stride=16), :]
                    shift = lax.rem(j * RIM - (cz - 1) + 2 * LANES, LANES)
                    rows = pltpu.roll(rows, shift, 1)
                    inside = (region_lane >= j * RIM) & (region_lane < (j + 1) * RIM)
                    total = jnp.where(inside, rows, total)
                packed[q, pl.ds(base + c * RIM, RIM), :] = total
    rank = lax.axis_index("gy") * lax.axis_size("gz") + gz
    for q in range(PAR):
        packed[q, 2 * ROWS_REGION : ROWS_PATCH, :] = jnp.zeros((ROWS_PATCH - 2 * ROWS_REGION, LANES), F32)
        packed[q, 2 * ROWS_REGION : 2 * ROWS_REGION + 1, :] = pad[pl.ds(at(1, full - 1) + tall, 1), :]
        packed[q, 2 * ROWS_REGION + 1 : 2 * ROWS_REGION + 2, :] = pad[pl.ds(at(0, 0) + 1, 1), :]
    for k, send in enumerate(sends):
        q = jnp.where(owners[0, rank, 0] == lax.bitwise_xor(rank, k), 0, 1)
        send[0:ROWS_PATCH, :] = packed[q]
    half = lane_iota((16, LANES)) < LANES // 2
    send = sends[1]
    send[ROWS_PATCH : ROWS_PATCH + 16, :] = jnp.where(half, plane(0, 0)[:, 0:LANES], plane(2, full - 1)[:, 0:LANES])
    low = jnp.where(gy_odd == 0, jnp.zeros_like(y_even[1]) if y_odd is None else y_odd[1], y_even[1])
    high = jnp.where(gy_odd == 0, y_even[2], jnp.zeros_like(y_even[2]) if y_odd is None else y_odd[2])
    send[ROWS_PATCH + 16 : ROWS_PATCH + 32, :] = jnp.zeros((16, LANES), F32)
    send[ROWS_PATCH + 16 : ROWS_PATCH + 16 + deep, :] = jnp.where(lane_iota((deep, LANES)) < LANES // 2, low, high)


def put(ref, g, c, m, value):
    for v in range(WIDE // LANES):
        ref[g, c * 3 + v, m * 8 : (m + 1) * 8, :] = value[:, v * LANES : (v + 1) * LANES]


def get(ref, g, c, m):
    return jnp.concatenate([ref[g, c * 3 + v, m * 8 : (m + 1) * 8, :] for v in range(WIDE // LANES)], axis=1)


def load_kernel(fine, perm, table, box, rate, lhs, wide, coefs):
    groups = fine.shape[2] // BATCH
    for g in range(groups):
        for s in range(BATCH):
            for x in range(PF):
                row = (s * PF + x) * 8
                lhs[row : row + 6, :] = fine[0, 0, g * BATCH + s, :, x * PF * PF : (x + 1) * PF * PF]
                lhs[row + 6 : row + 8, :] = jnp.zeros((2, PF * PF), F32)
        grown = move(lhs[...], table[...])
        for v in range(WIDE // LANES):
            wide[v] = grown[:, v * LANES : (v + 1) * LANES]
        zero = jnp.zeros((8, WIDE), F32)
        for c in range(6):
            put(box, g, c, 0, zero)
            put(box, g, c, PLANES - 1, zero)
            for s in range(BATCH):
                for xh in range(2):
                    source = pl.ds((s * PF + xh * 8) * 8 + c, 8, stride=8)
                    for v in range(WIDE // LANES):
                        target = pl.ds((1 - xh) * 8 + xh * BATCH + s, 8, stride=8)
                        box[g, c * 3 + v, target, :] = wide[v, source, :]
        coefs[...] = jnp.zeros_like(coefs)
        for x in range(PF):
            row = (x % 8 + (1 if x < 8 else 0)) * 8 + (0 if x < 8 else BATCH)
            cells = perm[0, 0, g * BATCH : (g + 1) * BATCH, x * PF * PF : (x + 1) * PF * PF]
            coefs[row : row + BATCH, :] = 0.5 / cells
        rate[g] = move(coefs[...], table[...])


def fine_kernel(ranks, *refs):
    regions, (box, rate, ghosts, means, out) = refs[:ranks], refs[ranks : ranks + 5]
    smalls = refs[ranks + 5 : 2 * ranks + 5]
    lhs, now, mag, halves, small = refs[2 * ranks + 5 :]
    groups = box.shape[0]
    rank = lax.axis_index("gy") * lax.axis_size("gz") + lax.axis_index("gz")
    flat = lane_iota((8, WIDE))
    yy = lax.shift_right_logical(flat * 3641, 16)
    zz = flat - yy * LINE
    inner = (yy >= 1) & (yy <= PF) & (zz >= 1) & (zz <= PF)
    upper = lax.broadcasted_iota(jnp.int32, (8, WIDE), 0) >= BATCH

    def inner_of(m):
        if m == 0:
            return inner & upper
        if m == PLANES - 1:
            return inner & jnp.logical_not(upper)
        return inner

    def up_y(a):
        return pltpu.roll(a, WIDE - LINE, 1)

    def up_z(a):
        return pltpu.roll(a, WIDE - 1, 1)

    def down_y(a):
        return pltpu.roll(a, LINE, 1)

    def down_z(a):
        return pltpu.roll(a, 1, 1)

    def rows_of(m):
        return pl.ds(m * 8, 8)

    for k, region in enumerate(regions):
        slot = lax.bitwise_xor(rank, k)
        start = (slot // BATCH) * 6 * ROWS_BOX + lax.rem(slot, BATCH)
        for c in range(6):
            old = region[c * RIM : (c + 1) * RIM, :]
            fresh = region[ROWS_REGION + c * RIM : ROWS_REGION + (c + 1) * RIM, :]
            for sub, value in enumerate((old, old + 0.5 * (fresh - old))):
                row = start + c * ROWS_BOX
                lhs[sub, pl.ds(row, 5, stride=16), :] = value[0:5]
                lhs[sub, pl.ds(row + 8, 4, stride=16), :] = value[1:5]
                lhs[sub, pl.ds(row + BATCH, 5, stride=16), :] = value[5:10]
                lhs[sub, pl.ds(row + BATCH + 8, 4, stride=16), :] = value[5:9]
    for g in range(groups):
        for sub in range(2):
            source = box if sub == 0 else out
            for c in range(6):
                ghost = move(lhs[sub, pl.ds((g * 6 + c) * ROWS_BOX, ROWS_BOX), :], ghosts[...])
                for m in range(PLANES):
                    now[c, rows_of(m), :] = jnp.where(
                        inner_of(m), get(source, g, c, m), ghost[m * 8 : (m + 1) * 8]
                    )

            def next_x(c, m):
                if m == PLANES - 1:
                    return pltpu.roll(now[c, rows_of(0), :], BATCH, 0)
                return now[c, rows_of(m + 1), :]

            def last_x(c, m):
                if m == 0:
                    return pltpu.roll(mag[c, rows_of(PLANES - 1), :], BATCH, 0)
                return mag[c, rows_of(m - 1), :]

            for m in range(PLANES):
                e0, e1, e2 = (now[c, rows_of(m), :] for c in range(3))
                h0, h1, h2 = (now[c, rows_of(m), :] for c in range(3, 6))
                mag[0, rows_of(m), :] = h0 - 0.5 * ((up_y(e2) - e2) - (up_z(e1) - e1))
                mag[1, rows_of(m), :] = h1 - 0.5 * ((up_z(e0) - e0) - (next_x(2, m) - e2))
                mag[2, rows_of(m), :] = h2 - 0.5 * ((next_x(1, m) - e1) - (up_y(e0) - e0))
            for m in range(PLANES):
                h0, h1, h2 = (mag[c, rows_of(m), :] for c in range(3))
                coef = rate[g, rows_of(m), :]
                e0, e1, e2 = (now[c, rows_of(m), :] for c in range(3))
                put(out, g, 0, m, e0 + coef * ((h2 - down_y(h2)) - (h1 - down_z(h1))))
                put(out, g, 1, m, e1 + coef * ((h0 - down_z(h0)) - (h2 - last_x(2, m))))
                put(out, g, 2, m, e2 + coef * ((h1 - last_x(1, m)) - (h0 - down_y(h0))))
                for c, value in enumerate((h0, h1, h2)):
                    put(out, g, c + 3, m, value)
        for c in range(6):
            for k in range(4):
                other = jnp.where(upper, get(out, g, c, 2 * k), get(out, g, c, 2 * k + 2))
                pair = get(out, g, c, 2 * k + 1) + other
                halves[pl.ds((c * 2 + k // 2) * 8, 8), (k % 2) * WIDE : (k % 2 + 1) * WIDE] = pair
        small[pl.ds(g * 96, 96), :] = move(halves[...], means[...])
    for k, send in enumerate(smalls):
        slot = lax.bitwise_xor(rank, k)
        start = (slot // BATCH) * 96 + lax.rem(slot, BATCH)
        for xh in range(2):
            send[xh * 12 : (xh + 1) * 12, :] = small[pl.ds(start + xh * BATCH, 12, stride=8), :]


def store_kernel(box, fine, owners, table, out, cells):
    groups = box.shape[0]
    rank = lax.axis_index("gy") * lax.axis_size("gz") + lax.axis_index("gz")
    for g in range(groups):
        for c in range(6):
            rows = jnp.concatenate([box[g, c * 3 + v] for v in range(WIDE // LANES)], axis=1)
            flat = move(rows, table[...])
            for v in range(PF * PF // LANES):
                cells[v, pl.ds(c * ROWS_BOX, ROWS_BOX), :] = flat[:, v * LANES : (v + 1) * LANES]
        for s in range(BATCH):
            slot = g * BATCH + s
            live = (owners[0, slot, 0] == rank) | (owners[0, slot, 1] == rank)
            for x in range(PF):
                row = (x % 8 + (1 if x < 8 else 0)) * 8 + (0 if x < 8 else BATCH) + s
                for v in range(PF * PF // LANES):
                    cut = slice(x * PF * PF + v * LANES, x * PF * PF + (v + 1) * LANES)
                    value = cells[v, pl.ds(row, 6, stride=ROWS_BOX), :]
                    out[0, 0, slot, :, cut] = jnp.where(live, value, fine[0, 0, slot, :, cut])


def fix_kernel(new, perm, *refs):
    edges, out = refs[:-1], refs[-1]
    deep, tall = new.shape[1], new.shape[2]
    gz = lax.axis_index("gz")
    rank = lax.axis_index("gy") * 2 + gz
    out[...] = new[...]

    def add(c, x, rows, amount):
        out[c, x, rows, :] = out[c, x, rows, :] + 0.25 / perm[x, rows, :] * amount

    lower = higher = jnp.zeros((1, LANES), F32)
    for k, edge in enumerate(edges, 1):
        row = 2 * ROWS_REGION
        lower = jnp.where(lax.bitwise_xor(rank, k) == rank - 2, edge[row : row + 1, :], lower)
        higher = jnp.where(lax.bitwise_xor(rank, k) == rank + 2, edge[row + 1 : row + 2, :], higher)
    add(0, deep - 1, slice(0, 1), lower)
    add(1, 0, slice(tall - 1, tall), higher)
    lane = lane_iota((tall, LANES))
    tile = edges[0][ROWS_PATCH + 1 : ROWS_PATCH + 1 + tall, :]
    add(0, deep - 1, slice(0, tall), jnp.where((lane == 0) & (gz == 1), pltpu.roll(tile, 1, 1), 0.0))
    add(2, 0, slice(0, tall), jnp.where((lane == LANES - 1) & (gz == 0), pltpu.roll(tile, LANES - 1, 1), 0.0))
    lane = lane_iota((deep, LANES))
    tile = edges[0][ROWS_PATCH + 16 : ROWS_PATCH + 16 + deep, :]
    first = jnp.where((lane == LANES - 1) & (gz == 0), pltpu.roll(tile, LANES - 1, 1), 0.0)
    last = jnp.where((lane == 0) & (gz == 1), pltpu.roll(tile, 1, 1), 0.0)
    for x in range(deep):
        add(2, x, slice(0, 1), first[x : x + 1])
        add(1, x, slice(tall - 1, tall), last[x : x + 1])


def place_kernel(ranks, new, corner, owners, *refs):
    means, (out, spread, stage, gathered, sems) = refs[:ranks], refs[ranks:]
    rank = lax.axis_index("gy") * lax.axis_size("gz") + lax.axis_index("gz")
    for k, mean in enumerate(means):
        gathered[k] = mean[...]
    lane = lane_iota((HALF, LANES))
    spots = [tuple(corner[0, 0, q, d] for d in range(3)) for q in range(PAR)]
    for q, (cx, cy, cz) in enumerate(spots):
        k = lax.bitwise_xor(owners[0, rank, q], rank)
        for xh in range(2):
            rows = gathered[k, xh * 12 : (xh + 1) * 12, :]
            for odd in range(2):
                for y in range(HALF):
                    shift = lax.rem(cz - y * HALF - odd * HALF * HALF + 2 * LANES, LANES)
                    spread[q, pl.ds((xh * 2 + odd) * 96 + y, 12, stride=8), :] = pltpu.roll(rows, shift, 1)
    copies = []
    for c in range(6):
        stage[c] = new[c]
        for q, (cx, cy, cz) in enumerate(spots):
            inside = (lane >= cz) & (lane < cz + HALF)
            for x in range(HALF):
                xh, k = x // 4, x % 4
                tile = spread[q, pl.ds((xh * 2 + k % 2) * 96 + (c * 2 + k // 2) * 8, 8), :]
                spot = stage[c, cx + x, pl.ds(cy, HALF), :]
                stage[c, cx + x, pl.ds(cy, HALF), :] = jnp.where(inside, tile, spot)
        copies.append(pltpu.make_async_copy(stage.at[c], out.at[c], sems.at[c]))
        copies[-1].start()
    for copy in copies:
        copy.wait()


def local(coarse_fields, permittivity, fine_fields, fine_permittivity, patch_corner, patch_owner):
    deep, tall, cols = coarse_fields.shape[1:]
    slots = fine_fields.shape[2]
    groups = slots // BATCH
    count_x, count_y = lax.axis_size("gx"), lax.axis_size("gy")
    two_y = count_y > 2
    smem = whole(pltpu.SMEM)
    vmem = whole()
    shape = jax.ShapeDtypeStruct
    grow = grow_table()

    beside = lax.ppermute(coarse_fields, "gz", swap_pairs(2, 0))
    x_face = shape((5, tall, cols), F32)
    y_face = shape((5, deep, cols), F32)
    faces = call(
        functools.partial(faces_kernel, two_y),
        [x_face, x_face, y_face] + [y_face] * two_y,
        [whole(pl.ANY)],
        [pltpu.SemaphoreType.DMA((6 + 2 * two_y,))],
    )(coarse_fields)
    got = [
        lax.ppermute(faces[0], "gx", swap_pairs(count_x, 0)),
        lax.ppermute(faces[1], "gx", swap_pairs(count_x, 1)),
        lax.ppermute(faces[2], "gy", swap_pairs(count_y, 0)),
    ]
    if two_y:
        got.append(lax.ppermute(faces[3], "gy", swap_pairs(count_y, 1)))

    box, rate = call(
        load_kernel,
        [shape((groups, 18, ROWS_BOX, LANES), F32), shape((groups, ROWS_BOX, WIDE), F32)],
        [vmem] * 3,
        [pltpu.VMEM((512, PF * PF), F32), pltpu.VMEM((3, 512, LANES), F32), pltpu.VMEM((ROWS_BOX, PF * PF), F32)],
        size=4_000_000,
    )(fine_fields, fine_permittivity, jnp.asarray(grow, BF16))

    full = deep + 2
    ranks = count_y * lax.axis_size("gz")

    def exchange(parts):
        swaps = [[(r, r ^ k) for r in range(ranks)] for k in range(ranks)]
        return [parts[0]] + [lax.ppermute(parts[k], ("gy", "gz"), swaps[k]) for k in range(1, ranks)]

    patches = [shape((ROWS_BESIDE if k == 1 else ROWS_PATCH, LANES), F32) for k in range(ranks)]
    new, *sends = call(
        functools.partial(leap_kernel, two_y, ranks),
        [shape(coarse_fields.shape, F32)] + patches,
        [vmem] * 3 + [smem] * 2 + [vmem] * len(got),
        [
            pltpu.VMEM((6 * full * 16, LANES), F32),
            pltpu.VMEM((6 * full * 16, LANES), F32),
            pltpu.VMEM((3 * (full - 1) * 16, 2 * LANES), F32),
            pltpu.VMEM((deep * 16, LANES), F32),
            pltpu.VMEM((6 * deep * 16, LANES), F32),
            pltpu.VMEM((PAR, ROWS_PATCH, LANES), F32),
        ],
    )(coarse_fields, beside, permittivity, patch_corner, patch_owner, *got)
    regions = exchange(sends)

    box, *smalls = call(
        functools.partial(fine_kernel, ranks),
        [shape((groups, 18, ROWS_BOX, LANES), F32)] + [shape((24, LANES), F32)] * ranks,
        [vmem] * (ranks + 4),
        [
            pltpu.VMEM((2, groups * 6 * ROWS_BOX, LANES), F32),
            pltpu.VMEM((6, ROWS_BOX, WIDE), F32),
            pltpu.VMEM((3, ROWS_BOX, WIDE), F32),
            pltpu.VMEM((96, 2 * WIDE), F32),
            pltpu.VMEM((groups * 96, LANES), F32),
        ],
    )(*regions, box, rate, jnp.asarray(ghost_table(), BF16), jnp.asarray(mean_table(), BF16))
    means = exchange(smalls)

    fine = call(
        store_kernel,
        shape(fine_fields.shape, F32),
        [vmem, vmem, smem, vmem],
        [pltpu.VMEM((2, 6 * ROWS_BOX, LANES), F32)],
        size=4_000_000,
    )(box, fine_fields, patch_owner, jnp.asarray(grow.T, BF16))
    new = call(fix_kernel, shape(coarse_fields.shape, F32), [vmem] * (1 + ranks))(new, permittivity, *regions[1:])
    coarse = call(
        functools.partial(place_kernel, ranks),
        shape(coarse_fields.shape, F32),
        [vmem, smem, smem] + [vmem] * ranks,
        [
            pltpu.VMEM((PAR, 4 * 96, LANES), F32),
            pltpu.VMEM(coarse_fields.shape, F32),
            pltpu.VMEM((ranks, 24, LANES), F32),
            pltpu.SemaphoreType.DMA((6,)),
        ],
        out_specs=whole(pl.ANY),
    )(new, patch_corner, patch_owner, *means)
    return coarse, fine


def solution(mesh):
    in_specs = (
        P(None, ("groups", "gx"), "gy", "gz"),
        P(("groups", "gx"), "gy", "gz"),
        P(("groups", "gx"), "gy", "gz", None, None),
        P(("groups", "gx"), "gy", "gz", None),
        P(("groups", "gx"), "gy", "gz", None),
        P(("groups", "gx"), None, None),
    )
    out_specs = (P(None, ("groups", "gx"), "gy", "gz"), P(("groups", "gx"), "gy", "gz", None, None))
    return jax.shard_map(local, mesh=mesh, in_specs=in_specs, out_specs=out_specs, check_vma=False)
```

```python
import functools
import jax
import jax.numpy as jnp
import numpy as np
from jax import lax
from jax.experimental import pallas as pl
from jax.experimental.pallas import tpu as pltpu
from jax.sharding import PartitionSpec as P

PF = 16
PAR = 2
HALF = PF // 2
RIM = HALF + 2
PLANES = 9
LINE = PF + 2
LANES = 128
WIDE = 384
BATCH = 4
ROWS_BOX = PLANES * 8
ROWS_RIM = 48
ROW_EDGE = 64
ROWS_PATCH = 72
ROWS_BESIDE = 104
X_COMPS = (0, 1, 2, 4, 5)
Y_COMPS = (0, 1, 2, 3, 5)
VMEM_BYTES = 48 * 1024 * 1024
F32 = jnp.float32
BF16 = jnp.bfloat16


def rim_lane(time, j, k):
    if 0 < j < RIM - 1:
        return j * RIM + k + 3 * time
    if j == 0 and time == 0:
        return k
    return (RIM - 1) * RIM + 3 + (2 * time + j // (RIM - 1) - 1) * RIM + k


def grow_table():
    table = np.zeros((PF * PF, WIDE), np.float32)
    for y in range(PF):
        for z in range(PF):
            table[y * PF + z, (y + 1) * LINE + z + 1] = 1.0
    return table


def ghost_table():
    table = np.zeros((2, 2 * LANES, WIDE), np.float32)
    for y in range(LINE):
        for z in range(LINE):
            j, k, lane = (y + 1) // 2, (z + 1) // 2, y * LINE + z
            table[:, LANES + j * RIM + k, lane] = 1.0
            if y in (0, LINE - 1) or z in (0, LINE - 1):
                table[0, rim_lane(0, j, k), lane] = 1.0
                table[1, rim_lane(0, j, k), lane] = 0.5
                table[1, rim_lane(1, j, k), lane] = 0.5
    return table


def mean_table():
    table = np.zeros((2, WIDE, LANES), np.float32)
    for odd in range(2):
        for y in range(PF):
            for z in range(PF):
                lane = odd * HALF * HALF + (y // 2) * HALF + z // 2
                table[odd, (y + 1) * LINE + z + 1, lane] = 0.125
    return table.reshape(2 * WIDE, LANES)


def move(rows, table):
    high = rows.astype(BF16)
    low = (rows - high.astype(F32)).astype(BF16)
    out = jnp.dot(high, table, preferred_element_type=F32)
    return out + jnp.dot(low, table, preferred_element_type=F32)


def lane_iota(shape):
    return lax.broadcasted_iota(jnp.int32, shape, len(shape) - 1)


def whole(memory_space=pltpu.VMEM):
    return pl.BlockSpec(memory_space=memory_space)


def call(kernel, outs, in_specs, scratch=(), flops=1_000_000, size=1_000_000, out_specs=None, **extra):
    return pl.pallas_call(
        kernel,
        out_shape=outs,
        in_specs=in_specs,
        out_specs=jax.tree.map(lambda _: whole(), outs) if out_specs is None else out_specs,
        scratch_shapes=list(scratch),
        compiler_params=pltpu.CompilerParams(vmem_limit_bytes=VMEM_BYTES),
        cost_estimate=pl.CostEstimate(flops=flops, bytes_accessed=size, transcendentals=0),
        **extra,
    )


def swap_pairs(count, first):
    pairs = []
    for i in range(first, count - 1, 2):
        pairs += [(i, i + 1), (i + 1, i)]
    return pairs


def faces_kernel(two_y, block, *refs):
    outs, sems = refs[:-1], refs[-1]
    deep, tall = block.shape[1], block.shape[2]
    gx_odd = lax.rem(lax.axis_index("gx"), 2)
    gy_odd = lax.rem(lax.axis_index("gy"), 2)
    copies = []
    for n, place in enumerate(((1 - gx_odd) * (deep - 1), gx_odd * (deep - 1))):
        for low, high, k in ((0, 3, 0), (4, 6, 3)):
            source = block.at[low:high, place]
            copies.append((source, outs[n].at[k : k + high - low]))
    for n, place in enumerate(((1 - gy_odd) * (tall - 1), gy_odd * (tall - 1))[: 1 + two_y]):
        for low, high, k in ((0, 4, 0), (5, 6, 4)):
            source = block.at[low:high, :, place]
            copies.append((source, outs[2 + n].at[k : k + high - low]))
    copies = [pltpu.make_async_copy(a, b, sems.at[i]) for i, (a, b) in enumerate(copies)]
    for copy in copies:
        copy.start()
    for copy in copies:
        copy.wait()


def leap_kernel(two_y, ranks, *refs):
    block, beside, perm, corner, owners, ahead, x_even, x_odd, y_even = refs[:9]
    y_odd = refs[9] if two_y else None
    refs = refs[9 + two_y :]
    new, sends = refs[0], refs[1 : 1 + ranks]
    pad, side, mag, rate, fresh, packed, sem = refs[1 + ranks :]
    deep, tall = block.shape[1], block.shape[2]
    full = deep + 2
    fetch = pltpu.make_async_copy(perm, rate, sem)
    fetch.start()
    gx_odd = lax.rem(lax.axis_index("gx"), 2)
    gy_odd = lax.rem(lax.axis_index("gy"), 2)
    gz = lax.axis_index("gz")
    rank = lax.axis_index("gy") * lax.axis_size("gz") + gz
    lane = lane_iota((tall, LANES))
    keep = ((lane == 0) & (gz == 0)) | ((lane == LANES - 1) & (gz == 1))
    lane = lane_iota((16, LANES))
    none = jnp.zeros((16, LANES), F32)

    def at(c, x):
        return (c * full + x) * 16

    for c in range(6):
        for x in (0, full - 1):
            pad[pl.ds(at(c, x), 16), :] = none
        for x in range(deep):
            pad[pl.ds(at(c, x + 1), tall), :] = block[c, x]
        pad[pl.ds(at(c, 1) + tall, deep, stride=16), :] = none[0:deep]
        pad[pl.ds(at(c, 1) + 15, deep, stride=16), :] = none[0:deep]
    for c in range(5):
        for x in (0, full - 1):
            side[pl.ds(at(c, x), 16), :] = none
        for x in range(deep):
            side[pl.ds(at(c, x + 1), 16), :] = none
            side[pl.ds(at(c, x + 1), tall), :] = jnp.where(keep, beside[c, x], 0.0)
    for k, c in enumerate(X_COMPS):
        even, odd = x_even[k], x_odd[k]
        pad[pl.ds(at(c, 0), tall), :] = jnp.where(gx_odd == 0, odd, even)
        if c in (1, 2):
            pad[pl.ds(at(c, full - 1), tall), :] = jnp.where(gx_odd == 0, even, odd)
    for k, c in enumerate(Y_COMPS):
        even = y_even[k]
        odd = jnp.zeros_like(even) if y_odd is None else y_odd[k]
        pad[pl.ds(at(c, 1) + 15, deep, stride=16), :] = jnp.where(gy_odd == 0, odd, even)
        if c in (0, 2):
            pad[pl.ds(at(c, 1) + tall, deep, stride=16), :] = jnp.where(gy_odd == 0, even, odd)

    def up_y(a):
        return pltpu.roll(a, 15, 0)

    def down_y(a):
        return pltpu.roll(a, 1, 0)

    def plane(c, x):
        return pad[pl.ds(at(c, x), 16), :]

    def edge(c, x):
        return side[pl.ds(at(c, x), 16), :]

    def field(c, x):
        return mag[pl.ds((c * (full - 1) + x) * 16, 16), :]

    for x in range(full - 1):
        e0, e1, e2 = plane(0, x), plane(1, x), plane(2, x)
        s0, s1, s2 = edge(0, x), edge(1, x), edge(2, x)
        r0, r1 = pltpu.roll(e0, LANES - 1, 1), pltpu.roll(e1, LANES - 1, 1)
        u0 = jnp.where(lane == LANES - 1, pltpu.roll(s0, LANES - 1, 1), r0)
        u1 = jnp.where(lane == LANES - 1, pltpu.roll(s1, LANES - 1, 1), r1)
        h0 = plane(3, x) - 0.5 * ((up_y(e2) - e2) - (u1 - e1))
        h1 = plane(4, x) - 0.5 * ((u0 - e0) - (plane(2, x + 1) - e2))
        h2 = plane(5, x) - 0.5 * ((plane(1, x + 1) - e1) - (up_y(e0) - e0))
        t0 = edge(3, x) - 0.5 * ((up_y(s2) - s2) - (r1 - s1))
        t1 = edge(4, x) - 0.5 * ((r0 - s0) - (edge(2, x + 1) - s2))
        d0 = pltpu.roll(jnp.where(lane == LANES - 1, t0, h0), 1, 1)
        d1 = pltpu.roll(jnp.where(lane == LANES - 1, t1, h1), 1, 1)
        for c, value in enumerate((h0, h1, h2, d0, d1)):
            mag[pl.ds((c * (full - 1) + x) * 16, 16), :] = value
    fetch.wait()
    for x in range(deep):
        h0, h1, h2, d0, d1 = (field(c, x + 1) for c in range(5))
        coef = 0.5 / rate[x]
        c0 = (h2 - down_y(h2)) - (h1 - d1)
        c1 = (h0 - d0) - (h2 - field(2, x))
        c2 = (h1 - field(1, x)) - (h0 - down_y(h0))
        for c, curl in enumerate((c0, c1, c2)):
            value = plane(c, x + 1)[0:tall] + coef * curl[0:tall]
            new[c, x] = value
            new[c + 3, x] = (h0, h1, h2)[c][0:tall]
            fresh[pl.ds((c * deep + x) * 16, tall), :] = value
            fresh[pl.ds(((c + 3) * deep + x) * 16, tall), :] = (h0, h1, h2)[c][0:tall]
    lane = lane_iota((8, LANES))
    for q in range(PAR):
        cx, cy, cz = corner[0, 0, q, 0], corner[0, 0, q, 1], corner[0, 0, q, 2]

        def rows_of(time, c, k, j, count, over_c):
            source, depth, start = (pad, full, cx) if time == 0 else (fresh, deep, cx - 1)
            step = depth * 16 if over_c else 16
            return source[pl.ds((c * depth + start + k) * 16 + cy + (j - 1), count, stride=step), :]

        def aim(rows, target):
            return pltpu.roll(rows, lax.rem(target - (cz - 1) + 2 * LANES, LANES), 1)

        for c in range(6):
            total = jnp.zeros((8, LANES), F32)
            for j in range(RIM):
                if (j == 0 and c == 4) or (j == RIM - 1 and c not in (0, 2)) or (0 < j < RIM - 1 and c == 5):
                    continue
                for time in range(2):
                    first = rim_lane(time, j, 0)
                    rows = aim(rows_of(time, c, 1, j, 8, False), first)
                    if j in (0, RIM - 1):
                        inside = (lane >= first) & (lane < first + RIM)
                    else:
                        inside = (lane == first) | (lane == first + RIM - 1)
                    total = jnp.where(inside, rows, total)
            packed[q, c * 8 : c * 8 + 8, :] = total
        for time in range(2):
            low = jnp.zeros((6, LANES), F32)
            high = jnp.zeros((2, LANES), F32)
            for j in range(RIM):
                first = j * RIM
                inside = (lane >= first) & (lane < first + RIM)
                low = jnp.where(inside[0:6], aim(rows_of(time, 0, 0, j, 6, True), first), low)
                high = jnp.where(inside[0:2], aim(rows_of(time, 1, RIM - 1, j, 2, True), first), high)
            base = ROWS_RIM + time * 8
            packed[q, base : base + 6, :] = low
            packed[q, base + 6 : base + 8, :] = high
        packed[q, ROW_EDGE:ROWS_PATCH, :] = jnp.zeros((ROWS_PATCH - ROW_EDGE, LANES), F32)
        packed[q, ROW_EDGE : ROW_EDGE + 1, :] = pad[pl.ds(at(1, full - 1) + tall - 1, 1), :]
        packed[q, ROW_EDGE + 1 : ROW_EDGE + 2, :] = pad[pl.ds(at(0, 0), 1), :]
    for k, send in enumerate(sends):
        q = jnp.where(owners[0, 0, rank] == lax.bitwise_xor(rank, k), 0, 1)
        send[0:ROWS_PATCH, :] = packed[q]
    half = lane_iota((16, LANES)) < LANES // 2
    send = sends[1]
    send[ROWS_PATCH : ROWS_PATCH + 16, :] = jnp.where(half, plane(0, 0), plane(2, full - 1))
    low = jnp.where(gy_odd == 0, jnp.zeros_like(y_even[1]) if y_odd is None else y_odd[1], y_even[1])
    high = jnp.where(gy_odd == 0, y_even[2], jnp.zeros_like(y_even[2]) if y_odd is None else y_odd[2])
    send[ROWS_PATCH + 16 : ROWS_PATCH + 32, :] = jnp.zeros((16, LANES), F32)
    send[ROWS_PATCH + 16 : ROWS_PATCH + 16 + deep, :] = jnp.where(half[0:deep], low, high)


def places():
    for x in range(PF):
        yield x, (x % 8 + 1) * 8 if x < 8 else (x % 8) * 8 + BATCH


def load_kernel(fine, perm, table, box, rate, lhs, coefs):
    groups = fine.shape[3] // BATCH
    blank = jnp.zeros((8, PF * PF), F32)
    for g in range(groups):
        slots = slice(g * BATCH, (g + 1) * BATCH)
        for c in range(6):
            for row in (0, ROWS_BOX - 8):
                lhs[c * ROWS_BOX + row : c * ROWS_BOX + row + 8, :] = blank
            for x, row in places():
                row += c * ROWS_BOX
                lhs[row : row + BATCH, :] = fine[0, 0, c, slots, x * PF * PF : (x + 1) * PF * PF]
            grown = move(lhs[c * ROWS_BOX : (c + 1) * ROWS_BOX, :], table[...])
            box[g, c] = grown
        for row in (0, ROWS_BOX - 8):
            coefs[row : row + 8, :] = blank
        for x, row in places():
            coefs[row : row + BATCH, :] = 0.5 / perm[0, 0, slots, x * PF * PF : (x + 1) * PF * PF]
        rate[g] = move(coefs[...], table[...])


def fine_kernel(ranks, *refs):
    regions, (box, rate, ghosts, means, out) = refs[:ranks], refs[ranks : ranks + 5]
    smalls = refs[ranks + 5 : 2 * ranks + 5]
    rims, walls, now, mag, halves, small = refs[2 * ranks + 5 :]
    groups = box.shape[0]
    rank = lax.axis_index("gy") * lax.axis_size("gz") + lax.axis_index("gz")
    flat = lane_iota((8, WIDE))
    yy = lax.shift_right_logical(flat * 3641, 16)
    zz = flat - yy * LINE
    inner = (yy >= 1) & (yy <= PF) & (zz >= 1) & (zz <= PF)
    upper = lax.broadcasted_iota(jnp.int32, (8, WIDE), 0) >= BATCH

    def inner_of(m):
        if m == 0:
            return inner & upper
        if m == PLANES - 1:
            return inner & jnp.logical_not(upper)
        return inner

    def up_y(a):
        return pltpu.roll(a, WIDE - LINE, 1)

    def up_z(a):
        return pltpu.roll(a, WIDE - 1, 1)

    def down_y(a):
        return pltpu.roll(a, LINE, 1)

    def down_z(a):
        return pltpu.roll(a, 1, 1)

    def rows_of(m):
        return pl.ds(m * 8, 8)

    blank = jnp.zeros((8, LANES), F32)
    for g in range(groups):
        for c in range(6):
            for m in range(PLANES):
                row = ((g * 6 + c) * PLANES + m) * 8
                if m in (0, PLANES - 1):
                    rims[row : row + 8, :] = blank
                walls[0, row : row + 8, :] = blank
                walls[1, row : row + 8, :] = blank
    for k, region in enumerate(regions):
        slot = lax.bitwise_xor(rank, k)
        start = (slot // BATCH) * 6 * ROWS_BOX + lax.rem(slot, BATCH)
        for c in range(6):
            rows = region[c * 8 : c * 8 + 8, :]
            row = start + c * ROWS_BOX
            rims[pl.ds(row + 8, 4, stride=16), :] = rows[0:4]
            rims[pl.ds(row + 16, 4, stride=16), :] = rows[0:4]
            rims[pl.ds(row + BATCH, 4, stride=16), :] = rows[4:8]
            rims[pl.ds(row + BATCH + 8, 4, stride=16), :] = rows[4:8]
        old = region[ROWS_RIM : ROWS_RIM + 8, :]
        fresh = region[ROWS_RIM + 8 : ROWS_RIM + 16, :]
        for sub, value in enumerate((old, old + 0.5 * (fresh - old))):
            walls[sub, pl.ds(start, 6, stride=ROWS_BOX), :] = value[0:6]
            last = start + ROWS_BOX + (PLANES - 1) * 8 + BATCH
            walls[sub, pl.ds(last, 2, stride=ROWS_BOX), :] = value[6:8]
    for g in range(groups):
        for sub in range(2):
            source = box if sub == 0 else out
            for c in range(6):
                rows = pl.ds((g * 6 + c) * ROWS_BOX, ROWS_BOX)
                ghost = move(jnp.concatenate([rims[rows, :], walls[sub, rows, :]], axis=1), ghosts[sub])
                for m in range(PLANES):
                    now[c, rows_of(m), :] = jnp.where(
                        inner_of(m), source[g, c, rows_of(m), :], ghost[m * 8 : (m + 1) * 8]
                    )

            def next_x(c, m):
                if m == PLANES - 1:
                    return pltpu.roll(now[c, rows_of(0), :], BATCH, 0)
                return now[c, rows_of(m + 1), :]

            def last_x(c, m):
                if m == 0:
                    return pltpu.roll(mag[c, rows_of(PLANES - 1), :], BATCH, 0)
                return mag[c, rows_of(m - 1), :]

            for m in range(PLANES):
                e0, e1, e2 = (now[c, rows_of(m), :] for c in range(3))
                h0, h1, h2 = (now[c, rows_of(m), :] for c in range(3, 6))
                mag[0, rows_of(m), :] = h0 - 0.5 * ((up_y(e2) - e2) - (up_z(e1) - e1))
                mag[1, rows_of(m), :] = h1 - 0.5 * ((up_z(e0) - e0) - (next_x(2, m) - e2))
                mag[2, rows_of(m), :] = h2 - 0.5 * ((next_x(1, m) - e1) - (up_y(e0) - e0))
            for m in range(PLANES):
                h0, h1, h2 = (mag[c, rows_of(m), :] for c in range(3))
                coef = rate[g, rows_of(m), :]
                e0, e1, e2 = (now[c, rows_of(m), :] for c in range(3))
                out[g, 0, rows_of(m), :] = e0 + coef * ((h2 - down_y(h2)) - (h1 - down_z(h1)))
                out[g, 1, rows_of(m), :] = e1 + coef * ((h0 - down_z(h0)) - (h2 - last_x(2, m)))
                out[g, 2, rows_of(m), :] = e2 + coef * ((h1 - last_x(1, m)) - (h0 - down_y(h0)))
                for c, value in enumerate((h0, h1, h2)):
                    out[g, c + 3, rows_of(m), :] = value
        for c in range(6):
            for k in range(4):
                other = jnp.where(upper, out[g, c, rows_of(2 * k), :], out[g, c, rows_of(2 * k + 2), :])
                pair = out[g, c, rows_of(2 * k + 1), :] + other
                halves[pl.ds((c * 2 + k // 2) * 8, 8), (k % 2) * WIDE : (k % 2 + 1) * WIDE] = pair
        small[pl.ds(g * 96, 96), :] = move(halves[...], means[...])
    for k, send in enumerate(smalls):
        slot = lax.bitwise_xor(rank, k)
        start = (slot // BATCH) * 96 + lax.rem(slot, BATCH)
        for xh in range(2):
            send[xh * 12 : (xh + 1) * 12, :] = small[pl.ds(start + xh * BATCH, 12, stride=8), :]


def store_kernel(box, fine, owners, table, out, stage, sems):
    groups = box.shape[0]
    slots = groups * BATCH
    rank = lax.axis_index("gy") * lax.axis_size("gz") + lax.axis_index("gz")
    slot = lax.broadcasted_iota(jnp.int32, (slots, PF * PF), 0)
    live = slot < 0
    for s in range(slots):
        live = live | ((slot == s) & ((owners[0, 0, s] == rank) | (owners[0, 1, s] == rank)))
    copies = []
    for c in range(6):
        flats = [move(box[g, c], table[...]) for g in range(groups)]
        for x, row in places():
            cut = slice(x * PF * PF, (x + 1) * PF * PF)
            for g, flat in enumerate(flats):
                some = slice(g * BATCH, (g + 1) * BATCH)
                stage[0, 0, c, some, cut] = jnp.where(live[some], flat[row : row + BATCH], fine[0, 0, c, some, cut])
        copies.append(pltpu.make_async_copy(stage.at[:, :, c], out.at[:, :, c], sems.at[c]))
        copies[-1].start()
    for copy in copies:
        copy.wait()


def fix_kernel(new, perm, *refs):
    edges, out = refs[:-1], refs[-1]
    deep, tall = new.shape[1], new.shape[2]
    gz = lax.axis_index("gz")
    rank = lax.axis_index("gy") * 2 + gz
    out[...] = new[...]

    def add(c, x, rows, amount):
        out[c, x, rows, :] = out[c, x, rows, :] + 0.25 / perm[x, rows, :] * amount

    lower = higher = jnp.zeros((1, LANES), F32)
    for k, edge in enumerate(edges, 1):
        row = ROW_EDGE
        lower = jnp.where(lax.bitwise_xor(rank, k) == rank - 2, edge[row : row + 1, :], lower)
        higher = jnp.where(lax.bitwise_xor(rank, k) == rank + 2, edge[row + 1 : row + 2, :], higher)
    add(0, deep - 1, slice(0, 1), lower)
    add(1, 0, slice(tall - 1, tall), higher)
    lane = lane_iota((tall, LANES))
    tile = edges[0][ROWS_PATCH : ROWS_PATCH + tall, :]
    add(0, deep - 1, slice(0, tall), jnp.where((lane == 0) & (gz == 1), pltpu.roll(tile, 1, 1), 0.0))
    add(2, 0, slice(0, tall), jnp.where((lane == LANES - 1) & (gz == 0), pltpu.roll(tile, LANES - 1, 1), 0.0))
    lane = lane_iota((deep, LANES))
    tile = edges[0][ROWS_PATCH + 16 : ROWS_PATCH + 16 + deep, :]
    first = jnp.where((lane == LANES - 1) & (gz == 0), pltpu.roll(tile, LANES - 1, 1), 0.0)
    last = jnp.where((lane == 0) & (gz == 1), pltpu.roll(tile, 1, 1), 0.0)
    for x in range(deep):
        add(2, x, slice(0, 1), first[x : x + 1])
        add(1, x, slice(tall - 1, tall), last[x : x + 1])


def place_kernel(ranks, new, corner, owners, *refs):
    means, (out, spread, stage, gathered, sems) = refs[:ranks], refs[ranks:]
    rank = lax.axis_index("gy") * lax.axis_size("gz") + lax.axis_index("gz")
    for k, mean in enumerate(means):
        gathered[k] = mean[...]
    lane = lane_iota((HALF, LANES))
    spots = [tuple(corner[0, 0, q, d] for d in range(3)) for q in range(PAR)]
    for q, (cx, cy, cz) in enumerate(spots):
        k = lax.bitwise_xor(owners[0, q, rank], rank)
        rows = gathered[k]
        for odd in range(2):
            for y in range(HALF):
                shift = lax.rem(cz - y * HALF - odd * HALF * HALF + 2 * LANES, LANES)
                spread[q, pl.ds(odd * 192 + y, 24, stride=8), :] = pltpu.roll(rows, shift, 1)
    copies = []
    for c in range(6):
        stage[c] = new[c]
        for q, (cx, cy, cz) in enumerate(spots):
            inside = (lane >= cz) & (lane < cz + HALF)
            for x in range(HALF):
                xh, k = x // 4, x % 4
                tile = spread[q, pl.ds((k % 2) * 192 + (xh * 12 + c * 2 + k // 2) * 8, 8), :]
                spot = stage[c, cx + x, pl.ds(cy, HALF), :]
                stage[c, cx + x, pl.ds(cy, HALF), :] = jnp.where(inside, tile, spot)
        copies.append(pltpu.make_async_copy(stage.at[c], out.at[c], sems.at[c]))
        copies[-1].start()
    for copy in copies:
        copy.wait()


def local(coarse_fields, permittivity, fine_fields, fine_permittivity, patch_corner, patch_owner):
    deep, tall, cols = coarse_fields.shape[1:]
    slots = fine_fields.shape[2]
    groups = slots // BATCH
    count_x, count_y = lax.axis_size("gx"), lax.axis_size("gy")
    two_y = count_y > 2
    smem = whole(pltpu.SMEM)
    vmem = whole()
    shape = jax.ShapeDtypeStruct
    grow = grow_table()

    beside = lax.ppermute(coarse_fields, "gz", swap_pairs(2, 0))
    x_face = shape((5, tall, cols), F32)
    y_face = shape((5, deep, cols), F32)
    faces = call(
        functools.partial(faces_kernel, two_y),
        [x_face, x_face, y_face] + [y_face] * two_y,
        [whole(pltpu.HBM)],
        [pltpu.SemaphoreType.DMA((6 + 2 * two_y,))],
    )(coarse_fields)
    got = [
        lax.ppermute(faces[0], "gx", swap_pairs(count_x, 0)),
        lax.ppermute(faces[1], "gx", swap_pairs(count_x, 1)),
        lax.ppermute(faces[2], "gy", swap_pairs(count_y, 0)),
    ]
    if two_y:
        got.append(lax.ppermute(faces[3], "gy", swap_pairs(count_y, 1)))

    fine = fine_fields.transpose(0, 1, 3, 2, 4)
    owners = patch_owner.transpose(0, 2, 1)
    box, rate = call(
        load_kernel,
        [shape((groups, 6, ROWS_BOX, WIDE), F32), shape((groups, ROWS_BOX, WIDE), F32)],
        [vmem] * 3,
        [pltpu.VMEM((6 * ROWS_BOX, PF * PF), F32), pltpu.VMEM((ROWS_BOX, PF * PF), F32)],
        size=4_000_000,
    )(fine, fine_permittivity, jnp.asarray(grow, BF16))

    full = deep + 2
    ranks = count_y * lax.axis_size("gz")

    def exchange(parts):
        swaps = [[(r, r ^ k) for r in range(ranks)] for k in range(ranks)]
        return [parts[0]] + [lax.ppermute(parts[k], ("gy", "gz"), swaps[k]) for k in range(1, ranks)]

    patches = [shape((ROWS_BESIDE if k == 1 else ROWS_PATCH, LANES), F32) for k in range(ranks)]
    new, *sends = call(
        functools.partial(leap_kernel, two_y, ranks),
        [shape(coarse_fields.shape, F32)] + patches,
        [vmem, vmem, whole(pltpu.HBM), smem, smem, whole(pl.ANY)] + [vmem] * len(got),
        [
            pltpu.VMEM((6 * full * 16, LANES), F32),
            pltpu.VMEM((6 * full * 16, LANES), F32),
            pltpu.VMEM((5 * (full - 1) * 16, LANES), F32),
            pltpu.VMEM(permittivity.shape, F32),
            pltpu.VMEM((6 * deep * 16, LANES), F32),
            pltpu.VMEM((PAR, ROWS_PATCH, LANES), F32),
            pltpu.SemaphoreType.DMA,
        ],
    )(coarse_fields, beside, permittivity, patch_corner, owners, rate, *got)
    regions = exchange(sends)

    box, *smalls = call(
        functools.partial(fine_kernel, ranks),
        [shape((groups, 6, ROWS_BOX, WIDE), F32)] + [shape((24, LANES), F32)] * ranks,
        [vmem] * (ranks + 4),
        [
            pltpu.VMEM((groups * 6 * ROWS_BOX, LANES), F32),
            pltpu.VMEM((2, groups * 6 * ROWS_BOX, LANES), F32),
            pltpu.VMEM((6, ROWS_BOX, WIDE), F32),
            pltpu.VMEM((3, ROWS_BOX, WIDE), F32),
            pltpu.VMEM((96, 2 * WIDE), F32),
            pltpu.VMEM((groups * 96, LANES), F32),
        ],
    )(*regions, box, rate, jnp.asarray(ghost_table(), BF16), jnp.asarray(mean_table(), BF16))
    means = exchange(smalls)

    fine = call(
        store_kernel,
        shape(fine.shape, F32),
        [vmem, vmem, smem, vmem],
        [pltpu.VMEM(fine.shape, F32), pltpu.SemaphoreType.DMA((6,))],
        size=4_000_000,
        out_specs=whole(pltpu.HBM),
    )(box, fine, owners, jnp.asarray(grow.T, BF16))
    new = call(fix_kernel, shape(coarse_fields.shape, F32), [vmem] * (1 + ranks))(new, permittivity, *regions[1:])
    coarse = call(
        functools.partial(place_kernel, ranks),
        shape(coarse_fields.shape, F32),
        [vmem, smem, smem] + [vmem] * ranks,
        [
            pltpu.VMEM((PAR, 4 * 96, LANES), F32),
            pltpu.VMEM(coarse_fields.shape, F32),
            pltpu.VMEM((ranks, 24, LANES), F32),
            pltpu.SemaphoreType.DMA((6,)),
        ],
        out_specs=whole(pltpu.HBM),
    )(new, patch_corner, owners, *means)
    return coarse, fine.transpose(0, 1, 3, 2, 4)


def solution(mesh):
    in_specs = (
        P(None, ("groups", "gx"), "gy", "gz"),
        P(("groups", "gx"), "gy", "gz"),
        P(("groups", "gx"), "gy", "gz", None, None),
        P(("groups", "gx"), "gy", "gz", None),
        P(("groups", "gx"), "gy", "gz", None),
        P(("groups", "gx"), None, None),
    )
    out_specs = (P(None, ("groups", "gx"), "gy", "gz"), P(("groups", "gx"), "gy", "gz", None, None))
    return jax.shard_map(local, mesh=mesh, in_specs=in_specs, out_specs=out_specs, check_vma=False)
```

```python
import functools
import jax
import jax.numpy as jnp
import numpy as np
from jax import lax
from jax.experimental import pallas as pl
from jax.experimental.pallas import tpu as pltpu
from jax.sharding import PartitionSpec as P

PF = 16
PAR = 2
HALF = PF // 2
RIM = HALF + 2
PLANES = 9
LINE = PF + 2
LANES = 128
WIDE = 384
BATCH = 4
ROWS_BOX = PLANES * 8
ROWS_RIM = 48
ROW_EDGE = 64
ROWS_PATCH = 72
ROWS_BESIDE = 104
X_COMPS = (0, 1, 2, 4, 5)
Y_COMPS = (0, 1, 2, 3, 5)
VMEM_BYTES = 48 * 1024 * 1024
F32 = jnp.float32
BF16 = jnp.bfloat16


def rim_lane(time, j, k):
    if 0 < j < RIM - 1:
        return j * RIM + k + 3 * time
    if j == 0 and time == 0:
        return k
    return (RIM - 1) * RIM + 3 + (2 * time + j // (RIM - 1) - 1) * RIM + k


def grow_table():
    table = np.zeros((PF * PF, WIDE), np.float32)
    for y in range(PF):
        for z in range(PF):
            table[y * PF + z, (y + 1) * LINE + z + 1] = 1.0
    return table


def ghost_table():
    table = np.zeros((2, 2 * LANES, WIDE), np.float32)
    for y in range(LINE):
        for z in range(LINE):
            j, k, lane = (y + 1) // 2, (z + 1) // 2, y * LINE + z
            table[:, LANES + j * RIM + k, lane] = 1.0
            if y in (0, LINE - 1) or z in (0, LINE - 1):
                table[0, rim_lane(0, j, k), lane] = 1.0
                table[1, rim_lane(0, j, k), lane] = 0.5
                table[1, rim_lane(1, j, k), lane] = 0.5
    return table


def mean_table():
    table = np.zeros((2, WIDE, LANES), np.float32)
    for odd in range(2):
        for y in range(PF):
            for z in range(PF):
                lane = odd * HALF * HALF + (y // 2) * HALF + z // 2
                table[odd, (y + 1) * LINE + z + 1, lane] = 0.125
    return table.reshape(2 * WIDE, LANES)


def move(rows, table):
    high = rows.astype(BF16)
    low = (rows - high.astype(F32)).astype(BF16)
    out = jnp.dot(high, table, preferred_element_type=F32)
    return out + jnp.dot(low, table, preferred_element_type=F32)


def lane_iota(shape):
    return lax.broadcasted_iota(jnp.int32, shape, len(shape) - 1)


def whole(memory_space=pltpu.VMEM):
    return pl.BlockSpec(memory_space=memory_space)


def call(kernel, outs, in_specs, scratch=(), flops=1_000_000, size=1_000_000, out_specs=None, **extra):
    return pl.pallas_call(
        kernel,
        out_shape=outs,
        in_specs=in_specs,
        out_specs=jax.tree.map(lambda _: whole(), outs) if out_specs is None else out_specs,
        scratch_shapes=list(scratch),
        compiler_params=pltpu.CompilerParams(vmem_limit_bytes=VMEM_BYTES),
        cost_estimate=pl.CostEstimate(flops=flops, bytes_accessed=size, transcendentals=0),
        **extra,
    )


def swap_pairs(count, first):
    pairs = []
    for i in range(first, count - 1, 2):
        pairs += [(i, i + 1), (i + 1, i)]
    return pairs


def faces_kernel(two_y, block, perm, kept, coef, x_even, x_odd, y_even, *y_odd):
    deep, tall = block.shape[1], block.shape[2]
    gx_odd = lax.rem(lax.axis_index("gx"), 2)
    gy_odd = lax.rem(lax.axis_index("gy"), 2)
    for k, c in enumerate(X_COMPS):
        x_even[k] = block[c, (1 - gx_odd) * (deep - 1)]
        x_odd[k] = block[c, gx_odd * (deep - 1)]
    for k, c in enumerate(Y_COMPS):
        for x in range(deep):
            first = block[c, x, 0:1, :]
            last = block[c, x, tall - 1 : tall, :]
            y_even[k, x : x + 1, :] = jnp.where(gy_odd == 0, last, first)
            if two_y:
                y_odd[0][k, x : x + 1, :] = jnp.where(gy_odd == 0, first, last)
    kept[...] = block[...]
    coef[...] = 0.5 / perm[...]


def notes_kernel(corner, owners, notes):
    rank = lax.axis_index("gy") * lax.axis_size("gz") + lax.axis_index("gz")

    def note(row, value):
        notes[row : row + 1, :] = jnp.full((1, LANES), value, jnp.int32)

    for q in range(PAR):
        for d in range(3):
            note(q * 4 + d, corner[0, 0, q, d])
        note(q * 4 + 3, lax.bitwise_xor(owners[0, q, rank], rank))
    for slot in range(notes.shape[0] - 8):
        live = (owners[0, 0, slot] == rank) | (owners[0, 1, slot] == rank)
        note(8 + slot, live.astype(jnp.int32))


def leap_kernel(two_y, ranks, *refs):
    block, beside, rate, notes, x_even, x_odd, y_even = refs[:7]
    y_odd = refs[7] if two_y else None
    refs = refs[7 + two_y :]
    new, sends = refs[0], refs[1 : 1 + ranks]
    pad, side, mag, fresh, packed = refs[1 + ranks :]
    deep, tall = block.shape[1], block.shape[2]
    full = deep + 2
    gx_odd = lax.rem(lax.axis_index("gx"), 2)
    gy_odd = lax.rem(lax.axis_index("gy"), 2)
    gz = lax.axis_index("gz")
    noted = notes[0:8, :]
    spots = [[noted[q * 4 + d, 0] for d in range(3)] for q in range(PAR)]
    chosen = noted[3, 0]
    lane = lane_iota((tall, LANES))
    keep = ((lane == 0) & (gz == 0)) | ((lane == LANES - 1) & (gz == 1))
    lane = lane_iota((16, LANES))
    none = jnp.zeros((16, LANES), F32)

    def at(c, x):
        return (c * full + x) * 16

    for c in range(6):
        for x in (0, full - 1):
            pad[pl.ds(at(c, x), 16), :] = none
        for x in range(deep):
            pad[pl.ds(at(c, x + 1), tall), :] = block[c, x]
        pad[pl.ds(at(c, 1) + tall, deep, stride=16), :] = none[0:deep]
        pad[pl.ds(at(c, 1) + 15, deep, stride=16), :] = none[0:deep]
    for c in range(5):
        for x in (0, full - 1):
            side[pl.ds(at(c, x), 16), :] = none
        for x in range(deep):
            side[pl.ds(at(c, x + 1), 16), :] = none
            side[pl.ds(at(c, x + 1), tall), :] = jnp.where(keep, beside[c, x], 0.0)
    for k, c in enumerate(X_COMPS):
        even, odd = x_even[k], x_odd[k]
        pad[pl.ds(at(c, 0), tall), :] = jnp.where(gx_odd == 0, odd, even)
        if c in (1, 2):
            pad[pl.ds(at(c, full - 1), tall), :] = jnp.where(gx_odd == 0, even, odd)
    for k, c in enumerate(Y_COMPS):
        even = y_even[k]
        odd = jnp.zeros_like(even) if y_odd is None else y_odd[k]
        pad[pl.ds(at(c, 1) + 15, deep, stride=16), :] = jnp.where(gy_odd == 0, odd, even)
        if c in (0, 2):
            pad[pl.ds(at(c, 1) + tall, deep, stride=16), :] = jnp.where(gy_odd == 0, even, odd)

    def up_y(a):
        return pltpu.roll(a, 15, 0)

    def down_y(a):
        return pltpu.roll(a, 1, 0)

    def plane(c, x):
        return pad[pl.ds(at(c, x), 16), :]

    def edge(c, x):
        return side[pl.ds(at(c, x), 16), :]

    def field(c, x):
        return mag[pl.ds((c * (full - 1) + x) * 16, 16), :]

    for x in range(full - 1):
        e0, e1, e2 = plane(0, x), plane(1, x), plane(2, x)
        s0, s1, s2 = edge(0, x), edge(1, x), edge(2, x)
        r0, r1 = pltpu.roll(e0, LANES - 1, 1), pltpu.roll(e1, LANES - 1, 1)
        u0 = jnp.where(lane == LANES - 1, pltpu.roll(s0, LANES - 1, 1), r0)
        u1 = jnp.where(lane == LANES - 1, pltpu.roll(s1, LANES - 1, 1), r1)
        h0 = plane(3, x) - 0.5 * ((up_y(e2) - e2) - (u1 - e1))
        h1 = plane(4, x) - 0.5 * ((u0 - e0) - (plane(2, x + 1) - e2))
        h2 = plane(5, x) - 0.5 * ((plane(1, x + 1) - e1) - (up_y(e0) - e0))
        t0 = edge(3, x) - 0.5 * ((up_y(s2) - s2) - (r1 - s1))
        t1 = edge(4, x) - 0.5 * ((r0 - s0) - (edge(2, x + 1) - s2))
        d0 = pltpu.roll(jnp.where(lane == LANES - 1, t0, h0), 1, 1)
        d1 = pltpu.roll(jnp.where(lane == LANES - 1, t1, h1), 1, 1)
        for c, value in enumerate((h0, h1, h2, d0, d1)):
            mag[pl.ds((c * (full - 1) + x) * 16, 16), :] = value
    for x in range(deep):
        h0, h1, h2, d0, d1 = (field(c, x + 1) for c in range(5))
        coef = rate[x]
        c0 = (h2 - down_y(h2)) - (h1 - d1)
        c1 = (h0 - d0) - (h2 - field(2, x))
        c2 = (h1 - field(1, x)) - (h0 - down_y(h0))
        for c, curl in enumerate((c0, c1, c2)):
            value = plane(c, x + 1)[0:tall] + coef * curl[0:tall]
            new[c, x] = value
            new[c + 3, x] = (h0, h1, h2)[c][0:tall]
            fresh[pl.ds((c * deep + x) * 16, tall), :] = value
            fresh[pl.ds(((c + 3) * deep + x) * 16, tall), :] = (h0, h1, h2)[c][0:tall]
    lane = lane_iota((8, LANES))
    for q in range(PAR):
        cx, cy, cz = spots[q]

        def rows_of(time, c, k, j, count, over_c):
            source, depth, start = (pad, full, cx) if time == 0 else (fresh, deep, cx - 1)
            step = depth * 16 if over_c else 16
            return source[pl.ds((c * depth + start + k) * 16 + cy + (j - 1), count, stride=step), :]

        def aim(rows, target):
            return pltpu.roll(rows, lax.rem(target - (cz - 1) + 2 * LANES, LANES), 1)

        for c in range(6):
            total = jnp.zeros((8, LANES), F32)
            for j in range(RIM):
                if (j == 0 and c == 4) or (j == RIM - 1 and c not in (0, 2)) or (0 < j < RIM - 1 and c == 5):
                    continue
                for time in range(2):
                    first = rim_lane(time, j, 0)
                    rows = aim(rows_of(time, c, 1, j, 8, False), first)
                    if j in (0, RIM - 1):
                        inside = (lane >= first) & (lane < first + RIM)
                    else:
                        inside = (lane == first) | (lane == first + RIM - 1)
                    total = jnp.where(inside, rows, total)
            packed[q, c * 8 : c * 8 + 8, :] = total
        for time in range(2):
            low = jnp.zeros((6, LANES), F32)
            high = jnp.zeros((2, LANES), F32)
            for j in range(RIM):
                first = j * RIM
                inside = (lane >= first) & (lane < first + RIM)
                low = jnp.where(inside[0:6], aim(rows_of(time, 0, 0, j, 6, True), first), low)
                high = jnp.where(inside[0:2], aim(rows_of(time, 1, RIM - 1, j, 2, True), first), high)
            base = ROWS_RIM + time * 8
            packed[q, base : base + 6, :] = low
            packed[q, base + 6 : base + 8, :] = high
        packed[q, ROW_EDGE:ROWS_PATCH, :] = jnp.zeros((ROWS_PATCH - ROW_EDGE, LANES), F32)
        packed[q, ROW_EDGE : ROW_EDGE + 1, :] = pad[pl.ds(at(1, full - 1) + tall - 1, 1), :]
        packed[q, ROW_EDGE + 1 : ROW_EDGE + 2, :] = pad[pl.ds(at(0, 0), 1), :]
    for k, send in enumerate(sends):
        q = jnp.where(chosen == k, 0, 1)
        send[0:ROWS_PATCH, :] = packed[q]
    half = lane_iota((16, LANES)) < LANES // 2
    send = sends[1]
    send[ROWS_PATCH : ROWS_PATCH + 16, :] = jnp.where(half, plane(0, 0), plane(2, full - 1))
    low = jnp.where(gy_odd == 0, jnp.zeros_like(y_even[1]) if y_odd is None else y_odd[1], y_even[1])
    high = jnp.where(gy_odd == 0, y_even[2], jnp.zeros_like(y_even[2]) if y_odd is None else y_odd[2])
    send[ROWS_PATCH + 16 : ROWS_PATCH + 32, :] = jnp.zeros((16, LANES), F32)
    send[ROWS_PATCH + 16 : ROWS_PATCH + 16 + deep, :] = jnp.where(half[0:deep], low, high)


def places():
    for x in range(PF):
        yield x, (x % 8 + 1) * 8 if x < 8 else (x % 8) * 8 + BATCH


def load_kernel(fine, perm, table, box, rate, lhs, coefs):
    groups = fine.shape[3] // BATCH
    blank = jnp.zeros((8, PF * PF), F32)
    for g in range(groups):
        slots = slice(g * BATCH, (g + 1) * BATCH)
        for c in range(6):
            for row in (0, ROWS_BOX - 8):
                lhs[c * ROWS_BOX + row : c * ROWS_BOX + row + 8, :] = blank
            for x, row in places():
                row += c * ROWS_BOX
                lhs[row : row + BATCH, :] = fine[0, 0, c, slots, x * PF * PF : (x + 1) * PF * PF]
            grown = move(lhs[c * ROWS_BOX : (c + 1) * ROWS_BOX, :], table[...])
            box[g, c] = grown
        for row in (0, ROWS_BOX - 8):
            coefs[row : row + 8, :] = blank
        for x, row in places():
            coefs[row : row + BATCH, :] = 0.5 / perm[0, 0, slots, x * PF * PF : (x + 1) * PF * PF]
        rate[g] = move(coefs[...], table[...])


def fine_kernel(ranks, *refs):
    regions, (box, rate, ghosts, means, out) = refs[:ranks], refs[ranks : ranks + 5]
    smalls = refs[ranks + 5 : 2 * ranks + 5]
    rims, walls, now, mag, halves, small = refs[2 * ranks + 5 :]
    groups = box.shape[0]
    rank = lax.axis_index("gy") * lax.axis_size("gz") + lax.axis_index("gz")
    flat = lane_iota((8, WIDE))
    yy = lax.shift_right_logical(flat * 3641, 16)
    zz = flat - yy * LINE
    inner = (yy >= 1) & (yy <= PF) & (zz >= 1) & (zz <= PF)
    upper = lax.broadcasted_iota(jnp.int32, (8, WIDE), 0) >= BATCH

    def inner_of(m):
        if m == 0:
            return inner & upper
        if m == PLANES - 1:
            return inner & jnp.logical_not(upper)
        return inner

    def up_y(a):
        return pltpu.roll(a, WIDE - LINE, 1)

    def up_z(a):
        return pltpu.roll(a, WIDE - 1, 1)

    def down_y(a):
        return pltpu.roll(a, LINE, 1)

    def down_z(a):
        return pltpu.roll(a, 1, 1)

    def rows_of(m):
        return pl.ds(m * 8, 8)

    blank = jnp.zeros((8, LANES), F32)
    for g in range(groups):
        for c in range(6):
            for m in range(PLANES):
                row = ((g * 6 + c) * PLANES + m) * 8
                if m in (0, PLANES - 1):
                    rims[row : row + 8, :] = blank
                walls[0, row : row + 8, :] = blank
                walls[1, row : row + 8, :] = blank
    for k, region in enumerate(regions):
        slot = lax.bitwise_xor(rank, k)
        start = (slot // BATCH) * 6 * ROWS_BOX + lax.rem(slot, BATCH)
        for c in range(6):
            rows = region[c * 8 : c * 8 + 8, :]
            row = start + c * ROWS_BOX
            rims[pl.ds(row + 8, 4, stride=16), :] = rows[0:4]
            rims[pl.ds(row + 16, 4, stride=16), :] = rows[0:4]
            rims[pl.ds(row + BATCH, 4, stride=16), :] = rows[4:8]
            rims[pl.ds(row + BATCH + 8, 4, stride=16), :] = rows[4:8]
        old = region[ROWS_RIM : ROWS_RIM + 8, :]
        fresh = region[ROWS_RIM + 8 : ROWS_RIM + 16, :]
        for sub, value in enumerate((old, old + 0.5 * (fresh - old))):
            walls[sub, pl.ds(start, 6, stride=ROWS_BOX), :] = value[0:6]
            last = start + ROWS_BOX + (PLANES - 1) * 8 + BATCH
            walls[sub, pl.ds(last, 2, stride=ROWS_BOX), :] = value[6:8]
    for g in range(groups):
        for sub in range(2):
            source = box if sub == 0 else out
            for c in range(6):
                rows = pl.ds((g * 6 + c) * ROWS_BOX, ROWS_BOX)
                ghost = move(jnp.concatenate([rims[rows, :], walls[sub, rows, :]], axis=1), ghosts[sub])
                for m in range(PLANES):
                    now[c, rows_of(m), :] = jnp.where(
                        inner_of(m), source[g, c, rows_of(m), :], ghost[m * 8 : (m + 1) * 8]
                    )

            def next_x(c, m):
                if m == PLANES - 1:
                    return pltpu.roll(now[c, rows_of(0), :], BATCH, 0)
                return now[c, rows_of(m + 1), :]

            def last_x(c, m):
                if m == 0:
                    return pltpu.roll(mag[c, rows_of(PLANES - 1), :], BATCH, 0)
                return mag[c, rows_of(m - 1), :]

            for m in range(PLANES):
                e0, e1, e2 = (now[c, rows_of(m), :] for c in range(3))
                h0, h1, h2 = (now[c, rows_of(m), :] for c in range(3, 6))
                mag[0, rows_of(m), :] = h0 - 0.5 * ((up_y(e2) - e2) - (up_z(e1) - e1))
                mag[1, rows_of(m), :] = h1 - 0.5 * ((up_z(e0) - e0) - (next_x(2, m) - e2))
                mag[2, rows_of(m), :] = h2 - 0.5 * ((next_x(1, m) - e1) - (up_y(e0) - e0))
            for m in range(PLANES):
                h0, h1, h2 = (mag[c, rows_of(m), :] for c in range(3))
                coef = rate[g, rows_of(m), :]
                e0, e1, e2 = (now[c, rows_of(m), :] for c in range(3))
                out[g, 0, rows_of(m), :] = e0 + coef * ((h2 - down_y(h2)) - (h1 - down_z(h1)))
                out[g, 1, rows_of(m), :] = e1 + coef * ((h0 - down_z(h0)) - (h2 - last_x(2, m)))
                out[g, 2, rows_of(m), :] = e2 + coef * ((h1 - last_x(1, m)) - (h0 - down_y(h0)))
                for c, value in enumerate((h0, h1, h2)):
                    out[g, c + 3, rows_of(m), :] = value
        for c in range(6):
            for k in range(4):
                other = jnp.where(upper, out[g, c, rows_of(2 * k), :], out[g, c, rows_of(2 * k + 2), :])
                pair = out[g, c, rows_of(2 * k + 1), :] + other
                halves[pl.ds((c * 2 + k // 2) * 8, 8), (k % 2) * WIDE : (k % 2 + 1) * WIDE] = pair
        small[pl.ds(g * 96, 96), :] = move(halves[...], means[...])
    for k, send in enumerate(smalls):
        slot = lax.bitwise_xor(rank, k)
        start = (slot // BATCH) * 96 + lax.rem(slot, BATCH)
        for xh in range(2):
            send[xh * 12 : (xh + 1) * 12, :] = small[pl.ds(start + xh * BATCH, 12, stride=8), :]


def store_kernel(box, fine, notes, table, out, stage, sems):
    groups = box.shape[0]
    slots = groups * BATCH
    live = jnp.concatenate([notes[8 : 8 + slots, :]] * (PF * PF // LANES), axis=1) > 0
    copies = []
    for c in range(6):
        flats = [move(box[g, c], table[...]) for g in range(groups)]
        for x, row in places():
            cut = slice(x * PF * PF, (x + 1) * PF * PF)
            for g, flat in enumerate(flats):
                some = slice(g * BATCH, (g + 1) * BATCH)
                stage[0, 0, c, some, cut] = jnp.where(live[some], flat[row : row + BATCH], fine[0, 0, c, some, cut])
        copies.append(pltpu.make_async_copy(stage.at[:, :, c], out.at[:, :, c], sems.at[c]))
        copies[-1].start()
    for copy in copies:
        copy.wait()


def fix_kernel(new, rate, *refs):
    edges, out = refs[:-1], refs[-1]
    deep, tall = new.shape[1], new.shape[2]
    gz = lax.axis_index("gz")
    rank = lax.axis_index("gy") * 2 + gz
    out[...] = new[...]

    def add(c, x, rows, amount):
        out[c, x, rows, :] = out[c, x, rows, :] + 0.5 * rate[x, rows, :] * amount

    lower = higher = jnp.zeros((1, LANES), F32)
    for k, edge in enumerate(edges, 1):
        row = ROW_EDGE
        lower = jnp.where(lax.bitwise_xor(rank, k) == rank - 2, edge[row : row + 1, :], lower)
        higher = jnp.where(lax.bitwise_xor(rank, k) == rank + 2, edge[row + 1 : row + 2, :], higher)
    add(0, deep - 1, slice(0, 1), lower)
    add(1, 0, slice(tall - 1, tall), higher)
    lane = lane_iota((tall, LANES))
    tile = edges[0][ROWS_PATCH : ROWS_PATCH + tall, :]
    add(0, deep - 1, slice(0, tall), jnp.where((lane == 0) & (gz == 1), pltpu.roll(tile, 1, 1), 0.0))
    add(2, 0, slice(0, tall), jnp.where((lane == LANES - 1) & (gz == 0), pltpu.roll(tile, LANES - 1, 1), 0.0))
    lane = lane_iota((deep, LANES))
    tile = edges[0][ROWS_PATCH + 16 : ROWS_PATCH + 16 + deep, :]
    first = jnp.where((lane == LANES - 1) & (gz == 0), pltpu.roll(tile, LANES - 1, 1), 0.0)
    last = jnp.where((lane == 0) & (gz == 1), pltpu.roll(tile, 1, 1), 0.0)
    for x in range(deep):
        add(2, x, slice(0, 1), first[x : x + 1])
        add(1, x, slice(tall - 1, tall), last[x : x + 1])


def place_kernel(ranks, new, notes, *refs):
    means, (out, spread, stage, gathered, sems) = refs[:ranks], refs[ranks:]
    noted = notes[0:8, :]
    for k, mean in enumerate(means):
        gathered[k] = mean[...]
    lane = lane_iota((HALF, LANES))
    spots = [tuple(noted[q * 4 + d, 0] for d in range(3)) for q in range(PAR)]
    for q, (cx, cy, cz) in enumerate(spots):
        k = noted[q * 4 + 3, 0]
        rows = gathered[k]
        for odd in range(2):
            for y in range(HALF):
                shift = lax.rem(cz - y * HALF - odd * HALF * HALF + 2 * LANES, LANES)
                spread[q, pl.ds(odd * 192 + y, 24, stride=8), :] = pltpu.roll(rows, shift, 1)
    copies = []
    for c in range(6):
        stage[c] = new[c]
        for q, (cx, cy, cz) in enumerate(spots):
            inside = (lane >= cz) & (lane < cz + HALF)
            for x in range(HALF):
                xh, k = x // 4, x % 4
                tile = spread[q, pl.ds((k % 2) * 192 + (xh * 12 + c * 2 + k // 2) * 8, 8), :]
                spot = stage[c, cx + x, pl.ds(cy, HALF), :]
                stage[c, cx + x, pl.ds(cy, HALF), :] = jnp.where(inside, tile, spot)
        copies.append(pltpu.make_async_copy(stage.at[c], out.at[c], sems.at[c]))
        copies[-1].start()
    for copy in copies:
        copy.wait()


def local(coarse_fields, permittivity, fine_fields, fine_permittivity, patch_corner, patch_owner):
    deep, tall, cols = coarse_fields.shape[1:]
    slots = fine_fields.shape[2]
    groups = slots // BATCH
    count_x, count_y = lax.axis_size("gx"), lax.axis_size("gy")
    two_y = count_y > 2
    vmem = whole()
    shape = jax.ShapeDtypeStruct
    grow = grow_table()

    x_face = shape((5, tall, cols), F32)
    y_face = shape((5, deep, cols), F32)
    kept, rate, *faces = call(
        functools.partial(faces_kernel, two_y),
        [shape(coarse_fields.shape, F32), shape(permittivity.shape, F32), x_face, x_face, y_face] + [y_face] * two_y,
        [vmem, vmem],
    )(coarse_fields, permittivity)
    got = [
        lax.ppermute(faces[0], "gx", swap_pairs(count_x, 0)),
        lax.ppermute(faces[1], "gx", swap_pairs(count_x, 1)),
        lax.ppermute(faces[2], "gy", swap_pairs(count_y, 0)),
    ]
    if two_y:
        got.append(lax.ppermute(faces[3], "gy", swap_pairs(count_y, 1)))
    beside = lax.ppermute(kept, "gz", swap_pairs(2, 0))

    fine = fine_fields.transpose(0, 1, 3, 2, 4)
    notes = call(
        notes_kernel,
        shape((8 + slots, LANES), jnp.int32),
        [whole(pltpu.SMEM)] * 2,
    )(patch_corner, patch_owner.transpose(0, 2, 1))
    box, fine_rate = call(
        load_kernel,
        [shape((groups, 6, ROWS_BOX, WIDE), F32), shape((groups, ROWS_BOX, WIDE), F32)],
        [vmem] * 3,
        [pltpu.VMEM((6 * ROWS_BOX, PF * PF), F32), pltpu.VMEM((ROWS_BOX, PF * PF), F32)],
        size=4_000_000,
    )(fine, fine_permittivity, jnp.asarray(grow, BF16))

    full = deep + 2
    ranks = count_y * lax.axis_size("gz")

    def exchange(parts):
        swaps = [[(r, r ^ k) for r in range(ranks)] for k in range(ranks)]
        return [parts[0]] + [lax.ppermute(parts[k], ("gy", "gz"), swaps[k]) for k in range(1, ranks)]

    patches = [shape((ROWS_BESIDE if k == 1 else ROWS_PATCH, LANES), F32) for k in range(ranks)]
    new, *sends = call(
        functools.partial(leap_kernel, two_y, ranks),
        [shape(coarse_fields.shape, F32)] + patches,
        [vmem] * (4 + len(got)),
        [
            pltpu.VMEM((6 * full * 16, LANES), F32),
            pltpu.VMEM((6 * full * 16, LANES), F32),
            pltpu.VMEM((5 * (full - 1) * 16, LANES), F32),
            pltpu.VMEM((6 * deep * 16, LANES), F32),
            pltpu.VMEM((PAR, ROWS_PATCH, LANES), F32),
        ],
    )(kept, beside, rate, notes, *got)
    regions = exchange(sends)

    box, *smalls = call(
        functools.partial(fine_kernel, ranks),
        [shape((groups, 6, ROWS_BOX, WIDE), F32)] + [shape((24, LANES), F32)] * ranks,
        [vmem] * (ranks + 4),
        [
            pltpu.VMEM((groups * 6 * ROWS_BOX, LANES), F32),
            pltpu.VMEM((2, groups * 6 * ROWS_BOX, LANES), F32),
            pltpu.VMEM((6, ROWS_BOX, WIDE), F32),
            pltpu.VMEM((3, ROWS_BOX, WIDE), F32),
            pltpu.VMEM((96, 2 * WIDE), F32),
            pltpu.VMEM((groups * 96, LANES), F32),
        ],
    )(*regions, box, fine_rate, jnp.asarray(ghost_table(), BF16), jnp.asarray(mean_table(), BF16))
    means = exchange(smalls)

    fine = call(
        store_kernel,
        shape(fine.shape, F32),
        [vmem] * 4,
        [pltpu.VMEM(fine.shape, F32), pltpu.SemaphoreType.DMA((6,))],
        size=4_000_000,
        out_specs=whole(pltpu.HBM),
    )(box, fine, notes, jnp.asarray(grow.T, BF16))
    new = call(fix_kernel, shape(coarse_fields.shape, F32), [vmem] * (1 + ranks))(new, rate, *regions[1:])
    coarse = call(
        functools.partial(place_kernel, ranks),
        shape(coarse_fields.shape, F32),
        [vmem] * (2 + ranks),
        [
            pltpu.VMEM((PAR, 4 * 96, LANES), F32),
            pltpu.VMEM(coarse_fields.shape, F32),
            pltpu.VMEM((ranks, 24, LANES), F32),
            pltpu.SemaphoreType.DMA((6,)),
        ],
        out_specs=whole(pltpu.HBM),
    )(new, notes, *means)
    return coarse, fine.transpose(0, 1, 3, 2, 4)


def solution(mesh):
    in_specs = (
        P(None, ("groups", "gx"), "gy", "gz"),
        P(("groups", "gx"), "gy", "gz"),
        P(("groups", "gx"), "gy", "gz", None, None),
        P(("groups", "gx"), "gy", "gz", None),
        P(("groups", "gx"), "gy", "gz", None),
        P(("groups", "gx"), None, None),
    )
    out_specs = (P(None, ("groups", "gx"), "gy", "gz"), P(("groups", "gx"), "gy", "gz", None, None))
    return jax.shard_map(local, mesh=mesh, in_specs=in_specs, out_specs=out_specs, check_vma=False)
```

```python
import functools
import jax
import jax.numpy as jnp
import numpy as np
from jax import lax
from jax.experimental import pallas as pl
from jax.experimental.pallas import tpu as pltpu
from jax.sharding import PartitionSpec as P

PF = 16
PAR = 2
HALF = PF // 2
RIM = HALF + 2
PLANES = 9
LINE = PF + 2
LANES = 128
WIDE = 384
BATCH = 4
ROWS_BOX = PLANES * 8
ROWS_RIM = 48
ROW_EDGE = 64
ROWS_PATCH = 72
ROWS_BESIDE = 104
X_COMPS = (0, 1, 2, 4, 5)
Y_COMPS = (0, 1, 2, 3, 5)
VMEM_BYTES = 48 * 1024 * 1024
F32 = jnp.float32
BF16 = jnp.bfloat16


def rim_lane(time, j, k):
    if 0 < j < RIM - 1:
        return j * RIM + k + 3 * time
    if j == 0 and time == 0:
        return k
    return (RIM - 1) * RIM + 3 + (2 * time + j // (RIM - 1) - 1) * RIM + k


def grow_table():
    table = np.zeros((PF * PF, WIDE), np.float32)
    for y in range(PF):
        for z in range(PF):
            table[y * PF + z, (y + 1) * LINE + z + 1] = 1.0
    return table


def ghost_table():
    table = np.zeros((2, 2 * LANES, WIDE), np.float32)
    for y in range(LINE):
        for z in range(LINE):
            j, k, lane = (y + 1) // 2, (z + 1) // 2, y * LINE + z
            table[:, LANES + j * RIM + k, lane] = 1.0
            if y in (0, LINE - 1) or z in (0, LINE - 1):
                table[0, rim_lane(0, j, k), lane] = 1.0
                table[1, rim_lane(0, j, k), lane] = 0.5
                table[1, rim_lane(1, j, k), lane] = 0.5
    return table


def mean_table():
    table = np.zeros((2, WIDE, LANES), np.float32)
    for odd in range(2):
        for y in range(PF):
            for z in range(PF):
                lane = odd * HALF * HALF + (y // 2) * HALF + z // 2
                table[odd, (y + 1) * LINE + z + 1, lane] = 0.125
    return table.reshape(2 * WIDE, LANES)


def move(rows, table):
    high = rows.astype(BF16)
    low = (rows - high.astype(F32)).astype(BF16)
    out = jnp.dot(high, table, preferred_element_type=F32)
    return out + jnp.dot(low, table, preferred_element_type=F32)


def lane_iota(shape):
    return lax.broadcasted_iota(jnp.int32, shape, len(shape) - 1)


def whole(memory_space=pltpu.VMEM):
    return pl.BlockSpec(memory_space=memory_space)


def call(kernel, outs, in_specs, scratch=(), flops=1_000_000, size=1_000_000, out_specs=None, **extra):
    return pl.pallas_call(
        kernel,
        out_shape=outs,
        in_specs=in_specs,
        out_specs=jax.tree.map(lambda _: whole(), outs) if out_specs is None else out_specs,
        scratch_shapes=list(scratch),
        compiler_params=pltpu.CompilerParams(vmem_limit_bytes=VMEM_BYTES),
        cost_estimate=pl.CostEstimate(flops=flops, bytes_accessed=size, transcendentals=0),
        **extra,
    )


def swap_pairs(count, first):
    pairs = []
    for i in range(first, count - 1, 2):
        pairs += [(i, i + 1), (i + 1, i)]
    return pairs


def faces_kernel(two_y, block, kept, x_even, x_odd, y_even, *y_odd):
    deep, tall = block.shape[1], block.shape[2]
    gx_odd = lax.rem(lax.axis_index("gx"), 2)
    gy_odd = lax.rem(lax.axis_index("gy"), 2)
    for k, c in enumerate(X_COMPS):
        x_even[k] = block[c, (1 - gx_odd) * (deep - 1)]
        x_odd[k] = block[c, gx_odd * (deep - 1)]
    for k, c in enumerate(Y_COMPS):
        for x in range(deep):
            first = block[c, x, 0:1, :]
            last = block[c, x, tall - 1 : tall, :]
            y_even[k, x : x + 1, :] = jnp.where(gy_odd == 0, last, first)
            if two_y:
                y_odd[0][k, x : x + 1, :] = jnp.where(gy_odd == 0, first, last)
    kept[...] = block[...]


def notes_kernel(corner, owners, perm, notes, rate):
    rank = lax.axis_index("gy") * lax.axis_size("gz") + lax.axis_index("gz")

    def note(row, value):
        notes[row : row + 1, :] = jnp.full((1, LANES), value, jnp.int32)

    for q in range(PAR):
        for d in range(3):
            note(q * 4 + d, corner[0, 0, q, d])
        note(q * 4 + 3, lax.bitwise_xor(owners[0, q, rank], rank))
    for slot in range(notes.shape[0] - 8):
        live = (owners[0, 0, slot] == rank) | (owners[0, 1, slot] == rank)
        note(8 + slot, live.astype(jnp.int32))
    rate[...] = 0.5 / perm[...]


def leap_kernel(two_y, ranks, *refs):
    block, beside, rate, notes, x_even, x_odd, y_even = refs[:7]
    y_odd = refs[7] if two_y else None
    refs = refs[7 + two_y :]
    new, sends = refs[0], refs[1 : 1 + ranks]
    pad, side, mag, fresh, packed = refs[1 + ranks :]
    deep, tall = block.shape[1], block.shape[2]
    full = deep + 2
    gx_odd = lax.rem(lax.axis_index("gx"), 2)
    gy_odd = lax.rem(lax.axis_index("gy"), 2)
    gz = lax.axis_index("gz")
    noted = notes[0:8, :]
    spots = [[noted[q * 4 + d, 0] for d in range(3)] for q in range(PAR)]
    chosen = noted[3, 0]
    lane = lane_iota((tall, LANES))
    keep = ((lane == 0) & (gz == 0)) | ((lane == LANES - 1) & (gz == 1))
    lane = lane_iota((16, LANES))
    none = jnp.zeros((16, LANES), F32)

    def at(c, x):
        return (c * full + x) * 16

    for c in range(6):
        for x in (0, full - 1):
            pad[pl.ds(at(c, x), 16), :] = none
        for x in range(deep):
            pad[pl.ds(at(c, x + 1), tall), :] = block[c, x]
        pad[pl.ds(at(c, 1) + tall, deep, stride=16), :] = none[0:deep]
        pad[pl.ds(at(c, 1) + 15, deep, stride=16), :] = none[0:deep]
    for c in range(5):
        for x in (0, full - 1):
            side[pl.ds(at(c, x), 16), :] = none
        for x in range(deep):
            side[pl.ds(at(c, x + 1), 16), :] = none
            side[pl.ds(at(c, x + 1), tall), :] = jnp.where(keep, beside[c, x], 0.0)
    for k, c in enumerate(X_COMPS):
        even, odd = x_even[k], x_odd[k]
        pad[pl.ds(at(c, 0), tall), :] = jnp.where(gx_odd == 0, odd, even)
        if c in (1, 2):
            pad[pl.ds(at(c, full - 1), tall), :] = jnp.where(gx_odd == 0, even, odd)
    for k, c in enumerate(Y_COMPS):
        even = y_even[k]
        odd = jnp.zeros_like(even) if y_odd is None else y_odd[k]
        pad[pl.ds(at(c, 1) + 15, deep, stride=16), :] = jnp.where(gy_odd == 0, odd, even)
        if c in (0, 2):
            pad[pl.ds(at(c, 1) + tall, deep, stride=16), :] = jnp.where(gy_odd == 0, even, odd)

    def up_y(a):
        return pltpu.roll(a, 15, 0)

    def down_y(a):
        return pltpu.roll(a, 1, 0)

    def plane(c, x):
        return pad[pl.ds(at(c, x), 16), :]

    def edge(c, x):
        return side[pl.ds(at(c, x), 16), :]

    def field(c, x):
        return mag[pl.ds((c * (full - 1) + x) * 16, 16), :]

    for x in range(full - 1):
        e0, e1, e2 = plane(0, x), plane(1, x), plane(2, x)
        s0, s1, s2 = edge(0, x), edge(1, x), edge(2, x)
        r0, r1 = pltpu.roll(e0, LANES - 1, 1), pltpu.roll(e1, LANES - 1, 1)
        u0 = jnp.where(lane == LANES - 1, pltpu.roll(s0, LANES - 1, 1), r0)
        u1 = jnp.where(lane == LANES - 1, pltpu.roll(s1, LANES - 1, 1), r1)
        h0 = plane(3, x) - 0.5 * ((up_y(e2) - e2) - (u1 - e1))
        h1 = plane(4, x) - 0.5 * ((u0 - e0) - (plane(2, x + 1) - e2))
        h2 = plane(5, x) - 0.5 * ((plane(1, x + 1) - e1) - (up_y(e0) - e0))
        t0 = edge(3, x) - 0.5 * ((up_y(s2) - s2) - (r1 - s1))
        t1 = edge(4, x) - 0.5 * ((r0 - s0) - (edge(2, x + 1) - s2))
        d0 = pltpu.roll(jnp.where(lane == LANES - 1, t0, h0), 1, 1)
        d1 = pltpu.roll(jnp.where(lane == LANES - 1, t1, h1), 1, 1)
        for c, value in enumerate((h0, h1, h2, d0, d1)):
            mag[pl.ds((c * (full - 1) + x) * 16, 16), :] = value
    for x in range(deep):
        h0, h1, h2, d0, d1 = (field(c, x + 1) for c in range(5))
        coef = rate[x]
        c0 = (h2 - down_y(h2)) - (h1 - d1)
        c1 = (h0 - d0) - (h2 - field(2, x))
        c2 = (h1 - field(1, x)) - (h0 - down_y(h0))
        for c, curl in enumerate((c0, c1, c2)):
            value = plane(c, x + 1)[0:tall] + coef * curl[0:tall]
            new[c, x] = value
            new[c + 3, x] = (h0, h1, h2)[c][0:tall]
            fresh[pl.ds((c * deep + x) * 16, tall), :] = value
            fresh[pl.ds(((c + 3) * deep + x) * 16, tall), :] = (h0, h1, h2)[c][0:tall]
    lane = lane_iota((8, LANES))
    for q in range(PAR):
        cx, cy, cz = spots[q]

        def rows_of(time, c, k, j, count, over_c):
            source, depth, start = (pad, full, cx) if time == 0 else (fresh, deep, cx - 1)
            step = depth * 16 if over_c else 16
            return source[pl.ds((c * depth + start + k) * 16 + cy + (j - 1), count, stride=step), :]

        def aim(rows, target):
            return pltpu.roll(rows, lax.rem(target - (cz - 1) + 2 * LANES, LANES), 1)

        for c in range(6):
            total = jnp.zeros((8, LANES), F32)
            for j in range(RIM):
                if (j == 0 and c == 4) or (j == RIM - 1 and c not in (0, 2)) or (0 < j < RIM - 1 and c == 5):
                    continue
                for time in range(2):
                    first = rim_lane(time, j, 0)
                    rows = aim(rows_of(time, c, 1, j, 8, False), first)
                    if j in (0, RIM - 1):
                        inside = (lane >= first) & (lane < first + RIM)
                    else:
                        inside = (lane == first) | (lane == first + RIM - 1)
                    total = jnp.where(inside, rows, total)
            packed[q, c * 8 : c * 8 + 8, :] = total
        for time in range(2):
            low = jnp.zeros((6, LANES), F32)
            high = jnp.zeros((2, LANES), F32)
            for j in range(RIM):
                first = j * RIM
                inside = (lane >= first) & (lane < first + RIM)
                low = jnp.where(inside[0:6], aim(rows_of(time, 0, 0, j, 6, True), first), low)
                high = jnp.where(inside[0:2], aim(rows_of(time, 1, RIM - 1, j, 2, True), first), high)
            base = ROWS_RIM + time * 8
            packed[q, base : base + 6, :] = low
            packed[q, base + 6 : base + 8, :] = high
        packed[q, ROW_EDGE:ROWS_PATCH, :] = jnp.zeros((ROWS_PATCH - ROW_EDGE, LANES), F32)
        packed[q, ROW_EDGE : ROW_EDGE + 1, :] = pad[pl.ds(at(1, full - 1) + tall - 1, 1), :]
        packed[q, ROW_EDGE + 1 : ROW_EDGE + 2, :] = pad[pl.ds(at(0, 0), 1), :]
    for k, send in enumerate(sends):
        q = jnp.where(chosen == k, 0, 1)
        send[0:ROWS_PATCH, :] = packed[q]
    half = lane_iota((16, LANES)) < LANES // 2
    send = sends[1]
    send[ROWS_PATCH : ROWS_PATCH + 16, :] = jnp.where(half, plane(0, 0), plane(2, full - 1))
    low = jnp.where(gy_odd == 0, jnp.zeros_like(y_even[1]) if y_odd is None else y_odd[1], y_even[1])
    high = jnp.where(gy_odd == 0, y_even[2], jnp.zeros_like(y_even[2]) if y_odd is None else y_odd[2])
    send[ROWS_PATCH + 16 : ROWS_PATCH + 32, :] = jnp.zeros((16, LANES), F32)
    send[ROWS_PATCH + 16 : ROWS_PATCH + 16 + deep, :] = jnp.where(half[0:deep], low, high)


def places():
    for x in range(PF):
        yield x, (x % 8 + 1) * 8 if x < 8 else (x % 8) * 8 + BATCH


def load_kernel(fine, perm, table, box, rate, lhs, coefs):
    groups = fine.shape[3] // BATCH
    blank = jnp.zeros((8, PF * PF), F32)
    for g in range(groups):
        slots = slice(g * BATCH, (g + 1) * BATCH)
        for c in range(6):
            for row in (0, ROWS_BOX - 8):
                lhs[c * ROWS_BOX + row : c * ROWS_BOX + row + 8, :] = blank
            for x, row in places():
                row += c * ROWS_BOX
                lhs[row : row + BATCH, :] = fine[0, 0, c, slots, x * PF * PF : (x + 1) * PF * PF]
            grown = move(lhs[c * ROWS_BOX : (c + 1) * ROWS_BOX, :], table[...])
            box[g, c] = grown
        for row in (0, ROWS_BOX - 8):
            coefs[row : row + 8, :] = blank
        for x, row in places():
            coefs[row : row + BATCH, :] = 0.5 / perm[0, 0, slots, x * PF * PF : (x + 1) * PF * PF]
        rate[g] = move(coefs[...], table[...])


def fine_kernel(ranks, *refs):
    regions, (box, rate, ghosts, means, out) = refs[:ranks], refs[ranks : ranks + 5]
    smalls = refs[ranks + 5 : 2 * ranks + 5]
    rims, walls, now, mag, halves, small = refs[2 * ranks + 5 :]
    groups = box.shape[0]
    rank = lax.axis_index("gy") * lax.axis_size("gz") + lax.axis_index("gz")
    flat = lane_iota((8, WIDE))
    yy = lax.shift_right_logical(flat * 3641, 16)
    zz = flat - yy * LINE
    inner = (yy >= 1) & (yy <= PF) & (zz >= 1) & (zz <= PF)
    upper = lax.broadcasted_iota(jnp.int32, (8, WIDE), 0) >= BATCH

    def inner_of(m):
        if m == 0:
            return inner & upper
        if m == PLANES - 1:
            return inner & jnp.logical_not(upper)
        return inner

    def up_y(a):
        return pltpu.roll(a, WIDE - LINE, 1)

    def up_z(a):
        return pltpu.roll(a, WIDE - 1, 1)

    def down_y(a):
        return pltpu.roll(a, LINE, 1)

    def down_z(a):
        return pltpu.roll(a, 1, 1)

    def rows_of(m):
        return pl.ds(m * 8, 8)

    blank = jnp.zeros((8, LANES), F32)
    for g in range(groups):
        for c in range(6):
            for m in range(PLANES):
                row = ((g * 6 + c) * PLANES + m) * 8
                if m in (0, PLANES - 1):
                    rims[row : row + 8, :] = blank
                walls[0, row : row + 8, :] = blank
                walls[1, row : row + 8, :] = blank
    for k, region in enumerate(regions):
        slot = lax.bitwise_xor(rank, k)
        start = (slot // BATCH) * 6 * ROWS_BOX + lax.rem(slot, BATCH)
        for c in range(6):
            rows = region[c * 8 : c * 8 + 8, :]
            row = start + c * ROWS_BOX
            rims[pl.ds(row + 8, 4, stride=16), :] = rows[0:4]
            rims[pl.ds(row + 16, 4, stride=16), :] = rows[0:4]
            rims[pl.ds(row + BATCH, 4, stride=16), :] = rows[4:8]
            rims[pl.ds(row + BATCH + 8, 4, stride=16), :] = rows[4:8]
        old = region[ROWS_RIM : ROWS_RIM + 8, :]
        fresh = region[ROWS_RIM + 8 : ROWS_RIM + 16, :]
        for sub, value in enumerate((old, old + 0.5 * (fresh - old))):
            walls[sub, pl.ds(start, 6, stride=ROWS_BOX), :] = value[0:6]
            last = start + ROWS_BOX + (PLANES - 1) * 8 + BATCH
            walls[sub, pl.ds(last, 2, stride=ROWS_BOX), :] = value[6:8]
    for g in range(groups):
        for sub in range(2):
            source = box if sub == 0 else out
            for c in range(6):
                rows = pl.ds((g * 6 + c) * ROWS_BOX, ROWS_BOX)
                ghost = move(jnp.concatenate([rims[rows, :], walls[sub, rows, :]], axis=1), ghosts[sub])
                for m in range(PLANES):
                    now[c, rows_of(m), :] = jnp.where(
                        inner_of(m), source[g, c, rows_of(m), :], ghost[m * 8 : (m + 1) * 8]
                    )

            def next_x(c, m):
                if m == PLANES - 1:
                    return pltpu.roll(now[c, rows_of(0), :], BATCH, 0)
                return now[c, rows_of(m + 1), :]

            def last_x(c, m):
                if m == 0:
                    return pltpu.roll(mag[c, rows_of(PLANES - 1), :], BATCH, 0)
                return mag[c, rows_of(m - 1), :]

            for m in range(PLANES):
                e0, e1, e2 = (now[c, rows_of(m), :] for c in range(3))
                h0, h1, h2 = (now[c, rows_of(m), :] for c in range(3, 6))
                mag[0, rows_of(m), :] = h0 - 0.5 * ((up_y(e2) - e2) - (up_z(e1) - e1))
                mag[1, rows_of(m), :] = h1 - 0.5 * ((up_z(e0) - e0) - (next_x(2, m) - e2))
                mag[2, rows_of(m), :] = h2 - 0.5 * ((next_x(1, m) - e1) - (up_y(e0) - e0))
            for m in range(PLANES):
                h0, h1, h2 = (mag[c, rows_of(m), :] for c in range(3))
                coef = rate[g, rows_of(m), :]
                e0, e1, e2 = (now[c, rows_of(m), :] for c in range(3))
                out[g, 0, rows_of(m), :] = e0 + coef * ((h2 - down_y(h2)) - (h1 - down_z(h1)))
                out[g, 1, rows_of(m), :] = e1 + coef * ((h0 - down_z(h0)) - (h2 - last_x(2, m)))
                out[g, 2, rows_of(m), :] = e2 + coef * ((h1 - last_x(1, m)) - (h0 - down_y(h0)))
                for c, value in enumerate((h0, h1, h2)):
                    out[g, c + 3, rows_of(m), :] = value
        for c in range(6):
            for k in range(4):
                other = jnp.where(upper, out[g, c, rows_of(2 * k), :], out[g, c, rows_of(2 * k + 2), :])
                pair = out[g, c, rows_of(2 * k + 1), :] + other
                halves[pl.ds((c * 2 + k // 2) * 8, 8), (k % 2) * WIDE : (k % 2 + 1) * WIDE] = pair
        small[pl.ds(g * 96, 96), :] = move(halves[...], means[...])
    for k, send in enumerate(smalls):
        slot = lax.bitwise_xor(rank, k)
        start = (slot // BATCH) * 96 + lax.rem(slot, BATCH)
        for xh in range(2):
            send[xh * 12 : (xh + 1) * 12, :] = small[pl.ds(start + xh * BATCH, 12, stride=8), :]


def store_kernel(box, fine, notes, table, out, stage, sems):
    groups = box.shape[0]
    slots = groups * BATCH
    live = jnp.concatenate([notes[8 : 8 + slots, :]] * (PF * PF // LANES), axis=1) > 0
    copies = []
    for c in range(6):
        flats = [move(box[g, c], table[...]) for g in range(groups)]
        for x, row in places():
            cut = slice(x * PF * PF, (x + 1) * PF * PF)
            for g, flat in enumerate(flats):
                some = slice(g * BATCH, (g + 1) * BATCH)
                stage[0, 0, c, some, cut] = jnp.where(live[some], flat[row : row + BATCH], fine[0, 0, c, some, cut])
        copies.append(pltpu.make_async_copy(stage.at[:, :, c], out.at[:, :, c], sems.at[c]))
        copies[-1].start()
    for copy in copies:
        copy.wait()


def fix_kernel(new, rate, *refs):
    edges, out = refs[:-1], refs[-1]
    deep, tall = new.shape[1], new.shape[2]
    gz = lax.axis_index("gz")
    rank = lax.axis_index("gy") * 2 + gz
    out[...] = new[...]

    def add(c, x, rows, amount):
        out[c, x, rows, :] = out[c, x, rows, :] + 0.5 * rate[x, rows, :] * amount

    lower = higher = jnp.zeros((1, LANES), F32)
    for k, edge in enumerate(edges, 1):
        row = ROW_EDGE
        lower = jnp.where(lax.bitwise_xor(rank, k) == rank - 2, edge[row : row + 1, :], lower)
        higher = jnp.where(lax.bitwise_xor(rank, k) == rank + 2, edge[row + 1 : row + 2, :], higher)
    add(0, deep - 1, slice(0, 1), lower)
    add(1, 0, slice(tall - 1, tall), higher)
    lane = lane_iota((tall, LANES))
    tile = edges[0][ROWS_PATCH : ROWS_PATCH + tall, :]
    add(0, deep - 1, slice(0, tall), jnp.where((lane == 0) & (gz == 1), pltpu.roll(tile, 1, 1), 0.0))
    add(2, 0, slice(0, tall), jnp.where((lane == LANES - 1) & (gz == 0), pltpu.roll(tile, LANES - 1, 1), 0.0))
    lane = lane_iota((deep, LANES))
    tile = edges[0][ROWS_PATCH + 16 : ROWS_PATCH + 16 + deep, :]
    first = jnp.where((lane == LANES - 1) & (gz == 0), pltpu.roll(tile, LANES - 1, 1), 0.0)
    last = jnp.where((lane == 0) & (gz == 1), pltpu.roll(tile, 1, 1), 0.0)
    for x in range(deep):
        add(2, x, slice(0, 1), first[x : x + 1])
        add(1, x, slice(tall - 1, tall), last[x : x + 1])


def place_kernel(ranks, new, notes, *refs):
    means, (out, spread, stage, gathered, sems) = refs[:ranks], refs[ranks:]
    noted = notes[0:8, :]
    for k, mean in enumerate(means):
        gathered[k] = mean[...]
    lane = lane_iota((HALF, LANES))
    spots = [tuple(noted[q * 4 + d, 0] for d in range(3)) for q in range(PAR)]
    for q, (cx, cy, cz) in enumerate(spots):
        k = noted[q * 4 + 3, 0]
        rows = gathered[k]
        for odd in range(2):
            for y in range(HALF):
                shift = lax.rem(cz - y * HALF - odd * HALF * HALF + 2 * LANES, LANES)
                spread[q, pl.ds(odd * 192 + y, 24, stride=8), :] = pltpu.roll(rows, shift, 1)
    copies = []
    for c in range(6):
        stage[c] = new[c]
        for q, (cx, cy, cz) in enumerate(spots):
            inside = (lane >= cz) & (lane < cz + HALF)
            for x in range(HALF):
                xh, k = x // 4, x % 4
                tile = spread[q, pl.ds((k % 2) * 192 + (xh * 12 + c * 2 + k // 2) * 8, 8), :]
                spot = stage[c, cx + x, pl.ds(cy, HALF), :]
                stage[c, cx + x, pl.ds(cy, HALF), :] = jnp.where(inside, tile, spot)
        copies.append(pltpu.make_async_copy(stage.at[c], out.at[c], sems.at[c]))
        copies[-1].start()
    for copy in copies:
        copy.wait()


def local(coarse_fields, permittivity, fine_fields, fine_permittivity, patch_corner, patch_owner):
    deep, tall, cols = coarse_fields.shape[1:]
    slots = fine_fields.shape[2]
    groups = slots // BATCH
    count_x, count_y = lax.axis_size("gx"), lax.axis_size("gy")
    two_y = count_y > 2
    vmem = whole()
    shape = jax.ShapeDtypeStruct
    grow = grow_table()

    x_face = shape((5, tall, cols), F32)
    y_face = shape((5, deep, cols), F32)
    kept, *faces = call(
        functools.partial(faces_kernel, two_y),
        [shape(coarse_fields.shape, F32), x_face, x_face, y_face] + [y_face] * two_y,
        [vmem],
    )(coarse_fields)
    got = [
        lax.ppermute(faces[0], "gx", swap_pairs(count_x, 0)),
        lax.ppermute(faces[1], "gx", swap_pairs(count_x, 1)),
        lax.ppermute(faces[2], "gy", swap_pairs(count_y, 0)),
    ]
    if two_y:
        got.append(lax.ppermute(faces[3], "gy", swap_pairs(count_y, 1)))
    beside = lax.ppermute(kept, "gz", swap_pairs(2, 0))

    fine = fine_fields.transpose(0, 1, 3, 2, 4)
    notes, rate = call(
        notes_kernel,
        [shape((8 + slots, LANES), jnp.int32), shape(permittivity.shape, F32)],
        [whole(pltpu.SMEM)] * 2 + [vmem],
    )(patch_corner, patch_owner.transpose(0, 2, 1), permittivity)
    box, fine_rate = call(
        load_kernel,
        [shape((groups, 6, ROWS_BOX, WIDE), F32), shape((groups, ROWS_BOX, WIDE), F32)],
        [vmem] * 3,
        [pltpu.VMEM((6 * ROWS_BOX, PF * PF), F32), pltpu.VMEM((ROWS_BOX, PF * PF), F32)],
        size=4_000_000,
    )(fine, fine_permittivity, jnp.asarray(grow, BF16))

    full = deep + 2
    ranks = count_y * lax.axis_size("gz")

    def exchange(parts):
        swaps = [[(r, r ^ k) for r in range(ranks)] for k in range(ranks)]
        got = list(parts)
        for k in [*range(2, ranks), 1]:
            got[k] = lax.ppermute(parts[k], ("gy", "gz"), swaps[k])
        return got

    patches = [shape((ROWS_BESIDE if k == 1 else ROWS_PATCH, LANES), F32) for k in range(ranks)]
    new, *sends = call(
        functools.partial(leap_kernel, two_y, ranks),
        [shape(coarse_fields.shape, F32)] + patches,
        [vmem] * (4 + len(got)),
        [
            pltpu.VMEM((6 * full * 16, LANES), F32),
            pltpu.VMEM((6 * full * 16, LANES), F32),
            pltpu.VMEM((5 * (full - 1) * 16, LANES), F32),
            pltpu.VMEM((6 * deep * 16, LANES), F32),
            pltpu.VMEM((PAR, ROWS_PATCH, LANES), F32),
        ],
    )(kept, beside, rate, notes, *got)
    regions = exchange(sends)

    box, *smalls = call(
        functools.partial(fine_kernel, ranks),
        [shape((groups, 6, ROWS_BOX, WIDE), F32)] + [shape((24, LANES), F32)] * ranks,
        [vmem] * (ranks + 4),
        [
            pltpu.VMEM((groups * 6 * ROWS_BOX, LANES), F32),
            pltpu.VMEM((2, groups * 6 * ROWS_BOX, LANES), F32),
            pltpu.VMEM((6, ROWS_BOX, WIDE), F32),
            pltpu.VMEM((3, ROWS_BOX, WIDE), F32),
            pltpu.VMEM((96, 2 * WIDE), F32),
            pltpu.VMEM((groups * 96, LANES), F32),
        ],
    )(*regions, box, fine_rate, jnp.asarray(ghost_table(), BF16), jnp.asarray(mean_table(), BF16))
    means = exchange(smalls)

    fine = call(
        store_kernel,
        shape(fine.shape, F32),
        [vmem] * 4,
        [pltpu.VMEM(fine.shape, F32), pltpu.SemaphoreType.DMA((6,))],
        size=4_000_000,
        out_specs=whole(pltpu.HBM),
    )(box, fine, notes, jnp.asarray(grow.T, BF16))
    new = call(fix_kernel, shape(coarse_fields.shape, F32), [vmem] * (1 + ranks))(new, rate, *regions[1:])
    coarse = call(
        functools.partial(place_kernel, ranks),
        shape(coarse_fields.shape, F32),
        [vmem] * (2 + ranks),
        [
            pltpu.VMEM((PAR, 4 * 96, LANES), F32),
            pltpu.VMEM(coarse_fields.shape, F32),
            pltpu.VMEM((ranks, 24, LANES), F32),
            pltpu.SemaphoreType.DMA((6,)),
        ],
        out_specs=whole(pltpu.HBM),
    )(new, notes, *means)
    return coarse, fine.transpose(0, 1, 3, 2, 4)


def solution(mesh):
    in_specs = (
        P(None, ("groups", "gx"), "gy", "gz"),
        P(("groups", "gx"), "gy", "gz"),
        P(("groups", "gx"), "gy", "gz", None, None),
        P(("groups", "gx"), "gy", "gz", None),
        P(("groups", "gx"), "gy", "gz", None),
        P(("groups", "gx"), None, None),
    )
    out_specs = (P(None, ("groups", "gx"), "gy", "gz"), P(("groups", "gx"), "gy", "gz", None, None))
    return jax.shard_map(local, mesh=mesh, in_specs=in_specs, out_specs=out_specs, check_vma=False)
```

```python
import functools
import jax
import jax.numpy as jnp
import numpy as np
from jax import lax
from jax.experimental import pallas as pl
from jax.experimental.pallas import tpu as pltpu
from jax.sharding import PartitionSpec as P

PF = 16
PAR = 2
HALF = PF // 2
RIM = HALF + 2
PLANES = 9
LINE = PF + 2
LANES = 128
WIDE = 384
BATCH = 4
ROWS_BOX = PLANES * 8
ROWS_RIM = 48
ROW_EDGE = 64
ROWS_PATCH = 72
ROWS_BESIDE = 104
X_COMPS = (0, 1, 2, 4, 5)
Y_COMPS = (0, 1, 2, 3, 5)
VMEM_BYTES = 48 * 1024 * 1024
F32 = jnp.float32
BF16 = jnp.bfloat16


def rim_lane(time, j, k):
    if 0 < j < RIM - 1:
        return j * RIM + k + 3 * time
    if j == 0 and time == 0:
        return k
    return (RIM - 1) * RIM + 3 + (2 * time + j // (RIM - 1) - 1) * RIM + k


def grow_table():
    table = np.zeros((PF * PF, WIDE), np.float32)
    for y in range(PF):
        for z in range(PF):
            table[y * PF + z, (y + 1) * LINE + z + 1] = 1.0
    return table


def ghost_table():
    table = np.zeros((2, 2 * LANES, WIDE), np.float32)
    for y in range(LINE):
        for z in range(LINE):
            j, k, lane = (y + 1) // 2, (z + 1) // 2, y * LINE + z
            table[:, LANES + j * RIM + k, lane] = 1.0
            if y in (0, LINE - 1) or z in (0, LINE - 1):
                table[0, rim_lane(0, j, k), lane] = 1.0
                table[1, rim_lane(0, j, k), lane] = 0.5
                table[1, rim_lane(1, j, k), lane] = 0.5
    return table


def mean_table():
    table = np.zeros((2, WIDE, LANES), np.float32)
    for odd in range(2):
        for y in range(PF):
            for z in range(PF):
                lane = odd * HALF * HALF + (y // 2) * HALF + z // 2
                table[odd, (y + 1) * LINE + z + 1, lane] = 0.125
    return table.reshape(2 * WIDE, LANES)


def move(rows, table):
    high = rows.astype(BF16)
    low = (rows - high.astype(F32)).astype(BF16)
    out = jnp.dot(high, table, preferred_element_type=F32)
    return out + jnp.dot(low, table, preferred_element_type=F32)


def lane_iota(shape):
    return lax.broadcasted_iota(jnp.int32, shape, len(shape) - 1)


def whole(memory_space=pltpu.VMEM):
    return pl.BlockSpec(memory_space=memory_space)


def call(kernel, outs, in_specs, scratch=(), flops=1_000_000, size=1_000_000, out_specs=None, **extra):
    return pl.pallas_call(
        kernel,
        out_shape=outs,
        in_specs=in_specs,
        out_specs=jax.tree.map(lambda _: whole(), outs) if out_specs is None else out_specs,
        scratch_shapes=list(scratch),
        compiler_params=pltpu.CompilerParams(vmem_limit_bytes=VMEM_BYTES),
        cost_estimate=pl.CostEstimate(flops=flops, bytes_accessed=size, transcendentals=0),
        **extra,
    )


def swap_pairs(count, first):
    pairs = []
    for i in range(first, count - 1, 2):
        pairs += [(i, i + 1), (i + 1, i)]
    return pairs


def far_first(parts):
    return [parts[0], *parts[2:], parts[1]]


def by_rank(parts):
    return [parts[0], parts[-1], *parts[1:-1]]


def faces_kernel(two_y, block, kept, x_odd, x_even, y_even, *y_odd):
    deep, tall = block.shape[1], block.shape[2]
    gx_odd = lax.rem(lax.axis_index("gx"), 2)
    gy_odd = lax.rem(lax.axis_index("gy"), 2)
    for k, c in enumerate(X_COMPS):
        x_even[k] = block[c, (1 - gx_odd) * (deep - 1)]
        x_odd[k] = block[c, gx_odd * (deep - 1)]
    for k, c in enumerate(Y_COMPS):
        for x in range(deep):
            first = block[c, x, 0:1, :]
            last = block[c, x, tall - 1 : tall, :]
            y_even[k, x : x + 1, :] = jnp.where(gy_odd == 0, last, first)
            if two_y:
                y_odd[0][k, x : x + 1, :] = jnp.where(gy_odd == 0, first, last)
    kept[...] = block[...]


def notes_kernel(corner, owners, perm, notes, rate):
    rank = lax.axis_index("gy") * lax.axis_size("gz") + lax.axis_index("gz")

    def note(row, value):
        notes[row : row + 1, :] = jnp.full((1, LANES), value, jnp.int32)

    for q in range(PAR):
        for d in range(3):
            note(q * 4 + d, corner[0, 0, q, d])
        note(q * 4 + 3, lax.bitwise_xor(owners[0, q, rank], rank))
    for slot in range(notes.shape[0] - 8):
        live = (owners[0, 0, slot] == rank) | (owners[0, 1, slot] == rank)
        note(8 + slot, live.astype(jnp.int32))
    rate[...] = 0.5 / perm[...]


def leap_kernel(two_y, ranks, *refs):
    block, beside, rate, notes, x_odd, x_even, y_even = refs[:7]
    y_odd = refs[7] if two_y else None
    refs = refs[7 + two_y :]
    new, sends = refs[0], by_rank(refs[1 : 1 + ranks])
    pad, side, mag, fresh, packed = refs[1 + ranks :]
    deep, tall = block.shape[1], block.shape[2]
    full = deep + 2
    gx_odd = lax.rem(lax.axis_index("gx"), 2)
    gy_odd = lax.rem(lax.axis_index("gy"), 2)
    gz = lax.axis_index("gz")
    noted = notes[0:8, :]
    spots = [[noted[q * 4 + d, 0] for d in range(3)] for q in range(PAR)]
    chosen = noted[3, 0]
    lane = lane_iota((tall, LANES))
    keep = ((lane == 0) & (gz == 0)) | ((lane == LANES - 1) & (gz == 1))
    lane = lane_iota((16, LANES))
    none = jnp.zeros((16, LANES), F32)

    def at(c, x):
        return (c * full + x) * 16

    for c in range(6):
        for x in (0, full - 1):
            pad[pl.ds(at(c, x), 16), :] = none
        for x in range(deep):
            pad[pl.ds(at(c, x + 1), tall), :] = block[c, x]
        pad[pl.ds(at(c, 1) + tall, deep, stride=16), :] = none[0:deep]
        pad[pl.ds(at(c, 1) + 15, deep, stride=16), :] = none[0:deep]
    for c in range(5):
        for x in (0, full - 1):
            side[pl.ds(at(c, x), 16), :] = none
        for x in range(deep):
            side[pl.ds(at(c, x + 1), 16), :] = none
            side[pl.ds(at(c, x + 1), tall), :] = jnp.where(keep, beside[c, x], 0.0)
    for k, c in enumerate(X_COMPS):
        even, odd = x_even[k], x_odd[k]
        pad[pl.ds(at(c, 0), tall), :] = jnp.where(gx_odd == 0, odd, even)
        if c in (1, 2):
            pad[pl.ds(at(c, full - 1), tall), :] = jnp.where(gx_odd == 0, even, odd)
    for k, c in enumerate(Y_COMPS):
        even = y_even[k]
        odd = jnp.zeros_like(even) if y_odd is None else y_odd[k]
        pad[pl.ds(at(c, 1) + 15, deep, stride=16), :] = jnp.where(gy_odd == 0, odd, even)
        if c in (0, 2):
            pad[pl.ds(at(c, 1) + tall, deep, stride=16), :] = jnp.where(gy_odd == 0, even, odd)

    def up_y(a):
        return pltpu.roll(a, 15, 0)

    def down_y(a):
        return pltpu.roll(a, 1, 0)

    def plane(c, x):
        return pad[pl.ds(at(c, x), 16), :]

    def edge(c, x):
        return side[pl.ds(at(c, x), 16), :]

    def field(c, x):
        return mag[pl.ds((c * (full - 1) + x) * 16, 16), :]

    for x in range(full - 1):
        e0, e1, e2 = plane(0, x), plane(1, x), plane(2, x)
        s0, s1, s2 = edge(0, x), edge(1, x), edge(2, x)
        r0, r1 = pltpu.roll(e0, LANES - 1, 1), pltpu.roll(e1, LANES - 1, 1)
        u0 = jnp.where(lane == LANES - 1, pltpu.roll(s0, LANES - 1, 1), r0)
        u1 = jnp.where(lane == LANES - 1, pltpu.roll(s1, LANES - 1, 1), r1)
        h0 = plane(3, x) - 0.5 * ((up_y(e2) - e2) - (u1 - e1))
        h1 = plane(4, x) - 0.5 * ((u0 - e0) - (plane(2, x + 1) - e2))
        h2 = plane(5, x) - 0.5 * ((plane(1, x + 1) - e1) - (up_y(e0) - e0))
        t0 = edge(3, x) - 0.5 * ((up_y(s2) - s2) - (r1 - s1))
        t1 = edge(4, x) - 0.5 * ((r0 - s0) - (edge(2, x + 1) - s2))
        d0 = pltpu.roll(jnp.where(lane == LANES - 1, t0, h0), 1, 1)
        d1 = pltpu.roll(jnp.where(lane == LANES - 1, t1, h1), 1, 1)
        for c, value in enumerate((h0, h1, h2, d0, d1)):
            mag[pl.ds((c * (full - 1) + x) * 16, 16), :] = value
    for x in range(deep):
        h0, h1, h2, d0, d1 = (field(c, x + 1) for c in range(5))
        coef = rate[x]
        c0 = (h2 - down_y(h2)) - (h1 - d1)
        c1 = (h0 - d0) - (h2 - field(2, x))
        c2 = (h1 - field(1, x)) - (h0 - down_y(h0))
        for c, curl in enumerate((c0, c1, c2)):
            value = plane(c, x + 1)[0:tall] + coef * curl[0:tall]
            new[c, x] = value
            new[c + 3, x] = (h0, h1, h2)[c][0:tall]
            fresh[pl.ds((c * deep + x) * 16, tall), :] = value
            fresh[pl.ds(((c + 3) * deep + x) * 16, tall), :] = (h0, h1, h2)[c][0:tall]
    lane = lane_iota((8, LANES))
    for q in range(PAR):
        cx, cy, cz = spots[q]

        def rows_of(time, c, k, j, count, over_c):
            source, depth, start = (pad, full, cx) if time == 0 else (fresh, deep, cx - 1)
            step = depth * 16 if over_c else 16
            return source[pl.ds((c * depth + start + k) * 16 + cy + (j - 1), count, stride=step), :]

        def aim(rows, target):
            return pltpu.roll(rows, lax.rem(target - (cz - 1) + 2 * LANES, LANES), 1)

        for c in range(6):
            total = jnp.zeros((8, LANES), F32)
            for j in range(RIM):
                if (j == 0 and c == 4) or (j == RIM - 1 and c not in (0, 2)) or (0 < j < RIM - 1 and c == 5):
                    continue
                for time in range(2):
                    first = rim_lane(time, j, 0)
                    rows = aim(rows_of(time, c, 1, j, 8, False), first)
                    if j in (0, RIM - 1):
                        inside = (lane >= first) & (lane < first + RIM)
                    else:
                        inside = (lane == first) | (lane == first + RIM - 1)
                    total = jnp.where(inside, rows, total)
            packed[q, c * 8 : c * 8 + 8, :] = total
        for time in range(2):
            low = jnp.zeros((6, LANES), F32)
            high = jnp.zeros((2, LANES), F32)
            for j in range(RIM):
                first = j * RIM
                inside = (lane >= first) & (lane < first + RIM)
                low = jnp.where(inside[0:6], aim(rows_of(time, 0, 0, j, 6, True), first), low)
                high = jnp.where(inside[0:2], aim(rows_of(time, 1, RIM - 1, j, 2, True), first), high)
            base = ROWS_RIM + time * 8
            packed[q, base : base + 6, :] = low
            packed[q, base + 6 : base + 8, :] = high
        packed[q, ROW_EDGE:ROWS_PATCH, :] = jnp.zeros((ROWS_PATCH - ROW_EDGE, LANES), F32)
        packed[q, ROW_EDGE : ROW_EDGE + 1, :] = pad[pl.ds(at(1, full - 1) + tall - 1, 1), :]
        packed[q, ROW_EDGE + 1 : ROW_EDGE + 2, :] = pad[pl.ds(at(0, 0), 1), :]
    for k, send in enumerate(sends):
        q = jnp.where(chosen == k, 0, 1)
        send[0:ROWS_PATCH, :] = packed[q]
    half = lane_iota((16, LANES)) < LANES // 2
    send = sends[1]
    send[ROWS_PATCH : ROWS_PATCH + 16, :] = jnp.where(half, plane(0, 0), plane(2, full - 1))
    low = jnp.where(gy_odd == 0, jnp.zeros_like(y_even[1]) if y_odd is None else y_odd[1], y_even[1])
    high = jnp.where(gy_odd == 0, y_even[2], jnp.zeros_like(y_even[2]) if y_odd is None else y_odd[2])
    send[ROWS_PATCH + 16 : ROWS_PATCH + 32, :] = jnp.zeros((16, LANES), F32)
    send[ROWS_PATCH + 16 : ROWS_PATCH + 16 + deep, :] = jnp.where(half[0:deep], low, high)


def places():
    for x in range(PF):
        yield x, (x % 8 + 1) * 8 if x < 8 else (x % 8) * 8 + BATCH


def load_kernel(fine, perm, table, box, rate, lhs, coefs):
    groups = fine.shape[3] // BATCH
    blank = jnp.zeros((8, PF * PF), F32)
    for g in range(groups):
        slots = slice(g * BATCH, (g + 1) * BATCH)
        for c in range(6):
            for row in (0, ROWS_BOX - 8):
                lhs[c * ROWS_BOX + row : c * ROWS_BOX + row + 8, :] = blank
            for x, row in places():
                row += c * ROWS_BOX
                lhs[row : row + BATCH, :] = fine[0, 0, c, slots, x * PF * PF : (x + 1) * PF * PF]
            grown = move(lhs[c * ROWS_BOX : (c + 1) * ROWS_BOX, :], table[...])
            box[g, c] = grown
        for row in (0, ROWS_BOX - 8):
            coefs[row : row + 8, :] = blank
        for x, row in places():
            coefs[row : row + BATCH, :] = 0.5 / perm[0, 0, slots, x * PF * PF : (x + 1) * PF * PF]
        rate[g] = move(coefs[...], table[...])


def fine_kernel(ranks, *refs):
    regions, (box, rate, ghosts, means, out) = refs[:ranks], refs[ranks : ranks + 5]
    smalls = by_rank(refs[ranks + 5 : 2 * ranks + 5])
    rims, walls, now, mag, halves, small = refs[2 * ranks + 5 :]
    groups = box.shape[0]
    rank = lax.axis_index("gy") * lax.axis_size("gz") + lax.axis_index("gz")
    flat = lane_iota((8, WIDE))
    yy = lax.shift_right_logical(flat * 3641, 16)
    zz = flat - yy * LINE
    inner = (yy >= 1) & (yy <= PF) & (zz >= 1) & (zz <= PF)
    upper = lax.broadcasted_iota(jnp.int32, (8, WIDE), 0) >= BATCH

    def inner_of(m):
        if m == 0:
            return inner & upper
        if m == PLANES - 1:
            return inner & jnp.logical_not(upper)
        return inner

    def up_y(a):
        return pltpu.roll(a, WIDE - LINE, 1)

    def up_z(a):
        return pltpu.roll(a, WIDE - 1, 1)

    def down_y(a):
        return pltpu.roll(a, LINE, 1)

    def down_z(a):
        return pltpu.roll(a, 1, 1)

    def rows_of(m):
        return pl.ds(m * 8, 8)

    blank = jnp.zeros((8, LANES), F32)
    for g in range(groups):
        for c in range(6):
            for m in range(PLANES):
                row = ((g * 6 + c) * PLANES + m) * 8
                if m in (0, PLANES - 1):
                    rims[row : row + 8, :] = blank
                walls[0, row : row + 8, :] = blank
                walls[1, row : row + 8, :] = blank
    for k, region in enumerate(regions):
        slot = lax.bitwise_xor(rank, k)
        start = (slot // BATCH) * 6 * ROWS_BOX + lax.rem(slot, BATCH)
        for c in range(6):
            rows = region[c * 8 : c * 8 + 8, :]
            row = start + c * ROWS_BOX
            rims[pl.ds(row + 8, 4, stride=16), :] = rows[0:4]
            rims[pl.ds(row + 16, 4, stride=16), :] = rows[0:4]
            rims[pl.ds(row + BATCH, 4, stride=16), :] = rows[4:8]
            rims[pl.ds(row + BATCH + 8, 4, stride=16), :] = rows[4:8]
        old = region[ROWS_RIM : ROWS_RIM + 8, :]
        fresh = region[ROWS_RIM + 8 : ROWS_RIM + 16, :]
        for sub, value in enumerate((old, old + 0.5 * (fresh - old))):
            walls[sub, pl.ds(start, 6, stride=ROWS_BOX), :] = value[0:6]
            last = start + ROWS_BOX + (PLANES - 1) * 8 + BATCH
            walls[sub, pl.ds(last, 2, stride=ROWS_BOX), :] = value[6:8]
    for g in range(groups):
        for sub in range(2):
            source = box if sub == 0 else out
            for c in range(6):
                rows = pl.ds((g * 6 + c) * ROWS_BOX, ROWS_BOX)
                ghost = move(jnp.concatenate([rims[rows, :], walls[sub, rows, :]], axis=1), ghosts[sub])
                for m in range(PLANES):
                    now[c, rows_of(m), :] = jnp.where(
                        inner_of(m), source[g, c, rows_of(m), :], ghost[m * 8 : (m + 1) * 8]
                    )

            def next_x(c, m):
                if m == PLANES - 1:
                    return pltpu.roll(now[c, rows_of(0), :], BATCH, 0)
                return now[c, rows_of(m + 1), :]

            def last_x(c, m):
                if m == 0:
                    return pltpu.roll(mag[c, rows_of(PLANES - 1), :], BATCH, 0)
                return mag[c, rows_of(m - 1), :]

            for m in range(PLANES):
                e0, e1, e2 = (now[c, rows_of(m), :] for c in range(3))
                h0, h1, h2 = (now[c, rows_of(m), :] for c in range(3, 6))
                mag[0, rows_of(m), :] = h0 - 0.5 * ((up_y(e2) - e2) - (up_z(e1) - e1))
                mag[1, rows_of(m), :] = h1 - 0.5 * ((up_z(e0) - e0) - (next_x(2, m) - e2))
                mag[2, rows_of(m), :] = h2 - 0.5 * ((next_x(1, m) - e1) - (up_y(e0) - e0))
            for m in range(PLANES):
                h0, h1, h2 = (mag[c, rows_of(m), :] for c in range(3))
                coef = rate[g, rows_of(m), :]
                e0, e1, e2 = (now[c, rows_of(m), :] for c in range(3))
                out[g, 0, rows_of(m), :] = e0 + coef * ((h2 - down_y(h2)) - (h1 - down_z(h1)))
                out[g, 1, rows_of(m), :] = e1 + coef * ((h0 - down_z(h0)) - (h2 - last_x(2, m)))
                out[g, 2, rows_of(m), :] = e2 + coef * ((h1 - last_x(1, m)) - (h0 - down_y(h0)))
                for c, value in enumerate((h0, h1, h2)):
                    out[g, c + 3, rows_of(m), :] = value
        for c in range(6):
            for k in range(4):
                other = jnp.where(upper, out[g, c, rows_of(2 * k), :], out[g, c, rows_of(2 * k + 2), :])
                pair = out[g, c, rows_of(2 * k + 1), :] + other
                halves[pl.ds((c * 2 + k // 2) * 8, 8), (k % 2) * WIDE : (k % 2 + 1) * WIDE] = pair
        small[pl.ds(g * 96, 96), :] = move(halves[...], means[...])
    for k, send in enumerate(smalls):
        slot = lax.bitwise_xor(rank, k)
        start = (slot // BATCH) * 96 + lax.rem(slot, BATCH)
        for xh in range(2):
            send[xh * 12 : (xh + 1) * 12, :] = small[pl.ds(start + xh * BATCH, 12, stride=8), :]


def store_kernel(box, fine, notes, table, out, stage, sems):
    groups = box.shape[0]
    slots = groups * BATCH
    live = jnp.concatenate([notes[8 : 8 + slots, :]] * (PF * PF // LANES), axis=1) > 0
    copies = []
    for c in range(6):
        flats = [move(box[g, c], table[...]) for g in range(groups)]
        for x, row in places():
            cut = slice(x * PF * PF, (x + 1) * PF * PF)
            for g, flat in enumerate(flats):
                some = slice(g * BATCH, (g + 1) * BATCH)
                stage[0, 0, c, some, cut] = jnp.where(live[some], flat[row : row + BATCH], fine[0, 0, c, some, cut])
        copies.append(pltpu.make_async_copy(stage.at[:, :, c], out.at[:, :, c], sems.at[c]))
        copies[-1].start()
    for copy in copies:
        copy.wait()


def fix_kernel(new, rate, *refs):
    edges, out = refs[:-1], refs[-1]
    deep, tall = new.shape[1], new.shape[2]
    gz = lax.axis_index("gz")
    rank = lax.axis_index("gy") * 2 + gz
    out[...] = new[...]

    def add(c, x, rows, amount):
        out[c, x, rows, :] = out[c, x, rows, :] + 0.5 * rate[x, rows, :] * amount

    lower = higher = jnp.zeros((1, LANES), F32)
    for k, edge in enumerate(edges, 1):
        row = ROW_EDGE
        lower = jnp.where(lax.bitwise_xor(rank, k) == rank - 2, edge[row : row + 1, :], lower)
        higher = jnp.where(lax.bitwise_xor(rank, k) == rank + 2, edge[row + 1 : row + 2, :], higher)
    add(0, deep - 1, slice(0, 1), lower)
    add(1, 0, slice(tall - 1, tall), higher)
    lane = lane_iota((tall, LANES))
    tile = edges[0][ROWS_PATCH : ROWS_PATCH + tall, :]
    add(0, deep - 1, slice(0, tall), jnp.where((lane == 0) & (gz == 1), pltpu.roll(tile, 1, 1), 0.0))
    add(2, 0, slice(0, tall), jnp.where((lane == LANES - 1) & (gz == 0), pltpu.roll(tile, LANES - 1, 1), 0.0))
    lane = lane_iota((deep, LANES))
    tile = edges[0][ROWS_PATCH + 16 : ROWS_PATCH + 16 + deep, :]
    first = jnp.where((lane == LANES - 1) & (gz == 0), pltpu.roll(tile, LANES - 1, 1), 0.0)
    last = jnp.where((lane == 0) & (gz == 1), pltpu.roll(tile, 1, 1), 0.0)
    for x in range(deep):
        add(2, x, slice(0, 1), first[x : x + 1])
        add(1, x, slice(tall - 1, tall), last[x : x + 1])


def place_kernel(ranks, new, notes, *refs):
    means, (out, spread, stage, gathered, sems) = refs[:ranks], refs[ranks:]
    noted = notes[0:8, :]
    for k, mean in enumerate(means):
        gathered[k] = mean[...]
    lane = lane_iota((HALF, LANES))
    spots = [tuple(noted[q * 4 + d, 0] for d in range(3)) for q in range(PAR)]
    for q, (cx, cy, cz) in enumerate(spots):
        k = noted[q * 4 + 3, 0]
        rows = gathered[k]
        for odd in range(2):
            for y in range(HALF):
                shift = lax.rem(cz - y * HALF - odd * HALF * HALF + 2 * LANES, LANES)
                spread[q, pl.ds(odd * 192 + y, 24, stride=8), :] = pltpu.roll(rows, shift, 1)
    copies = []
    for c in range(6):
        stage[c] = new[c]
        for q, (cx, cy, cz) in enumerate(spots):
            inside = (lane >= cz) & (lane < cz + HALF)
            for x in range(HALF):
                xh, k = x // 4, x % 4
                tile = spread[q, pl.ds((k % 2) * 192 + (xh * 12 + c * 2 + k // 2) * 8, 8), :]
                spot = stage[c, cx + x, pl.ds(cy, HALF), :]
                stage[c, cx + x, pl.ds(cy, HALF), :] = jnp.where(inside, tile, spot)
        copies.append(pltpu.make_async_copy(stage.at[c], out.at[c], sems.at[c]))
        copies[-1].start()
    for copy in copies:
        copy.wait()


def local(coarse_fields, permittivity, fine_fields, fine_permittivity, patch_corner, patch_owner):
    deep, tall, cols = coarse_fields.shape[1:]
    slots = fine_fields.shape[2]
    groups = slots // BATCH
    count_x, count_y = lax.axis_size("gx"), lax.axis_size("gy")
    two_y = count_y > 2
    vmem = whole()
    shape = jax.ShapeDtypeStruct
    grow = grow_table()

    x_face = shape((5, tall, cols), F32)
    y_face = shape((5, deep, cols), F32)
    kept, *faces = call(
        functools.partial(faces_kernel, two_y),
        [shape(coarse_fields.shape, F32), x_face, x_face, y_face] + [y_face] * two_y,
        [vmem],
    )(coarse_fields)
    got = [
        lax.ppermute(faces[0], "gx", swap_pairs(count_x, 1)),
        lax.ppermute(faces[1], "gx", swap_pairs(count_x, 0)),
        lax.ppermute(faces[2], "gy", swap_pairs(count_y, 0)),
    ]
    if two_y:
        got.append(lax.ppermute(faces[3], "gy", swap_pairs(count_y, 1)))
    beside = lax.ppermute(kept, "gz", swap_pairs(2, 0))

    fine = fine_fields.transpose(0, 1, 3, 2, 4)
    notes, rate = call(
        notes_kernel,
        [shape((8 + slots, LANES), jnp.int32), shape(permittivity.shape, F32)],
        [whole(pltpu.SMEM)] * 2 + [vmem],
    )(patch_corner, patch_owner.transpose(0, 2, 1), permittivity)
    box, fine_rate = call(
        load_kernel,
        [shape((groups, 6, ROWS_BOX, WIDE), F32), shape((groups, ROWS_BOX, WIDE), F32)],
        [vmem] * 3,
        [pltpu.VMEM((6 * ROWS_BOX, PF * PF), F32), pltpu.VMEM((ROWS_BOX, PF * PF), F32)],
        size=4_000_000,
    )(fine, fine_permittivity, jnp.asarray(grow, BF16))

    full = deep + 2
    ranks = count_y * lax.axis_size("gz")

    def exchange(parts):
        swaps = [[(r, r ^ k) for r in range(ranks)] for k in range(ranks)]
        got = list(parts)
        for k in [*range(2, ranks), 1]:
            got[k] = lax.ppermute(parts[k], ("gy", "gz"), swaps[k])
        return got

    patches = [shape((ROWS_BESIDE if k == 1 else ROWS_PATCH, LANES), F32) for k in range(ranks)]
    new, *sends = call(
        functools.partial(leap_kernel, two_y, ranks),
        [shape(coarse_fields.shape, F32)] + far_first(patches),
        [vmem] * (4 + len(got)),
        [
            pltpu.VMEM((6 * full * 16, LANES), F32),
            pltpu.VMEM((6 * full * 16, LANES), F32),
            pltpu.VMEM((5 * (full - 1) * 16, LANES), F32),
            pltpu.VMEM((6 * deep * 16, LANES), F32),
            pltpu.VMEM((PAR, ROWS_PATCH, LANES), F32),
        ],
    )(kept, beside, rate, notes, *got)
    regions = exchange(by_rank(sends))

    box, *smalls = call(
        functools.partial(fine_kernel, ranks),
        [shape((groups, 6, ROWS_BOX, WIDE), F32)] + [shape((24, LANES), F32)] * ranks,
        [vmem] * (ranks + 4),
        [
            pltpu.VMEM((groups * 6 * ROWS_BOX, LANES), F32),
            pltpu.VMEM((2, groups * 6 * ROWS_BOX, LANES), F32),
            pltpu.VMEM((6, ROWS_BOX, WIDE), F32),
            pltpu.VMEM((3, ROWS_BOX, WIDE), F32),
            pltpu.VMEM((96, 2 * WIDE), F32),
            pltpu.VMEM((groups * 96, LANES), F32),
        ],
    )(*regions, box, fine_rate, jnp.asarray(ghost_table(), BF16), jnp.asarray(mean_table(), BF16))
    means = exchange(by_rank(smalls))

    fine = call(
        store_kernel,
        shape(fine.shape, F32),
        [vmem] * 4,
        [pltpu.VMEM(fine.shape, F32), pltpu.SemaphoreType.DMA((6,))],
        size=4_000_000,
        out_specs=whole(pltpu.HBM),
    )(box, fine, notes, jnp.asarray(grow.T, BF16))
    new = call(fix_kernel, shape(coarse_fields.shape, F32), [vmem] * (1 + ranks))(new, rate, *regions[1:])
    coarse = call(
        functools.partial(place_kernel, ranks),
        shape(coarse_fields.shape, F32),
        [vmem] * (2 + ranks),
        [
            pltpu.VMEM((PAR, 4 * 96, LANES), F32),
            pltpu.VMEM(coarse_fields.shape, F32),
            pltpu.VMEM((ranks, 24, LANES), F32),
            pltpu.SemaphoreType.DMA((6,)),
        ],
        out_specs=whole(pltpu.HBM),
    )(new, notes, *means)
    return coarse, fine.transpose(0, 1, 3, 2, 4)


def solution(mesh):
    in_specs = (
        P(None, ("groups", "gx"), "gy", "gz"),
        P(("groups", "gx"), "gy", "gz"),
        P(("groups", "gx"), "gy", "gz", None, None),
        P(("groups", "gx"), "gy", "gz", None),
        P(("groups", "gx"), "gy", "gz", None),
        P(("groups", "gx"), None, None),
    )
    out_specs = (P(None, ("groups", "gx"), "gy", "gz"), P(("groups", "gx"), "gy", "gz", None, None))
    return jax.shard_map(local, mesh=mesh, in_specs=in_specs, out_specs=out_specs, check_vma=False)
```

```python
import functools
import jax
import jax.numpy as jnp
import numpy as np
from jax import lax
from jax.experimental import pallas as pl
from jax.experimental.pallas import tpu as pltpu
from jax.sharding import PartitionSpec as P

PF = 16
PAR = 2
HALF = PF // 2
RIM = HALF + 2
PLANES = 9
LINE = PF + 2
LANES = 128
WIDE = 384
BATCH = 4
ROWS_BOX = PLANES * 8
ROWS_RIM = 48
ROW_EDGE = 64
ROWS_PATCH = 72
ROWS_BESIDE = 104
X_COMPS = (0, 1, 2, 4, 5)
Y_COMPS = (0, 1, 2, 3, 5)
VMEM_BYTES = 48 * 1024 * 1024
F32 = jnp.float32
BF16 = jnp.bfloat16


def rim_lane(time, j, k):
    if 0 < j < RIM - 1:
        return j * RIM + k + 3 * time
    if j == 0 and time == 0:
        return k
    return (RIM - 1) * RIM + 3 + (2 * time + j // (RIM - 1) - 1) * RIM + k


def grow_table():
    table = np.zeros((PF * PF, WIDE), np.float32)
    for y in range(PF):
        for z in range(PF):
            table[y * PF + z, (y + 1) * LINE + z + 1] = 1.0
    return table


def ghost_table():
    table = np.zeros((2, 2 * LANES, WIDE), np.float32)
    for y in range(LINE):
        for z in range(LINE):
            j, k, lane = (y + 1) // 2, (z + 1) // 2, y * LINE + z
            table[:, LANES + j * RIM + k, lane] = 1.0
            if y in (0, LINE - 1) or z in (0, LINE - 1):
                table[0, rim_lane(0, j, k), lane] = 1.0
                table[1, rim_lane(0, j, k), lane] = 0.5
                table[1, rim_lane(1, j, k), lane] = 0.5
    return table


def mean_table():
    table = np.zeros((2, WIDE, LANES), np.float32)
    for odd in range(2):
        for y in range(PF):
            for z in range(PF):
                lane = odd * HALF * HALF + (y // 2) * HALF + z // 2
                table[odd, (y + 1) * LINE + z + 1, lane] = 0.125
    return table.reshape(2 * WIDE, LANES)


def move(rows, table):
    high = rows.astype(BF16)
    low = (rows - high.astype(F32)).astype(BF16)
    out = jnp.dot(high, table, preferred_element_type=F32)
    return out + jnp.dot(low, table, preferred_element_type=F32)


def lane_iota(shape):
    return lax.broadcasted_iota(jnp.int32, shape, len(shape) - 1)


def whole(memory_space=pltpu.VMEM):
    return pl.BlockSpec(memory_space=memory_space)


def call(kernel, outs, in_specs, scratch=(), flops=1_000_000, size=1_000_000, out_specs=None, **extra):
    return pl.pallas_call(
        kernel,
        out_shape=outs,
        in_specs=in_specs,
        out_specs=jax.tree.map(lambda _: whole(), outs) if out_specs is None else out_specs,
        scratch_shapes=list(scratch),
        compiler_params=pltpu.CompilerParams(vmem_limit_bytes=VMEM_BYTES),
        cost_estimate=pl.CostEstimate(flops=flops, bytes_accessed=size, transcendentals=0),
        **extra,
    )


def swap_pairs(count, first):
    pairs = []
    for i in range(first, count - 1, 2):
        pairs += [(i, i + 1), (i + 1, i)]
    return pairs


def far_first(parts):
    return [parts[0], *parts[2:], parts[1]]


def by_rank(parts):
    return [parts[0], parts[-1], *parts[1:-1]]


def faces_kernel(two_y, block, kept, x_even, x_odd, y_even, *more):
    y_odd, z_face = more[:-1], more[-1]
    deep, tall = block.shape[1], block.shape[2]
    gx_odd = lax.rem(lax.axis_index("gx"), 2)
    gy_odd = lax.rem(lax.axis_index("gy"), 2)
    for k, c in enumerate(X_COMPS):
        x_even[k] = block[c, (1 - gx_odd) * (deep - 1)]
        x_odd[k] = block[c, gx_odd * (deep - 1)]
    for k, c in enumerate(Y_COMPS):
        for x in range(deep):
            first = block[c, x, 0:1, :]
            last = block[c, x, tall - 1 : tall, :]
            y_even[k, x : x + 1, :] = jnp.where(gy_odd == 0, last, first)
            if two_y:
                y_odd[0][k, x : x + 1, :] = jnp.where(gy_odd == 0, first, last)
    gz = lax.axis_index("gz")
    lane = lane_iota((tall, LANES))
    for c in range(5):
        total = jnp.zeros((tall, LANES), F32)
        for x in range(deep):
            total = jnp.where(lane == x, pltpu.roll(block[c, x], x + 1 - gz, 1), total)
        z_face[c] = total
    kept[...] = block[...]


def notes_kernel(corner, owners, perm, notes, rate):
    rank = lax.axis_index("gy") * lax.axis_size("gz") + lax.axis_index("gz")

    def note(row, value):
        notes[row : row + 1, :] = jnp.full((1, LANES), value, jnp.int32)

    for q in range(PAR):
        for d in range(3):
            note(q * 4 + d, corner[0, 0, q, d])
        note(q * 4 + 3, lax.bitwise_xor(owners[0, q, rank], rank))
    for slot in range(notes.shape[0] - 8):
        live = (owners[0, 0, slot] == rank) | (owners[0, 1, slot] == rank)
        note(8 + slot, live.astype(jnp.int32))
    rate[...] = 0.5 / perm[...]


def leap_kernel(two_y, ranks, *refs):
    block, beside, rate, notes, x_even, x_odd, y_even = refs[:7]
    y_odd = refs[7] if two_y else None
    refs = refs[7 + two_y :]
    new, sends = refs[0], by_rank(refs[1 : 1 + ranks])
    pad, side, mag, fresh, packed = refs[1 + ranks :]
    deep, tall = block.shape[1], block.shape[2]
    full = deep + 2
    gx_odd = lax.rem(lax.axis_index("gx"), 2)
    gy_odd = lax.rem(lax.axis_index("gy"), 2)
    gz = lax.axis_index("gz")
    noted = notes[0:8, :]
    spots = [[noted[q * 4 + d, 0] for d in range(3)] for q in range(PAR)]
    chosen = noted[3, 0]
    lane = lane_iota((tall, LANES))
    keep = ((lane == 0) & (gz == 0)) | ((lane == LANES - 1) & (gz == 1))
    lane = lane_iota((16, LANES))
    none = jnp.zeros((16, LANES), F32)

    def at(c, x):
        return (c * full + x) * 16

    for c in range(6):
        for x in (0, full - 1):
            pad[pl.ds(at(c, x), 16), :] = none
        for x in range(deep):
            pad[pl.ds(at(c, x + 1), tall), :] = block[c, x]
        pad[pl.ds(at(c, 1) + tall, deep, stride=16), :] = none[0:deep]
        pad[pl.ds(at(c, 1) + 15, deep, stride=16), :] = none[0:deep]
    for c in range(5):
        for x in (0, full - 1):
            side[pl.ds(at(c, x), 16), :] = none
        for x in range(deep):
            side[pl.ds(at(c, x + 1), 16), :] = none
            turned = pltpu.roll(beside[c], lax.rem(LANES - x + (LANES - 1) * gz, LANES), 1)
            side[pl.ds(at(c, x + 1), tall), :] = jnp.where(keep, turned, 0.0)
    for k, c in enumerate(X_COMPS):
        even, odd = x_even[k], x_odd[k]
        pad[pl.ds(at(c, 0), tall), :] = jnp.where(gx_odd == 0, odd, even)
        if c in (1, 2):
            pad[pl.ds(at(c, full - 1), tall), :] = jnp.where(gx_odd == 0, even, odd)
    for k, c in enumerate(Y_COMPS):
        even = y_even[k]
        odd = jnp.zeros_like(even) if y_odd is None else y_odd[k]
        pad[pl.ds(at(c, 1) + 15, deep, stride=16), :] = jnp.where(gy_odd == 0, odd, even)
        if c in (0, 2):
            pad[pl.ds(at(c, 1) + tall, deep, stride=16), :] = jnp.where(gy_odd == 0, even, odd)

    def up_y(a):
        return pltpu.roll(a, 15, 0)

    def down_y(a):
        return pltpu.roll(a, 1, 0)

    def plane(c, x):
        return pad[pl.ds(at(c, x), 16), :]

    def edge(c, x):
        return side[pl.ds(at(c, x), 16), :]

    def field(c, x):
        return mag[pl.ds((c * (full - 1) + x) * 16, 16), :]

    for x in range(full - 1):
        e0, e1, e2 = plane(0, x), plane(1, x), plane(2, x)
        s0, s1, s2 = edge(0, x), edge(1, x), edge(2, x)
        r0, r1 = pltpu.roll(e0, LANES - 1, 1), pltpu.roll(e1, LANES - 1, 1)
        u0 = jnp.where(lane == LANES - 1, pltpu.roll(s0, LANES - 1, 1), r0)
        u1 = jnp.where(lane == LANES - 1, pltpu.roll(s1, LANES - 1, 1), r1)
        h0 = plane(3, x) - 0.5 * ((up_y(e2) - e2) - (u1 - e1))
        h1 = plane(4, x) - 0.5 * ((u0 - e0) - (plane(2, x + 1) - e2))
        h2 = plane(5, x) - 0.5 * ((plane(1, x + 1) - e1) - (up_y(e0) - e0))
        t0 = edge(3, x) - 0.5 * ((up_y(s2) - s2) - (r1 - s1))
        t1 = edge(4, x) - 0.5 * ((r0 - s0) - (edge(2, x + 1) - s2))
        d0 = pltpu.roll(jnp.where(lane == LANES - 1, t0, h0), 1, 1)
        d1 = pltpu.roll(jnp.where(lane == LANES - 1, t1, h1), 1, 1)
        for c, value in enumerate((h0, h1, h2, d0, d1)):
            mag[pl.ds((c * (full - 1) + x) * 16, 16), :] = value
    for x in range(deep):
        h0, h1, h2, d0, d1 = (field(c, x + 1) for c in range(5))
        coef = rate[x]
        c0 = (h2 - down_y(h2)) - (h1 - d1)
        c1 = (h0 - d0) - (h2 - field(2, x))
        c2 = (h1 - field(1, x)) - (h0 - down_y(h0))
        for c, curl in enumerate((c0, c1, c2)):
            value = plane(c, x + 1)[0:tall] + coef * curl[0:tall]
            new[c, x] = value
            new[c + 3, x] = (h0, h1, h2)[c][0:tall]
            fresh[pl.ds((c * deep + x) * 16, tall), :] = value
            fresh[pl.ds(((c + 3) * deep + x) * 16, tall), :] = (h0, h1, h2)[c][0:tall]
    lane = lane_iota((8, LANES))
    for q in range(PAR):
        cx, cy, cz = spots[q]

        def rows_of(time, c, k, j, count, over_c):
            source, depth, start = (pad, full, cx) if time == 0 else (fresh, deep, cx - 1)
            step = depth * 16 if over_c else 16
            return source[pl.ds((c * depth + start + k) * 16 + cy + (j - 1), count, stride=step), :]

        def aim(rows, target):
            return pltpu.roll(rows, lax.rem(target - (cz - 1) + 2 * LANES, LANES), 1)

        for c in range(6):
            total = jnp.zeros((8, LANES), F32)
            for j in range(RIM):
                if (j == 0 and c == 4) or (j == RIM - 1 and c not in (0, 2)) or (0 < j < RIM - 1 and c == 5):
                    continue
                for time in range(2):
                    first = rim_lane(time, j, 0)
                    rows = aim(rows_of(time, c, 1, j, 8, False), first)
                    if j in (0, RIM - 1):
                        inside = (lane >= first) & (lane < first + RIM)
                    else:
                        inside = (lane == first) | (lane == first + RIM - 1)
                    total = jnp.where(inside, rows, total)
            packed[q, c * 8 : c * 8 + 8, :] = total
        for time in range(2):
            low = jnp.zeros((6, LANES), F32)
            high = jnp.zeros((2, LANES), F32)
            for j in range(RIM):
                first = j * RIM
                inside = (lane >= first) & (lane < first + RIM)
                low = jnp.where(inside[0:6], aim(rows_of(time, 0, 0, j, 6, True), first), low)
                high = jnp.where(inside[0:2], aim(rows_of(time, 1, RIM - 1, j, 2, True), first), high)
            base = ROWS_RIM + time * 8
            packed[q, base : base + 6, :] = low
            packed[q, base + 6 : base + 8, :] = high
        packed[q, ROW_EDGE:ROWS_PATCH, :] = jnp.zeros((ROWS_PATCH - ROW_EDGE, LANES), F32)
        packed[q, ROW_EDGE : ROW_EDGE + 1, :] = pad[pl.ds(at(1, full - 1) + tall - 1, 1), :]
        packed[q, ROW_EDGE + 1 : ROW_EDGE + 2, :] = pad[pl.ds(at(0, 0), 1), :]
    for k, send in enumerate(sends):
        q = jnp.where(chosen == k, 0, 1)
        send[0:ROWS_PATCH, :] = packed[q]
    half = lane_iota((16, LANES)) < LANES // 2
    send = sends[1]
    send[ROWS_PATCH : ROWS_PATCH + 16, :] = jnp.where(half, plane(0, 0), plane(2, full - 1))
    low = jnp.where(gy_odd == 0, jnp.zeros_like(y_even[1]) if y_odd is None else y_odd[1], y_even[1])
    high = jnp.where(gy_odd == 0, y_even[2], jnp.zeros_like(y_even[2]) if y_odd is None else y_odd[2])
    send[ROWS_PATCH + 16 : ROWS_PATCH + 32, :] = jnp.zeros((16, LANES), F32)
    send[ROWS_PATCH + 16 : ROWS_PATCH + 16 + deep, :] = jnp.where(half[0:deep], low, high)


def places():
    for x in range(PF):
        yield x, (x % 8 + 1) * 8 if x < 8 else (x % 8) * 8 + BATCH


def load_kernel(fine, perm, table, box, rate, lhs, coefs):
    groups = fine.shape[3] // BATCH
    blank = jnp.zeros((8, PF * PF), F32)
    for g in range(groups):
        slots = slice(g * BATCH, (g + 1) * BATCH)
        for c in range(6):
            for row in (0, ROWS_BOX - 8):
                lhs[c * ROWS_BOX + row : c * ROWS_BOX + row + 8, :] = blank
            for x, row in places():
                row += c * ROWS_BOX
                lhs[row : row + BATCH, :] = fine[0, 0, c, slots, x * PF * PF : (x + 1) * PF * PF]
            grown = move(lhs[c * ROWS_BOX : (c + 1) * ROWS_BOX, :], table[...])
            box[g, c] = grown
        for row in (0, ROWS_BOX - 8):
            coefs[row : row + 8, :] = blank
        for x, row in places():
            coefs[row : row + BATCH, :] = 0.5 / perm[0, 0, slots, x * PF * PF : (x + 1) * PF * PF]
        rate[g] = move(coefs[...], table[...])


def fine_kernel(ranks, *refs):
    regions, (box, rate, ghosts, means, out) = refs[:ranks], refs[ranks : ranks + 5]
    smalls = by_rank(refs[ranks + 5 : 2 * ranks + 5])
    rims, walls, now, mag, halves, small = refs[2 * ranks + 5 :]
    groups = box.shape[0]
    rank = lax.axis_index("gy") * lax.axis_size("gz") + lax.axis_index("gz")
    flat = lane_iota((8, WIDE))
    yy = lax.shift_right_logical(flat * 3641, 16)
    zz = flat - yy * LINE
    inner = (yy >= 1) & (yy <= PF) & (zz >= 1) & (zz <= PF)
    upper = lax.broadcasted_iota(jnp.int32, (8, WIDE), 0) >= BATCH

    def inner_of(m):
        if m == 0:
            return inner & upper
        if m == PLANES - 1:
            return inner & jnp.logical_not(upper)
        return inner

    def up_y(a):
        return pltpu.roll(a, WIDE - LINE, 1)

    def up_z(a):
        return pltpu.roll(a, WIDE - 1, 1)

    def down_y(a):
        return pltpu.roll(a, LINE, 1)

    def down_z(a):
        return pltpu.roll(a, 1, 1)

    def rows_of(m):
        return pl.ds(m * 8, 8)

    blank = jnp.zeros((8, LANES), F32)
    for g in range(groups):
        for c in range(6):
            for m in range(PLANES):
                row = ((g * 6 + c) * PLANES + m) * 8
                if m in (0, PLANES - 1):
                    rims[row : row + 8, :] = blank
                walls[0, row : row + 8, :] = blank
                walls[1, row : row + 8, :] = blank
    for k, region in enumerate(regions):
        slot = lax.bitwise_xor(rank, k)
        start = (slot // BATCH) * 6 * ROWS_BOX + lax.rem(slot, BATCH)
        for c in range(6):
            rows = region[c * 8 : c * 8 + 8, :]
            row = start + c * ROWS_BOX
            rims[pl.ds(row + 8, 4, stride=16), :] = rows[0:4]
            rims[pl.ds(row + 16, 4, stride=16), :] = rows[0:4]
            rims[pl.ds(row + BATCH, 4, stride=16), :] = rows[4:8]
            rims[pl.ds(row + BATCH + 8, 4, stride=16), :] = rows[4:8]
        old = region[ROWS_RIM : ROWS_RIM + 8, :]
        fresh = region[ROWS_RIM + 8 : ROWS_RIM + 16, :]
        for sub, value in enumerate((old, old + 0.5 * (fresh - old))):
            walls[sub, pl.ds(start, 6, stride=ROWS_BOX), :] = value[0:6]
            last = start + ROWS_BOX + (PLANES - 1) * 8 + BATCH
            walls[sub, pl.ds(last, 2, stride=ROWS_BOX), :] = value[6:8]
    for g in range(groups):
        for sub in range(2):
            source = box if sub == 0 else out
            for c in range(6):
                rows = pl.ds((g * 6 + c) * ROWS_BOX, ROWS_BOX)
                ghost = move(jnp.concatenate([rims[rows, :], walls[sub, rows, :]], axis=1), ghosts[sub])
                for m in range(PLANES):
                    now[c, rows_of(m), :] = jnp.where(
                        inner_of(m), source[g, c, rows_of(m), :], ghost[m * 8 : (m + 1) * 8]
                    )

            def next_x(c, m):
                if m == PLANES - 1:
                    return pltpu.roll(now[c, rows_of(0), :], BATCH, 0)
                return now[c, rows_of(m + 1), :]

            def last_x(c, m):
                if m == 0:
                    return pltpu.roll(mag[c, rows_of(PLANES - 1), :], BATCH, 0)
                return mag[c, rows_of(m - 1), :]

            for m in range(PLANES):
                e0, e1, e2 = (now[c, rows_of(m), :] for c in range(3))
                h0, h1, h2 = (now[c, rows_of(m), :] for c in range(3, 6))
                mag[0, rows_of(m), :] = h0 - 0.5 * ((up_y(e2) - e2) - (up_z(e1) - e1))
                mag[1, rows_of(m), :] = h1 - 0.5 * ((up_z(e0) - e0) - (next_x(2, m) - e2))
                mag[2, rows_of(m), :] = h2 - 0.5 * ((next_x(1, m) - e1) - (up_y(e0) - e0))
            for m in range(PLANES):
                h0, h1, h2 = (mag[c, rows_of(m), :] for c in range(3))
                coef = rate[g, rows_of(m), :]
                e0, e1, e2 = (now[c, rows_of(m), :] for c in range(3))
                out[g, 0, rows_of(m), :] = e0 + coef * ((h2 - down_y(h2)) - (h1 - down_z(h1)))
                out[g, 1, rows_of(m), :] = e1 + coef * ((h0 - down_z(h0)) - (h2 - last_x(2, m)))
                out[g, 2, rows_of(m), :] = e2 + coef * ((h1 - last_x(1, m)) - (h0 - down_y(h0)))
                for c, value in enumerate((h0, h1, h2)):
                    out[g, c + 3, rows_of(m), :] = value
        for c in range(6):
            for k in range(4):
                other = jnp.where(upper, out[g, c, rows_of(2 * k), :], out[g, c, rows_of(2 * k + 2), :])
                pair = out[g, c, rows_of(2 * k + 1), :] + other
                halves[pl.ds((c * 2 + k // 2) * 8, 8), (k % 2) * WIDE : (k % 2 + 1) * WIDE] = pair
        small[pl.ds(g * 96, 96), :] = move(halves[...], means[...])
    for k, send in enumerate(smalls):
        slot = lax.bitwise_xor(rank, k)
        start = (slot // BATCH) * 96 + lax.rem(slot, BATCH)
        for xh in range(2):
            send[xh * 12 : (xh + 1) * 12, :] = small[pl.ds(start + xh * BATCH, 12, stride=8), :]


def store_kernel(box, fine, notes, table, out, stage, sems):
    groups = box.shape[0]
    slots = groups * BATCH
    live = jnp.concatenate([notes[8 : 8 + slots, :]] * (PF * PF // LANES), axis=1) > 0
    copies = []
    for c in range(6):
        flats = [move(box[g, c], table[...]) for g in range(groups)]
        for x, row in places():
            cut = slice(x * PF * PF, (x + 1) * PF * PF)
            for g, flat in enumerate(flats):
                some = slice(g * BATCH, (g + 1) * BATCH)
                stage[0, 0, c, some, cut] = jnp.where(live[some], flat[row : row + BATCH], fine[0, 0, c, some, cut])
        copies.append(pltpu.make_async_copy(stage.at[:, :, c], out.at[:, :, c], sems.at[c]))
        copies[-1].start()
    for copy in copies:
        copy.wait()


def fix_kernel(new, rate, *refs):
    edges, out = refs[:-1], refs[-1]
    deep, tall = new.shape[1], new.shape[2]
    gz = lax.axis_index("gz")
    rank = lax.axis_index("gy") * 2 + gz
    out[...] = new[...]

    def add(c, x, rows, amount):
        out[c, x, rows, :] = out[c, x, rows, :] + 0.5 * rate[x, rows, :] * amount

    lower = higher = jnp.zeros((1, LANES), F32)
    for k, edge in enumerate(edges, 1):
        row = ROW_EDGE
        lower = jnp.where(lax.bitwise_xor(rank, k) == rank - 2, edge[row : row + 1, :], lower)
        higher = jnp.where(lax.bitwise_xor(rank, k) == rank + 2, edge[row + 1 : row + 2, :], higher)
    add(0, deep - 1, slice(0, 1), lower)
    add(1, 0, slice(tall - 1, tall), higher)
    lane = lane_iota((tall, LANES))
    tile = edges[0][ROWS_PATCH : ROWS_PATCH + tall, :]
    add(0, deep - 1, slice(0, tall), jnp.where((lane == 0) & (gz == 1), pltpu.roll(tile, 1, 1), 0.0))
    add(2, 0, slice(0, tall), jnp.where((lane == LANES - 1) & (gz == 0), pltpu.roll(tile, LANES - 1, 1), 0.0))
    lane = lane_iota((deep, LANES))
    tile = edges[0][ROWS_PATCH + 16 : ROWS_PATCH + 16 + deep, :]
    first = jnp.where((lane == LANES - 1) & (gz == 0), pltpu.roll(tile, LANES - 1, 1), 0.0)
    last = jnp.where((lane == 0) & (gz == 1), pltpu.roll(tile, 1, 1), 0.0)
    for x in range(deep):
        add(2, x, slice(0, 1), first[x : x + 1])
        add(1, x, slice(tall - 1, tall), last[x : x + 1])


def place_kernel(ranks, new, notes, *refs):
    means, (out, spread, stage, gathered, sems) = refs[:ranks], refs[ranks:]
    noted = notes[0:8, :]
    for k, mean in enumerate(means):
        gathered[k] = mean[...]
    lane = lane_iota((HALF, LANES))
    spots = [tuple(noted[q * 4 + d, 0] for d in range(3)) for q in range(PAR)]
    for q, (cx, cy, cz) in enumerate(spots):
        k = noted[q * 4 + 3, 0]
        rows = gathered[k]
        for odd in range(2):
            for y in range(HALF):
                shift = lax.rem(cz - y * HALF - odd * HALF * HALF + 2 * LANES, LANES)
                spread[q, pl.ds(odd * 192 + y, 24, stride=8), :] = pltpu.roll(rows, shift, 1)
    copies = []
    for c in range(6):
        stage[c] = new[c]
        for q, (cx, cy, cz) in enumerate(spots):
            inside = (lane >= cz) & (lane < cz + HALF)
            for x in range(HALF):
                xh, k = x // 4, x % 4
                tile = spread[q, pl.ds((k % 2) * 192 + (xh * 12 + c * 2 + k // 2) * 8, 8), :]
                spot = stage[c, cx + x, pl.ds(cy, HALF), :]
                stage[c, cx + x, pl.ds(cy, HALF), :] = jnp.where(inside, tile, spot)
        copies.append(pltpu.make_async_copy(stage.at[c], out.at[c], sems.at[c]))
        copies[-1].start()
    for copy in copies:
        copy.wait()


def local(coarse_fields, permittivity, fine_fields, fine_permittivity, patch_corner, patch_owner):
    deep, tall, cols = coarse_fields.shape[1:]
    slots = fine_fields.shape[2]
    groups = slots // BATCH
    count_x, count_y = lax.axis_size("gx"), lax.axis_size("gy")
    two_y = count_y > 2
    vmem = whole()
    shape = jax.ShapeDtypeStruct
    grow = grow_table()

    x_face = shape((5, tall, cols), F32)
    y_face = shape((5, deep, cols), F32)
    kept, *faces = call(
        functools.partial(faces_kernel, two_y),
        [shape(coarse_fields.shape, F32), x_face, x_face, y_face] + [y_face] * two_y + [shape((5, tall, cols), F32)],
        [vmem],
    )(coarse_fields)
    got = [
        lax.ppermute(faces[0], "gx", swap_pairs(count_x, 0)),
        lax.ppermute(faces[1], "gx", swap_pairs(count_x, 1)),
        lax.ppermute(faces[2], "gy", swap_pairs(count_y, 0)),
    ]
    if two_y:
        got.append(lax.ppermute(faces[3], "gy", swap_pairs(count_y, 1)))
    beside = lax.ppermute(faces[-1], "gz", swap_pairs(2, 0))

    fine = fine_fields.transpose(0, 1, 3, 2, 4)
    notes, rate = call(
        notes_kernel,
        [shape((8 + slots, LANES), jnp.int32), shape(permittivity.shape, F32)],
        [whole(pltpu.SMEM)] * 2 + [vmem],
    )(patch_corner, patch_owner.transpose(0, 2, 1), permittivity)
    box, fine_rate = call(
        load_kernel,
        [shape((groups, 6, ROWS_BOX, WIDE), F32), shape((groups, ROWS_BOX, WIDE), F32)],
        [vmem] * 3,
        [pltpu.VMEM((6 * ROWS_BOX, PF * PF), F32), pltpu.VMEM((ROWS_BOX, PF * PF), F32)],
        size=4_000_000,
    )(fine, fine_permittivity, jnp.asarray(grow, BF16))

    full = deep + 2
    ranks = count_y * lax.axis_size("gz")

    def exchange(parts):
        swaps = [[(r, r ^ k) for r in range(ranks)] for k in range(ranks)]
        got = list(parts)
        for k in [*range(2, ranks), 1]:
            got[k] = lax.ppermute(parts[k], ("gy", "gz"), swaps[k])
        return got

    patches = [shape((ROWS_BESIDE if k == 1 else ROWS_PATCH, LANES), F32) for k in range(ranks)]
    new, *sends = call(
        functools.partial(leap_kernel, two_y, ranks),
        [shape(coarse_fields.shape, F32)] + far_first(patches),
        [vmem] * (4 + len(got)),
        [
            pltpu.VMEM((6 * full * 16, LANES), F32),
            pltpu.VMEM((6 * full * 16, LANES), F32),
            pltpu.VMEM((5 * (full - 1) * 16, LANES), F32),
            pltpu.VMEM((6 * deep * 16, LANES), F32),
            pltpu.VMEM((PAR, ROWS_PATCH, LANES), F32),
        ],
    )(kept, beside, rate, notes, *got)
    regions = exchange(by_rank(sends))

    box, *smalls = call(
        functools.partial(fine_kernel, ranks),
        [shape((groups, 6, ROWS_BOX, WIDE), F32)] + [shape((24, LANES), F32)] * ranks,
        [vmem] * (ranks + 4),
        [
            pltpu.VMEM((groups * 6 * ROWS_BOX, LANES), F32),
            pltpu.VMEM((2, groups * 6 * ROWS_BOX, LANES), F32),
            pltpu.VMEM((6, ROWS_BOX, WIDE), F32),
            pltpu.VMEM((3, ROWS_BOX, WIDE), F32),
            pltpu.VMEM((96, 2 * WIDE), F32),
            pltpu.VMEM((groups * 96, LANES), F32),
        ],
    )(*regions, box, fine_rate, jnp.asarray(ghost_table(), BF16), jnp.asarray(mean_table(), BF16))
    means = exchange(by_rank(smalls))

    fine = call(
        store_kernel,
        shape(fine.shape, F32),
        [vmem] * 4,
        [pltpu.VMEM(fine.shape, F32), pltpu.SemaphoreType.DMA((6,))],
        size=4_000_000,
        out_specs=whole(pltpu.HBM),
    )(box, fine, notes, jnp.asarray(grow.T, BF16))
    new = call(fix_kernel, shape(coarse_fields.shape, F32), [vmem] * (1 + ranks))(new, rate, *regions[1:])
    coarse = call(
        functools.partial(place_kernel, ranks),
        shape(coarse_fields.shape, F32),
        [vmem] * (2 + ranks),
        [
            pltpu.VMEM((PAR, 4 * 96, LANES), F32),
            pltpu.VMEM(coarse_fields.shape, F32),
            pltpu.VMEM((ranks, 24, LANES), F32),
            pltpu.SemaphoreType.DMA((6,)),
        ],
        out_specs=whole(pltpu.HBM),
    )(new, notes, *means)
    return coarse, fine.transpose(0, 1, 3, 2, 4)


def solution(mesh):
    in_specs = (
        P(None, ("groups", "gx"), "gy", "gz"),
        P(("groups", "gx"), "gy", "gz"),
        P(("groups", "gx"), "gy", "gz", None, None),
        P(("groups", "gx"), "gy", "gz", None),
        P(("groups", "gx"), "gy", "gz", None),
        P(("groups", "gx"), None, None),
    )
    out_specs = (P(None, ("groups", "gx"), "gy", "gz"), P(("groups", "gx"), "gy", "gz", None, None))
    return jax.shard_map(local, mesh=mesh, in_specs=in_specs, out_specs=out_specs, check_vma=False)
```

```python
import functools
import jax
import jax.numpy as jnp
import numpy as np
from jax import lax
from jax.experimental import pallas as pl
from jax.experimental.pallas import tpu as pltpu
from jax.sharding import PartitionSpec as P

PF = 16
PAR = 2
HALF = PF // 2
RIM = HALF + 2
PLANES = 9
LINE = PF + 2
LANES = 128
WIDE = 384
BATCH = 4
ROWS_BOX = PLANES * 8
ROWS_RIM = 48
ROW_EDGE = 64
ROWS_PATCH = 72
ROWS_BESIDE = 104
X_COMPS = (0, 1, 2, 4, 5)
Y_COMPS = (0, 1, 2, 3, 5)
VMEM_BYTES = 48 * 1024 * 1024
F32 = jnp.float32
BF16 = jnp.bfloat16


def rim_lane(time, j, k):
    if 0 < j < RIM - 1:
        return j * RIM + k + 3 * time
    if j == 0 and time == 0:
        return k
    return (RIM - 1) * RIM + 3 + (2 * time + j // (RIM - 1) - 1) * RIM + k


def grow_table():
    table = np.zeros((PF * PF, WIDE), np.float32)
    for y in range(PF):
        for z in range(PF):
            table[y * PF + z, (y + 1) * LINE + z + 1] = 1.0
    return table


def ghost_table():
    table = np.zeros((2, 2 * LANES, WIDE), np.float32)
    for y in range(LINE):
        for z in range(LINE):
            j, k, lane = (y + 1) // 2, (z + 1) // 2, y * LINE + z
            table[:, LANES + j * RIM + k, lane] = 1.0
            if y in (0, LINE - 1) or z in (0, LINE - 1):
                table[0, rim_lane(0, j, k), lane] = 1.0
                table[1, rim_lane(0, j, k), lane] = 0.5
                table[1, rim_lane(1, j, k), lane] = 0.5
    return table


def mean_table():
    table = np.zeros((2, WIDE, LANES), np.float32)
    for odd in range(2):
        for y in range(PF):
            for z in range(PF):
                lane = odd * HALF * HALF + (y // 2) * HALF + z // 2
                table[odd, (y + 1) * LINE + z + 1, lane] = 0.125
    return table.reshape(2 * WIDE, LANES)


def move(rows, table):
    high = rows.astype(BF16)
    low = (rows - high.astype(F32)).astype(BF16)
    out = jnp.dot(high, table, preferred_element_type=F32)
    return out + jnp.dot(low, table, preferred_element_type=F32)


def lane_iota(shape):
    return lax.broadcasted_iota(jnp.int32, shape, len(shape) - 1)


def whole(memory_space=pltpu.VMEM):
    return pl.BlockSpec(memory_space=memory_space)


def call(kernel, outs, in_specs, scratch=(), flops=1_000_000, size=1_000_000, out_specs=None, **extra):
    return pl.pallas_call(
        kernel,
        out_shape=outs,
        in_specs=in_specs,
        out_specs=jax.tree.map(lambda _: whole(), outs) if out_specs is None else out_specs,
        scratch_shapes=list(scratch),
        compiler_params=pltpu.CompilerParams(vmem_limit_bytes=VMEM_BYTES),
        cost_estimate=pl.CostEstimate(flops=flops, bytes_accessed=size, transcendentals=0),
        **extra,
    )


def swap_pairs(count, first):
    pairs = []
    for i in range(first, count - 1, 2):
        pairs += [(i, i + 1), (i + 1, i)]
    return pairs


def full_pairs(count_x, count_y):
    pairs = []
    for i in range(count_x):
        for j in range(count_y):
            if 0 < i < count_x - 1:
                target = (i + 1 if i % 2 else i - 1) * count_y + j
            else:
                target = i * count_y + (j ^ 1)
            pairs.append((i * count_y + j, target))
    return pairs


def faces_kernel(two_y, block, kept, x_even, x_odd, y_even, *y_odd):
    deep, tall = block.shape[1], block.shape[2]
    gx_odd = lax.rem(lax.axis_index("gx"), 2)
    gy_odd = lax.rem(lax.axis_index("gy"), 2)
    for k, c in enumerate(X_COMPS):
        x_even[k] = block[c, (1 - gx_odd) * (deep - 1)]
        x_odd[k] = block[c, gx_odd * (deep - 1)]
    for k, c in enumerate(Y_COMPS):
        for x in range(deep):
            first = block[c, x, 0:1, :]
            last = block[c, x, tall - 1 : tall, :]
            y_even[k, x : x + 1, :] = jnp.where(gy_odd == 0, last, first)
            if two_y:
                y_odd[0][k, x : x + 1, :] = jnp.where(gy_odd == 0, first, last)
    kept[...] = block[...]


def notes_kernel(corner, owners, perm, notes, rate):
    rank = lax.axis_index("gy") * lax.axis_size("gz") + lax.axis_index("gz")

    def note(row, value):
        notes[row : row + 1, :] = jnp.full((1, LANES), value, jnp.int32)

    for q in range(PAR):
        for d in range(3):
            note(q * 4 + d, corner[0, 0, q, d])
        note(q * 4 + 3, lax.bitwise_xor(owners[0, q, rank], rank))
    for slot in range(notes.shape[0] - 8):
        live = (owners[0, 0, slot] == rank) | (owners[0, 1, slot] == rank)
        note(8 + slot, live.astype(jnp.int32))
    rate[...] = 0.5 / perm[...]


def leap_kernel(two_y, ranks, *refs):
    block, beside, rate, notes, x_even, x_odd, y_even = refs[:7]
    y_odd = refs[7] if two_y else None
    refs = refs[7 + two_y :]
    new, sends = refs[0], refs[1 : 1 + ranks]
    pad, side, mag, fresh, packed = refs[1 + ranks :]
    deep, tall = block.shape[1], block.shape[2]
    full = deep + 2
    gx = lax.axis_index("gx")
    gx_odd = lax.rem(gx, 2)
    gy_odd = lax.rem(lax.axis_index("gy"), 2)
    gz = lax.axis_index("gz")
    noted = notes[0:8, :]
    spots = [[noted[q * 4 + d, 0] for d in range(3)] for q in range(PAR)]
    chosen = noted[3, 0]
    lane = lane_iota((tall, LANES))
    keep = ((lane == 0) & (gz == 0)) | ((lane == LANES - 1) & (gz == 1))
    lane = lane_iota((16, LANES))
    none = jnp.zeros((16, LANES), F32)

    def at(c, x):
        return (c * full + x) * 16

    for c in range(6):
        for x in (0, full - 1):
            pad[pl.ds(at(c, x), 16), :] = none
        for x in range(deep):
            pad[pl.ds(at(c, x + 1), tall), :] = block[c, x]
        pad[pl.ds(at(c, 1) + tall, deep, stride=16), :] = none[0:deep]
        pad[pl.ds(at(c, 1) + 15, deep, stride=16), :] = none[0:deep]
    for c in range(5):
        for x in (0, full - 1):
            side[pl.ds(at(c, x), 16), :] = none
        for x in range(deep):
            side[pl.ds(at(c, x + 1), 16), :] = none
            side[pl.ds(at(c, x + 1), tall), :] = jnp.where(keep, beside[c, x], 0.0)
    for k, c in enumerate(X_COMPS):
        even, odd = x_even[k], x_odd[k]
        low, high = jnp.where(gx_odd == 0, odd, even), jnp.where(gx_odd == 0, even, odd)
        pad[pl.ds(at(c, 0), tall), :] = jnp.where(gx == 0, 0.0, low)
        if c in (1, 2):
            pad[pl.ds(at(c, full - 1), tall), :] = jnp.where(gx == lax.axis_size("gx") - 1, 0.0, high)
    for k, c in enumerate(Y_COMPS):
        even = y_even[k]
        odd = jnp.zeros_like(even) if y_odd is None else y_odd[k]
        pad[pl.ds(at(c, 1) + 15, deep, stride=16), :] = jnp.where(gy_odd == 0, odd, even)
        if c in (0, 2):
            pad[pl.ds(at(c, 1) + tall, deep, stride=16), :] = jnp.where(gy_odd == 0, even, odd)

    def up_y(a):
        return pltpu.roll(a, 15, 0)

    def down_y(a):
        return pltpu.roll(a, 1, 0)

    def plane(c, x):
        return pad[pl.ds(at(c, x), 16), :]

    def edge(c, x):
        return side[pl.ds(at(c, x), 16), :]

    def field(c, x):
        return mag[pl.ds((c * (full - 1) + x) * 16, 16), :]

    for x in range(full - 1):
        e0, e1, e2 = plane(0, x), plane(1, x), plane(2, x)
        s0, s1, s2 = edge(0, x), edge(1, x), edge(2, x)
        r0, r1 = pltpu.roll(e0, LANES - 1, 1), pltpu.roll(e1, LANES - 1, 1)
        u0 = jnp.where(lane == LANES - 1, pltpu.roll(s0, LANES - 1, 1), r0)
        u1 = jnp.where(lane == LANES - 1, pltpu.roll(s1, LANES - 1, 1), r1)
        h0 = plane(3, x) - 0.5 * ((up_y(e2) - e2) - (u1 - e1))
        h1 = plane(4, x) - 0.5 * ((u0 - e0) - (plane(2, x + 1) - e2))
        h2 = plane(5, x) - 0.5 * ((plane(1, x + 1) - e1) - (up_y(e0) - e0))
        t0 = edge(3, x) - 0.5 * ((up_y(s2) - s2) - (r1 - s1))
        t1 = edge(4, x) - 0.5 * ((r0 - s0) - (edge(2, x + 1) - s2))
        d0 = pltpu.roll(jnp.where(lane == LANES - 1, t0, h0), 1, 1)
        d1 = pltpu.roll(jnp.where(lane == LANES - 1, t1, h1), 1, 1)
        for c, value in enumerate((h0, h1, h2, d0, d1)):
            mag[pl.ds((c * (full - 1) + x) * 16, 16), :] = value
    for x in range(deep):
        h0, h1, h2, d0, d1 = (field(c, x + 1) for c in range(5))
        coef = rate[x]
        c0 = (h2 - down_y(h2)) - (h1 - d1)
        c1 = (h0 - d0) - (h2 - field(2, x))
        c2 = (h1 - field(1, x)) - (h0 - down_y(h0))
        for c, curl in enumerate((c0, c1, c2)):
            value = plane(c, x + 1)[0:tall] + coef * curl[0:tall]
            new[c, x] = value
            new[c + 3, x] = (h0, h1, h2)[c][0:tall]
            fresh[pl.ds((c * deep + x) * 16, tall), :] = value
            fresh[pl.ds(((c + 3) * deep + x) * 16, tall), :] = (h0, h1, h2)[c][0:tall]
    lane = lane_iota((8, LANES))
    for q in range(PAR):
        cx, cy, cz = spots[q]

        def rows_of(time, c, k, j, count, over_c):
            source, depth, start = (pad, full, cx) if time == 0 else (fresh, deep, cx - 1)
            step = depth * 16 if over_c else 16
            return source[pl.ds((c * depth + start + k) * 16 + cy + (j - 1), count, stride=step), :]

        def aim(rows, target):
            return pltpu.roll(rows, lax.rem(target - (cz - 1) + 2 * LANES, LANES), 1)

        for c in range(6):
            total = jnp.zeros((8, LANES), F32)
            for j in range(RIM):
                if (j == 0 and c == 4) or (j == RIM - 1 and c not in (0, 2)) or (0 < j < RIM - 1 and c == 5):
                    continue
                for time in range(2):
                    first = rim_lane(time, j, 0)
                    rows = aim(rows_of(time, c, 1, j, 8, False), first)
                    if j in (0, RIM - 1):
                        inside = (lane >= first) & (lane < first + RIM)
                    else:
                        inside = (lane == first) | (lane == first + RIM - 1)
                    total = jnp.where(inside, rows, total)
            packed[q, c * 8 : c * 8 + 8, :] = total
        for time in range(2):
            low = jnp.zeros((6, LANES), F32)
            high = jnp.zeros((2, LANES), F32)
            for j in range(RIM):
                first = j * RIM
                inside = (lane >= first) & (lane < first + RIM)
                low = jnp.where(inside[0:6], aim(rows_of(time, 0, 0, j, 6, True), first), low)
                high = jnp.where(inside[0:2], aim(rows_of(time, 1, RIM - 1, j, 2, True), first), high)
            base = ROWS_RIM + time * 8
            packed[q, base : base + 6, :] = low
            packed[q, base + 6 : base + 8, :] = high
        packed[q, ROW_EDGE:ROWS_PATCH, :] = jnp.zeros((ROWS_PATCH - ROW_EDGE, LANES), F32)
        packed[q, ROW_EDGE : ROW_EDGE + 1, :] = pad[pl.ds(at(1, full - 1) + tall - 1, 1), :]
        packed[q, ROW_EDGE + 1 : ROW_EDGE + 2, :] = pad[pl.ds(at(0, 0), 1), :]
    for k, send in enumerate(sends):
        q = jnp.where(chosen == k, 0, 1)
        send[0:ROWS_PATCH, :] = packed[q]
    half = lane_iota((16, LANES)) < LANES // 2
    send = sends[1]
    send[ROWS_PATCH : ROWS_PATCH + 16, :] = jnp.where(half, plane(0, 0), plane(2, full - 1))
    low = jnp.where(gy_odd == 0, jnp.zeros_like(y_even[1]) if y_odd is None else y_odd[1], y_even[1])
    high = jnp.where(gy_odd == 0, y_even[2], jnp.zeros_like(y_even[2]) if y_odd is None else y_odd[2])
    send[ROWS_PATCH + 16 : ROWS_PATCH + 32, :] = jnp.zeros((16, LANES), F32)
    send[ROWS_PATCH + 16 : ROWS_PATCH + 16 + deep, :] = jnp.where(half[0:deep], low, high)


def places():
    for x in range(PF):
        yield x, (x % 8 + 1) * 8 if x < 8 else (x % 8) * 8 + BATCH


def load_kernel(fine, perm, table, box, rate, lhs, coefs):
    groups = fine.shape[3] // BATCH
    blank = jnp.zeros((8, PF * PF), F32)
    for g in range(groups):
        slots = slice(g * BATCH, (g + 1) * BATCH)
        for c in range(6):
            for row in (0, ROWS_BOX - 8):
                lhs[c * ROWS_BOX + row : c * ROWS_BOX + row + 8, :] = blank
            for x, row in places():
                row += c * ROWS_BOX
                lhs[row : row + BATCH, :] = fine[0, 0, c, slots, x * PF * PF : (x + 1) * PF * PF]
            grown = move(lhs[c * ROWS_BOX : (c + 1) * ROWS_BOX, :], table[...])
            box[g, c] = grown
        for row in (0, ROWS_BOX - 8):
            coefs[row : row + 8, :] = blank
        for x, row in places():
            coefs[row : row + BATCH, :] = 0.5 / perm[0, 0, slots, x * PF * PF : (x + 1) * PF * PF]
        rate[g] = move(coefs[...], table[...])


def fine_kernel(ranks, *refs):
    regions, (box, rate, ghosts, means, out) = refs[:ranks], refs[ranks : ranks + 5]
    smalls = refs[ranks + 5 : 2 * ranks + 5]
    rims, walls, now, mag, halves, small = refs[2 * ranks + 5 :]
    groups = box.shape[0]
    rank = lax.axis_index("gy") * lax.axis_size("gz") + lax.axis_index("gz")
    flat = lane_iota((8, WIDE))
    yy = lax.shift_right_logical(flat * 3641, 16)
    zz = flat - yy * LINE
    inner = (yy >= 1) & (yy <= PF) & (zz >= 1) & (zz <= PF)
    upper = lax.broadcasted_iota(jnp.int32, (8, WIDE), 0) >= BATCH

    def inner_of(m):
        if m == 0:
            return inner & upper
        if m == PLANES - 1:
            return inner & jnp.logical_not(upper)
        return inner

    def up_y(a):
        return pltpu.roll(a, WIDE - LINE, 1)

    def up_z(a):
        return pltpu.roll(a, WIDE - 1, 1)

    def down_y(a):
        return pltpu.roll(a, LINE, 1)

    def down_z(a):
        return pltpu.roll(a, 1, 1)

    def rows_of(m):
        return pl.ds(m * 8, 8)

    blank = jnp.zeros((8, LANES), F32)
    for g in range(groups):
        for c in range(6):
            for m in range(PLANES):
                row = ((g * 6 + c) * PLANES + m) * 8
                if m in (0, PLANES - 1):
                    rims[row : row + 8, :] = blank
                walls[0, row : row + 8, :] = blank
                walls[1, row : row + 8, :] = blank
    for k, region in enumerate(regions):
        slot = lax.bitwise_xor(rank, k)
        start = (slot // BATCH) * 6 * ROWS_BOX + lax.rem(slot, BATCH)
        for c in range(6):
            rows = region[c * 8 : c * 8 + 8, :]
            row = start + c * ROWS_BOX
            rims[pl.ds(row + 8, 4, stride=16), :] = rows[0:4]
            rims[pl.ds(row + 16, 4, stride=16), :] = rows[0:4]
            rims[pl.ds(row + BATCH, 4, stride=16), :] = rows[4:8]
            rims[pl.ds(row + BATCH + 8, 4, stride=16), :] = rows[4:8]
        old = region[ROWS_RIM : ROWS_RIM + 8, :]
        fresh = region[ROWS_RIM + 8 : ROWS_RIM + 16, :]
        for sub, value in enumerate((old, old + 0.5 * (fresh - old))):
            walls[sub, pl.ds(start, 6, stride=ROWS_BOX), :] = value[0:6]
            last = start + ROWS_BOX + (PLANES - 1) * 8 + BATCH
            walls[sub, pl.ds(last, 2, stride=ROWS_BOX), :] = value[6:8]
    for g in range(groups):
        for sub in range(2):
            source = box if sub == 0 else out
            for c in range(6):
                rows = pl.ds((g * 6 + c) * ROWS_BOX, ROWS_BOX)
                ghost = move(jnp.concatenate([rims[rows, :], walls[sub, rows, :]], axis=1), ghosts[sub])
                for m in range(PLANES):
                    now[c, rows_of(m), :] = jnp.where(
                        inner_of(m), source[g, c, rows_of(m), :], ghost[m * 8 : (m + 1) * 8]
                    )

            def next_x(c, m):
                if m == PLANES - 1:
                    return pltpu.roll(now[c, rows_of(0), :], BATCH, 0)
                return now[c, rows_of(m + 1), :]

            def last_x(c, m):
                if m == 0:
                    return pltpu.roll(mag[c, rows_of(PLANES - 1), :], BATCH, 0)
                return mag[c, rows_of(m - 1), :]

            for m in range(PLANES):
                e0, e1, e2 = (now[c, rows_of(m), :] for c in range(3))
                h0, h1, h2 = (now[c, rows_of(m), :] for c in range(3, 6))
                mag[0, rows_of(m), :] = h0 - 0.5 * ((up_y(e2) - e2) - (up_z(e1) - e1))
                mag[1, rows_of(m), :] = h1 - 0.5 * ((up_z(e0) - e0) - (next_x(2, m) - e2))
                mag[2, rows_of(m), :] = h2 - 0.5 * ((next_x(1, m) - e1) - (up_y(e0) - e0))
            for m in range(PLANES):
                h0, h1, h2 = (mag[c, rows_of(m), :] for c in range(3))
                coef = rate[g, rows_of(m), :]
                e0, e1, e2 = (now[c, rows_of(m), :] for c in range(3))
                out[g, 0, rows_of(m), :] = e0 + coef * ((h2 - down_y(h2)) - (h1 - down_z(h1)))
                out[g, 1, rows_of(m), :] = e1 + coef * ((h0 - down_z(h0)) - (h2 - last_x(2, m)))
                out[g, 2, rows_of(m), :] = e2 + coef * ((h1 - last_x(1, m)) - (h0 - down_y(h0)))
                for c, value in enumerate((h0, h1, h2)):
                    out[g, c + 3, rows_of(m), :] = value
        for c in range(6):
            for k in range(4):
                other = jnp.where(upper, out[g, c, rows_of(2 * k), :], out[g, c, rows_of(2 * k + 2), :])
                pair = out[g, c, rows_of(2 * k + 1), :] + other
                halves[pl.ds((c * 2 + k // 2) * 8, 8), (k % 2) * WIDE : (k % 2 + 1) * WIDE] = pair
        small[pl.ds(g * 96, 96), :] = move(halves[...], means[...])
    for k, send in enumerate(smalls):
        slot = lax.bitwise_xor(rank, k)
        start = (slot // BATCH) * 96 + lax.rem(slot, BATCH)
        for xh in range(2):
            send[xh * 12 : (xh + 1) * 12, :] = small[pl.ds(start + xh * BATCH, 12, stride=8), :]


def store_kernel(box, fine, notes, table, out, stage, sems):
    groups = box.shape[0]
    slots = groups * BATCH
    live = jnp.concatenate([notes[8 : 8 + slots, :]] * (PF * PF // LANES), axis=1) > 0
    copies = []
    for c in range(6):
        flats = [move(box[g, c], table[...]) for g in range(groups)]
        for x, row in places():
            cut = slice(x * PF * PF, (x + 1) * PF * PF)
            for g, flat in enumerate(flats):
                some = slice(g * BATCH, (g + 1) * BATCH)
                stage[0, 0, c, some, cut] = jnp.where(live[some], flat[row : row + BATCH], fine[0, 0, c, some, cut])
        copies.append(pltpu.make_async_copy(stage.at[:, :, c], out.at[:, :, c], sems.at[c]))
        copies[-1].start()
    for copy in copies:
        copy.wait()


def fix_kernel(new, rate, *refs):
    edges, out = refs[:-1], refs[-1]
    deep, tall = new.shape[1], new.shape[2]
    gz = lax.axis_index("gz")
    rank = lax.axis_index("gy") * 2 + gz
    out[...] = new[...]

    def add(c, x, rows, amount):
        out[c, x, rows, :] = out[c, x, rows, :] + 0.5 * rate[x, rows, :] * amount

    lower = higher = jnp.zeros((1, LANES), F32)
    for k, edge in enumerate(edges, 1):
        row = ROW_EDGE
        lower = jnp.where(lax.bitwise_xor(rank, k) == rank - 2, edge[row : row + 1, :], lower)
        higher = jnp.where(lax.bitwise_xor(rank, k) == rank + 2, edge[row + 1 : row + 2, :], higher)
    add(0, deep - 1, slice(0, 1), lower)
    add(1, 0, slice(tall - 1, tall), higher)
    lane = lane_iota((tall, LANES))
    tile = edges[0][ROWS_PATCH : ROWS_PATCH + tall, :]
    add(0, deep - 1, slice(0, tall), jnp.where((lane == 0) & (gz == 1), pltpu.roll(tile, 1, 1), 0.0))
    add(2, 0, slice(0, tall), jnp.where((lane == LANES - 1) & (gz == 0), pltpu.roll(tile, LANES - 1, 1), 0.0))
    lane = lane_iota((deep, LANES))
    tile = edges[0][ROWS_PATCH + 16 : ROWS_PATCH + 16 + deep, :]
    first = jnp.where((lane == LANES - 1) & (gz == 0), pltpu.roll(tile, LANES - 1, 1), 0.0)
    last = jnp.where((lane == 0) & (gz == 1), pltpu.roll(tile, 1, 1), 0.0)
    for x in range(deep):
        add(2, x, slice(0, 1), first[x : x + 1])
        add(1, x, slice(tall - 1, tall), last[x : x + 1])


def place_kernel(ranks, new, notes, *refs):
    means, (out, spread, stage, gathered, sems) = refs[:ranks], refs[ranks:]
    noted = notes[0:8, :]
    for k, mean in enumerate(means):
        gathered[k] = mean[...]
    lane = lane_iota((HALF, LANES))
    spots = [tuple(noted[q * 4 + d, 0] for d in range(3)) for q in range(PAR)]
    for q, (cx, cy, cz) in enumerate(spots):
        k = noted[q * 4 + 3, 0]
        rows = gathered[k]
        for odd in range(2):
            for y in range(HALF):
                shift = lax.rem(cz - y * HALF - odd * HALF * HALF + 2 * LANES, LANES)
                spread[q, pl.ds(odd * 192 + y, 24, stride=8), :] = pltpu.roll(rows, shift, 1)
    copies = []
    for c in range(6):
        stage[c] = new[c]
        for q, (cx, cy, cz) in enumerate(spots):
            inside = (lane >= cz) & (lane < cz + HALF)
            for x in range(HALF):
                xh, k = x // 4, x % 4
                tile = spread[q, pl.ds((k % 2) * 192 + (xh * 12 + c * 2 + k // 2) * 8, 8), :]
                spot = stage[c, cx + x, pl.ds(cy, HALF), :]
                stage[c, cx + x, pl.ds(cy, HALF), :] = jnp.where(inside, tile, spot)
        copies.append(pltpu.make_async_copy(stage.at[c], out.at[c], sems.at[c]))
        copies[-1].start()
    for copy in copies:
        copy.wait()


def local(coarse_fields, permittivity, fine_fields, fine_permittivity, patch_corner, patch_owner):
    deep, tall, cols = coarse_fields.shape[1:]
    slots = fine_fields.shape[2]
    groups = slots // BATCH
    count_x, count_y = lax.axis_size("gx"), lax.axis_size("gy")
    two_y = count_y > 2
    vmem = whole()
    shape = jax.ShapeDtypeStruct
    grow = grow_table()

    x_face = shape((5, tall, cols), F32)
    y_face = shape((5, deep, cols), F32)
    kept, *faces = call(
        functools.partial(faces_kernel, two_y),
        [shape(coarse_fields.shape, F32), x_face, x_face, y_face] + [y_face] * two_y,
        [vmem],
    )(coarse_fields)
    got = [
        lax.ppermute(faces[0], "gx", swap_pairs(count_x, 0)),
        lax.ppermute(faces[1], ("gx", "gy"), full_pairs(count_x, count_y)),
        lax.ppermute(faces[2], "gy", swap_pairs(count_y, 0)),
    ]
    if two_y:
        got.append(lax.ppermute(faces[3], "gy", swap_pairs(count_y, 1)))
    beside = lax.ppermute(kept, "gz", swap_pairs(2, 0))

    fine = fine_fields.transpose(0, 1, 3, 2, 4)
    notes, rate = call(
        notes_kernel,
        [shape((8 + slots, LANES), jnp.int32), shape(permittivity.shape, F32)],
        [whole(pltpu.SMEM)] * 2 + [vmem],
    )(patch_corner, patch_owner.transpose(0, 2, 1), permittivity)
    box, fine_rate = call(
        load_kernel,
        [shape((groups, 6, ROWS_BOX, WIDE), F32), shape((groups, ROWS_BOX, WIDE), F32)],
        [vmem] * 3,
        [pltpu.VMEM((6 * ROWS_BOX, PF * PF), F32), pltpu.VMEM((ROWS_BOX, PF * PF), F32)],
        size=4_000_000,
    )(fine, fine_permittivity, jnp.asarray(grow, BF16))

    full = deep + 2
    ranks = count_y * lax.axis_size("gz")

    def exchange(parts):
        swaps = [[(r, r ^ k) for r in range(ranks)] for k in range(ranks)]
        got = list(parts)
        for k in [*range(2, ranks), 1]:
            got[k] = lax.ppermute(parts[k], ("gy", "gz"), swaps[k])
        return got

    patches = [shape((ROWS_BESIDE if k == 1 else ROWS_PATCH, LANES), F32) for k in range(ranks)]
    new, *sends = call(
        functools.partial(leap_kernel, two_y, ranks),
        [shape(coarse_fields.shape, F32)] + patches,
        [vmem] * (4 + len(got)),
        [
            pltpu.VMEM((6 * full * 16, LANES), F32),
            pltpu.VMEM((6 * full * 16, LANES), F32),
            pltpu.VMEM((5 * (full - 1) * 16, LANES), F32),
            pltpu.VMEM((6 * deep * 16, LANES), F32),
            pltpu.VMEM((PAR, ROWS_PATCH, LANES), F32),
        ],
    )(kept, beside, rate, notes, *got)
    regions = exchange(sends)

    box, *smalls = call(
        functools.partial(fine_kernel, ranks),
        [shape((groups, 6, ROWS_BOX, WIDE), F32)] + [shape((24, LANES), F32)] * ranks,
        [vmem] * (ranks + 4),
        [
            pltpu.VMEM((groups * 6 * ROWS_BOX, LANES), F32),
            pltpu.VMEM((2, groups * 6 * ROWS_BOX, LANES), F32),
            pltpu.VMEM((6, ROWS_BOX, WIDE), F32),
            pltpu.VMEM((3, ROWS_BOX, WIDE), F32),
            pltpu.VMEM((96, 2 * WIDE), F32),
            pltpu.VMEM((groups * 96, LANES), F32),
        ],
    )(*regions, box, fine_rate, jnp.asarray(ghost_table(), BF16), jnp.asarray(mean_table(), BF16))
    means = exchange(smalls)

    fine = call(
        store_kernel,
        shape(fine.shape, F32),
        [vmem] * 4,
        [pltpu.VMEM(fine.shape, F32), pltpu.SemaphoreType.DMA((6,))],
        size=4_000_000,
        out_specs=whole(pltpu.HBM),
    )(box, fine, notes, jnp.asarray(grow.T, BF16))
    new = call(fix_kernel, shape(coarse_fields.shape, F32), [vmem] * (1 + ranks))(new, rate, *regions[1:])
    coarse = call(
        functools.partial(place_kernel, ranks),
        shape(coarse_fields.shape, F32),
        [vmem] * (2 + ranks),
        [
            pltpu.VMEM((PAR, 4 * 96, LANES), F32),
            pltpu.VMEM(coarse_fields.shape, F32),
            pltpu.VMEM((ranks, 24, LANES), F32),
            pltpu.SemaphoreType.DMA((6,)),
        ],
        out_specs=whole(pltpu.HBM),
    )(new, notes, *means)
    return coarse, fine.transpose(0, 1, 3, 2, 4)


def solution(mesh):
    in_specs = (
        P(None, ("groups", "gx"), "gy", "gz"),
        P(("groups", "gx"), "gy", "gz"),
        P(("groups", "gx"), "gy", "gz", None, None),
        P(("groups", "gx"), "gy", "gz", None),
        P(("groups", "gx"), "gy", "gz", None),
        P(("groups", "gx"), None, None),
    )
    out_specs = (P(None, ("groups", "gx"), "gy", "gz"), P(("groups", "gx"), "gy", "gz", None, None))
    return jax.shard_map(local, mesh=mesh, in_specs=in_specs, out_specs=out_specs, check_vma=False)
```

```python
import functools
import jax
import jax.numpy as jnp
import numpy as np
from jax import lax
from jax.experimental import pallas as pl
from jax.experimental.pallas import tpu as pltpu
from jax.sharding import PartitionSpec as P

PF = 16
PAR = 2
HALF = PF // 2
RIM = HALF + 2
PLANES = 9
LINE = PF + 2
LANES = 128
WIDE = 384
BATCH = 4
ROWS_BOX = PLANES * 8
ROWS_RIM = 48
ROW_EDGE = 64
ROWS_PATCH = 72
ROWS_BESIDE = 104
X_COMPS = (0, 1, 2, 4, 5)
Y_COMPS = (0, 1, 2, 3, 5)
VMEM_BYTES = 48 * 1024 * 1024
F32 = jnp.float32
BF16 = jnp.bfloat16


def rim_lane(time, j, k):
    if 0 < j < RIM - 1:
        return j * RIM + k + 3 * time
    if j == 0 and time == 0:
        return k
    return (RIM - 1) * RIM + 3 + (2 * time + j // (RIM - 1) - 1) * RIM + k


def grow_table():
    table = np.zeros((PF * PF, WIDE), np.float32)
    for y in range(PF):
        for z in range(PF):
            table[y * PF + z, (y + 1) * LINE + z + 1] = 1.0
    return table


def ghost_table():
    table = np.zeros((2, 2 * LANES, WIDE), np.float32)
    for y in range(LINE):
        for z in range(LINE):
            j, k, lane = (y + 1) // 2, (z + 1) // 2, y * LINE + z
            table[:, LANES + j * RIM + k, lane] = 1.0
            if y in (0, LINE - 1) or z in (0, LINE - 1):
                table[0, rim_lane(0, j, k), lane] = 1.0
                table[1, rim_lane(0, j, k), lane] = 0.5
                table[1, rim_lane(1, j, k), lane] = 0.5
    return table


def mean_table():
    table = np.zeros((2, WIDE, LANES), np.float32)
    for odd in range(2):
        for y in range(PF):
            for z in range(PF):
                lane = odd * HALF * HALF + (y // 2) * HALF + z // 2
                table[odd, (y + 1) * LINE + z + 1, lane] = 0.125
    return table.reshape(2 * WIDE, LANES)


def move(rows, table):
    high = rows.astype(BF16)
    low = (rows - high.astype(F32)).astype(BF16)
    out = jnp.dot(high, table, preferred_element_type=F32)
    return out + jnp.dot(low, table, preferred_element_type=F32)


def lane_iota(shape):
    return lax.broadcasted_iota(jnp.int32, shape, len(shape) - 1)


def whole(memory_space=pltpu.VMEM):
    return pl.BlockSpec(memory_space=memory_space)


def call(kernel, outs, in_specs, scratch=(), flops=1_000_000, size=1_000_000, out_specs=None, **extra):
    return pl.pallas_call(
        kernel,
        out_shape=outs,
        in_specs=in_specs,
        out_specs=jax.tree.map(lambda _: whole(), outs) if out_specs is None else out_specs,
        scratch_shapes=list(scratch),
        compiler_params=pltpu.CompilerParams(vmem_limit_bytes=VMEM_BYTES),
        cost_estimate=pl.CostEstimate(flops=flops, bytes_accessed=size, transcendentals=0),
        **extra,
    )


def swap_pairs(count, first):
    pairs = []
    for i in range(first, count - 1, 2):
        pairs += [(i, i + 1), (i + 1, i)]
    return pairs


def full_pairs(count_x):
    pairs = []
    for i in range(count_x):
        for j in range(2):
            if 0 < i < count_x - 1:
                target = (i + 1 if i % 2 else i - 1) * 2 + j
            else:
                target = i * 2 + 1 - j
            pairs.append((i * 2 + j, target))
    return pairs


def faces_kernel(two_y, block, kept, x_even, y_even, x_odd, *y_odd):
    deep, tall = block.shape[1], block.shape[2]
    gx_odd = lax.rem(lax.axis_index("gx"), 2)
    gy_odd = lax.rem(lax.axis_index("gy"), 2)
    for k, c in enumerate(X_COMPS):
        x_even[k] = block[c, (1 - gx_odd) * (deep - 1)]
        x_odd[k] = block[c, gx_odd * (deep - 1)]
    for k, c in enumerate(Y_COMPS):
        for x in range(deep):
            first = block[c, x, 0:1, :]
            last = block[c, x, tall - 1 : tall, :]
            y_even[k, x : x + 1, :] = jnp.where(gy_odd == 0, last, first)
            if two_y:
                y_odd[0][k, x : x + 1, :] = jnp.where(gy_odd == 0, first, last)
    kept[...] = block[...]


def notes_kernel(corner, owners, perm, notes, rate):
    rank = lax.axis_index("gy") * lax.axis_size("gz") + lax.axis_index("gz")

    def note(row, value):
        notes[row : row + 1, :] = jnp.full((1, LANES), value, jnp.int32)

    for q in range(PAR):
        for d in range(3):
            note(q * 4 + d, corner[0, 0, q, d])
        note(q * 4 + 3, lax.bitwise_xor(owners[0, q, rank], rank))
    for slot in range(notes.shape[0] - 8):
        live = (owners[0, 0, slot] == rank) | (owners[0, 1, slot] == rank)
        note(8 + slot, live.astype(jnp.int32))
    rate[...] = 0.5 / perm[...]


def leap_kernel(two_y, ranks, *refs):
    block, beside, rate, notes, x_even, y_even, x_odd = refs[:7]
    y_odd = refs[7] if two_y else None
    refs = refs[7 + two_y :]
    new, sends = refs[0], refs[1 : 1 + ranks]
    pad, side, mag, fresh, packed = refs[1 + ranks :]
    deep, tall = block.shape[1], block.shape[2]
    full = deep + 2
    gx = lax.axis_index("gx")
    gx_odd = lax.rem(gx, 2)
    gy_odd = lax.rem(lax.axis_index("gy"), 2)
    gz = lax.axis_index("gz")
    noted = notes[0:8, :]
    spots = [[noted[q * 4 + d, 0] for d in range(3)] for q in range(PAR)]
    chosen = noted[3, 0]
    lane = lane_iota((tall, LANES))
    keep = ((lane == 0) & (gz == 0)) | ((lane == LANES - 1) & (gz == 1))
    lane = lane_iota((16, LANES))
    none = jnp.zeros((16, LANES), F32)

    def at(c, x):
        return (c * full + x) * 16

    for c in range(6):
        for x in (0, full - 1):
            pad[pl.ds(at(c, x), 16), :] = none
        for x in range(deep):
            pad[pl.ds(at(c, x + 1), tall), :] = block[c, x]
        pad[pl.ds(at(c, 1) + tall, deep, stride=16), :] = none[0:deep]
        pad[pl.ds(at(c, 1) + 15, deep, stride=16), :] = none[0:deep]
    for c in range(5):
        for x in (0, full - 1):
            side[pl.ds(at(c, x), 16), :] = none
        for x in range(deep):
            side[pl.ds(at(c, x + 1), 16), :] = none
            side[pl.ds(at(c, x + 1), tall), :] = jnp.where(keep, beside[c, x], 0.0)
    for k, c in enumerate(X_COMPS):
        even, odd = x_even[k], x_odd[k]
        low, high = jnp.where(gx_odd == 0, odd, even), jnp.where(gx_odd == 0, even, odd)
        pad[pl.ds(at(c, 0), tall), :] = jnp.where(gx == 0, 0.0, low)
        if c in (1, 2):
            pad[pl.ds(at(c, full - 1), tall), :] = jnp.where(gx == lax.axis_size("gx") - 1, 0.0, high)
    for k, c in enumerate(Y_COMPS):
        even = y_even[k]
        odd = jnp.zeros_like(even) if y_odd is None else y_odd[k]
        pad[pl.ds(at(c, 1) + 15, deep, stride=16), :] = jnp.where(gy_odd == 0, odd, even)
        if c in (0, 2):
            pad[pl.ds(at(c, 1) + tall, deep, stride=16), :] = jnp.where(gy_odd == 0, even, odd)

    def up_y(a):
        return pltpu.roll(a, 15, 0)

    def down_y(a):
        return pltpu.roll(a, 1, 0)

    def plane(c, x):
        return pad[pl.ds(at(c, x), 16), :]

    def edge(c, x):
        return side[pl.ds(at(c, x), 16), :]

    def field(c, x):
        return mag[pl.ds((c * (full - 1) + x) * 16, 16), :]

    for x in range(full - 1):
        e0, e1, e2 = plane(0, x), plane(1, x), plane(2, x)
        s0, s1, s2 = edge(0, x), edge(1, x), edge(2, x)
        r0, r1 = pltpu.roll(e0, LANES - 1, 1), pltpu.roll(e1, LANES - 1, 1)
        u0 = jnp.where(lane == LANES - 1, pltpu.roll(s0, LANES - 1, 1), r0)
        u1 = jnp.where(lane == LANES - 1, pltpu.roll(s1, LANES - 1, 1), r1)
        h0 = plane(3, x) - 0.5 * ((up_y(e2) - e2) - (u1 - e1))
        h1 = plane(4, x) - 0.5 * ((u0 - e0) - (plane(2, x + 1) - e2))
        h2 = plane(5, x) - 0.5 * ((plane(1, x + 1) - e1) - (up_y(e0) - e0))
        t0 = edge(3, x) - 0.5 * ((up_y(s2) - s2) - (r1 - s1))
        t1 = edge(4, x) - 0.5 * ((r0 - s0) - (edge(2, x + 1) - s2))
        d0 = pltpu.roll(jnp.where(lane == LANES - 1, t0, h0), 1, 1)
        d1 = pltpu.roll(jnp.where(lane == LANES - 1, t1, h1), 1, 1)
        for c, value in enumerate((h0, h1, h2, d0, d1)):
            mag[pl.ds((c * (full - 1) + x) * 16, 16), :] = value
    for x in range(deep):
        h0, h1, h2, d0, d1 = (field(c, x + 1) for c in range(5))
        coef = rate[x]
        c0 = (h2 - down_y(h2)) - (h1 - d1)
        c1 = (h0 - d0) - (h2 - field(2, x))
        c2 = (h1 - field(1, x)) - (h0 - down_y(h0))
        for c, curl in enumerate((c0, c1, c2)):
            value = plane(c, x + 1)[0:tall] + coef * curl[0:tall]
            new[c, x] = value
            new[c + 3, x] = (h0, h1, h2)[c][0:tall]
            fresh[pl.ds((c * deep + x) * 16, tall), :] = value
            fresh[pl.ds(((c + 3) * deep + x) * 16, tall), :] = (h0, h1, h2)[c][0:tall]
    lane = lane_iota((8, LANES))
    for q in range(PAR):
        cx, cy, cz = spots[q]

        def rows_of(time, c, k, j, count, over_c):
            source, depth, start = (pad, full, cx) if time == 0 else (fresh, deep, cx - 1)
            step = depth * 16 if over_c else 16
            return source[pl.ds((c * depth + start + k) * 16 + cy + (j - 1), count, stride=step), :]

        def aim(rows, target):
            return pltpu.roll(rows, lax.rem(target - (cz - 1) + 2 * LANES, LANES), 1)

        for c in range(6):
            total = jnp.zeros((8, LANES), F32)
            for j in range(RIM):
                if (j == 0 and c == 4) or (j == RIM - 1 and c not in (0, 2)) or (0 < j < RIM - 1 and c == 5):
                    continue
                for time in range(2):
                    first = rim_lane(time, j, 0)
                    rows = aim(rows_of(time, c, 1, j, 8, False), first)
                    if j in (0, RIM - 1):
                        inside = (lane >= first) & (lane < first + RIM)
                    else:
                        inside = (lane == first) | (lane == first + RIM - 1)
                    total = jnp.where(inside, rows, total)
            packed[q, c * 8 : c * 8 + 8, :] = total
        for time in range(2):
            low = jnp.zeros((6, LANES), F32)
            high = jnp.zeros((2, LANES), F32)
            for j in range(RIM):
                first = j * RIM
                inside = (lane >= first) & (lane < first + RIM)
                low = jnp.where(inside[0:6], aim(rows_of(time, 0, 0, j, 6, True), first), low)
                high = jnp.where(inside[0:2], aim(rows_of(time, 1, RIM - 1, j, 2, True), first), high)
            base = ROWS_RIM + time * 8
            packed[q, base : base + 6, :] = low
            packed[q, base + 6 : base + 8, :] = high
        packed[q, ROW_EDGE:ROWS_PATCH, :] = jnp.zeros((ROWS_PATCH - ROW_EDGE, LANES), F32)
        packed[q, ROW_EDGE : ROW_EDGE + 1, :] = pad[pl.ds(at(1, full - 1) + tall - 1, 1), :]
        packed[q, ROW_EDGE + 1 : ROW_EDGE + 2, :] = pad[pl.ds(at(0, 0), 1), :]
    for k, send in enumerate(sends):
        q = jnp.where(chosen == k, 0, 1)
        send[0:ROWS_PATCH, :] = packed[q]
    half = lane_iota((16, LANES)) < LANES // 2
    send = sends[1]
    send[ROWS_PATCH : ROWS_PATCH + 16, :] = jnp.where(half, plane(0, 0), plane(2, full - 1))
    low = jnp.where(gy_odd == 0, jnp.zeros_like(y_even[1]) if y_odd is None else y_odd[1], y_even[1])
    high = jnp.where(gy_odd == 0, y_even[2], jnp.zeros_like(y_even[2]) if y_odd is None else y_odd[2])
    send[ROWS_PATCH + 16 : ROWS_PATCH + 32, :] = jnp.zeros((16, LANES), F32)
    send[ROWS_PATCH + 16 : ROWS_PATCH + 16 + deep, :] = jnp.where(half[0:deep], low, high)


def places():
    for x in range(PF):
        yield x, (x % 8 + 1) * 8 if x < 8 else (x % 8) * 8 + BATCH


def load_kernel(fine, perm, table, box, rate, lhs, coefs):
    groups = fine.shape[3] // BATCH
    blank = jnp.zeros((8, PF * PF), F32)
    for g in range(groups):
        slots = slice(g * BATCH, (g + 1) * BATCH)
        for c in range(6):
            for row in (0, ROWS_BOX - 8):
                lhs[c * ROWS_BOX + row : c * ROWS_BOX + row + 8, :] = blank
            for x, row in places():
                row += c * ROWS_BOX
                lhs[row : row + BATCH, :] = fine[0, 0, c, slots, x * PF * PF : (x + 1) * PF * PF]
            grown = move(lhs[c * ROWS_BOX : (c + 1) * ROWS_BOX, :], table[...])
            box[g, c] = grown
        for row in (0, ROWS_BOX - 8):
            coefs[row : row + 8, :] = blank
        for x, row in places():
            coefs[row : row + BATCH, :] = 0.5 / perm[0, 0, slots, x * PF * PF : (x + 1) * PF * PF]
        rate[g] = move(coefs[...], table[...])


def fine_kernel(ranks, *refs):
    regions, (box, rate, ghosts, means, out) = refs[:ranks], refs[ranks : ranks + 5]
    smalls = refs[ranks + 5 : 2 * ranks + 5]
    rims, walls, now, mag, halves, small = refs[2 * ranks + 5 :]
    groups = box.shape[0]
    rank = lax.axis_index("gy") * lax.axis_size("gz") + lax.axis_index("gz")
    flat = lane_iota((8, WIDE))
    yy = lax.shift_right_logical(flat * 3641, 16)
    zz = flat - yy * LINE
    inner = (yy >= 1) & (yy <= PF) & (zz >= 1) & (zz <= PF)
    upper = lax.broadcasted_iota(jnp.int32, (8, WIDE), 0) >= BATCH

    def inner_of(m):
        if m == 0:
            return inner & upper
        if m == PLANES - 1:
            return inner & jnp.logical_not(upper)
        return inner

    def up_y(a):
        return pltpu.roll(a, WIDE - LINE, 1)

    def up_z(a):
        return pltpu.roll(a, WIDE - 1, 1)

    def down_y(a):
        return pltpu.roll(a, LINE, 1)

    def down_z(a):
        return pltpu.roll(a, 1, 1)

    def rows_of(m):
        return pl.ds(m * 8, 8)

    blank = jnp.zeros((8, LANES), F32)
    for g in range(groups):
        for c in range(6):
            for m in range(PLANES):
                row = ((g * 6 + c) * PLANES + m) * 8
                if m in (0, PLANES - 1):
                    rims[row : row + 8, :] = blank
                walls[0, row : row + 8, :] = blank
                walls[1, row : row + 8, :] = blank
    for k, region in enumerate(regions):
        slot = lax.bitwise_xor(rank, k)
        start = (slot // BATCH) * 6 * ROWS_BOX + lax.rem(slot, BATCH)
        for c in range(6):
            rows = region[c * 8 : c * 8 + 8, :]
            row = start + c * ROWS_BOX
            rims[pl.ds(row + 8, 4, stride=16), :] = rows[0:4]
            rims[pl.ds(row + 16, 4, stride=16), :] = rows[0:4]
            rims[pl.ds(row + BATCH, 4, stride=16), :] = rows[4:8]
            rims[pl.ds(row + BATCH + 8, 4, stride=16), :] = rows[4:8]
        old = region[ROWS_RIM : ROWS_RIM + 8, :]
        fresh = region[ROWS_RIM + 8 : ROWS_RIM + 16, :]
        for sub, value in enumerate((old, old + 0.5 * (fresh - old))):
            walls[sub, pl.ds(start, 6, stride=ROWS_BOX), :] = value[0:6]
            last = start + ROWS_BOX + (PLANES - 1) * 8 + BATCH
            walls[sub, pl.ds(last, 2, stride=ROWS_BOX), :] = value[6:8]
    for g in range(groups):
        for sub in range(2):
            source = box if sub == 0 else out
            for c in range(6):
                rows = pl.ds((g * 6 + c) * ROWS_BOX, ROWS_BOX)
                ghost = move(jnp.concatenate([rims[rows, :], walls[sub, rows, :]], axis=1), ghosts[sub])
                for m in range(PLANES):
                    now[c, rows_of(m), :] = jnp.where(
                        inner_of(m), source[g, c, rows_of(m), :], ghost[m * 8 : (m + 1) * 8]
                    )

            def next_x(c, m):
                if m == PLANES - 1:
                    return pltpu.roll(now[c, rows_of(0), :], BATCH, 0)
                return now[c, rows_of(m + 1), :]

            def last_x(c, m):
                if m == 0:
                    return pltpu.roll(mag[c, rows_of(PLANES - 1), :], BATCH, 0)
                return mag[c, rows_of(m - 1), :]

            for m in range(PLANES):
                e0, e1, e2 = (now[c, rows_of(m), :] for c in range(3))
                h0, h1, h2 = (now[c, rows_of(m), :] for c in range(3, 6))
                mag[0, rows_of(m), :] = h0 - 0.5 * ((up_y(e2) - e2) - (up_z(e1) - e1))
                mag[1, rows_of(m), :] = h1 - 0.5 * ((up_z(e0) - e0) - (next_x(2, m) - e2))
                mag[2, rows_of(m), :] = h2 - 0.5 * ((next_x(1, m) - e1) - (up_y(e0) - e0))
            for m in range(PLANES):
                h0, h1, h2 = (mag[c, rows_of(m), :] for c in range(3))
                coef = rate[g, rows_of(m), :]
                e0, e1, e2 = (now[c, rows_of(m), :] for c in range(3))
                out[g, 0, rows_of(m), :] = e0 + coef * ((h2 - down_y(h2)) - (h1 - down_z(h1)))
                out[g, 1, rows_of(m), :] = e1 + coef * ((h0 - down_z(h0)) - (h2 - last_x(2, m)))
                out[g, 2, rows_of(m), :] = e2 + coef * ((h1 - last_x(1, m)) - (h0 - down_y(h0)))
                for c, value in enumerate((h0, h1, h2)):
                    out[g, c + 3, rows_of(m), :] = value
        for c in range(6):
            for k in range(4):
                other = jnp.where(upper, out[g, c, rows_of(2 * k), :], out[g, c, rows_of(2 * k + 2), :])
                pair = out[g, c, rows_of(2 * k + 1), :] + other
                halves[pl.ds((c * 2 + k // 2) * 8, 8), (k % 2) * WIDE : (k % 2 + 1) * WIDE] = pair
        small[pl.ds(g * 96, 96), :] = move(halves[...], means[...])
    for k, send in enumerate(smalls):
        slot = lax.bitwise_xor(rank, k)
        start = (slot // BATCH) * 96 + lax.rem(slot, BATCH)
        for xh in range(2):
            send[xh * 12 : (xh + 1) * 12, :] = small[pl.ds(start + xh * BATCH, 12, stride=8), :]


def store_kernel(box, fine, notes, table, out, stage, sems):
    groups = box.shape[0]
    slots = groups * BATCH
    live = jnp.concatenate([notes[8 : 8 + slots, :]] * (PF * PF // LANES), axis=1) > 0
    copies = []
    for c in range(6):
        flats = [move(box[g, c], table[...]) for g in range(groups)]
        for x, row in places():
            cut = slice(x * PF * PF, (x + 1) * PF * PF)
            for g, flat in enumerate(flats):
                some = slice(g * BATCH, (g + 1) * BATCH)
                stage[0, 0, c, some, cut] = jnp.where(live[some], flat[row : row + BATCH], fine[0, 0, c, some, cut])
        copies.append(pltpu.make_async_copy(stage.at[:, :, c], out.at[:, :, c], sems.at[c]))
        copies[-1].start()
    for copy in copies:
        copy.wait()


def fix_kernel(new, rate, *refs):
    edges, out = refs[:-1], refs[-1]
    deep, tall = new.shape[1], new.shape[2]
    gz = lax.axis_index("gz")
    rank = lax.axis_index("gy") * 2 + gz
    out[...] = new[...]

    def add(c, x, rows, amount):
        out[c, x, rows, :] = out[c, x, rows, :] + 0.5 * rate[x, rows, :] * amount

    lower = higher = jnp.zeros((1, LANES), F32)
    for k, edge in enumerate(edges, 1):
        row = ROW_EDGE
        lower = jnp.where(lax.bitwise_xor(rank, k) == rank - 2, edge[row : row + 1, :], lower)
        higher = jnp.where(lax.bitwise_xor(rank, k) == rank + 2, edge[row + 1 : row + 2, :], higher)
    add(0, deep - 1, slice(0, 1), lower)
    add(1, 0, slice(tall - 1, tall), higher)
    lane = lane_iota((tall, LANES))
    tile = edges[0][ROWS_PATCH : ROWS_PATCH + tall, :]
    add(0, deep - 1, slice(0, tall), jnp.where((lane == 0) & (gz == 1), pltpu.roll(tile, 1, 1), 0.0))
    add(2, 0, slice(0, tall), jnp.where((lane == LANES - 1) & (gz == 0), pltpu.roll(tile, LANES - 1, 1), 0.0))
    lane = lane_iota((deep, LANES))
    tile = edges[0][ROWS_PATCH + 16 : ROWS_PATCH + 16 + deep, :]
    first = jnp.where((lane == LANES - 1) & (gz == 0), pltpu.roll(tile, LANES - 1, 1), 0.0)
    last = jnp.where((lane == 0) & (gz == 1), pltpu.roll(tile, 1, 1), 0.0)
    for x in range(deep):
        add(2, x, slice(0, 1), first[x : x + 1])
        add(1, x, slice(tall - 1, tall), last[x : x + 1])


def place_kernel(ranks, new, notes, *refs):
    means, (out, spread, stage, gathered, sems) = refs[:ranks], refs[ranks:]
    noted = notes[0:8, :]
    for k, mean in enumerate(means):
        gathered[k] = mean[...]
    lane = lane_iota((HALF, LANES))
    spots = [tuple(noted[q * 4 + d, 0] for d in range(3)) for q in range(PAR)]
    for q, (cx, cy, cz) in enumerate(spots):
        k = noted[q * 4 + 3, 0]
        rows = gathered[k]
        for odd in range(2):
            for y in range(HALF):
                shift = lax.rem(cz - y * HALF - odd * HALF * HALF + 2 * LANES, LANES)
                spread[q, pl.ds(odd * 192 + y, 24, stride=8), :] = pltpu.roll(rows, shift, 1)
    copies = []
    for c in range(6):
        stage[c] = new[c]
        for q, (cx, cy, cz) in enumerate(spots):
            inside = (lane >= cz) & (lane < cz + HALF)
            for x in range(HALF):
                xh, k = x // 4, x % 4
                tile = spread[q, pl.ds((k % 2) * 192 + (xh * 12 + c * 2 + k // 2) * 8, 8), :]
                spot = stage[c, cx + x, pl.ds(cy, HALF), :]
                stage[c, cx + x, pl.ds(cy, HALF), :] = jnp.where(inside, tile, spot)
        copies.append(pltpu.make_async_copy(stage.at[c], out.at[c], sems.at[c]))
        copies[-1].start()
    for copy in copies:
        copy.wait()


def local(coarse_fields, permittivity, fine_fields, fine_permittivity, patch_corner, patch_owner):
    deep, tall, cols = coarse_fields.shape[1:]
    slots = fine_fields.shape[2]
    groups = slots // BATCH
    count_x, count_y = lax.axis_size("gx"), lax.axis_size("gy")
    two_y = count_y > 2
    vmem = whole()
    shape = jax.ShapeDtypeStruct
    grow = grow_table()

    x_face = shape((5, tall, cols), F32)
    y_face = shape((5, deep, cols), F32)
    kept, *faces = call(
        functools.partial(faces_kernel, two_y),
        [shape(coarse_fields.shape, F32), x_face, y_face, x_face] + [y_face] * two_y,
        [vmem],
    )(coarse_fields)
    got = [
        lax.ppermute(faces[0], "gx", swap_pairs(count_x, 0)),
        lax.ppermute(faces[1], "gy", swap_pairs(count_y, 0)),
        lax.ppermute(faces[2], ("gx", "gz"), full_pairs(count_x)),
    ]
    if two_y:
        got.append(lax.ppermute(faces[3], "gy", swap_pairs(count_y, 1)))
    beside = lax.ppermute(kept, "gz", swap_pairs(2, 0))

    fine = fine_fields.transpose(0, 1, 3, 2, 4)
    notes, rate = call(
        notes_kernel,
        [shape((8 + slots, LANES), jnp.int32), shape(permittivity.shape, F32)],
        [whole(pltpu.SMEM)] * 2 + [vmem],
    )(patch_corner, patch_owner.transpose(0, 2, 1), permittivity)
    box, fine_rate = call(
        load_kernel,
        [shape((groups, 6, ROWS_BOX, WIDE), F32), shape((groups, ROWS_BOX, WIDE), F32)],
        [vmem] * 3,
        [pltpu.VMEM((6 * ROWS_BOX, PF * PF), F32), pltpu.VMEM((ROWS_BOX, PF * PF), F32)],
        size=4_000_000,
    )(fine, fine_permittivity, jnp.asarray(grow, BF16))

    full = deep + 2
    ranks = count_y * lax.axis_size("gz")

    def exchange(parts):
        swaps = [[(r, r ^ k) for r in range(ranks)] for k in range(ranks)]
        got = list(parts)
        for k in [*range(2, ranks), 1]:
            got[k] = lax.ppermute(parts[k], ("gy", "gz"), swaps[k])
        return got

    patches = [shape((ROWS_BESIDE if k == 1 else ROWS_PATCH, LANES), F32) for k in range(ranks)]
    new, *sends = call(
        functools.partial(leap_kernel, two_y, ranks),
        [shape(coarse_fields.shape, F32)] + patches,
        [vmem] * (4 + len(got)),
        [
            pltpu.VMEM((6 * full * 16, LANES), F32),
            pltpu.VMEM((6 * full * 16, LANES), F32),
            pltpu.VMEM((5 * (full - 1) * 16, LANES), F32),
            pltpu.VMEM((6 * deep * 16, LANES), F32),
            pltpu.VMEM((PAR, ROWS_PATCH, LANES), F32),
        ],
    )(kept, beside, rate, notes, *got)
    regions = exchange(sends)

    box, *smalls = call(
        functools.partial(fine_kernel, ranks),
        [shape((groups, 6, ROWS_BOX, WIDE), F32)] + [shape((24, LANES), F32)] * ranks,
        [vmem] * (ranks + 4),
        [
            pltpu.VMEM((groups * 6 * ROWS_BOX, LANES), F32),
            pltpu.VMEM((2, groups * 6 * ROWS_BOX, LANES), F32),
            pltpu.VMEM((6, ROWS_BOX, WIDE), F32),
            pltpu.VMEM((3, ROWS_BOX, WIDE), F32),
            pltpu.VMEM((96, 2 * WIDE), F32),
            pltpu.VMEM((groups * 96, LANES), F32),
        ],
    )(*regions, box, fine_rate, jnp.asarray(ghost_table(), BF16), jnp.asarray(mean_table(), BF16))
    means = exchange(smalls)

    fine = call(
        store_kernel,
        shape(fine.shape, F32),
        [vmem] * 4,
        [pltpu.VMEM(fine.shape, F32), pltpu.SemaphoreType.DMA((6,))],
        size=4_000_000,
        out_specs=whole(pltpu.HBM),
    )(box, fine, notes, jnp.asarray(grow.T, BF16))
    new = call(fix_kernel, shape(coarse_fields.shape, F32), [vmem] * (1 + ranks))(new, rate, *regions[1:])
    coarse = call(
        functools.partial(place_kernel, ranks),
        shape(coarse_fields.shape, F32),
        [vmem] * (2 + ranks),
        [
            pltpu.VMEM((PAR, 4 * 96, LANES), F32),
            pltpu.VMEM(coarse_fields.shape, F32),
            pltpu.VMEM((ranks, 24, LANES), F32),
            pltpu.SemaphoreType.DMA((6,)),
        ],
        out_specs=whole(pltpu.HBM),
    )(new, notes, *means)
    return coarse, fine.transpose(0, 1, 3, 2, 4)


def solution(mesh):
    in_specs = (
        P(None, ("groups", "gx"), "gy", "gz"),
        P(("groups", "gx"), "gy", "gz"),
        P(("groups", "gx"), "gy", "gz", None, None),
        P(("groups", "gx"), "gy", "gz", None),
        P(("groups", "gx"), "gy", "gz", None),
        P(("groups", "gx"), None, None),
    )
    out_specs = (P(None, ("groups", "gx"), "gy", "gz"), P(("groups", "gx"), "gy", "gz", None, None))
    return jax.shard_map(local, mesh=mesh, in_specs=in_specs, out_specs=out_specs, check_vma=False)
```

```python
import functools
import jax
import jax.numpy as jnp
import numpy as np
from jax import lax
from jax.experimental import pallas as pl
from jax.experimental.pallas import tpu as pltpu
from jax.sharding import PartitionSpec as P

PF = 16
PAR = 2
HALF = PF // 2
RIM = HALF + 2
PLANES = 9
LINE = PF + 2
LANES = 128
WIDE = 384
BATCH = 4
ROWS_BOX = PLANES * 8
ROWS_RIM = 48
ROW_EDGE = 64
ROWS_PATCH = 72
ROWS_BESIDE = 104
X_COMPS = (0, 1, 2, 4, 5)
Y_COMPS = (0, 1, 2, 3, 5)
VMEM_BYTES = 48 * 1024 * 1024
F32 = jnp.float32
BF16 = jnp.bfloat16


def rim_lane(time, j, k):
    if 0 < j < RIM - 1:
        return j * RIM + k + 3 * time
    if j == 0 and time == 0:
        return k
    return (RIM - 1) * RIM + 3 + (2 * time + j // (RIM - 1) - 1) * RIM + k


def grow_table():
    table = np.zeros((PF * PF, WIDE), np.float32)
    for y in range(PF):
        for z in range(PF):
            table[y * PF + z, (y + 1) * LINE + z + 1] = 1.0
    return table


def ghost_table():
    table = np.zeros((2, 2 * LANES, WIDE), np.float32)
    for y in range(LINE):
        for z in range(LINE):
            j, k, lane = (y + 1) // 2, (z + 1) // 2, y * LINE + z
            table[:, LANES + j * RIM + k, lane] = 1.0
            if y in (0, LINE - 1) or z in (0, LINE - 1):
                table[0, rim_lane(0, j, k), lane] = 1.0
                table[1, rim_lane(0, j, k), lane] = 0.5
                table[1, rim_lane(1, j, k), lane] = 0.5
    return table


def mean_table():
    table = np.zeros((2, WIDE, LANES), np.float32)
    for odd in range(2):
        for y in range(PF):
            for z in range(PF):
                lane = odd * HALF * HALF + (y // 2) * HALF + z // 2
                table[odd, (y + 1) * LINE + z + 1, lane] = 0.125
    return table.reshape(2 * WIDE, LANES)


def move(rows, table):
    high = rows.astype(BF16)
    low = (rows - high.astype(F32)).astype(BF16)
    out = jnp.dot(jnp.concatenate([high, low], axis=0), table, preferred_element_type=F32)
    return out[: rows.shape[0]] + out[rows.shape[0] :]


def lane_iota(shape):
    return lax.broadcasted_iota(jnp.int32, shape, len(shape) - 1)


def whole(memory_space=pltpu.VMEM):
    return pl.BlockSpec(memory_space=memory_space)


def call(kernel, outs, in_specs, scratch=(), flops=1_000_000, size=1_000_000, out_specs=None, **extra):
    return pl.pallas_call(
        kernel,
        out_shape=outs,
        in_specs=in_specs,
        out_specs=jax.tree.map(lambda _: whole(), outs) if out_specs is None else out_specs,
        scratch_shapes=list(scratch),
        compiler_params=pltpu.CompilerParams(vmem_limit_bytes=VMEM_BYTES),
        cost_estimate=pl.CostEstimate(flops=flops, bytes_accessed=size, transcendentals=0),
        **extra,
    )


def swap_pairs(count, first):
    pairs = []
    for i in range(first, count - 1, 2):
        pairs += [(i, i + 1), (i + 1, i)]
    return pairs


def full_pairs(count_x):
    pairs = []
    for i in range(count_x):
        for j in range(2):
            if 0 < i < count_x - 1:
                target = (i + 1 if i % 2 else i - 1) * 2 + j
            else:
                target = i * 2 + 1 - j
            pairs.append((i * 2 + j, target))
    return pairs


def faces_kernel(two_y, block, kept, x_even, y_even, x_odd, *y_odd):
    deep, tall = block.shape[1], block.shape[2]
    gx_odd = lax.rem(lax.axis_index("gx"), 2)
    gy_odd = lax.rem(lax.axis_index("gy"), 2)
    for k, c in enumerate(X_COMPS):
        x_even[k] = block[c, (1 - gx_odd) * (deep - 1)]
        x_odd[k] = block[c, gx_odd * (deep - 1)]
    for k, c in enumerate(Y_COMPS):
        for x in range(deep):
            first = block[c, x, 0:1, :]
            last = block[c, x, tall - 1 : tall, :]
            y_even[k, x : x + 1, :] = jnp.where(gy_odd == 0, last, first)
            if two_y:
                y_odd[0][k, x : x + 1, :] = jnp.where(gy_odd == 0, first, last)
    kept[...] = block[...]


def notes_kernel(corner, owners, perm, notes, rate):
    rank = lax.axis_index("gy") * lax.axis_size("gz") + lax.axis_index("gz")

    def note(row, value):
        notes[row : row + 1, :] = jnp.full((1, LANES), value, jnp.int32)

    for q in range(PAR):
        for d in range(3):
            note(q * 4 + d, corner[0, 0, q, d])
        note(q * 4 + 3, lax.bitwise_xor(owners[0, q, rank], rank))
    for slot in range(notes.shape[0] - 8):
        live = (owners[0, 0, slot] == rank) | (owners[0, 1, slot] == rank)
        note(8 + slot, live.astype(jnp.int32))
    rate[...] = 0.5 / perm[...]


def leap_kernel(two_y, ranks, *refs):
    block, beside, rate, notes, x_even, y_even, x_odd = refs[:7]
    y_odd = refs[7] if two_y else None
    refs = refs[7 + two_y :]
    new, sends = refs[0], refs[1 : 1 + ranks]
    pad, side, mag, fresh, packed = refs[1 + ranks :]
    deep, tall = block.shape[1], block.shape[2]
    full = deep + 2
    gx = lax.axis_index("gx")
    gx_odd = lax.rem(gx, 2)
    gy_odd = lax.rem(lax.axis_index("gy"), 2)
    gz = lax.axis_index("gz")
    noted = notes[0:8, :]
    spots = [[noted[q * 4 + d, 0] for d in range(3)] for q in range(PAR)]
    chosen = noted[3, 0]
    lane = lane_iota((tall, LANES))
    keep = ((lane == 0) & (gz == 0)) | ((lane == LANES - 1) & (gz == 1))
    lane = lane_iota((16, LANES))
    none = jnp.zeros((16, LANES), F32)

    def at(c, x):
        return (c * full + x) * 16

    for c in range(6):
        for x in (0, full - 1):
            pad[pl.ds(at(c, x), 16), :] = none
        for x in range(deep):
            pad[pl.ds(at(c, x + 1), tall), :] = block[c, x]
        pad[pl.ds(at(c, 1) + tall, deep, stride=16), :] = none[0:deep]
        pad[pl.ds(at(c, 1) + 15, deep, stride=16), :] = none[0:deep]
    for c in range(5):
        for x in (0, full - 1):
            side[pl.ds(at(c, x), 16), :] = none
        for x in range(deep):
            side[pl.ds(at(c, x + 1), 16), :] = none
            side[pl.ds(at(c, x + 1), tall), :] = jnp.where(keep, beside[c, x], 0.0)
    for k, c in enumerate(X_COMPS):
        even, odd = x_even[k], x_odd[k]
        low, high = jnp.where(gx_odd == 0, odd, even), jnp.where(gx_odd == 0, even, odd)
        pad[pl.ds(at(c, 0), tall), :] = jnp.where(gx == 0, 0.0, low)
        if c in (1, 2):
            pad[pl.ds(at(c, full - 1), tall), :] = jnp.where(gx == lax.axis_size("gx") - 1, 0.0, high)
    for k, c in enumerate(Y_COMPS):
        even = y_even[k]
        odd = jnp.zeros_like(even) if y_odd is None else y_odd[k]
        pad[pl.ds(at(c, 1) + 15, deep, stride=16), :] = jnp.where(gy_odd == 0, odd, even)
        if c in (0, 2):
            pad[pl.ds(at(c, 1) + tall, deep, stride=16), :] = jnp.where(gy_odd == 0, even, odd)

    def up_y(a):
        return pltpu.roll(a, 15, 0)

    def down_y(a):
        return pltpu.roll(a, 1, 0)

    def plane(c, x):
        return pad[pl.ds(at(c, x), 16), :]

    def edge(c, x):
        return side[pl.ds(at(c, x), 16), :]

    def field(c, x):
        return mag[pl.ds((c * (full - 1) + x) * 16, 16), :]

    for x in range(full - 1):
        e0, e1, e2 = plane(0, x), plane(1, x), plane(2, x)
        s0, s1, s2 = edge(0, x), edge(1, x), edge(2, x)
        r0, r1 = pltpu.roll(e0, LANES - 1, 1), pltpu.roll(e1, LANES - 1, 1)
        u0 = jnp.where(lane == LANES - 1, pltpu.roll(s0, LANES - 1, 1), r0)
        u1 = jnp.where(lane == LANES - 1, pltpu.roll(s1, LANES - 1, 1), r1)
        h0 = plane(3, x) - 0.5 * ((up_y(e2) - e2) - (u1 - e1))
        h1 = plane(4, x) - 0.5 * ((u0 - e0) - (plane(2, x + 1) - e2))
        h2 = plane(5, x) - 0.5 * ((plane(1, x + 1) - e1) - (up_y(e0) - e0))
        t0 = edge(3, x) - 0.5 * ((up_y(s2) - s2) - (r1 - s1))
        t1 = edge(4, x) - 0.5 * ((r0 - s0) - (edge(2, x + 1) - s2))
        d0 = pltpu.roll(jnp.where(lane == LANES - 1, t0, h0), 1, 1)
        d1 = pltpu.roll(jnp.where(lane == LANES - 1, t1, h1), 1, 1)
        for c, value in enumerate((h0, h1, h2, d0, d1)):
            mag[pl.ds((c * (full - 1) + x) * 16, 16), :] = value
    for x in range(deep):
        h0, h1, h2, d0, d1 = (field(c, x + 1) for c in range(5))
        coef = rate[x]
        c0 = (h2 - down_y(h2)) - (h1 - d1)
        c1 = (h0 - d0) - (h2 - field(2, x))
        c2 = (h1 - field(1, x)) - (h0 - down_y(h0))
        for c, curl in enumerate((c0, c1, c2)):
            value = plane(c, x + 1)[0:tall] + coef * curl[0:tall]
            new[c, x] = value
            new[c + 3, x] = (h0, h1, h2)[c][0:tall]
            fresh[pl.ds((c * deep + x) * 16, tall), :] = value
            fresh[pl.ds(((c + 3) * deep + x) * 16, tall), :] = (h0, h1, h2)[c][0:tall]
    lane = lane_iota((8, LANES))
    for q in range(PAR):
        cx, cy, cz = spots[q]

        def rows_of(time, c, k, j, count, over_c):
            source, depth, start = (pad, full, cx) if time == 0 else (fresh, deep, cx - 1)
            step = depth * 16 if over_c else 16
            return source[pl.ds((c * depth + start + k) * 16 + cy + (j - 1), count, stride=step), :]

        def aim(rows, target):
            return pltpu.roll(rows, lax.rem(target - (cz - 1) + 2 * LANES, LANES), 1)

        for c in range(6):
            total = jnp.zeros((8, LANES), F32)
            for j in range(RIM):
                if (j == 0 and c == 4) or (j == RIM - 1 and c not in (0, 2)) or (0 < j < RIM - 1 and c == 5):
                    continue
                for time in range(2):
                    first = rim_lane(time, j, 0)
                    rows = aim(rows_of(time, c, 1, j, 8, False), first)
                    if j in (0, RIM - 1):
                        inside = (lane >= first) & (lane < first + RIM)
                    else:
                        inside = (lane == first) | (lane == first + RIM - 1)
                    total = jnp.where(inside, rows, total)
            packed[q, c * 8 : c * 8 + 8, :] = total
        for time in range(2):
            low = jnp.zeros((6, LANES), F32)
            high = jnp.zeros((2, LANES), F32)
            for j in range(RIM):
                first = j * RIM
                inside = (lane >= first) & (lane < first + RIM)
                low = jnp.where(inside[0:6], aim(rows_of(time, 0, 0, j, 6, True), first), low)
                high = jnp.where(inside[0:2], aim(rows_of(time, 1, RIM - 1, j, 2, True), first), high)
            base = ROWS_RIM + time * 8
            packed[q, base : base + 6, :] = low
            packed[q, base + 6 : base + 8, :] = high
        packed[q, ROW_EDGE:ROWS_PATCH, :] = jnp.zeros((ROWS_PATCH - ROW_EDGE, LANES), F32)
        packed[q, ROW_EDGE : ROW_EDGE + 1, :] = pad[pl.ds(at(1, full - 1) + tall - 1, 1), :]
        packed[q, ROW_EDGE + 1 : ROW_EDGE + 2, :] = pad[pl.ds(at(0, 0), 1), :]
    for k, send in enumerate(sends):
        q = jnp.where(chosen == k, 0, 1)
        send[0:ROWS_PATCH, :] = packed[q]
    half = lane_iota((16, LANES)) < LANES // 2
    send = sends[1]
    send[ROWS_PATCH : ROWS_PATCH + 16, :] = jnp.where(half, plane(0, 0), plane(2, full - 1))
    low = jnp.where(gy_odd == 0, jnp.zeros_like(y_even[1]) if y_odd is None else y_odd[1], y_even[1])
    high = jnp.where(gy_odd == 0, y_even[2], jnp.zeros_like(y_even[2]) if y_odd is None else y_odd[2])
    send[ROWS_PATCH + 16 : ROWS_PATCH + 32, :] = jnp.zeros((16, LANES), F32)
    send[ROWS_PATCH + 16 : ROWS_PATCH + 16 + deep, :] = jnp.where(half[0:deep], low, high)


def places():
    for x in range(PF):
        yield x, (x % 8 + 1) * 8 if x < 8 else (x % 8) * 8 + BATCH


def load_kernel(fine, perm, table, box, rate, lhs, coefs):
    groups = fine.shape[3] // BATCH
    blank = jnp.zeros((8, PF * PF), F32)
    for g in range(groups):
        slots = slice(g * BATCH, (g + 1) * BATCH)
        for c in range(6):
            for row in (0, ROWS_BOX - 8):
                lhs[c * ROWS_BOX + row : c * ROWS_BOX + row + 8, :] = blank
            for x, row in places():
                row += c * ROWS_BOX
                lhs[row : row + BATCH, :] = fine[0, 0, c, slots, x * PF * PF : (x + 1) * PF * PF]
            grown = move(lhs[c * ROWS_BOX : (c + 1) * ROWS_BOX, :], table[...])
            box[g, c] = grown
        for row in (0, ROWS_BOX - 8):
            coefs[row : row + 8, :] = blank
        for x, row in places():
            coefs[row : row + BATCH, :] = 0.5 / perm[0, 0, slots, x * PF * PF : (x + 1) * PF * PF]
        rate[g] = move(coefs[...], table[...])


def fine_kernel(ranks, *refs):
    regions, (box, rate, ghosts, means, out) = refs[:ranks], refs[ranks : ranks + 5]
    smalls = refs[ranks + 5 : 2 * ranks + 5]
    rims, walls, now, halves, small = refs[2 * ranks + 5 :]
    groups = box.shape[0]
    rank = lax.axis_index("gy") * lax.axis_size("gz") + lax.axis_index("gz")
    flat = lane_iota((8, WIDE))
    yy = lax.shift_right_logical(flat * 3641, 16)
    zz = flat - yy * LINE
    inner = (yy >= 1) & (yy <= PF) & (zz >= 1) & (zz <= PF)
    upper = lax.broadcasted_iota(jnp.int32, (8, WIDE), 0) >= BATCH

    def inner_of(m):
        if m == 0:
            return inner & upper
        if m == PLANES - 1:
            return inner & jnp.logical_not(upper)
        return inner

    def up_y(a):
        return pltpu.roll(a, WIDE - LINE, 1)

    def up_z(a):
        return pltpu.roll(a, WIDE - 1, 1)

    def down_y(a):
        return pltpu.roll(a, LINE, 1)

    def down_z(a):
        return pltpu.roll(a, 1, 1)

    def rows_of(m):
        return pl.ds(m * 8, 8)

    blank = jnp.zeros((8, LANES), F32)
    for g in range(groups):
        for c in range(6):
            for m in range(PLANES):
                row = ((g * 6 + c) * PLANES + m) * 8
                if m in (0, PLANES - 1):
                    rims[row : row + 8, :] = blank
                walls[0, row : row + 8, :] = blank
                walls[1, row : row + 8, :] = blank
    for k, region in enumerate(regions):
        slot = lax.bitwise_xor(rank, k)
        start = (slot // BATCH) * 6 * ROWS_BOX + lax.rem(slot, BATCH)
        for c in range(6):
            rows = region[c * 8 : c * 8 + 8, :]
            row = start + c * ROWS_BOX
            rims[pl.ds(row + 8, 4, stride=16), :] = rows[0:4]
            rims[pl.ds(row + 16, 4, stride=16), :] = rows[0:4]
            rims[pl.ds(row + BATCH, 4, stride=16), :] = rows[4:8]
            rims[pl.ds(row + BATCH + 8, 4, stride=16), :] = rows[4:8]
        old = region[ROWS_RIM : ROWS_RIM + 8, :]
        fresh = region[ROWS_RIM + 8 : ROWS_RIM + 16, :]
        for sub, value in enumerate((old, old + 0.5 * (fresh - old))):
            walls[sub, pl.ds(start, 6, stride=ROWS_BOX), :] = value[0:6]
            last = start + ROWS_BOX + (PLANES - 1) * 8 + BATCH
            walls[sub, pl.ds(last, 2, stride=ROWS_BOX), :] = value[6:8]
    for g in range(groups):
        for sub in range(2):
            source = box if sub == 0 else out
            rows = pl.ds(g * 6 * ROWS_BOX, 6 * ROWS_BOX)
            ghost = move(jnp.concatenate([rims[rows, :], walls[sub, rows, :]], axis=1), ghosts[sub])
            for c in range(6):
                for m in range(PLANES):
                    row = c * ROWS_BOX + m * 8
                    now[c, rows_of(m), :] = jnp.where(
                        inner_of(m), source[g, c, rows_of(m), :], ghost[row : row + 8]
                    )

            def next_x(c, m):
                if m == PLANES - 1:
                    return pltpu.roll(now[c, rows_of(0), :], BATCH, 0)
                return now[c, rows_of(m + 1), :]

            def last_x(c, m):
                if m == 0:
                    return pltpu.roll(out[g, c + 3, rows_of(PLANES - 1), :], BATCH, 0)
                return out[g, c + 3, rows_of(m - 1), :]

            for m in range(PLANES):
                e0, e1, e2 = (now[c, rows_of(m), :] for c in range(3))
                h0, h1, h2 = (now[c, rows_of(m), :] for c in range(3, 6))
                out[g, 3, rows_of(m), :] = h0 - 0.5 * ((up_y(e2) - e2) - (up_z(e1) - e1))
                out[g, 4, rows_of(m), :] = h1 - 0.5 * ((up_z(e0) - e0) - (next_x(2, m) - e2))
                out[g, 5, rows_of(m), :] = h2 - 0.5 * ((next_x(1, m) - e1) - (up_y(e0) - e0))
            for m in range(PLANES):
                h0, h1, h2 = (out[g, c, rows_of(m), :] for c in range(3, 6))
                coef = rate[g, rows_of(m), :]
                e0, e1, e2 = (now[c, rows_of(m), :] for c in range(3))
                out[g, 0, rows_of(m), :] = e0 + coef * ((h2 - down_y(h2)) - (h1 - down_z(h1)))
                out[g, 1, rows_of(m), :] = e1 + coef * ((h0 - down_z(h0)) - (h2 - last_x(2, m)))
                out[g, 2, rows_of(m), :] = e2 + coef * ((h1 - last_x(1, m)) - (h0 - down_y(h0)))
        for c in range(6):
            for k in range(4):
                other = jnp.where(upper, out[g, c, rows_of(2 * k), :], out[g, c, rows_of(2 * k + 2), :])
                pair = out[g, c, rows_of(2 * k + 1), :] + other
                halves[pl.ds((c * 2 + k // 2) * 8, 8), (k % 2) * WIDE : (k % 2 + 1) * WIDE] = pair
        small[pl.ds(g * 96, 96), :] = move(halves[...], means[...])
    for k, send in enumerate(smalls):
        slot = lax.bitwise_xor(rank, k)
        start = (slot // BATCH) * 96 + lax.rem(slot, BATCH)
        for xh in range(2):
            send[xh * 12 : (xh + 1) * 12, :] = small[pl.ds(start + xh * BATCH, 12, stride=8), :]


def store_kernel(box, fine, notes, table, out, stage, sems):
    groups = box.shape[0]
    slots = groups * BATCH
    live = jnp.concatenate([notes[8 : 8 + slots, :]] * (PF * PF // LANES), axis=1) > 0
    copies = []
    for c in range(6):
        flats = [move(box[g, c], table[...]) for g in range(groups)]
        for x, row in places():
            cut = slice(x * PF * PF, (x + 1) * PF * PF)
            for g, flat in enumerate(flats):
                some = slice(g * BATCH, (g + 1) * BATCH)
                stage[0, 0, c, some, cut] = jnp.where(live[some], flat[row : row + BATCH], fine[0, 0, c, some, cut])
        copies.append(pltpu.make_async_copy(stage.at[:, :, c], out.at[:, :, c], sems.at[c]))
        copies[-1].start()
    for copy in copies:
        copy.wait()


def fix_kernel(new, rate, *refs):
    edges, out = refs[:-1], refs[-1]
    deep, tall = new.shape[1], new.shape[2]
    gz = lax.axis_index("gz")
    rank = lax.axis_index("gy") * 2 + gz
    out[...] = new[...]

    def add(c, x, rows, amount):
        out[c, x, rows, :] = out[c, x, rows, :] + 0.5 * rate[x, rows, :] * amount

    lower = higher = jnp.zeros((1, LANES), F32)
    for k, edge in enumerate(edges, 1):
        row = ROW_EDGE
        lower = jnp.where(lax.bitwise_xor(rank, k) == rank - 2, edge[row : row + 1, :], lower)
        higher = jnp.where(lax.bitwise_xor(rank, k) == rank + 2, edge[row + 1 : row + 2, :], higher)
    add(0, deep - 1, slice(0, 1), lower)
    add(1, 0, slice(tall - 1, tall), higher)
    lane = lane_iota((tall, LANES))
    tile = edges[0][ROWS_PATCH : ROWS_PATCH + tall, :]
    add(0, deep - 1, slice(0, tall), jnp.where((lane == 0) & (gz == 1), pltpu.roll(tile, 1, 1), 0.0))
    add(2, 0, slice(0, tall), jnp.where((lane == LANES - 1) & (gz == 0), pltpu.roll(tile, LANES - 1, 1), 0.0))
    lane = lane_iota((deep, LANES))
    tile = edges[0][ROWS_PATCH + 16 : ROWS_PATCH + 16 + deep, :]
    first = jnp.where((lane == LANES - 1) & (gz == 0), pltpu.roll(tile, LANES - 1, 1), 0.0)
    last = jnp.where((lane == 0) & (gz == 1), pltpu.roll(tile, 1, 1), 0.0)
    for x in range(deep):
        add(2, x, slice(0, 1), first[x : x + 1])
        add(1, x, slice(tall - 1, tall), last[x : x + 1])


def place_kernel(ranks, new, notes, *refs):
    means, (out, spread, stage, gathered, sems) = refs[:ranks], refs[ranks:]
    noted = notes[0:8, :]
    for k, mean in enumerate(means):
        gathered[k] = mean[...]
    lane = lane_iota((HALF, LANES))
    spots = [tuple(noted[q * 4 + d, 0] for d in range(3)) for q in range(PAR)]
    for q, (cx, cy, cz) in enumerate(spots):
        k = noted[q * 4 + 3, 0]
        rows = gathered[k]
        for odd in range(2):
            for y in range(HALF):
                shift = lax.rem(cz - y * HALF - odd * HALF * HALF + 2 * LANES, LANES)
                spread[q, pl.ds(odd * 192 + y, 24, stride=8), :] = pltpu.roll(rows, shift, 1)
    copies = []
    for c in range(6):
        stage[c] = new[c]
        for q, (cx, cy, cz) in enumerate(spots):
            inside = (lane >= cz) & (lane < cz + HALF)
            for x in range(HALF):
                xh, k = x // 4, x % 4
                tile = spread[q, pl.ds((k % 2) * 192 + (xh * 12 + c * 2 + k // 2) * 8, 8), :]
                spot = stage[c, cx + x, pl.ds(cy, HALF), :]
                stage[c, cx + x, pl.ds(cy, HALF), :] = jnp.where(inside, tile, spot)
        copies.append(pltpu.make_async_copy(stage.at[c], out.at[c], sems.at[c]))
        copies[-1].start()
    for copy in copies:
        copy.wait()


def local(coarse_fields, permittivity, fine_fields, fine_permittivity, patch_corner, patch_owner):
    deep, tall, cols = coarse_fields.shape[1:]
    slots = fine_fields.shape[2]
    groups = slots // BATCH
    count_x, count_y = lax.axis_size("gx"), lax.axis_size("gy")
    two_y = count_y > 2
    vmem = whole()
    shape = jax.ShapeDtypeStruct
    grow = grow_table()

    x_face = shape((5, tall, cols), F32)
    y_face = shape((5, deep, cols), F32)
    kept, *faces = call(
        functools.partial(faces_kernel, two_y),
        [shape(coarse_fields.shape, F32), x_face, y_face, x_face] + [y_face] * two_y,
        [vmem],
    )(coarse_fields)
    got = [
        lax.ppermute(faces[0], "gx", swap_pairs(count_x, 0)),
        lax.ppermute(faces[1], "gy", swap_pairs(count_y, 0)),
        lax.ppermute(faces[2], ("gx", "gz"), full_pairs(count_x)),
    ]
    if two_y:
        got.append(lax.ppermute(faces[3], "gy", swap_pairs(count_y, 1)))
    beside = lax.ppermute(kept, "gz", swap_pairs(2, 0))

    fine = fine_fields.transpose(0, 1, 3, 2, 4)
    notes, rate = call(
        notes_kernel,
        [shape((8 + slots, LANES), jnp.int32), shape(permittivity.shape, F32)],
        [whole(pltpu.SMEM)] * 2 + [vmem],
    )(patch_corner, patch_owner.transpose(0, 2, 1), permittivity)
    box, fine_rate = call(
        load_kernel,
        [shape((groups, 6, ROWS_BOX, WIDE), F32), shape((groups, ROWS_BOX, WIDE), F32)],
        [vmem] * 3,
        [pltpu.VMEM((6 * ROWS_BOX, PF * PF), F32), pltpu.VMEM((ROWS_BOX, PF * PF), F32)],
        size=4_000_000,
    )(fine, fine_permittivity, jnp.asarray(grow, BF16))

    full = deep + 2
    ranks = count_y * lax.axis_size("gz")

    def exchange(parts):
        swaps = [[(r, r ^ k) for r in range(ranks)] for k in range(ranks)]
        got = list(parts)
        for k in [*range(2, ranks), 1]:
            got[k] = lax.ppermute(parts[k], ("gy", "gz"), swaps[k])
        return got

    patches = [shape((ROWS_BESIDE if k == 1 else ROWS_PATCH, LANES), F32) for k in range(ranks)]
    new, *sends = call(
        functools.partial(leap_kernel, two_y, ranks),
        [shape(coarse_fields.shape, F32)] + patches,
        [vmem] * (4 + len(got)),
        [
            pltpu.VMEM((6 * full * 16, LANES), F32),
            pltpu.VMEM((6 * full * 16, LANES), F32),
            pltpu.VMEM((5 * (full - 1) * 16, LANES), F32),
            pltpu.VMEM((6 * deep * 16, LANES), F32),
            pltpu.VMEM((PAR, ROWS_PATCH, LANES), F32),
        ],
    )(kept, beside, rate, notes, *got)
    regions = exchange(sends)

    box, *smalls = call(
        functools.partial(fine_kernel, ranks),
        [shape((groups, 6, ROWS_BOX, WIDE), F32)] + [shape((24, LANES), F32)] * ranks,
        [vmem] * (ranks + 4),
        [
            pltpu.VMEM((groups * 6 * ROWS_BOX, LANES), F32),
            pltpu.VMEM((2, groups * 6 * ROWS_BOX, LANES), F32),
            pltpu.VMEM((6, ROWS_BOX, WIDE), F32),
            pltpu.VMEM((96, 2 * WIDE), F32),
            pltpu.VMEM((groups * 96, LANES), F32),
        ],
    )(*regions, box, fine_rate, jnp.asarray(ghost_table(), BF16), jnp.asarray(mean_table(), BF16))
    means = exchange(smalls)

    fine = call(
        store_kernel,
        shape(fine.shape, F32),
        [vmem] * 4,
        [pltpu.VMEM(fine.shape, F32), pltpu.SemaphoreType.DMA((6,))],
        size=4_000_000,
        out_specs=whole(pltpu.HBM),
    )(box, fine, notes, jnp.asarray(grow.T, BF16))
    new = call(fix_kernel, shape(coarse_fields.shape, F32), [vmem] * (1 + ranks))(new, rate, *regions[1:])
    coarse = call(
        functools.partial(place_kernel, ranks),
        shape(coarse_fields.shape, F32),
        [vmem] * (2 + ranks),
        [
            pltpu.VMEM((PAR, 4 * 96, LANES), F32),
            pltpu.VMEM(coarse_fields.shape, F32),
            pltpu.VMEM((ranks, 24, LANES), F32),
            pltpu.SemaphoreType.DMA((6,)),
        ],
        out_specs=whole(pltpu.HBM),
    )(new, notes, *means)
    return coarse, fine.transpose(0, 1, 3, 2, 4)


def solution(mesh):
    in_specs = (
        P(None, ("groups", "gx"), "gy", "gz"),
        P(("groups", "gx"), "gy", "gz"),
        P(("groups", "gx"), "gy", "gz", None, None),
        P(("groups", "gx"), "gy", "gz", None),
        P(("groups", "gx"), "gy", "gz", None),
        P(("groups", "gx"), None, None),
    )
    out_specs = (P(None, ("groups", "gx"), "gy", "gz"), P(("groups", "gx"), "gy", "gz", None, None))
    return jax.shard_map(local, mesh=mesh, in_specs=in_specs, out_specs=out_specs, check_vma=False)
```

```python
import functools
import jax
import jax.numpy as jnp
import numpy as np
from jax import lax
from jax.experimental import pallas as pl
from jax.experimental.pallas import tpu as pltpu
from jax.sharding import PartitionSpec as P

PF = 16
PAR = 2
HALF = PF // 2
RIM = HALF + 2
PLANES = 9
LINE = PF + 2
LANES = 128
WIDE = 384
BATCH = 4
ROWS_BOX = PLANES * 8
ROWS_RIM = 48
ROW_EDGE = 64
ROWS_PATCH = 72
ROWS_BESIDE = 104
X_COMPS = (0, 1, 2, 4, 5)
Y_COMPS = (0, 1, 2, 3, 5)
VMEM_BYTES = 48 * 1024 * 1024
F32 = jnp.float32
BF16 = jnp.bfloat16


def rim_lane(time, j, k):
    if 0 < j < RIM - 1:
        return j * RIM + k + 3 * time
    if j == 0 and time == 0:
        return k
    return (RIM - 1) * RIM + 3 + (2 * time + j // (RIM - 1) - 1) * RIM + k


def grow_table():
    table = np.zeros((PF * PF, WIDE), np.float32)
    for y in range(PF):
        for z in range(PF):
            table[y * PF + z, (y + 1) * LINE + z + 1] = 1.0
    return table


def ghost_table():
    table = np.zeros((2, 2 * LANES, WIDE), np.float32)
    for y in range(LINE):
        for z in range(LINE):
            j, k, lane = (y + 1) // 2, (z + 1) // 2, y * LINE + z
            table[:, LANES + j * RIM + k, lane] = 1.0
            if y in (0, LINE - 1) or z in (0, LINE - 1):
                table[0, rim_lane(0, j, k), lane] = 1.0
                table[1, rim_lane(0, j, k), lane] = 0.5
                table[1, rim_lane(1, j, k), lane] = 0.5
    return table


def mean_table():
    table = np.zeros((2, WIDE, LANES), np.float32)
    for odd in range(2):
        for y in range(PF):
            for z in range(PF):
                lane = odd * HALF * HALF + (y // 2) * HALF + z // 2
                table[odd, (y + 1) * LINE + z + 1, lane] = 0.125
    return table.reshape(2 * WIDE, LANES)


def move(rows, table):
    high = rows.astype(BF16)
    low = (rows - high.astype(F32)).astype(BF16)
    out = jnp.dot(jnp.concatenate([high, low], axis=0), table, preferred_element_type=F32)
    return out[: rows.shape[0]] + out[rows.shape[0] :]


def lane_iota(shape):
    return lax.broadcasted_iota(jnp.int32, shape, len(shape) - 1)


def whole(memory_space=pltpu.VMEM):
    return pl.BlockSpec(memory_space=memory_space)


def call(kernel, outs, in_specs, scratch=(), flops=1_000_000, size=1_000_000, out_specs=None, **extra):
    return pl.pallas_call(
        kernel,
        out_shape=outs,
        in_specs=in_specs,
        out_specs=jax.tree.map(lambda _: whole(), outs) if out_specs is None else out_specs,
        scratch_shapes=list(scratch),
        compiler_params=pltpu.CompilerParams(vmem_limit_bytes=VMEM_BYTES),
        cost_estimate=pl.CostEstimate(flops=flops, bytes_accessed=size, transcendentals=0),
        **extra,
    )


def swap_pairs(count, first):
    pairs = []
    for i in range(first, count - 1, 2):
        pairs += [(i, i + 1), (i + 1, i)]
    return pairs


def full_pairs(count_x):
    pairs = []
    for i in range(count_x):
        for j in range(2):
            if 0 < i < count_x - 1:
                target = (i + 1 if i % 2 else i - 1) * 2 + j
            else:
                target = i * 2 + 1 - j
            pairs.append((i * 2 + j, target))
    return pairs


def faces_kernel(two_y, block, kept, x_even, y_even, x_odd, *y_odd):
    deep, tall = block.shape[1], block.shape[2]
    gx_odd = lax.rem(lax.axis_index("gx"), 2)
    gy_odd = lax.rem(lax.axis_index("gy"), 2)
    for k, c in enumerate(X_COMPS):
        x_even[k] = block[c, (1 - gx_odd) * (deep - 1)]
        x_odd[k] = block[c, gx_odd * (deep - 1)]
    for k, c in enumerate(Y_COMPS):
        for x in range(deep):
            first = block[c, x, 0:1, :]
            last = block[c, x, tall - 1 : tall, :]
            y_even[k, x : x + 1, :] = jnp.where(gy_odd == 0, last, first)
            if two_y:
                y_odd[0][k, x : x + 1, :] = jnp.where(gy_odd == 0, first, last)
    kept[...] = block[...]


def pack(source, deep, spot, time, packed, q, early):
    lane = lane_iota((8, LANES))
    cx, cy, cz = spot

    def rows_of(c, k, j, count, over_c):
        step = deep * 16 if over_c else 16
        return source[pl.ds((c * deep + cx - 1 + k) * 16 + cy + (j - 1), count, stride=step), :]

    def aim(rows, target):
        return pltpu.roll(rows, lax.rem(target - (cz - 1) + 2 * LANES, LANES), 1)

    for c in range(6):
        total = jnp.zeros((8, LANES), F32) if early is None else early[q, c * 8 : c * 8 + 8, :]
        for j in range(RIM):
            if (j == 0 and c == 4) or (j == RIM - 1 and c not in (0, 2)) or (0 < j < RIM - 1 and c == 5):
                continue
            first = rim_lane(time, j, 0)
            if j in (0, RIM - 1):
                inside = (lane >= first) & (lane < first + RIM)
            else:
                inside = (lane == first) | (lane == first + RIM - 1)
            total = jnp.where(inside, aim(rows_of(c, 1, j, 8, False), first), total)
        packed[q, c * 8 : c * 8 + 8, :] = total
    low = jnp.zeros((6, LANES), F32)
    high = jnp.zeros((2, LANES), F32)
    for j in range(RIM):
        first = j * RIM
        inside = (lane >= first) & (lane < first + RIM)
        low = jnp.where(inside[0:6], aim(rows_of(0, 0, j, 6, True), first), low)
        high = jnp.where(inside[0:2], aim(rows_of(1, RIM - 1, j, 2, True), first), high)
    base = ROWS_RIM + time * 8
    packed[q, base : base + 6, :] = low
    packed[q, base + 6 : base + 8, :] = high
    if early is not None:
        packed[q, ROWS_RIM:base, :] = early[q, ROWS_RIM:base, :]


def notes_kernel(corner, owners, perm, block, notes, rate, early, flat):
    rank = lax.axis_index("gy") * lax.axis_size("gz") + lax.axis_index("gz")

    def note(row, value):
        notes[row : row + 1, :] = jnp.full((1, LANES), value, jnp.int32)

    for q in range(PAR):
        for d in range(3):
            note(q * 4 + d, corner[0, 0, q, d])
        note(q * 4 + 3, lax.bitwise_xor(owners[0, q, rank], rank))
    for slot in range(notes.shape[0] - 8):
        live = (owners[0, 0, slot] == rank) | (owners[0, 1, slot] == rank)
        note(8 + slot, live.astype(jnp.int32))
    rate[...] = 0.5 / perm[...]
    deep, tall = block.shape[1], block.shape[2]
    for c in range(6):
        for x in range(deep):
            flat[pl.ds((c * deep + x) * 16, tall), :] = block[c, x]
    for q in range(PAR):
        spot = [corner[0, 0, q, d] for d in range(3)]
        pack(flat, deep, spot, 0, early, q, None)


def leap_kernel(two_y, ranks, *refs):
    block, beside, rate, notes, early, x_even, y_even, x_odd = refs[:8]
    y_odd = refs[8] if two_y else None
    refs = refs[8 + two_y :]
    new, sends = refs[0], refs[1 : 1 + ranks]
    pad, side, mag, fresh, packed = refs[1 + ranks :]
    deep, tall = block.shape[1], block.shape[2]
    full = deep + 2
    gx = lax.axis_index("gx")
    gx_odd = lax.rem(gx, 2)
    gy_odd = lax.rem(lax.axis_index("gy"), 2)
    gz = lax.axis_index("gz")
    noted = notes[0:8, :]
    spots = [[noted[q * 4 + d, 0] for d in range(3)] for q in range(PAR)]
    chosen = noted[3, 0]
    lane = lane_iota((tall, LANES))
    keep = ((lane == 0) & (gz == 0)) | ((lane == LANES - 1) & (gz == 1))
    lane = lane_iota((16, LANES))
    none = jnp.zeros((16, LANES), F32)

    def at(c, x):
        return (c * full + x) * 16

    for c in range(6):
        for x in (0, full - 1):
            pad[pl.ds(at(c, x), 16), :] = none
        for x in range(deep):
            pad[pl.ds(at(c, x + 1), tall), :] = block[c, x]
        pad[pl.ds(at(c, 1) + tall, deep, stride=16), :] = none[0:deep]
        pad[pl.ds(at(c, 1) + 15, deep, stride=16), :] = none[0:deep]
    for c in range(5):
        for x in (0, full - 1):
            side[pl.ds(at(c, x), 16), :] = none
        for x in range(deep):
            side[pl.ds(at(c, x + 1), 16), :] = none
            side[pl.ds(at(c, x + 1), tall), :] = jnp.where(keep, beside[c, x], 0.0)
    for k, c in enumerate(X_COMPS):
        even, odd = x_even[k], x_odd[k]
        low, high = jnp.where(gx_odd == 0, odd, even), jnp.where(gx_odd == 0, even, odd)
        pad[pl.ds(at(c, 0), tall), :] = jnp.where(gx == 0, 0.0, low)
        if c in (1, 2):
            pad[pl.ds(at(c, full - 1), tall), :] = jnp.where(gx == lax.axis_size("gx") - 1, 0.0, high)
    for k, c in enumerate(Y_COMPS):
        even = y_even[k]
        odd = jnp.zeros_like(even) if y_odd is None else y_odd[k]
        pad[pl.ds(at(c, 1) + 15, deep, stride=16), :] = jnp.where(gy_odd == 0, odd, even)
        if c in (0, 2):
            pad[pl.ds(at(c, 1) + tall, deep, stride=16), :] = jnp.where(gy_odd == 0, even, odd)

    def up_y(a):
        return pltpu.roll(a, 15, 0)

    def down_y(a):
        return pltpu.roll(a, 1, 0)

    def plane(c, x):
        return pad[pl.ds(at(c, x), 16), :]

    def edge(c, x):
        return side[pl.ds(at(c, x), 16), :]

    def field(c, x):
        return mag[pl.ds((c * (full - 1) + x) * 16, 16), :]

    for x in range(full - 1):
        e0, e1, e2 = plane(0, x), plane(1, x), plane(2, x)
        s0, s1, s2 = edge(0, x), edge(1, x), edge(2, x)
        r0, r1 = pltpu.roll(e0, LANES - 1, 1), pltpu.roll(e1, LANES - 1, 1)
        u0 = jnp.where(lane == LANES - 1, pltpu.roll(s0, LANES - 1, 1), r0)
        u1 = jnp.where(lane == LANES - 1, pltpu.roll(s1, LANES - 1, 1), r1)
        h0 = plane(3, x) - 0.5 * ((up_y(e2) - e2) - (u1 - e1))
        h1 = plane(4, x) - 0.5 * ((u0 - e0) - (plane(2, x + 1) - e2))
        h2 = plane(5, x) - 0.5 * ((plane(1, x + 1) - e1) - (up_y(e0) - e0))
        t0 = edge(3, x) - 0.5 * ((up_y(s2) - s2) - (r1 - s1))
        t1 = edge(4, x) - 0.5 * ((r0 - s0) - (edge(2, x + 1) - s2))
        d0 = pltpu.roll(jnp.where(lane == LANES - 1, t0, h0), 1, 1)
        d1 = pltpu.roll(jnp.where(lane == LANES - 1, t1, h1), 1, 1)
        for c, value in enumerate((h0, h1, h2, d0, d1)):
            mag[pl.ds((c * (full - 1) + x) * 16, 16), :] = value
    for x in range(deep):
        h0, h1, h2, d0, d1 = (field(c, x + 1) for c in range(5))
        coef = rate[x]
        c0 = (h2 - down_y(h2)) - (h1 - d1)
        c1 = (h0 - d0) - (h2 - field(2, x))
        c2 = (h1 - field(1, x)) - (h0 - down_y(h0))
        for c, curl in enumerate((c0, c1, c2)):
            value = plane(c, x + 1)[0:tall] + coef * curl[0:tall]
            new[c, x] = value
            new[c + 3, x] = (h0, h1, h2)[c][0:tall]
            fresh[pl.ds((c * deep + x) * 16, tall), :] = value
            fresh[pl.ds(((c + 3) * deep + x) * 16, tall), :] = (h0, h1, h2)[c][0:tall]
    for q in range(PAR):
        pack(fresh, deep, spots[q], 1, packed, q, early)
        packed[q, ROW_EDGE:ROWS_PATCH, :] = jnp.zeros((ROWS_PATCH - ROW_EDGE, LANES), F32)
        packed[q, ROW_EDGE : ROW_EDGE + 1, :] = pad[pl.ds(at(1, full - 1) + tall - 1, 1), :]
        packed[q, ROW_EDGE + 1 : ROW_EDGE + 2, :] = pad[pl.ds(at(0, 0), 1), :]
    for k, send in enumerate(sends):
        q = jnp.where(chosen == k, 0, 1)
        send[0:ROWS_PATCH, :] = packed[q]
    half = lane_iota((16, LANES)) < LANES // 2
    send = sends[1]
    send[ROWS_PATCH : ROWS_PATCH + 16, :] = jnp.where(half, plane(0, 0), plane(2, full - 1))
    low = jnp.where(gy_odd == 0, jnp.zeros_like(y_even[1]) if y_odd is None else y_odd[1], y_even[1])
    high = jnp.where(gy_odd == 0, y_even[2], jnp.zeros_like(y_even[2]) if y_odd is None else y_odd[2])
    send[ROWS_PATCH + 16 : ROWS_PATCH + 32, :] = jnp.zeros((16, LANES), F32)
    send[ROWS_PATCH + 16 : ROWS_PATCH + 16 + deep, :] = jnp.where(half[0:deep], low, high)


def places():
    for x in range(PF):
        yield x, (x % 8 + 1) * 8 if x < 8 else (x % 8) * 8 + BATCH


def load_kernel(fine, perm, table, box, rate, lhs, coefs):
    groups = fine.shape[3] // BATCH
    blank = jnp.zeros((8, PF * PF), F32)
    for g in range(groups):
        slots = slice(g * BATCH, (g + 1) * BATCH)
        for c in range(6):
            for row in (0, ROWS_BOX - 8):
                lhs[c * ROWS_BOX + row : c * ROWS_BOX + row + 8, :] = blank
            for x, row in places():
                row += c * ROWS_BOX
                lhs[row : row + BATCH, :] = fine[0, 0, c, slots, x * PF * PF : (x + 1) * PF * PF]
            grown = move(lhs[c * ROWS_BOX : (c + 1) * ROWS_BOX, :], table[...])
            box[g, c] = grown
        for row in (0, ROWS_BOX - 8):
            coefs[row : row + 8, :] = blank
        for x, row in places():
            coefs[row : row + BATCH, :] = 0.5 / perm[0, 0, slots, x * PF * PF : (x + 1) * PF * PF]
        rate[g] = move(coefs[...], table[...])


def fine_kernel(ranks, *refs):
    regions, (box, rate, ghosts, means, out) = refs[:ranks], refs[ranks : ranks + 5]
    smalls = refs[ranks + 5 : 2 * ranks + 5]
    rims, walls, now, halves, small = refs[2 * ranks + 5 :]
    groups = box.shape[0]
    rank = lax.axis_index("gy") * lax.axis_size("gz") + lax.axis_index("gz")
    flat = lane_iota((8, WIDE))
    yy = lax.shift_right_logical(flat * 3641, 16)
    zz = flat - yy * LINE
    inner = (yy >= 1) & (yy <= PF) & (zz >= 1) & (zz <= PF)
    upper = lax.broadcasted_iota(jnp.int32, (8, WIDE), 0) >= BATCH

    def inner_of(m):
        if m == 0:
            return inner & upper
        if m == PLANES - 1:
            return inner & jnp.logical_not(upper)
        return inner

    def up_y(a):
        return pltpu.roll(a, WIDE - LINE, 1)

    def up_z(a):
        return pltpu.roll(a, WIDE - 1, 1)

    def down_y(a):
        return pltpu.roll(a, LINE, 1)

    def down_z(a):
        return pltpu.roll(a, 1, 1)

    def rows_of(m):
        return pl.ds(m * 8, 8)

    blank = jnp.zeros((8, LANES), F32)
    for g in range(groups):
        for c in range(6):
            for m in range(PLANES):
                row = ((g * 6 + c) * PLANES + m) * 8
                if m in (0, PLANES - 1):
                    rims[row : row + 8, :] = blank
                walls[0, row : row + 8, :] = blank
                walls[1, row : row + 8, :] = blank
    for k, region in enumerate(regions):
        slot = lax.bitwise_xor(rank, k)
        start = (slot // BATCH) * 6 * ROWS_BOX + lax.rem(slot, BATCH)
        for c in range(6):
            rows = region[c * 8 : c * 8 + 8, :]
            row = start + c * ROWS_BOX
            rims[pl.ds(row + 8, 4, stride=16), :] = rows[0:4]
            rims[pl.ds(row + 16, 4, stride=16), :] = rows[0:4]
            rims[pl.ds(row + BATCH, 4, stride=16), :] = rows[4:8]
            rims[pl.ds(row + BATCH + 8, 4, stride=16), :] = rows[4:8]
        old = region[ROWS_RIM : ROWS_RIM + 8, :]
        fresh = region[ROWS_RIM + 8 : ROWS_RIM + 16, :]
        for sub, value in enumerate((old, old + 0.5 * (fresh - old))):
            walls[sub, pl.ds(start, 6, stride=ROWS_BOX), :] = value[0:6]
            last = start + ROWS_BOX + (PLANES - 1) * 8 + BATCH
            walls[sub, pl.ds(last, 2, stride=ROWS_BOX), :] = value[6:8]
    for g in range(groups):
        for sub in range(2):
            source = box if sub == 0 else out
            rows = pl.ds(g * 6 * ROWS_BOX, 6 * ROWS_BOX)
            ghost = move(jnp.concatenate([rims[rows, :], walls[sub, rows, :]], axis=1), ghosts[sub])
            for c in range(6):
                for m in range(PLANES):
                    row = c * ROWS_BOX + m * 8
                    now[c, rows_of(m), :] = jnp.where(
                        inner_of(m), source[g, c, rows_of(m), :], ghost[row : row + 8]
                    )

            def next_x(c, m):
                if m == PLANES - 1:
                    return pltpu.roll(now[c, rows_of(0), :], BATCH, 0)
                return now[c, rows_of(m + 1), :]

            def last_x(c, m):
                if m == 0:
                    return pltpu.roll(out[g, c + 3, rows_of(PLANES - 1), :], BATCH, 0)
                return out[g, c + 3, rows_of(m - 1), :]

            for m in range(PLANES):
                e0, e1, e2 = (now[c, rows_of(m), :] for c in range(3))
                h0, h1, h2 = (now[c, rows_of(m), :] for c in range(3, 6))
                out[g, 3, rows_of(m), :] = h0 - 0.5 * ((up_y(e2) - e2) - (up_z(e1) - e1))
                out[g, 4, rows_of(m), :] = h1 - 0.5 * ((up_z(e0) - e0) - (next_x(2, m) - e2))
                out[g, 5, rows_of(m), :] = h2 - 0.5 * ((next_x(1, m) - e1) - (up_y(e0) - e0))
            for m in range(PLANES):
                h0, h1, h2 = (out[g, c, rows_of(m), :] for c in range(3, 6))
                coef = rate[g, rows_of(m), :]
                e0, e1, e2 = (now[c, rows_of(m), :] for c in range(3))
                out[g, 0, rows_of(m), :] = e0 + coef * ((h2 - down_y(h2)) - (h1 - down_z(h1)))
                out[g, 1, rows_of(m), :] = e1 + coef * ((h0 - down_z(h0)) - (h2 - last_x(2, m)))
                out[g, 2, rows_of(m), :] = e2 + coef * ((h1 - last_x(1, m)) - (h0 - down_y(h0)))
        for c in range(6):
            for k in range(4):
                other = jnp.where(upper, out[g, c, rows_of(2 * k), :], out[g, c, rows_of(2 * k + 2), :])
                pair = out[g, c, rows_of(2 * k + 1), :] + other
                halves[pl.ds((c * 2 + k // 2) * 8, 8), (k % 2) * WIDE : (k % 2 + 1) * WIDE] = pair
        small[pl.ds(g * 96, 96), :] = move(halves[...], means[...])
    for k, send in enumerate(smalls):
        slot = lax.bitwise_xor(rank, k)
        start = (slot // BATCH) * 96 + lax.rem(slot, BATCH)
        for xh in range(2):
            send[xh * 12 : (xh + 1) * 12, :] = small[pl.ds(start + xh * BATCH, 12, stride=8), :]


def store_kernel(box, fine, notes, table, out, stage, sems):
    groups = box.shape[0]
    slots = groups * BATCH
    live = jnp.concatenate([notes[8 : 8 + slots, :]] * (PF * PF // LANES), axis=1) > 0
    copies = []
    for c in range(6):
        flats = [move(box[g, c], table[...]) for g in range(groups)]
        for x, row in places():
            cut = slice(x * PF * PF, (x + 1) * PF * PF)
            for g, flat in enumerate(flats):
                some = slice(g * BATCH, (g + 1) * BATCH)
                stage[0, 0, c, some, cut] = jnp.where(live[some], flat[row : row + BATCH], fine[0, 0, c, some, cut])
        copies.append(pltpu.make_async_copy(stage.at[:, :, c], out.at[:, :, c], sems.at[c]))
        copies[-1].start()
    for copy in copies:
        copy.wait()


def fix_kernel(new, rate, *refs):
    edges, out = refs[:-1], refs[-1]
    deep, tall = new.shape[1], new.shape[2]
    gz = lax.axis_index("gz")
    rank = lax.axis_index("gy") * 2 + gz
    out[...] = new[...]

    def add(c, x, rows, amount):
        out[c, x, rows, :] = out[c, x, rows, :] + 0.5 * rate[x, rows, :] * amount

    lower = higher = jnp.zeros((1, LANES), F32)
    for k, edge in enumerate(edges, 1):
        row = ROW_EDGE
        lower = jnp.where(lax.bitwise_xor(rank, k) == rank - 2, edge[row : row + 1, :], lower)
        higher = jnp.where(lax.bitwise_xor(rank, k) == rank + 2, edge[row + 1 : row + 2, :], higher)
    add(0, deep - 1, slice(0, 1), lower)
    add(1, 0, slice(tall - 1, tall), higher)
    lane = lane_iota((tall, LANES))
    tile = edges[0][ROWS_PATCH : ROWS_PATCH + tall, :]
    add(0, deep - 1, slice(0, tall), jnp.where((lane == 0) & (gz == 1), pltpu.roll(tile, 1, 1), 0.0))
    add(2, 0, slice(0, tall), jnp.where((lane == LANES - 1) & (gz == 0), pltpu.roll(tile, LANES - 1, 1), 0.0))
    lane = lane_iota((deep, LANES))
    tile = edges[0][ROWS_PATCH + 16 : ROWS_PATCH + 16 + deep, :]
    first = jnp.where((lane == LANES - 1) & (gz == 0), pltpu.roll(tile, LANES - 1, 1), 0.0)
    last = jnp.where((lane == 0) & (gz == 1), pltpu.roll(tile, 1, 1), 0.0)
    for x in range(deep):
        add(2, x, slice(0, 1), first[x : x + 1])
        add(1, x, slice(tall - 1, tall), last[x : x + 1])


def place_kernel(ranks, new, notes, *refs):
    means, (out, spread, stage, gathered, sems) = refs[:ranks], refs[ranks:]
    noted = notes[0:8, :]
    for k, mean in enumerate(means):
        gathered[k] = mean[...]
    lane = lane_iota((HALF, LANES))
    spots = [tuple(noted[q * 4 + d, 0] for d in range(3)) for q in range(PAR)]
    for q, (cx, cy, cz) in enumerate(spots):
        k = noted[q * 4 + 3, 0]
        rows = gathered[k]
        for odd in range(2):
            for y in range(HALF):
                shift = lax.rem(cz - y * HALF - odd * HALF * HALF + 2 * LANES, LANES)
                spread[q, pl.ds(odd * 192 + y, 24, stride=8), :] = pltpu.roll(rows, shift, 1)
    copies = []
    for c in range(6):
        stage[c] = new[c]
        for q, (cx, cy, cz) in enumerate(spots):
            inside = (lane >= cz) & (lane < cz + HALF)
            for x in range(HALF):
                xh, k = x // 4, x % 4
                tile = spread[q, pl.ds((k % 2) * 192 + (xh * 12 + c * 2 + k // 2) * 8, 8), :]
                spot = stage[c, cx + x, pl.ds(cy, HALF), :]
                stage[c, cx + x, pl.ds(cy, HALF), :] = jnp.where(inside, tile, spot)
        copies.append(pltpu.make_async_copy(stage.at[c], out.at[c], sems.at[c]))
        copies[-1].start()
    for copy in copies:
        copy.wait()


def local(coarse_fields, permittivity, fine_fields, fine_permittivity, patch_corner, patch_owner):
    deep, tall, cols = coarse_fields.shape[1:]
    slots = fine_fields.shape[2]
    groups = slots // BATCH
    count_x, count_y = lax.axis_size("gx"), lax.axis_size("gy")
    two_y = count_y > 2
    vmem = whole()
    shape = jax.ShapeDtypeStruct
    grow = grow_table()

    x_face = shape((5, tall, cols), F32)
    y_face = shape((5, deep, cols), F32)
    kept, *faces = call(
        functools.partial(faces_kernel, two_y),
        [shape(coarse_fields.shape, F32), x_face, y_face, x_face] + [y_face] * two_y,
        [vmem],
    )(coarse_fields)
    got = [
        lax.ppermute(faces[0], "gx", swap_pairs(count_x, 0)),
        lax.ppermute(faces[1], "gy", swap_pairs(count_y, 0)),
        lax.ppermute(faces[2], ("gx", "gz"), full_pairs(count_x)),
    ]
    if two_y:
        got.append(lax.ppermute(faces[3], "gy", swap_pairs(count_y, 1)))
    beside = lax.ppermute(kept, "gz", swap_pairs(2, 0))

    fine = fine_fields.transpose(0, 1, 3, 2, 4)
    notes, rate, early = call(
        notes_kernel,
        [
            shape((8 + slots, LANES), jnp.int32),
            shape(permittivity.shape, F32),
            shape((PAR, ROWS_RIM + 8, LANES), F32),
        ],
        [whole(pltpu.SMEM)] * 2 + [vmem] * 2,
        [pltpu.VMEM((6 * deep * 16, LANES), F32)],
    )(patch_corner, patch_owner.transpose(0, 2, 1), permittivity, kept)
    box, fine_rate = call(
        load_kernel,
        [shape((groups, 6, ROWS_BOX, WIDE), F32), shape((groups, ROWS_BOX, WIDE), F32)],
        [vmem] * 3,
        [pltpu.VMEM((6 * ROWS_BOX, PF * PF), F32), pltpu.VMEM((ROWS_BOX, PF * PF), F32)],
        size=4_000_000,
    )(fine, fine_permittivity, jnp.asarray(grow, BF16))

    full = deep + 2
    ranks = count_y * lax.axis_size("gz")

    def exchange(parts):
        swaps = [[(r, r ^ k) for r in range(ranks)] for k in range(ranks)]
        got = list(parts)
        for k in [*range(2, ranks), 1]:
            got[k] = lax.ppermute(parts[k], ("gy", "gz"), swaps[k])
        return got

    patches = [shape((ROWS_BESIDE if k == 1 else ROWS_PATCH, LANES), F32) for k in range(ranks)]
    new, *sends = call(
        functools.partial(leap_kernel, two_y, ranks),
        [shape(coarse_fields.shape, F32)] + patches,
        [vmem] * (5 + len(got)),
        [
            pltpu.VMEM((6 * full * 16, LANES), F32),
            pltpu.VMEM((6 * full * 16, LANES), F32),
            pltpu.VMEM((5 * (full - 1) * 16, LANES), F32),
            pltpu.VMEM((6 * deep * 16, LANES), F32),
            pltpu.VMEM((PAR, ROWS_PATCH, LANES), F32),
        ],
    )(kept, beside, rate, notes, early, *got)
    regions = exchange(sends)

    box, *smalls = call(
        functools.partial(fine_kernel, ranks),
        [shape((groups, 6, ROWS_BOX, WIDE), F32)] + [shape((24, LANES), F32)] * ranks,
        [vmem] * (ranks + 4),
        [
            pltpu.VMEM((groups * 6 * ROWS_BOX, LANES), F32),
            pltpu.VMEM((2, groups * 6 * ROWS_BOX, LANES), F32),
            pltpu.VMEM((6, ROWS_BOX, WIDE), F32),
            pltpu.VMEM((96, 2 * WIDE), F32),
            pltpu.VMEM((groups * 96, LANES), F32),
        ],
    )(*regions, box, fine_rate, jnp.asarray(ghost_table(), BF16), jnp.asarray(mean_table(), BF16))
    means = exchange(smalls)

    fine = call(
        store_kernel,
        shape(fine.shape, F32),
        [vmem] * 4,
        [pltpu.VMEM(fine.shape, F32), pltpu.SemaphoreType.DMA((6,))],
        size=4_000_000,
        out_specs=whole(pltpu.HBM),
    )(box, fine, notes, jnp.asarray(grow.T, BF16))
    new = call(fix_kernel, shape(coarse_fields.shape, F32), [vmem] * (1 + ranks))(new, rate, *regions[1:])
    coarse = call(
        functools.partial(place_kernel, ranks),
        shape(coarse_fields.shape, F32),
        [vmem] * (2 + ranks),
        [
            pltpu.VMEM((PAR, 4 * 96, LANES), F32),
            pltpu.VMEM(coarse_fields.shape, F32),
            pltpu.VMEM((ranks, 24, LANES), F32),
            pltpu.SemaphoreType.DMA((6,)),
        ],
        out_specs=whole(pltpu.HBM),
    )(new, notes, *means)
    return coarse, fine.transpose(0, 1, 3, 2, 4)


def solution(mesh):
    in_specs = (
        P(None, ("groups", "gx"), "gy", "gz"),
        P(("groups", "gx"), "gy", "gz"),
        P(("groups", "gx"), "gy", "gz", None, None),
        P(("groups", "gx"), "gy", "gz", None),
        P(("groups", "gx"), "gy", "gz", None),
        P(("groups", "gx"), None, None),
    )
    out_specs = (P(None, ("groups", "gx"), "gy", "gz"), P(("groups", "gx"), "gy", "gz", None, None))
    return jax.shard_map(local, mesh=mesh, in_specs=in_specs, out_specs=out_specs, check_vma=False)
```

```python
import functools
import jax
import jax.numpy as jnp
import numpy as np
from jax import lax
from jax.experimental import pallas as pl
from jax.experimental.pallas import tpu as pltpu
from jax.sharding import PartitionSpec as P

PF = 16
PAR = 2
HALF = PF // 2
RIM = HALF + 2
PLANES = 9
LINE = PF + 2
LANES = 128
WIDE = 384
BATCH = 4
ROWS_BOX = PLANES * 8
ROWS_RIM = 48
ROW_EDGE = 64
ROWS_PATCH = 72
ROWS_BESIDE = 104
X_COMPS = (0, 1, 2, 4, 5)
Y_COMPS = (0, 1, 2, 3, 5)
VMEM_BYTES = 48 * 1024 * 1024
F32 = jnp.float32
BF16 = jnp.bfloat16


def rim_lane(time, j, k):
    if 0 < j < RIM - 1:
        return j * RIM + k + 3 * time
    if j == 0 and time == 0:
        return k
    return (RIM - 1) * RIM + 3 + (2 * time + j // (RIM - 1) - 1) * RIM + k


def grow_table():
    table = np.zeros((PF * PF, WIDE), np.float32)
    for y in range(PF):
        for z in range(PF):
            table[y * PF + z, (y + 1) * LINE + z + 1] = 1.0
    return table


def ghost_table():
    table = np.zeros((2, 2 * LANES, WIDE), np.float32)
    for y in range(LINE):
        for z in range(LINE):
            j, k, lane = (y + 1) // 2, (z + 1) // 2, y * LINE + z
            table[:, LANES + j * RIM + k, lane] = 1.0
            if y in (0, LINE - 1) or z in (0, LINE - 1):
                table[0, rim_lane(0, j, k), lane] = 1.0
                table[1, rim_lane(0, j, k), lane] = 0.5
                table[1, rim_lane(1, j, k), lane] = 0.5
    return table


def mean_table():
    table = np.zeros((2, WIDE, LANES), np.float32)
    for odd in range(2):
        for y in range(PF):
            for z in range(PF):
                lane = odd * HALF * HALF + (y // 2) * HALF + z // 2
                table[odd, (y + 1) * LINE + z + 1, lane] = 0.125
    return table.reshape(2 * WIDE, LANES)


def move(rows, table):
    high = rows.astype(BF16)
    low = (rows - high.astype(F32)).astype(BF16)
    out = jnp.dot(jnp.concatenate([high, low], axis=0), table, preferred_element_type=F32)
    return out[: rows.shape[0]] + out[rows.shape[0] :]


def lane_iota(shape):
    return lax.broadcasted_iota(jnp.int32, shape, len(shape) - 1)


def whole(memory_space=pltpu.VMEM):
    return pl.BlockSpec(memory_space=memory_space)


def call(kernel, outs, in_specs, scratch=(), flops=1_000_000, size=1_000_000, out_specs=None, **extra):
    return pl.pallas_call(
        kernel,
        out_shape=outs,
        in_specs=in_specs,
        out_specs=jax.tree.map(lambda _: whole(), outs) if out_specs is None else out_specs,
        scratch_shapes=list(scratch),
        compiler_params=pltpu.CompilerParams(vmem_limit_bytes=VMEM_BYTES),
        cost_estimate=pl.CostEstimate(flops=flops, bytes_accessed=size, transcendentals=0),
        **extra,
    )


def swap_pairs(count, first):
    pairs = []
    for i in range(first, count - 1, 2):
        pairs += [(i, i + 1), (i + 1, i)]
    return pairs


def full_pairs(count_x):
    pairs = []
    for i in range(count_x):
        for j in range(2):
            if 0 < i < count_x - 1:
                target = (i + 1 if i % 2 else i - 1) * 2 + j
            else:
                target = i * 2 + 1 - j
            pairs.append((i * 2 + j, target))
    return pairs


def far_first(parts):
    return [parts[0], *parts[2:], parts[1]]


def by_rank(parts):
    return [parts[0], parts[-1], *parts[1:-1]]


def faces_kernel(two_y, block, kept, x_even, y_even, x_odd, *y_odd):
    deep, tall = block.shape[1], block.shape[2]
    gx_odd = lax.rem(lax.axis_index("gx"), 2)
    gy_odd = lax.rem(lax.axis_index("gy"), 2)
    for k, c in enumerate(X_COMPS):
        x_even[k] = block[c, (1 - gx_odd) * (deep - 1)]
        x_odd[k] = block[c, gx_odd * (deep - 1)]
    for k, c in enumerate(Y_COMPS):
        for x in range(deep):
            first = block[c, x, 0:1, :]
            last = block[c, x, tall - 1 : tall, :]
            y_even[k, x : x + 1, :] = jnp.where(gy_odd == 0, last, first)
            if two_y:
                y_odd[0][k, x : x + 1, :] = jnp.where(gy_odd == 0, first, last)
    kept[...] = block[...]


def pack(source, deep, spot, time, packed, q, early):
    lane = lane_iota((8, LANES))
    cx, cy, cz = spot

    def rows_of(c, k, j, count, over_c):
        step = deep * 16 if over_c else 16
        return source[pl.ds((c * deep + cx - 1 + k) * 16 + cy + (j - 1), count, stride=step), :]

    def aim(rows, target):
        return pltpu.roll(rows, lax.rem(target - (cz - 1) + 2 * LANES, LANES), 1)

    for c in range(6):
        total = jnp.zeros((8, LANES), F32) if early is None else early[q, c * 8 : c * 8 + 8, :]
        for j in range(RIM):
            if (j == 0 and c == 4) or (j == RIM - 1 and c not in (0, 2)) or (0 < j < RIM - 1 and c == 5):
                continue
            first = rim_lane(time, j, 0)
            if j in (0, RIM - 1):
                inside = (lane >= first) & (lane < first + RIM)
            else:
                inside = (lane == first) | (lane == first + RIM - 1)
            total = jnp.where(inside, aim(rows_of(c, 1, j, 8, False), first), total)
        packed[q, c * 8 : c * 8 + 8, :] = total
    low = jnp.zeros((6, LANES), F32)
    high = jnp.zeros((2, LANES), F32)
    for j in range(RIM):
        first = j * RIM
        inside = (lane >= first) & (lane < first + RIM)
        low = jnp.where(inside[0:6], aim(rows_of(0, 0, j, 6, True), first), low)
        high = jnp.where(inside[0:2], aim(rows_of(1, RIM - 1, j, 2, True), first), high)
    base = ROWS_RIM + time * 8
    packed[q, base : base + 6, :] = low
    packed[q, base + 6 : base + 8, :] = high
    if early is not None:
        packed[q, ROWS_RIM:base, :] = early[q, ROWS_RIM:base, :]


def notes_kernel(corner, owners, perm, block, notes, rate, early, flat):
    rank = lax.axis_index("gy") * lax.axis_size("gz") + lax.axis_index("gz")

    def note(row, value):
        notes[row : row + 1, :] = jnp.full((1, LANES), value, jnp.int32)

    for q in range(PAR):
        for d in range(3):
            note(q * 4 + d, corner[0, 0, q, d])
        note(q * 4 + 3, lax.bitwise_xor(owners[0, q, rank], rank))
    for slot in range(notes.shape[0] - 8):
        live = (owners[0, 0, slot] == rank) | (owners[0, 1, slot] == rank)
        note(8 + slot, live.astype(jnp.int32))
    rate[...] = 0.5 / perm[...]
    deep, tall = block.shape[1], block.shape[2]
    for c in range(6):
        for x in range(deep):
            flat[pl.ds((c * deep + x) * 16, tall), :] = block[c, x]
    for q in range(PAR):
        spot = [corner[0, 0, q, d] for d in range(3)]
        pack(flat, deep, spot, 0, early, q, None)


def leap_kernel(two_y, ranks, *refs):
    block, rate, notes, early, x_even, y_even, x_odd = refs[:7]
    y_odd = refs[7] if two_y else None
    beside, refs = refs[7 + two_y], refs[8 + two_y :]
    new, sends = refs[0], by_rank(refs[1 : 1 + ranks])
    pad, side, mag, fresh, packed = refs[1 + ranks :]
    deep, tall = block.shape[1], block.shape[2]
    full = deep + 2
    gx = lax.axis_index("gx")
    gx_odd = lax.rem(gx, 2)
    gy_odd = lax.rem(lax.axis_index("gy"), 2)
    gz = lax.axis_index("gz")
    noted = notes[0:8, :]
    spots = [[noted[q * 4 + d, 0] for d in range(3)] for q in range(PAR)]
    chosen = noted[3, 0]
    lane = lane_iota((tall, LANES))
    keep = ((lane == 0) & (gz == 0)) | ((lane == LANES - 1) & (gz == 1))
    lane = lane_iota((16, LANES))
    none = jnp.zeros((16, LANES), F32)

    def at(c, x):
        return (c * full + x) * 16

    for c in range(6):
        for x in (0, full - 1):
            pad[pl.ds(at(c, x), 16), :] = none
        for x in range(deep):
            pad[pl.ds(at(c, x + 1), tall), :] = block[c, x]
        pad[pl.ds(at(c, 1) + tall, deep, stride=16), :] = none[0:deep]
        pad[pl.ds(at(c, 1) + 15, deep, stride=16), :] = none[0:deep]
    for c in range(5):
        for x in (0, full - 1):
            side[pl.ds(at(c, x), 16), :] = none
        for x in range(deep):
            side[pl.ds(at(c, x + 1), 16), :] = none
            side[pl.ds(at(c, x + 1), tall), :] = jnp.where(keep, beside[c, x], 0.0)
    for k, c in enumerate(X_COMPS):
        even, odd = x_even[k], x_odd[k]
        low, high = jnp.where(gx_odd == 0, odd, even), jnp.where(gx_odd == 0, even, odd)
        pad[pl.ds(at(c, 0), tall), :] = jnp.where(gx == 0, 0.0, low)
        if c in (1, 2):
            pad[pl.ds(at(c, full - 1), tall), :] = jnp.where(gx == lax.axis_size("gx") - 1, 0.0, high)
    for k, c in enumerate(Y_COMPS):
        even = y_even[k]
        odd = jnp.zeros_like(even) if y_odd is None else y_odd[k]
        pad[pl.ds(at(c, 1) + 15, deep, stride=16), :] = jnp.where(gy_odd == 0, odd, even)
        if c in (0, 2):
            pad[pl.ds(at(c, 1) + tall, deep, stride=16), :] = jnp.where(gy_odd == 0, even, odd)

    def up_y(a):
        return pltpu.roll(a, 15, 0)

    def down_y(a):
        return pltpu.roll(a, 1, 0)

    def plane(c, x):
        return pad[pl.ds(at(c, x), 16), :]

    def edge(c, x):
        return side[pl.ds(at(c, x), 16), :]

    def field(c, x):
        return mag[pl.ds((c * (full - 1) + x) * 16, 16), :]

    for x in range(full - 1):
        e0, e1, e2 = plane(0, x), plane(1, x), plane(2, x)
        s0, s1, s2 = edge(0, x), edge(1, x), edge(2, x)
        r0, r1 = pltpu.roll(e0, LANES - 1, 1), pltpu.roll(e1, LANES - 1, 1)
        u0 = jnp.where(lane == LANES - 1, pltpu.roll(s0, LANES - 1, 1), r0)
        u1 = jnp.where(lane == LANES - 1, pltpu.roll(s1, LANES - 1, 1), r1)
        h0 = plane(3, x) - 0.5 * ((up_y(e2) - e2) - (u1 - e1))
        h1 = plane(4, x) - 0.5 * ((u0 - e0) - (plane(2, x + 1) - e2))
        h2 = plane(5, x) - 0.5 * ((plane(1, x + 1) - e1) - (up_y(e0) - e0))
        t0 = edge(3, x) - 0.5 * ((up_y(s2) - s2) - (r1 - s1))
        t1 = edge(4, x) - 0.5 * ((r0 - s0) - (edge(2, x + 1) - s2))
        d0 = pltpu.roll(jnp.where(lane == LANES - 1, t0, h0), 1, 1)
        d1 = pltpu.roll(jnp.where(lane == LANES - 1, t1, h1), 1, 1)
        for c, value in enumerate((h0, h1, h2, d0, d1)):
            mag[pl.ds((c * (full - 1) + x) * 16, 16), :] = value
    for x in range(deep):
        h0, h1, h2, d0, d1 = (field(c, x + 1) for c in range(5))
        coef = rate[x]
        c0 = (h2 - down_y(h2)) - (h1 - d1)
        c1 = (h0 - d0) - (h2 - field(2, x))
        c2 = (h1 - field(1, x)) - (h0 - down_y(h0))
        for c, curl in enumerate((c0, c1, c2)):
            value = plane(c, x + 1)[0:tall] + coef * curl[0:tall]
            new[c, x] = value
            new[c + 3, x] = (h0, h1, h2)[c][0:tall]
            fresh[pl.ds((c * deep + x) * 16, tall), :] = value
            fresh[pl.ds(((c + 3) * deep + x) * 16, tall), :] = (h0, h1, h2)[c][0:tall]
    for q in range(PAR):
        pack(fresh, deep, spots[q], 1, packed, q, early)
        packed[q, ROW_EDGE:ROWS_PATCH, :] = jnp.zeros((ROWS_PATCH - ROW_EDGE, LANES), F32)
        packed[q, ROW_EDGE : ROW_EDGE + 1, :] = pad[pl.ds(at(1, full - 1) + tall - 1, 1), :]
        packed[q, ROW_EDGE + 1 : ROW_EDGE + 2, :] = pad[pl.ds(at(0, 0), 1), :]
    for k, send in enumerate(sends):
        q = jnp.where(chosen == k, 0, 1)
        send[0:ROWS_PATCH, :] = packed[q]
    half = lane_iota((16, LANES)) < LANES // 2
    send = sends[1]
    send[ROWS_PATCH : ROWS_PATCH + 16, :] = jnp.where(half, plane(0, 0), plane(2, full - 1))
    low = jnp.where(gy_odd == 0, jnp.zeros_like(y_even[1]) if y_odd is None else y_odd[1], y_even[1])
    high = jnp.where(gy_odd == 0, y_even[2], jnp.zeros_like(y_even[2]) if y_odd is None else y_odd[2])
    send[ROWS_PATCH + 16 : ROWS_PATCH + 32, :] = jnp.zeros((16, LANES), F32)
    send[ROWS_PATCH + 16 : ROWS_PATCH + 16 + deep, :] = jnp.where(half[0:deep], low, high)


def places():
    for x in range(PF):
        yield x, (x % 8 + 1) * 8 if x < 8 else (x % 8) * 8 + BATCH


def load_kernel(fine, perm, table, box, rate, lhs, coefs):
    groups = fine.shape[3] // BATCH
    blank = jnp.zeros((8, PF * PF), F32)
    for g in range(groups):
        slots = slice(g * BATCH, (g + 1) * BATCH)
        for c in range(6):
            for row in (0, ROWS_BOX - 8):
                lhs[c * ROWS_BOX + row : c * ROWS_BOX + row + 8, :] = blank
            for x, row in places():
                row += c * ROWS_BOX
                lhs[row : row + BATCH, :] = fine[0, 0, c, slots, x * PF * PF : (x + 1) * PF * PF]
            grown = move(lhs[c * ROWS_BOX : (c + 1) * ROWS_BOX, :], table[...])
            box[g, c] = grown
        for row in (0, ROWS_BOX - 8):
            coefs[row : row + 8, :] = blank
        for x, row in places():
            coefs[row : row + BATCH, :] = 0.5 / perm[0, 0, slots, x * PF * PF : (x + 1) * PF * PF]
        rate[g] = move(coefs[...], table[...])


def fine_kernel(ranks, *refs):
    regions, (box, rate, ghosts, means, out) = by_rank(refs[:ranks]), refs[ranks : ranks + 5]
    smalls = by_rank(refs[ranks + 5 : 2 * ranks + 5])
    rims, walls, now, halves, small = refs[2 * ranks + 5 :]
    groups = box.shape[0]
    rank = lax.axis_index("gy") * lax.axis_size("gz") + lax.axis_index("gz")
    flat = lane_iota((8, WIDE))
    yy = lax.shift_right_logical(flat * 3641, 16)
    zz = flat - yy * LINE
    inner = (yy >= 1) & (yy <= PF) & (zz >= 1) & (zz <= PF)
    upper = lax.broadcasted_iota(jnp.int32, (8, WIDE), 0) >= BATCH

    def inner_of(m):
        if m == 0:
            return inner & upper
        if m == PLANES - 1:
            return inner & jnp.logical_not(upper)
        return inner

    def up_y(a):
        return pltpu.roll(a, WIDE - LINE, 1)

    def up_z(a):
        return pltpu.roll(a, WIDE - 1, 1)

    def down_y(a):
        return pltpu.roll(a, LINE, 1)

    def down_z(a):
        return pltpu.roll(a, 1, 1)

    def rows_of(m):
        return pl.ds(m * 8, 8)

    blank = jnp.zeros((8, LANES), F32)
    for g in range(groups):
        for c in range(6):
            for m in range(PLANES):
                row = ((g * 6 + c) * PLANES + m) * 8
                if m in (0, PLANES - 1):
                    rims[row : row + 8, :] = blank
                walls[0, row : row + 8, :] = blank
                walls[1, row : row + 8, :] = blank
    for k, region in enumerate(regions):
        slot = lax.bitwise_xor(rank, k)
        start = (slot // BATCH) * 6 * ROWS_BOX + lax.rem(slot, BATCH)
        for c in range(6):
            rows = region[c * 8 : c * 8 + 8, :]
            row = start + c * ROWS_BOX
            rims[pl.ds(row + 8, 4, stride=16), :] = rows[0:4]
            rims[pl.ds(row + 16, 4, stride=16), :] = rows[0:4]
            rims[pl.ds(row + BATCH, 4, stride=16), :] = rows[4:8]
            rims[pl.ds(row + BATCH + 8, 4, stride=16), :] = rows[4:8]
        old = region[ROWS_RIM : ROWS_RIM + 8, :]
        fresh = region[ROWS_RIM + 8 : ROWS_RIM + 16, :]
        for sub, value in enumerate((old, old + 0.5 * (fresh - old))):
            walls[sub, pl.ds(start, 6, stride=ROWS_BOX), :] = value[0:6]
            last = start + ROWS_BOX + (PLANES - 1) * 8 + BATCH
            walls[sub, pl.ds(last, 2, stride=ROWS_BOX), :] = value[6:8]
    for g in range(groups):
        for sub in range(2):
            source = box if sub == 0 else out
            rows = pl.ds(g * 6 * ROWS_BOX, 6 * ROWS_BOX)
            ghost = move(jnp.concatenate([rims[rows, :], walls[sub, rows, :]], axis=1), ghosts[sub])
            for c in range(6):
                for m in range(PLANES):
                    row = c * ROWS_BOX + m * 8
                    now[c, rows_of(m), :] = jnp.where(
                        inner_of(m), source[g, c, rows_of(m), :], ghost[row : row + 8]
                    )

            def next_x(c, m):
                if m == PLANES - 1:
                    return pltpu.roll(now[c, rows_of(0), :], BATCH, 0)
                return now[c, rows_of(m + 1), :]

            def last_x(c, m):
                if m == 0:
                    return pltpu.roll(out[g, c + 3, rows_of(PLANES - 1), :], BATCH, 0)
                return out[g, c + 3, rows_of(m - 1), :]

            for m in range(PLANES):
                e0, e1, e2 = (now[c, rows_of(m), :] for c in range(3))
                h0, h1, h2 = (now[c, rows_of(m), :] for c in range(3, 6))
                out[g, 3, rows_of(m), :] = h0 - 0.5 * ((up_y(e2) - e2) - (up_z(e1) - e1))
                out[g, 4, rows_of(m), :] = h1 - 0.5 * ((up_z(e0) - e0) - (next_x(2, m) - e2))
                out[g, 5, rows_of(m), :] = h2 - 0.5 * ((next_x(1, m) - e1) - (up_y(e0) - e0))
            for m in range(PLANES):
                h0, h1, h2 = (out[g, c, rows_of(m), :] for c in range(3, 6))
                coef = rate[g, rows_of(m), :]
                e0, e1, e2 = (now[c, rows_of(m), :] for c in range(3))
                out[g, 0, rows_of(m), :] = e0 + coef * ((h2 - down_y(h2)) - (h1 - down_z(h1)))
                out[g, 1, rows_of(m), :] = e1 + coef * ((h0 - down_z(h0)) - (h2 - last_x(2, m)))
                out[g, 2, rows_of(m), :] = e2 + coef * ((h1 - last_x(1, m)) - (h0 - down_y(h0)))
        for c in range(6):
            for k in range(4):
                other = jnp.where(upper, out[g, c, rows_of(2 * k), :], out[g, c, rows_of(2 * k + 2), :])
                pair = out[g, c, rows_of(2 * k + 1), :] + other
                halves[pl.ds((c * 2 + k // 2) * 8, 8), (k % 2) * WIDE : (k % 2 + 1) * WIDE] = pair
        small[pl.ds(g * 96, 96), :] = move(halves[...], means[...])
    for k, send in enumerate(smalls):
        slot = lax.bitwise_xor(rank, k)
        start = (slot // BATCH) * 96 + lax.rem(slot, BATCH)
        for xh in range(2):
            send[xh * 12 : (xh + 1) * 12, :] = small[pl.ds(start + xh * BATCH, 12, stride=8), :]


def store_kernel(box, fine, notes, table, out, stage, sems):
    groups = box.shape[0]
    slots = groups * BATCH
    live = jnp.concatenate([notes[8 : 8 + slots, :]] * (PF * PF // LANES), axis=1) > 0
    copies = []
    for c in range(6):
        flats = [move(box[g, c], table[...]) for g in range(groups)]
        for x, row in places():
            cut = slice(x * PF * PF, (x + 1) * PF * PF)
            for g, flat in enumerate(flats):
                some = slice(g * BATCH, (g + 1) * BATCH)
                stage[0, 0, c, some, cut] = jnp.where(live[some], flat[row : row + BATCH], fine[0, 0, c, some, cut])
        copies.append(pltpu.make_async_copy(stage.at[:, :, c], out.at[:, :, c], sems.at[c]))
        copies[-1].start()
    for copy in copies:
        copy.wait()


def fix_kernel(new, rate, *refs):
    edges, out = refs[:-1], refs[-1]
    deep, tall = new.shape[1], new.shape[2]
    gz = lax.axis_index("gz")
    rank = lax.axis_index("gy") * 2 + gz
    out[...] = new[...]

    def add(c, x, rows, amount):
        out[c, x, rows, :] = out[c, x, rows, :] + 0.5 * rate[x, rows, :] * amount

    lower = higher = jnp.zeros((1, LANES), F32)
    for k, edge in enumerate(edges, 1):
        row = ROW_EDGE
        lower = jnp.where(lax.bitwise_xor(rank, k) == rank - 2, edge[row : row + 1, :], lower)
        higher = jnp.where(lax.bitwise_xor(rank, k) == rank + 2, edge[row + 1 : row + 2, :], higher)
    add(0, deep - 1, slice(0, 1), lower)
    add(1, 0, slice(tall - 1, tall), higher)
    lane = lane_iota((tall, LANES))
    tile = edges[0][ROWS_PATCH : ROWS_PATCH + tall, :]
    add(0, deep - 1, slice(0, tall), jnp.where((lane == 0) & (gz == 1), pltpu.roll(tile, 1, 1), 0.0))
    add(2, 0, slice(0, tall), jnp.where((lane == LANES - 1) & (gz == 0), pltpu.roll(tile, LANES - 1, 1), 0.0))
    lane = lane_iota((deep, LANES))
    tile = edges[0][ROWS_PATCH + 16 : ROWS_PATCH + 16 + deep, :]
    first = jnp.where((lane == LANES - 1) & (gz == 0), pltpu.roll(tile, LANES - 1, 1), 0.0)
    last = jnp.where((lane == 0) & (gz == 1), pltpu.roll(tile, 1, 1), 0.0)
    for x in range(deep):
        add(2, x, slice(0, 1), first[x : x + 1])
        add(1, x, slice(tall - 1, tall), last[x : x + 1])


def place_kernel(ranks, new, notes, *refs):
    means, (out, spread, stage, gathered, sems) = by_rank(refs[:ranks]), refs[ranks:]
    noted = notes[0:8, :]
    for k, mean in enumerate(means):
        gathered[k] = mean[...]
    lane = lane_iota((HALF, LANES))
    spots = [tuple(noted[q * 4 + d, 0] for d in range(3)) for q in range(PAR)]
    for q, (cx, cy, cz) in enumerate(spots):
        k = noted[q * 4 + 3, 0]
        rows = gathered[k]
        for odd in range(2):
            for y in range(HALF):
                shift = lax.rem(cz - y * HALF - odd * HALF * HALF + 2 * LANES, LANES)
                spread[q, pl.ds(odd * 192 + y, 24, stride=8), :] = pltpu.roll(rows, shift, 1)
    copies = []
    for c in range(6):
        stage[c] = new[c]
        for q, (cx, cy, cz) in enumerate(spots):
            inside = (lane >= cz) & (lane < cz + HALF)
            for x in range(HALF):
                xh, k = x // 4, x % 4
                tile = spread[q, pl.ds((k % 2) * 192 + (xh * 12 + c * 2 + k // 2) * 8, 8), :]
                spot = stage[c, cx + x, pl.ds(cy, HALF), :]
                stage[c, cx + x, pl.ds(cy, HALF), :] = jnp.where(inside, tile, spot)
        copies.append(pltpu.make_async_copy(stage.at[c], out.at[c], sems.at[c]))
        copies[-1].start()
    for copy in copies:
        copy.wait()


def local(coarse_fields, permittivity, fine_fields, fine_permittivity, patch_corner, patch_owner):
    deep, tall, cols = coarse_fields.shape[1:]
    slots = fine_fields.shape[2]
    groups = slots // BATCH
    count_x, count_y = lax.axis_size("gx"), lax.axis_size("gy")
    two_y = count_y > 2
    vmem = whole()
    shape = jax.ShapeDtypeStruct
    grow = grow_table()

    x_face = shape((5, tall, cols), F32)
    y_face = shape((5, deep, cols), F32)
    kept, *faces = call(
        functools.partial(faces_kernel, two_y),
        [shape(coarse_fields.shape, F32), x_face, y_face, x_face] + [y_face] * two_y,
        [vmem],
    )(coarse_fields)
    got = [
        lax.ppermute(faces[0], "gx", swap_pairs(count_x, 0)),
        lax.ppermute(faces[1], "gy", swap_pairs(count_y, 0)),
        lax.ppermute(faces[2], ("gx", "gz"), full_pairs(count_x)),
    ]
    if two_y:
        got.append(lax.ppermute(faces[3], "gy", swap_pairs(count_y, 1)))
    beside = lax.ppermute(kept, "gz", swap_pairs(2, 0))

    fine = fine_fields.transpose(0, 1, 3, 2, 4)
    notes, rate, early = call(
        notes_kernel,
        [
            shape((8 + slots, LANES), jnp.int32),
            shape(permittivity.shape, F32),
            shape((PAR, ROWS_RIM + 8, LANES), F32),
        ],
        [whole(pltpu.SMEM)] * 2 + [vmem] * 2,
        [pltpu.VMEM((6 * deep * 16, LANES), F32)],
    )(patch_corner, patch_owner.transpose(0, 2, 1), permittivity, kept)
    box, fine_rate = call(
        load_kernel,
        [shape((groups, 6, ROWS_BOX, WIDE), F32), shape((groups, ROWS_BOX, WIDE), F32)],
        [vmem] * 3,
        [pltpu.VMEM((6 * ROWS_BOX, PF * PF), F32), pltpu.VMEM((ROWS_BOX, PF * PF), F32)],
        size=4_000_000,
    )(fine, fine_permittivity, jnp.asarray(grow, BF16))

    full = deep + 2
    ranks = count_y * lax.axis_size("gz")

    def exchange(parts):
        swaps = [[(r, r ^ k) for r in range(ranks)] for k in range(ranks)]
        got = list(parts)
        for k in [*range(2, ranks), 1]:
            got[k] = lax.ppermute(parts[k], ("gy", "gz"), swaps[k])
        return got

    patches = [shape((ROWS_BESIDE if k == 1 else ROWS_PATCH, LANES), F32) for k in range(ranks)]
    new, *sends = call(
        functools.partial(leap_kernel, two_y, ranks),
        [shape(coarse_fields.shape, F32)] + far_first(patches),
        [vmem] * (5 + len(got)),
        [
            pltpu.VMEM((6 * full * 16, LANES), F32),
            pltpu.VMEM((6 * full * 16, LANES), F32),
            pltpu.VMEM((5 * (full - 1) * 16, LANES), F32),
            pltpu.VMEM((6 * deep * 16, LANES), F32),
            pltpu.VMEM((PAR, ROWS_PATCH, LANES), F32),
        ],
    )(kept, rate, notes, early, *got, beside)
    regions = exchange(by_rank(sends))

    box, *smalls = call(
        functools.partial(fine_kernel, ranks),
        [shape((groups, 6, ROWS_BOX, WIDE), F32)] + [shape((24, LANES), F32)] * ranks,
        [vmem] * (ranks + 4),
        [
            pltpu.VMEM((groups * 6 * ROWS_BOX, LANES), F32),
            pltpu.VMEM((2, groups * 6 * ROWS_BOX, LANES), F32),
            pltpu.VMEM((6, ROWS_BOX, WIDE), F32),
            pltpu.VMEM((96, 2 * WIDE), F32),
            pltpu.VMEM((groups * 96, LANES), F32),
        ],
    )(*far_first(regions), box, fine_rate, jnp.asarray(ghost_table(), BF16), jnp.asarray(mean_table(), BF16))
    means = exchange(by_rank(smalls))

    fine = call(
        store_kernel,
        shape(fine.shape, F32),
        [vmem] * 4,
        [pltpu.VMEM(fine.shape, F32), pltpu.SemaphoreType.DMA((6,))],
        size=4_000_000,
        out_specs=whole(pltpu.HBM),
    )(box, fine, notes, jnp.asarray(grow.T, BF16))
    new = call(fix_kernel, shape(coarse_fields.shape, F32), [vmem] * (1 + ranks))(new, rate, *regions[1:])
    coarse = call(
        functools.partial(place_kernel, ranks),
        shape(coarse_fields.shape, F32),
        [vmem] * (2 + ranks),
        [
            pltpu.VMEM((PAR, 4 * 96, LANES), F32),
            pltpu.VMEM(coarse_fields.shape, F32),
            pltpu.VMEM((ranks, 24, LANES), F32),
            pltpu.SemaphoreType.DMA((6,)),
        ],
        out_specs=whole(pltpu.HBM),
    )(new, notes, *far_first(means))
    return coarse, fine.transpose(0, 1, 3, 2, 4)


def solution(mesh):
    in_specs = (
        P(None, ("groups", "gx"), "gy", "gz"),
        P(("groups", "gx"), "gy", "gz"),
        P(("groups", "gx"), "gy", "gz", None, None),
        P(("groups", "gx"), "gy", "gz", None),
        P(("groups", "gx"), "gy", "gz", None),
        P(("groups", "gx"), None, None),
    )
    out_specs = (P(None, ("groups", "gx"), "gy", "gz"), P(("groups", "gx"), "gy", "gz", None, None))
    return jax.shard_map(local, mesh=mesh, in_specs=in_specs, out_specs=out_specs, check_vma=False)
```

```python
import functools
import jax
import jax.numpy as jnp
import numpy as np
from jax import lax
from jax.experimental import pallas as pl
from jax.experimental.pallas import tpu as pltpu
from jax.sharding import PartitionSpec as P

PF = 16
PAR = 2
HALF = PF // 2
RIM = HALF + 2
PLANES = 9
LINE = PF + 2
LANES = 128
WIDE = 384
BATCH = 4
ROWS_BOX = PLANES * 8
ROWS_RIM = 48
ROW_EDGE = 64
ROWS_PATCH = 72
ROWS_BESIDE = 104
X_COMPS = (0, 1, 2, 4, 5)
Y_COMPS = (0, 1, 2, 3, 5)
VMEM_BYTES = 48 * 1024 * 1024
F32 = jnp.float32
BF16 = jnp.bfloat16


def rim_lane(time, j, k):
    if 0 < j < RIM - 1:
        return j * RIM + k + 3 * time
    if j == 0 and time == 0:
        return k
    return (RIM - 1) * RIM + 3 + (2 * time + j // (RIM - 1) - 1) * RIM + k


def grow_table():
    table = np.zeros((PF * PF, WIDE), np.float32)
    for y in range(PF):
        for z in range(PF):
            table[y * PF + z, (y + 1) * LINE + z + 1] = 1.0
    return table


def ghost_table():
    table = np.zeros((2, 2 * LANES, WIDE), np.float32)
    for y in range(LINE):
        for z in range(LINE):
            j, k, lane = (y + 1) // 2, (z + 1) // 2, y * LINE + z
            table[:, LANES + j * RIM + k, lane] = 1.0
            if y in (0, LINE - 1) or z in (0, LINE - 1):
                table[0, rim_lane(0, j, k), lane] = 1.0
                table[1, rim_lane(0, j, k), lane] = 0.5
                table[1, rim_lane(1, j, k), lane] = 0.5
    return table


def mean_table():
    table = np.zeros((2, WIDE, LANES), np.float32)
    for odd in range(2):
        for y in range(PF):
            for z in range(PF):
                lane = odd * HALF * HALF + (y // 2) * HALF + z // 2
                table[odd, (y + 1) * LINE + z + 1, lane] = 0.125
    return table.reshape(2 * WIDE, LANES)


def move(rows, table):
    high = rows.astype(BF16)
    low = (rows - high.astype(F32)).astype(BF16)
    out = jnp.dot(jnp.concatenate([high, low], axis=0), table, preferred_element_type=F32)
    return out[: rows.shape[0]] + out[rows.shape[0] :]


def lane_iota(shape):
    return lax.broadcasted_iota(jnp.int32, shape, len(shape) - 1)


def whole(memory_space=pltpu.VMEM):
    return pl.BlockSpec(memory_space=memory_space)


def call(kernel, outs, in_specs, scratch=(), flops=1_000_000, size=1_000_000, out_specs=None, **extra):
    return pl.pallas_call(
        kernel,
        out_shape=outs,
        in_specs=in_specs,
        out_specs=jax.tree.map(lambda _: whole(), outs) if out_specs is None else out_specs,
        scratch_shapes=list(scratch),
        compiler_params=pltpu.CompilerParams(vmem_limit_bytes=VMEM_BYTES),
        cost_estimate=pl.CostEstimate(flops=flops, bytes_accessed=size, transcendentals=0),
        **extra,
    )


def swap_pairs(count, first):
    pairs = []
    for i in range(first, count - 1, 2):
        pairs += [(i, i + 1), (i + 1, i)]
    return pairs


def full_pairs(count_x):
    pairs = []
    for i in range(count_x):
        for j in range(2):
            if 0 < i < count_x - 1:
                target = (i + 1 if i % 2 else i - 1) * 2 + j
            else:
                target = i * 2 + 1 - j
            pairs.append((i * 2 + j, target))
    return pairs


def faces_kernel(two_y, block, kept, y_even, x_even, x_odd, *y_odd):
    deep, tall = block.shape[1], block.shape[2]
    gx_odd = lax.rem(lax.axis_index("gx"), 2)
    gy_odd = lax.rem(lax.axis_index("gy"), 2)
    for k, c in enumerate(X_COMPS):
        x_even[k] = block[c, (1 - gx_odd) * (deep - 1)]
        x_odd[k] = block[c, gx_odd * (deep - 1)]
    for k, c in enumerate(Y_COMPS):
        for x in range(deep):
            first = block[c, x, 0:1, :]
            last = block[c, x, tall - 1 : tall, :]
            y_even[k, x : x + 1, :] = jnp.where(gy_odd == 0, last, first)
            if two_y:
                y_odd[0][k, x : x + 1, :] = jnp.where(gy_odd == 0, first, last)
    kept[...] = block[...]


def pack(source, deep, spot, time, packed, q, early):
    lane = lane_iota((8, LANES))
    cx, cy, cz = spot

    def rows_of(c, k, j, count, over_c):
        step = deep * 16 if over_c else 16
        return source[pl.ds((c * deep + cx - 1 + k) * 16 + cy + (j - 1), count, stride=step), :]

    def aim(rows, target):
        return pltpu.roll(rows, lax.rem(target - (cz - 1) + 2 * LANES, LANES), 1)

    for c in range(6):
        total = jnp.zeros((8, LANES), F32) if early is None else early[q, c * 8 : c * 8 + 8, :]
        for j in range(RIM):
            if (j == 0 and c == 4) or (j == RIM - 1 and c not in (0, 2)) or (0 < j < RIM - 1 and c == 5):
                continue
            first = rim_lane(time, j, 0)
            if j in (0, RIM - 1):
                inside = (lane >= first) & (lane < first + RIM)
            else:
                inside = (lane == first) | (lane == first + RIM - 1)
            total = jnp.where(inside, aim(rows_of(c, 1, j, 8, False), first), total)
        packed[q, c * 8 : c * 8 + 8, :] = total
    low = jnp.zeros((6, LANES), F32)
    high = jnp.zeros((2, LANES), F32)
    for j in range(RIM):
        first = j * RIM
        inside = (lane >= first) & (lane < first + RIM)
        low = jnp.where(inside[0:6], aim(rows_of(0, 0, j, 6, True), first), low)
        high = jnp.where(inside[0:2], aim(rows_of(1, RIM - 1, j, 2, True), first), high)
    base = ROWS_RIM + time * 8
    packed[q, base : base + 6, :] = low
    packed[q, base + 6 : base + 8, :] = high
    if early is not None:
        packed[q, ROWS_RIM:base, :] = early[q, ROWS_RIM:base, :]


def notes_kernel(corner, owners, perm, block, notes, rate, early, flat):
    rank = lax.axis_index("gy") * lax.axis_size("gz") + lax.axis_index("gz")

    def note(row, value):
        notes[row : row + 1, :] = jnp.full((1, LANES), value, jnp.int32)

    for q in range(PAR):
        for d in range(3):
            note(q * 4 + d, corner[0, 0, q, d])
        note(q * 4 + 3, lax.bitwise_xor(owners[0, q, rank], rank))
    for slot in range(notes.shape[0] - 8):
        live = (owners[0, 0, slot] == rank) | (owners[0, 1, slot] == rank)
        note(8 + slot, live.astype(jnp.int32))
    rate[...] = 0.5 / perm[...]
    deep, tall = block.shape[1], block.shape[2]
    for c in range(6):
        for x in range(deep):
            flat[pl.ds((c * deep + x) * 16, tall), :] = block[c, x]
    for q in range(PAR):
        spot = [corner[0, 0, q, d] for d in range(3)]
        pack(flat, deep, spot, 0, early, q, None)


def leap_kernel(two_y, ranks, *refs):
    block, beside, rate, notes, early, y_even, x_even, x_odd = refs[:8]
    y_odd = refs[8] if two_y else None
    refs = refs[8 + two_y :]
    new, sends = refs[0], refs[1 : 1 + ranks]
    pad, side, mag, fresh, packed = refs[1 + ranks :]
    deep, tall = block.shape[1], block.shape[2]
    full = deep + 2
    gx = lax.axis_index("gx")
    gx_odd = lax.rem(gx, 2)
    gy_odd = lax.rem(lax.axis_index("gy"), 2)
    gz = lax.axis_index("gz")
    noted = notes[0:8, :]
    spots = [[noted[q * 4 + d, 0] for d in range(3)] for q in range(PAR)]
    chosen = noted[3, 0]
    lane = lane_iota((tall, LANES))
    keep = ((lane == 0) & (gz == 0)) | ((lane == LANES - 1) & (gz == 1))
    lane = lane_iota((16, LANES))
    none = jnp.zeros((16, LANES), F32)

    def at(c, x):
        return (c * full + x) * 16

    for c in range(6):
        for x in (0, full - 1):
            pad[pl.ds(at(c, x), 16), :] = none
        for x in range(deep):
            pad[pl.ds(at(c, x + 1), tall), :] = block[c, x]
        pad[pl.ds(at(c, 1) + tall, deep, stride=16), :] = none[0:deep]
        pad[pl.ds(at(c, 1) + 15, deep, stride=16), :] = none[0:deep]
    for c in range(5):
        for x in (0, full - 1):
            side[pl.ds(at(c, x), 16), :] = none
        for x in range(deep):
            side[pl.ds(at(c, x + 1), 16), :] = none
            side[pl.ds(at(c, x + 1), tall), :] = jnp.where(keep, beside[c, x], 0.0)
    for k, c in enumerate(X_COMPS):
        even, odd = x_even[k], x_odd[k]
        low, high = jnp.where(gx_odd == 0, odd, even), jnp.where(gx_odd == 0, even, odd)
        pad[pl.ds(at(c, 0), tall), :] = jnp.where(gx == 0, 0.0, low)
        if c in (1, 2):
            pad[pl.ds(at(c, full - 1), tall), :] = jnp.where(gx == lax.axis_size("gx") - 1, 0.0, high)
    for k, c in enumerate(Y_COMPS):
        even = y_even[k]
        odd = jnp.zeros_like(even) if y_odd is None else y_odd[k]
        pad[pl.ds(at(c, 1) + 15, deep, stride=16), :] = jnp.where(gy_odd == 0, odd, even)
        if c in (0, 2):
            pad[pl.ds(at(c, 1) + tall, deep, stride=16), :] = jnp.where(gy_odd == 0, even, odd)

    def up_y(a):
        return pltpu.roll(a, 15, 0)

    def down_y(a):
        return pltpu.roll(a, 1, 0)

    def plane(c, x):
        return pad[pl.ds(at(c, x), 16), :]

    def edge(c, x):
        return side[pl.ds(at(c, x), 16), :]

    def field(c, x):
        return mag[pl.ds((c * (full - 1) + x) * 16, 16), :]

    for x in range(full - 1):
        e0, e1, e2 = plane(0, x), plane(1, x), plane(2, x)
        s0, s1, s2 = edge(0, x), edge(1, x), edge(2, x)
        r0, r1 = pltpu.roll(e0, LANES - 1, 1), pltpu.roll(e1, LANES - 1, 1)
        u0 = jnp.where(lane == LANES - 1, pltpu.roll(s0, LANES - 1, 1), r0)
        u1 = jnp.where(lane == LANES - 1, pltpu.roll(s1, LANES - 1, 1), r1)
        h0 = plane(3, x) - 0.5 * ((up_y(e2) - e2) - (u1 - e1))
        h1 = plane(4, x) - 0.5 * ((u0 - e0) - (plane(2, x + 1) - e2))
        h2 = plane(5, x) - 0.5 * ((plane(1, x + 1) - e1) - (up_y(e0) - e0))
        t0 = edge(3, x) - 0.5 * ((up_y(s2) - s2) - (r1 - s1))
        t1 = edge(4, x) - 0.5 * ((r0 - s0) - (edge(2, x + 1) - s2))
        d0 = pltpu.roll(jnp.where(lane == LANES - 1, t0, h0), 1, 1)
        d1 = pltpu.roll(jnp.where(lane == LANES - 1, t1, h1), 1, 1)
        for c, value in enumerate((h0, h1, h2, d0, d1)):
            mag[pl.ds((c * (full - 1) + x) * 16, 16), :] = value
    for x in range(deep):
        h0, h1, h2, d0, d1 = (field(c, x + 1) for c in range(5))
        coef = rate[x]
        c0 = (h2 - down_y(h2)) - (h1 - d1)
        c1 = (h0 - d0) - (h2 - field(2, x))
        c2 = (h1 - field(1, x)) - (h0 - down_y(h0))
        for c, curl in enumerate((c0, c1, c2)):
            value = plane(c, x + 1)[0:tall] + coef * curl[0:tall]
            new[c, x] = value
            new[c + 3, x] = (h0, h1, h2)[c][0:tall]
            fresh[pl.ds((c * deep + x) * 16, tall), :] = value
            fresh[pl.ds(((c + 3) * deep + x) * 16, tall), :] = (h0, h1, h2)[c][0:tall]
    for q in range(PAR):
        pack(fresh, deep, spots[q], 1, packed, q, early)
        packed[q, ROW_EDGE:ROWS_PATCH, :] = jnp.zeros((ROWS_PATCH - ROW_EDGE, LANES), F32)
        packed[q, ROW_EDGE : ROW_EDGE + 1, :] = pad[pl.ds(at(1, full - 1) + tall - 1, 1), :]
        packed[q, ROW_EDGE + 1 : ROW_EDGE + 2, :] = pad[pl.ds(at(0, 0), 1), :]
    for k, send in enumerate(sends):
        q = jnp.where(chosen == k, 0, 1)
        send[0:ROWS_PATCH, :] = packed[q]
    half = lane_iota((16, LANES)) < LANES // 2
    send = sends[1]
    send[ROWS_PATCH : ROWS_PATCH + 16, :] = jnp.where(half, plane(0, 0), plane(2, full - 1))
    low = jnp.where(gy_odd == 0, jnp.zeros_like(y_even[1]) if y_odd is None else y_odd[1], y_even[1])
    high = jnp.where(gy_odd == 0, y_even[2], jnp.zeros_like(y_even[2]) if y_odd is None else y_odd[2])
    send[ROWS_PATCH + 16 : ROWS_PATCH + 32, :] = jnp.zeros((16, LANES), F32)
    send[ROWS_PATCH + 16 : ROWS_PATCH + 16 + deep, :] = jnp.where(half[0:deep], low, high)


def places():
    for x in range(PF):
        yield x, (x % 8 + 1) * 8 if x < 8 else (x % 8) * 8 + BATCH


def load_kernel(fine, perm, table, box, rate, lhs, coefs):
    groups = fine.shape[3] // BATCH
    blank = jnp.zeros((8, PF * PF), F32)
    for g in range(groups):
        slots = slice(g * BATCH, (g + 1) * BATCH)
        for c in range(6):
            for row in (0, ROWS_BOX - 8):
                lhs[c * ROWS_BOX + row : c * ROWS_BOX + row + 8, :] = blank
            for x, row in places():
                row += c * ROWS_BOX
                lhs[row : row + BATCH, :] = fine[0, 0, c, slots, x * PF * PF : (x + 1) * PF * PF]
            grown = move(lhs[c * ROWS_BOX : (c + 1) * ROWS_BOX, :], table[...])
            box[g, c] = grown
        for row in (0, ROWS_BOX - 8):
            coefs[row : row + 8, :] = blank
        for x, row in places():
            coefs[row : row + BATCH, :] = 0.5 / perm[0, 0, slots, x * PF * PF : (x + 1) * PF * PF]
        rate[g] = move(coefs[...], table[...])


def fine_kernel(ranks, *refs):
    regions, (box, rate, ghosts, means, out) = refs[:ranks], refs[ranks : ranks + 5]
    smalls = refs[ranks + 5 : 2 * ranks + 5]
    rims, walls, now, halves, small = refs[2 * ranks + 5 :]
    groups = box.shape[0]
    rank = lax.axis_index("gy") * lax.axis_size("gz") + lax.axis_index("gz")
    flat = lane_iota((8, WIDE))
    yy = lax.shift_right_logical(flat * 3641, 16)
    zz = flat - yy * LINE
    inner = (yy >= 1) & (yy <= PF) & (zz >= 1) & (zz <= PF)
    upper = lax.broadcasted_iota(jnp.int32, (8, WIDE), 0) >= BATCH

    def inner_of(m):
        if m == 0:
            return inner & upper
        if m == PLANES - 1:
            return inner & jnp.logical_not(upper)
        return inner

    def up_y(a):
        return pltpu.roll(a, WIDE - LINE, 1)

    def up_z(a):
        return pltpu.roll(a, WIDE - 1, 1)

    def down_y(a):
        return pltpu.roll(a, LINE, 1)

    def down_z(a):
        return pltpu.roll(a, 1, 1)

    def rows_of(m):
        return pl.ds(m * 8, 8)

    blank = jnp.zeros((8, LANES), F32)
    for g in range(groups):
        for c in range(6):
            for m in range(PLANES):
                row = ((g * 6 + c) * PLANES + m) * 8
                if m in (0, PLANES - 1):
                    rims[row : row + 8, :] = blank
                walls[0, row : row + 8, :] = blank
                walls[1, row : row + 8, :] = blank
    for k, region in enumerate(regions):
        slot = lax.bitwise_xor(rank, k)
        start = (slot // BATCH) * 6 * ROWS_BOX + lax.rem(slot, BATCH)
        for c in range(6):
            rows = region[c * 8 : c * 8 + 8, :]
            row = start + c * ROWS_BOX
            rims[pl.ds(row + 8, 4, stride=16), :] = rows[0:4]
            rims[pl.ds(row + 16, 4, stride=16), :] = rows[0:4]
            rims[pl.ds(row + BATCH, 4, stride=16), :] = rows[4:8]
            rims[pl.ds(row + BATCH + 8, 4, stride=16), :] = rows[4:8]
        old = region[ROWS_RIM : ROWS_RIM + 8, :]
        fresh = region[ROWS_RIM + 8 : ROWS_RIM + 16, :]
        for sub, value in enumerate((old, old + 0.5 * (fresh - old))):
            walls[sub, pl.ds(start, 6, stride=ROWS_BOX), :] = value[0:6]
            last = start + ROWS_BOX + (PLANES - 1) * 8 + BATCH
            walls[sub, pl.ds(last, 2, stride=ROWS_BOX), :] = value[6:8]
    for g in range(groups):
        for sub in range(2):
            source = box if sub == 0 else out
            rows = pl.ds(g * 6 * ROWS_BOX, 6 * ROWS_BOX)
            ghost = move(jnp.concatenate([rims[rows, :], walls[sub, rows, :]], axis=1), ghosts[sub])
            for c in range(6):
                for m in range(PLANES):
                    row = c * ROWS_BOX + m * 8
                    now[c, rows_of(m), :] = jnp.where(
                        inner_of(m), source[g, c, rows_of(m), :], ghost[row : row + 8]
                    )

            def next_x(c, m):
                if m == PLANES - 1:
                    return pltpu.roll(now[c, rows_of(0), :], BATCH, 0)
                return now[c, rows_of(m + 1), :]

            def last_x(c, m):
                if m == 0:
                    return pltpu.roll(out[g, c + 3, rows_of(PLANES - 1), :], BATCH, 0)
                return out[g, c + 3, rows_of(m - 1), :]

            for m in range(PLANES):
                e0, e1, e2 = (now[c, rows_of(m), :] for c in range(3))
                h0, h1, h2 = (now[c, rows_of(m), :] for c in range(3, 6))
                out[g, 3, rows_of(m), :] = h0 - 0.5 * ((up_y(e2) - e2) - (up_z(e1) - e1))
                out[g, 4, rows_of(m), :] = h1 - 0.5 * ((up_z(e0) - e0) - (next_x(2, m) - e2))
                out[g, 5, rows_of(m), :] = h2 - 0.5 * ((next_x(1, m) - e1) - (up_y(e0) - e0))
            for m in range(PLANES):
                h0, h1, h2 = (out[g, c, rows_of(m), :] for c in range(3, 6))
                coef = rate[g, rows_of(m), :]
                e0, e1, e2 = (now[c, rows_of(m), :] for c in range(3))
                out[g, 0, rows_of(m), :] = e0 + coef * ((h2 - down_y(h2)) - (h1 - down_z(h1)))
                out[g, 1, rows_of(m), :] = e1 + coef * ((h0 - down_z(h0)) - (h2 - last_x(2, m)))
                out[g, 2, rows_of(m), :] = e2 + coef * ((h1 - last_x(1, m)) - (h0 - down_y(h0)))
        for c in range(6):
            for k in range(4):
                other = jnp.where(upper, out[g, c, rows_of(2 * k), :], out[g, c, rows_of(2 * k + 2), :])
                pair = out[g, c, rows_of(2 * k + 1), :] + other
                halves[pl.ds((c * 2 + k // 2) * 8, 8), (k % 2) * WIDE : (k % 2 + 1) * WIDE] = pair
        small[pl.ds(g * 96, 96), :] = move(halves[...], means[...])
    for k, send in enumerate(smalls):
        slot = lax.bitwise_xor(rank, k)
        start = (slot // BATCH) * 96 + lax.rem(slot, BATCH)
        for xh in range(2):
            send[xh * 12 : (xh + 1) * 12, :] = small[pl.ds(start + xh * BATCH, 12, stride=8), :]


def store_kernel(box, fine, notes, table, out, stage, sems):
    groups = box.shape[0]
    slots = groups * BATCH
    live = jnp.concatenate([notes[8 : 8 + slots, :]] * (PF * PF // LANES), axis=1) > 0
    copies = []
    for c in range(6):
        flats = [move(box[g, c], table[...]) for g in range(groups)]
        for x, row in places():
            cut = slice(x * PF * PF, (x + 1) * PF * PF)
            for g, flat in enumerate(flats):
                some = slice(g * BATCH, (g + 1) * BATCH)
                stage[0, 0, c, some, cut] = jnp.where(live[some], flat[row : row + BATCH], fine[0, 0, c, some, cut])
        copies.append(pltpu.make_async_copy(stage.at[:, :, c], out.at[:, :, c], sems.at[c]))
        copies[-1].start()
    for copy in copies:
        copy.wait()


def fix_kernel(new, rate, *refs):
    edges, out = refs[:-1], refs[-1]
    deep, tall = new.shape[1], new.shape[2]
    gz = lax.axis_index("gz")
    rank = lax.axis_index("gy") * 2 + gz
    out[...] = new[...]

    def add(c, x, rows, amount):
        out[c, x, rows, :] = out[c, x, rows, :] + 0.5 * rate[x, rows, :] * amount

    lower = higher = jnp.zeros((1, LANES), F32)
    for k, edge in enumerate(edges, 1):
        row = ROW_EDGE
        lower = jnp.where(lax.bitwise_xor(rank, k) == rank - 2, edge[row : row + 1, :], lower)
        higher = jnp.where(lax.bitwise_xor(rank, k) == rank + 2, edge[row + 1 : row + 2, :], higher)
    add(0, deep - 1, slice(0, 1), lower)
    add(1, 0, slice(tall - 1, tall), higher)
    lane = lane_iota((tall, LANES))
    tile = edges[0][ROWS_PATCH : ROWS_PATCH + tall, :]
    add(0, deep - 1, slice(0, tall), jnp.where((lane == 0) & (gz == 1), pltpu.roll(tile, 1, 1), 0.0))
    add(2, 0, slice(0, tall), jnp.where((lane == LANES - 1) & (gz == 0), pltpu.roll(tile, LANES - 1, 1), 0.0))
    lane = lane_iota((deep, LANES))
    tile = edges[0][ROWS_PATCH + 16 : ROWS_PATCH + 16 + deep, :]
    first = jnp.where((lane == LANES - 1) & (gz == 0), pltpu.roll(tile, LANES - 1, 1), 0.0)
    last = jnp.where((lane == 0) & (gz == 1), pltpu.roll(tile, 1, 1), 0.0)
    for x in range(deep):
        add(2, x, slice(0, 1), first[x : x + 1])
        add(1, x, slice(tall - 1, tall), last[x : x + 1])


def place_kernel(ranks, new, notes, *refs):
    means, (out, spread, stage, gathered, sems) = refs[:ranks], refs[ranks:]
    noted = notes[0:8, :]
    for k, mean in enumerate(means):
        gathered[k] = mean[...]
    lane = lane_iota((HALF, LANES))
    spots = [tuple(noted[q * 4 + d, 0] for d in range(3)) for q in range(PAR)]
    for q, (cx, cy, cz) in enumerate(spots):
        k = noted[q * 4 + 3, 0]
        rows = gathered[k]
        for odd in range(2):
            for y in range(HALF):
                shift = lax.rem(cz - y * HALF - odd * HALF * HALF + 2 * LANES, LANES)
                spread[q, pl.ds(odd * 192 + y, 24, stride=8), :] = pltpu.roll(rows, shift, 1)
    copies = []
    for c in range(6):
        stage[c] = new[c]
        for q, (cx, cy, cz) in enumerate(spots):
            inside = (lane >= cz) & (lane < cz + HALF)
            for x in range(HALF):
                xh, k = x // 4, x % 4
                tile = spread[q, pl.ds((k % 2) * 192 + (xh * 12 + c * 2 + k // 2) * 8, 8), :]
                spot = stage[c, cx + x, pl.ds(cy, HALF), :]
                stage[c, cx + x, pl.ds(cy, HALF), :] = jnp.where(inside, tile, spot)
        copies.append(pltpu.make_async_copy(stage.at[c], out.at[c], sems.at[c]))
        copies[-1].start()
    for copy in copies:
        copy.wait()


def local(coarse_fields, permittivity, fine_fields, fine_permittivity, patch_corner, patch_owner):
    deep, tall, cols = coarse_fields.shape[1:]
    slots = fine_fields.shape[2]
    groups = slots // BATCH
    count_x, count_y = lax.axis_size("gx"), lax.axis_size("gy")
    two_y = count_y > 2
    vmem = whole()
    shape = jax.ShapeDtypeStruct
    grow = grow_table()

    x_face = shape((5, tall, cols), F32)
    y_face = shape((5, deep, cols), F32)
    kept, *faces = call(
        functools.partial(faces_kernel, two_y),
        [shape(coarse_fields.shape, F32), y_face, x_face, x_face] + [y_face] * two_y,
        [vmem],
    )(coarse_fields)
    got = [
        lax.ppermute(faces[0], "gy", swap_pairs(count_y, 0)),
        lax.ppermute(faces[1], "gx", swap_pairs(count_x, 0)),
        lax.ppermute(faces[2], ("gx", "gz"), full_pairs(count_x)),
    ]
    if two_y:
        got.append(lax.ppermute(faces[3], "gy", swap_pairs(count_y, 1)))
    beside = lax.ppermute(kept, "gz", swap_pairs(2, 0))

    fine = fine_fields.transpose(0, 1, 3, 2, 4)
    notes, rate, early = call(
        notes_kernel,
        [
            shape((8 + slots, LANES), jnp.int32),
            shape(permittivity.shape, F32),
            shape((PAR, ROWS_RIM + 8, LANES), F32),
        ],
        [whole(pltpu.SMEM)] * 2 + [vmem] * 2,
        [pltpu.VMEM((6 * deep * 16, LANES), F32)],
    )(patch_corner, patch_owner.transpose(0, 2, 1), permittivity, kept)
    box, fine_rate = call(
        load_kernel,
        [shape((groups, 6, ROWS_BOX, WIDE), F32), shape((groups, ROWS_BOX, WIDE), F32)],
        [vmem] * 3,
        [pltpu.VMEM((6 * ROWS_BOX, PF * PF), F32), pltpu.VMEM((ROWS_BOX, PF * PF), F32)],
        size=4_000_000,
    )(fine, fine_permittivity, jnp.asarray(grow, BF16))

    full = deep + 2
    ranks = count_y * lax.axis_size("gz")

    def exchange(parts):
        swaps = [[(r, r ^ k) for r in range(ranks)] for k in range(ranks)]
        got = list(parts)
        for k in [*range(2, ranks), 1]:
            got[k] = lax.ppermute(parts[k], ("gy", "gz"), swaps[k])
        return got

    patches = [shape((ROWS_BESIDE if k == 1 else ROWS_PATCH, LANES), F32) for k in range(ranks)]
    new, *sends = call(
        functools.partial(leap_kernel, two_y, ranks),
        [shape(coarse_fields.shape, F32)] + patches,
        [vmem] * (5 + len(got)),
        [
            pltpu.VMEM((6 * full * 16, LANES), F32),
            pltpu.VMEM((6 * full * 16, LANES), F32),
            pltpu.VMEM((5 * (full - 1) * 16, LANES), F32),
            pltpu.VMEM((6 * deep * 16, LANES), F32),
            pltpu.VMEM((PAR, ROWS_PATCH, LANES), F32),
        ],
    )(kept, beside, rate, notes, early, *got)
    regions = exchange(sends)

    box, *smalls = call(
        functools.partial(fine_kernel, ranks),
        [shape((groups, 6, ROWS_BOX, WIDE), F32)] + [shape((24, LANES), F32)] * ranks,
        [vmem] * (ranks + 4),
        [
            pltpu.VMEM((groups * 6 * ROWS_BOX, LANES), F32),
            pltpu.VMEM((2, groups * 6 * ROWS_BOX, LANES), F32),
            pltpu.VMEM((6, ROWS_BOX, WIDE), F32),
            pltpu.VMEM((96, 2 * WIDE), F32),
            pltpu.VMEM((groups * 96, LANES), F32),
        ],
    )(*regions, box, fine_rate, jnp.asarray(ghost_table(), BF16), jnp.asarray(mean_table(), BF16))
    means = exchange(smalls)

    fine = call(
        store_kernel,
        shape(fine.shape, F32),
        [vmem] * 4,
        [pltpu.VMEM(fine.shape, F32), pltpu.SemaphoreType.DMA((6,))],
        size=4_000_000,
        out_specs=whole(pltpu.HBM),
    )(box, fine, notes, jnp.asarray(grow.T, BF16))
    new = call(fix_kernel, shape(coarse_fields.shape, F32), [vmem] * (1 + ranks))(new, rate, *regions[1:])
    coarse = call(
        functools.partial(place_kernel, ranks),
        shape(coarse_fields.shape, F32),
        [vmem] * (2 + ranks),
        [
            pltpu.VMEM((PAR, 4 * 96, LANES), F32),
            pltpu.VMEM(coarse_fields.shape, F32),
            pltpu.VMEM((ranks, 24, LANES), F32),
            pltpu.SemaphoreType.DMA((6,)),
        ],
        out_specs=whole(pltpu.HBM),
    )(new, notes, *means)
    return coarse, fine.transpose(0, 1, 3, 2, 4)


def solution(mesh):
    in_specs = (
        P(None, ("groups", "gx"), "gy", "gz"),
        P(("groups", "gx"), "gy", "gz"),
        P(("groups", "gx"), "gy", "gz", None, None),
        P(("groups", "gx"), "gy", "gz", None),
        P(("groups", "gx"), "gy", "gz", None),
        P(("groups", "gx"), None, None),
    )
    out_specs = (P(None, ("groups", "gx"), "gy", "gz"), P(("groups", "gx"), "gy", "gz", None, None))
    return jax.shard_map(local, mesh=mesh, in_specs=in_specs, out_specs=out_specs, check_vma=False)
```

```python
import functools
import jax
import jax.numpy as jnp
import numpy as np
from jax import lax
from jax.experimental import pallas as pl
from jax.experimental.pallas import tpu as pltpu
from jax.sharding import PartitionSpec as P

PF = 16
PAR = 2
HALF = PF // 2
RIM = HALF + 2
PLANES = 9
LINE = PF + 2
LANES = 128
WIDE = 384
BATCH = 4
ROWS_BOX = PLANES * 8
ROWS_RIM = 40
ROW_EDGE = 43
ROWS_PATCH = 56
ROWS_BESIDE = 88
X_COMPS = (0, 1, 2, 4, 5)
Y_COMPS = (0, 1, 2, 3, 5)
VMEM_BYTES = 48 * 1024 * 1024
F32 = jnp.float32
BF16 = jnp.bfloat16


def rim_lane(time, j, k):
    if 0 < j < RIM - 1:
        return j * RIM + k + 3 * time
    if j == 0 and time == 0:
        return k
    return (RIM - 1) * RIM + 3 + (2 * time + j // (RIM - 1) - 1) * RIM + k


def grow_table():
    table = np.zeros((PF * PF, WIDE), np.float32)
    for y in range(PF):
        for z in range(PF):
            table[y * PF + z, (y + 1) * LINE + z + 1] = 1.0
    return table


def ghost_table():
    table = np.zeros((2, 2 * LANES, WIDE), np.float32)
    for y in range(LINE):
        for z in range(LINE):
            j, k, lane = (y + 1) // 2, (z + 1) // 2, y * LINE + z
            table[:, LANES + j * RIM + k, lane] = 1.0
            if y in (0, LINE - 1) or z in (0, LINE - 1):
                table[0, rim_lane(0, j, k), lane] = 1.0
                table[1, rim_lane(0, j, k), lane] = 0.5
                table[1, rim_lane(1, j, k), lane] = 0.5
    return table


def mean_table():
    table = np.zeros((2, WIDE, LANES), np.float32)
    for odd in range(2):
        for y in range(PF):
            for z in range(PF):
                lane = odd * HALF * HALF + (y // 2) * HALF + z // 2
                table[odd, (y + 1) * LINE + z + 1, lane] = 0.125
    return table.reshape(2 * WIDE, LANES)


def move(rows, table):
    high = rows.astype(BF16)
    low = (rows - high.astype(F32)).astype(BF16)
    out = jnp.dot(jnp.concatenate([high, low], axis=0), table, preferred_element_type=F32)
    return out[: rows.shape[0]] + out[rows.shape[0] :]


def lane_iota(shape):
    return lax.broadcasted_iota(jnp.int32, shape, len(shape) - 1)


def whole(memory_space=pltpu.VMEM):
    return pl.BlockSpec(memory_space=memory_space)


def call(kernel, outs, in_specs, scratch=(), flops=1_000_000, size=1_000_000, out_specs=None, **extra):
    return pl.pallas_call(
        kernel,
        out_shape=outs,
        in_specs=in_specs,
        out_specs=jax.tree.map(lambda _: whole(), outs) if out_specs is None else out_specs,
        scratch_shapes=list(scratch),
        compiler_params=pltpu.CompilerParams(vmem_limit_bytes=VMEM_BYTES),
        cost_estimate=pl.CostEstimate(flops=flops, bytes_accessed=size, transcendentals=0),
        **extra,
    )


def swap_pairs(count, first):
    pairs = []
    for i in range(first, count - 1, 2):
        pairs += [(i, i + 1), (i + 1, i)]
    return pairs


def full_pairs(count_x):
    pairs = []
    for i in range(count_x):
        for j in range(2):
            if 0 < i < count_x - 1:
                target = (i + 1 if i % 2 else i - 1) * 2 + j
            else:
                target = i * 2 + 1 - j
            pairs.append((i * 2 + j, target))
    return pairs


def faces_kernel(two_y, block, kept, x_even, y_even, x_odd, *y_odd):
    deep, tall = block.shape[1], block.shape[2]
    gx_odd = lax.rem(lax.axis_index("gx"), 2)
    gy_odd = lax.rem(lax.axis_index("gy"), 2)
    for k, c in enumerate(X_COMPS):
        x_even[k] = block[c, (1 - gx_odd) * (deep - 1)]
        x_odd[k] = block[c, gx_odd * (deep - 1)]
    for k, c in enumerate(Y_COMPS):
        for x in range(deep):
            first = block[c, x, 0:1, :]
            last = block[c, x, tall - 1 : tall, :]
            y_even[k, x : x + 1, :] = jnp.where(gy_odd == 0, last, first)
            if two_y:
                y_odd[0][k, x : x + 1, :] = jnp.where(gy_odd == 0, first, last)
    kept[...] = block[...]


def pack(source, deep, spot, time, packed, q, early):
    lane = lane_iota((8, LANES))
    cx, cy, cz = spot

    def rows_of(c, k, j, count, over_c):
        step = deep * 16 if over_c else 16
        return source[pl.ds((c * deep + cx - 1 + k) * 16 + cy + (j - 1), count, stride=step), :]

    def aim(rows, target):
        return pltpu.roll(rows, lax.rem(target - (cz - 1) + 2 * LANES, LANES), 1)

    for c in range(5):
        total = jnp.zeros((8, LANES), F32) if early is None else early[q, c * 8 : c * 8 + 8, :]
        for j in range(RIM):
            if j == RIM - 1 and c not in (0, 2):
                continue
            source_c = 5 if c == 4 and j == 0 else c
            first = rim_lane(time, j, 0)
            if j in (0, RIM - 1):
                inside = (lane >= first) & (lane < first + RIM)
            else:
                inside = (lane == first) | (lane == first + RIM - 1)
            total = jnp.where(inside, aim(rows_of(source_c, 1, j, 8, False), first), total)
        packed[q, c * 8 : c * 8 + 8, :] = total
    low = jnp.zeros((6, LANES), F32)
    high = jnp.zeros((2, LANES), F32)
    for j in range(RIM):
        first = j * RIM
        inside = (lane >= first) & (lane < first + RIM)
        low = jnp.where(inside[0:6], aim(rows_of(0, 0, j, 6, True), first), low)
        high = jnp.where(inside[0:2], aim(rows_of(1, RIM - 1, j, 2, True), first), high)
    base = ROWS_RIM + time * 8
    packed[q, base : base + 6, :] = low
    packed[q, base + 6 : base + 8, :] = high
    if early is not None:
        packed[q, ROWS_RIM:base, :] = early[q, ROWS_RIM:base, :]


def notes_kernel(corner, owners, perm, block, notes, rate, early, flat):
    rank = lax.axis_index("gy") * lax.axis_size("gz") + lax.axis_index("gz")

    def note(row, value):
        notes[row : row + 1, :] = jnp.full((1, LANES), value, jnp.int32)

    for q in range(PAR):
        for d in range(3):
            note(q * 4 + d, corner[0, 0, q, d])
        note(q * 4 + 3, lax.bitwise_xor(owners[0, q, rank], rank))
    for slot in range(notes.shape[0] - 8):
        live = (owners[0, 0, slot] == rank) | (owners[0, 1, slot] == rank)
        note(8 + slot, live.astype(jnp.int32))
    rate[...] = 0.5 / perm[...]
    deep, tall = block.shape[1], block.shape[2]
    for c in range(6):
        for x in range(deep):
            flat[pl.ds((c * deep + x) * 16, tall), :] = block[c, x]
    for q in range(PAR):
        spot = [corner[0, 0, q, d] for d in range(3)]
        pack(flat, deep, spot, 0, early, q, None)


def leap_kernel(two_y, ranks, *refs):
    block, beside, rate, notes, early, x_even, y_even, x_odd = refs[:8]
    y_odd = refs[8] if two_y else None
    refs = refs[8 + two_y :]
    new, sends = refs[0], refs[1 : 1 + ranks]
    pad, side, mag, fresh, packed = refs[1 + ranks :]
    deep, tall = block.shape[1], block.shape[2]
    full = deep + 2
    gx = lax.axis_index("gx")
    gx_odd = lax.rem(gx, 2)
    gy_odd = lax.rem(lax.axis_index("gy"), 2)
    gz = lax.axis_index("gz")
    noted = notes[0:8, :]
    spots = [[noted[q * 4 + d, 0] for d in range(3)] for q in range(PAR)]
    chosen = noted[3, 0]
    lane = lane_iota((tall, LANES))
    keep = ((lane == 0) & (gz == 0)) | ((lane == LANES - 1) & (gz == 1))
    lane = lane_iota((16, LANES))
    none = jnp.zeros((16, LANES), F32)

    def at(c, x):
        return (c * full + x) * 16

    for c in range(6):
        for x in (0, full - 1):
            pad[pl.ds(at(c, x), 16), :] = none
        for x in range(deep):
            pad[pl.ds(at(c, x + 1), tall), :] = block[c, x]
        pad[pl.ds(at(c, 1) + tall, deep, stride=16), :] = none[0:deep]
        pad[pl.ds(at(c, 1) + 15, deep, stride=16), :] = none[0:deep]
    for c in range(5):
        for x in (0, full - 1):
            side[pl.ds(at(c, x), 16), :] = none
        for x in range(deep):
            side[pl.ds(at(c, x + 1), 16), :] = none
            side[pl.ds(at(c, x + 1), tall), :] = jnp.where(keep, beside[c, x], 0.0)
    for k, c in enumerate(X_COMPS):
        even, odd = x_even[k], x_odd[k]
        low, high = jnp.where(gx_odd == 0, odd, even), jnp.where(gx_odd == 0, even, odd)
        pad[pl.ds(at(c, 0), tall), :] = jnp.where(gx == 0, 0.0, low)
        if c in (1, 2):
            pad[pl.ds(at(c, full - 1), tall), :] = jnp.where(gx == lax.axis_size("gx") - 1, 0.0, high)
    for k, c in enumerate(Y_COMPS):
        even = y_even[k]
        odd = jnp.zeros_like(even) if y_odd is None else y_odd[k]
        pad[pl.ds(at(c, 1) + 15, deep, stride=16), :] = jnp.where(gy_odd == 0, odd, even)
        if c in (0, 2):
            pad[pl.ds(at(c, 1) + tall, deep, stride=16), :] = jnp.where(gy_odd == 0, even, odd)

    def up_y(a):
        return pltpu.roll(a, 15, 0)

    def down_y(a):
        return pltpu.roll(a, 1, 0)

    def plane(c, x):
        return pad[pl.ds(at(c, x), 16), :]

    def edge(c, x):
        return side[pl.ds(at(c, x), 16), :]

    def field(c, x):
        return mag[pl.ds((c * (full - 1) + x) * 16, 16), :]

    for x in range(full - 1):
        e0, e1, e2 = plane(0, x), plane(1, x), plane(2, x)
        s0, s1, s2 = edge(0, x), edge(1, x), edge(2, x)
        r0, r1 = pltpu.roll(e0, LANES - 1, 1), pltpu.roll(e1, LANES - 1, 1)
        u0 = jnp.where(lane == LANES - 1, pltpu.roll(s0, LANES - 1, 1), r0)
        u1 = jnp.where(lane == LANES - 1, pltpu.roll(s1, LANES - 1, 1), r1)
        h0 = plane(3, x) - 0.5 * ((up_y(e2) - e2) - (u1 - e1))
        h1 = plane(4, x) - 0.5 * ((u0 - e0) - (plane(2, x + 1) - e2))
        h2 = plane(5, x) - 0.5 * ((plane(1, x + 1) - e1) - (up_y(e0) - e0))
        t0 = edge(3, x) - 0.5 * ((up_y(s2) - s2) - (r1 - s1))
        t1 = edge(4, x) - 0.5 * ((r0 - s0) - (edge(2, x + 1) - s2))
        d0 = pltpu.roll(jnp.where(lane == LANES - 1, t0, h0), 1, 1)
        d1 = pltpu.roll(jnp.where(lane == LANES - 1, t1, h1), 1, 1)
        for c, value in enumerate((h0, h1, h2, d0, d1)):
            mag[pl.ds((c * (full - 1) + x) * 16, 16), :] = value
    for x in range(deep):
        h0, h1, h2, d0, d1 = (field(c, x + 1) for c in range(5))
        coef = rate[x]
        c0 = (h2 - down_y(h2)) - (h1 - d1)
        c1 = (h0 - d0) - (h2 - field(2, x))
        c2 = (h1 - field(1, x)) - (h0 - down_y(h0))
        for c, curl in enumerate((c0, c1, c2)):
            value = plane(c, x + 1)[0:tall] + coef * curl[0:tall]
            new[c, x] = value
            new[c + 3, x] = (h0, h1, h2)[c][0:tall]
            fresh[pl.ds((c * deep + x) * 16, tall), :] = value
            fresh[pl.ds(((c + 3) * deep + x) * 16, tall), :] = (h0, h1, h2)[c][0:tall]
    for q in range(PAR):
        pack(fresh, deep, spots[q], 1, packed, q, early)
        packed[q, ROW_EDGE : ROW_EDGE + 1, :] = pad[pl.ds(at(1, full - 1) + tall - 1, 1), :]
        packed[q, ROW_EDGE + 8 : ROW_EDGE + 9, :] = pad[pl.ds(at(0, 0), 1), :]
    for k, send in enumerate(sends):
        q = jnp.where(chosen == k, 0, 1)
        send[0:ROWS_PATCH, :] = packed[q]
    half = lane_iota((16, LANES)) < LANES // 2
    send = sends[1]
    send[ROWS_PATCH : ROWS_PATCH + 16, :] = jnp.where(half, plane(0, 0), plane(2, full - 1))
    low = jnp.where(gy_odd == 0, jnp.zeros_like(y_even[1]) if y_odd is None else y_odd[1], y_even[1])
    high = jnp.where(gy_odd == 0, y_even[2], jnp.zeros_like(y_even[2]) if y_odd is None else y_odd[2])
    send[ROWS_PATCH + 16 : ROWS_PATCH + 32, :] = jnp.zeros((16, LANES), F32)
    send[ROWS_PATCH + 16 : ROWS_PATCH + 16 + deep, :] = jnp.where(half[0:deep], low, high)


def places():
    for x in range(PF):
        yield x, (x % 8 + 1) * 8 if x < 8 else (x % 8) * 8 + BATCH


def load_kernel(fine, perm, table, box, rate, lhs, coefs):
    groups = fine.shape[3] // BATCH
    blank = jnp.zeros((8, PF * PF), F32)
    for g in range(groups):
        slots = slice(g * BATCH, (g + 1) * BATCH)
        for c in range(6):
            for row in (0, ROWS_BOX - 8):
                lhs[c * ROWS_BOX + row : c * ROWS_BOX + row + 8, :] = blank
            for x, row in places():
                row += c * ROWS_BOX
                lhs[row : row + BATCH, :] = fine[0, 0, c, slots, x * PF * PF : (x + 1) * PF * PF]
            grown = move(lhs[c * ROWS_BOX : (c + 1) * ROWS_BOX, :], table[...])
            box[g, c] = grown
        for row in (0, ROWS_BOX - 8):
            coefs[row : row + 8, :] = blank
        for x, row in places():
            coefs[row : row + BATCH, :] = 0.5 / perm[0, 0, slots, x * PF * PF : (x + 1) * PF * PF]
        rate[g] = move(coefs[...], table[...])


def fine_kernel(ranks, *refs):
    regions, (box, rate, ghosts, means, out) = refs[:ranks], refs[ranks : ranks + 5]
    smalls = refs[ranks + 5 : 2 * ranks + 5]
    rims, walls, now, halves, small = refs[2 * ranks + 5 :]
    groups = box.shape[0]
    rank = lax.axis_index("gy") * lax.axis_size("gz") + lax.axis_index("gz")
    flat = lane_iota((8, WIDE))
    yy = lax.shift_right_logical(flat * 3641, 16)
    zz = flat - yy * LINE
    inner = (yy >= 1) & (yy <= PF) & (zz >= 1) & (zz <= PF)
    upper = lax.broadcasted_iota(jnp.int32, (8, WIDE), 0) >= BATCH

    def inner_of(m):
        if m == 0:
            return inner & upper
        if m == PLANES - 1:
            return inner & jnp.logical_not(upper)
        return inner

    def up_y(a):
        return pltpu.roll(a, WIDE - LINE, 1)

    def up_z(a):
        return pltpu.roll(a, WIDE - 1, 1)

    def down_y(a):
        return pltpu.roll(a, LINE, 1)

    def down_z(a):
        return pltpu.roll(a, 1, 1)

    def rows_of(m):
        return pl.ds(m * 8, 8)

    blank = jnp.zeros((8, LANES), F32)
    for g in range(groups):
        for c in range(6):
            for m in range(PLANES):
                row = ((g * 6 + c) * PLANES + m) * 8
                if m in (0, PLANES - 1):
                    rims[row : row + 8, :] = blank
                walls[0, row : row + 8, :] = blank
                walls[1, row : row + 8, :] = blank
    for k, region in enumerate(regions):
        slot = lax.bitwise_xor(rank, k)
        start = (slot // BATCH) * 6 * ROWS_BOX + lax.rem(slot, BATCH)
        for c in range(6):
            rows = region[min(c, 4) * 8 : min(c, 4) * 8 + 8, :]
            row = start + c * ROWS_BOX
            rims[pl.ds(row + 8, 4, stride=16), :] = rows[0:4]
            rims[pl.ds(row + 16, 4, stride=16), :] = rows[0:4]
            rims[pl.ds(row + BATCH, 4, stride=16), :] = rows[4:8]
            rims[pl.ds(row + BATCH + 8, 4, stride=16), :] = rows[4:8]
        old = region[ROWS_RIM : ROWS_RIM + 8, :]
        fresh = region[ROWS_RIM + 8 : ROWS_RIM + 16, :]
        for sub, value in enumerate((old, old + 0.5 * (fresh - old))):
            walls[sub, pl.ds(start, 6, stride=ROWS_BOX), :] = value[0:6]
            last = start + ROWS_BOX + (PLANES - 1) * 8 + BATCH
            walls[sub, pl.ds(last, 2, stride=ROWS_BOX), :] = value[6:8]
    for g in range(groups):
        for sub in range(2):
            source = box if sub == 0 else out
            rows = pl.ds(g * 6 * ROWS_BOX, 6 * ROWS_BOX)
            ghost = move(jnp.concatenate([rims[rows, :], walls[sub, rows, :]], axis=1), ghosts[sub])
            for c in range(6):
                for m in range(PLANES):
                    row = c * ROWS_BOX + m * 8
                    now[c, rows_of(m), :] = jnp.where(
                        inner_of(m), source[g, c, rows_of(m), :], ghost[row : row + 8]
                    )

            def next_x(c, m):
                if m == PLANES - 1:
                    return pltpu.roll(now[c, rows_of(0), :], BATCH, 0)
                return now[c, rows_of(m + 1), :]

            def last_x(c, m):
                if m == 0:
                    return pltpu.roll(out[g, c + 3, rows_of(PLANES - 1), :], BATCH, 0)
                return out[g, c + 3, rows_of(m - 1), :]

            for m in range(PLANES):
                e0, e1, e2 = (now[c, rows_of(m), :] for c in range(3))
                h0, h1, h2 = (now[c, rows_of(m), :] for c in range(3, 6))
                out[g, 3, rows_of(m), :] = h0 - 0.5 * ((up_y(e2) - e2) - (up_z(e1) - e1))
                out[g, 4, rows_of(m), :] = h1 - 0.5 * ((up_z(e0) - e0) - (next_x(2, m) - e2))
                out[g, 5, rows_of(m), :] = h2 - 0.5 * ((next_x(1, m) - e1) - (up_y(e0) - e0))
            for m in range(PLANES):
                h0, h1, h2 = (out[g, c, rows_of(m), :] for c in range(3, 6))
                coef = rate[g, rows_of(m), :]
                e0, e1, e2 = (now[c, rows_of(m), :] for c in range(3))
                out[g, 0, rows_of(m), :] = e0 + coef * ((h2 - down_y(h2)) - (h1 - down_z(h1)))
                out[g, 1, rows_of(m), :] = e1 + coef * ((h0 - down_z(h0)) - (h2 - last_x(2, m)))
                out[g, 2, rows_of(m), :] = e2 + coef * ((h1 - last_x(1, m)) - (h0 - down_y(h0)))
        for c in range(6):
            for k in range(4):
                other = jnp.where(upper, out[g, c, rows_of(2 * k), :], out[g, c, rows_of(2 * k + 2), :])
                pair = out[g, c, rows_of(2 * k + 1), :] + other
                halves[pl.ds((c * 2 + k // 2) * 8, 8), (k % 2) * WIDE : (k % 2 + 1) * WIDE] = pair
        small[pl.ds(g * 96, 96), :] = move(halves[...], means[...])
    for k, send in enumerate(smalls):
        slot = lax.bitwise_xor(rank, k)
        start = (slot // BATCH) * 96 + lax.rem(slot, BATCH)
        for xh in range(2):
            send[xh * 12 : (xh + 1) * 12, :] = small[pl.ds(start + xh * BATCH, 12, stride=8), :]


def store_kernel(box, fine, notes, table, out, stage, sems):
    groups = box.shape[0]
    slots = groups * BATCH
    live = jnp.concatenate([notes[8 : 8 + slots, :]] * (PF * PF // LANES), axis=1) > 0
    copies = []
    for c in range(6):
        flats = [move(box[g, c], table[...]) for g in range(groups)]
        for x, row in places():
            cut = slice(x * PF * PF, (x + 1) * PF * PF)
            for g, flat in enumerate(flats):
                some = slice(g * BATCH, (g + 1) * BATCH)
                stage[0, 0, c, some, cut] = jnp.where(live[some], flat[row : row + BATCH], fine[0, 0, c, some, cut])
        copies.append(pltpu.make_async_copy(stage.at[:, :, c], out.at[:, :, c], sems.at[c]))
        copies[-1].start()
    for copy in copies:
        copy.wait()


def fix_kernel(new, rate, *refs):
    edges, out = refs[:-1], refs[-1]
    deep, tall = new.shape[1], new.shape[2]
    gz = lax.axis_index("gz")
    rank = lax.axis_index("gy") * 2 + gz
    out[...] = new[...]

    def add(c, x, rows, amount):
        out[c, x, rows, :] = out[c, x, rows, :] + 0.5 * rate[x, rows, :] * amount

    lower = higher = jnp.zeros((1, LANES), F32)
    for k, edge in enumerate(edges, 1):
        row = ROW_EDGE
        lower = jnp.where(lax.bitwise_xor(rank, k) == rank - 2, edge[row : row + 1, :], lower)
        higher = jnp.where(lax.bitwise_xor(rank, k) == rank + 2, edge[row + 8 : row + 9, :], higher)
    add(0, deep - 1, slice(0, 1), lower)
    add(1, 0, slice(tall - 1, tall), higher)
    lane = lane_iota((tall, LANES))
    tile = edges[0][ROWS_PATCH : ROWS_PATCH + tall, :]
    add(0, deep - 1, slice(0, tall), jnp.where((lane == 0) & (gz == 1), pltpu.roll(tile, 1, 1), 0.0))
    add(2, 0, slice(0, tall), jnp.where((lane == LANES - 1) & (gz == 0), pltpu.roll(tile, LANES - 1, 1), 0.0))
    lane = lane_iota((deep, LANES))
    tile = edges[0][ROWS_PATCH + 16 : ROWS_PATCH + 16 + deep, :]
    first = jnp.where((lane == LANES - 1) & (gz == 0), pltpu.roll(tile, LANES - 1, 1), 0.0)
    last = jnp.where((lane == 0) & (gz == 1), pltpu.roll(tile, 1, 1), 0.0)
    for x in range(deep):
        add(2, x, slice(0, 1), first[x : x + 1])
        add(1, x, slice(tall - 1, tall), last[x : x + 1])


def place_kernel(ranks, new, notes, *refs):
    means, (out, spread, stage, gathered, sems) = refs[:ranks], refs[ranks:]
    noted = notes[0:8, :]
    for k, mean in enumerate(means):
        gathered[k] = mean[...]
    lane = lane_iota((HALF, LANES))
    spots = [tuple(noted[q * 4 + d, 0] for d in range(3)) for q in range(PAR)]
    for q, (cx, cy, cz) in enumerate(spots):
        k = noted[q * 4 + 3, 0]
        rows = gathered[k]
        for odd in range(2):
            for y in range(HALF):
                shift = lax.rem(cz - y * HALF - odd * HALF * HALF + 2 * LANES, LANES)
                spread[q, pl.ds(odd * 192 + y, 24, stride=8), :] = pltpu.roll(rows, shift, 1)
    copies = []
    for c in range(6):
        stage[c] = new[c]
        for q, (cx, cy, cz) in enumerate(spots):
            inside = (lane >= cz) & (lane < cz + HALF)
            for x in range(HALF):
                xh, k = x // 4, x % 4
                tile = spread[q, pl.ds((k % 2) * 192 + (xh * 12 + c * 2 + k // 2) * 8, 8), :]
                spot = stage[c, cx + x, pl.ds(cy, HALF), :]
                stage[c, cx + x, pl.ds(cy, HALF), :] = jnp.where(inside, tile, spot)
        copies.append(pltpu.make_async_copy(stage.at[c], out.at[c], sems.at[c]))
        copies[-1].start()
    for copy in copies:
        copy.wait()


def local(coarse_fields, permittivity, fine_fields, fine_permittivity, patch_corner, patch_owner):
    deep, tall, cols = coarse_fields.shape[1:]
    slots = fine_fields.shape[2]
    groups = slots // BATCH
    count_x, count_y = lax.axis_size("gx"), lax.axis_size("gy")
    two_y = count_y > 2
    vmem = whole()
    shape = jax.ShapeDtypeStruct
    grow = grow_table()

    x_face = shape((5, tall, cols), F32)
    y_face = shape((5, deep, cols), F32)
    kept, *faces = call(
        functools.partial(faces_kernel, two_y),
        [shape(coarse_fields.shape, F32), x_face, y_face, x_face] + [y_face] * two_y,
        [vmem],
    )(coarse_fields)
    got = [
        lax.ppermute(faces[0], "gx", swap_pairs(count_x, 0)),
        lax.ppermute(faces[1], "gy", swap_pairs(count_y, 0)),
        lax.ppermute(faces[2], ("gx", "gz"), full_pairs(count_x)),
    ]
    if two_y:
        got.append(lax.ppermute(faces[3], "gy", swap_pairs(count_y, 1)))
    beside = lax.ppermute(kept, "gz", swap_pairs(2, 0))

    fine = fine_fields.transpose(0, 1, 3, 2, 4)
    notes, rate, early = call(
        notes_kernel,
        [
            shape((8 + slots, LANES), jnp.int32),
            shape(permittivity.shape, F32),
            shape((PAR, ROWS_RIM + 8, LANES), F32),
        ],
        [whole(pltpu.SMEM)] * 2 + [vmem] * 2,
        [pltpu.VMEM((6 * deep * 16, LANES), F32)],
    )(patch_corner, patch_owner.transpose(0, 2, 1), permittivity, kept)
    box, fine_rate = call(
        load_kernel,
        [shape((groups, 6, ROWS_BOX, WIDE), F32), shape((groups, ROWS_BOX, WIDE), F32)],
        [vmem] * 3,
        [pltpu.VMEM((6 * ROWS_BOX, PF * PF), F32), pltpu.VMEM((ROWS_BOX, PF * PF), F32)],
        size=4_000_000,
    )(fine, fine_permittivity, jnp.asarray(grow, BF16))

    full = deep + 2
    ranks = count_y * lax.axis_size("gz")

    def exchange(parts):
        swaps = [[(r, r ^ k) for r in range(ranks)] for k in range(ranks)]
        got = list(parts)
        for k in [*range(2, ranks), 1]:
            got[k] = lax.ppermute(parts[k], ("gy", "gz"), swaps[k])
        return got

    patches = [shape((ROWS_BESIDE if k == 1 else ROWS_PATCH, LANES), F32) for k in range(ranks)]
    new, *sends = call(
        functools.partial(leap_kernel, two_y, ranks),
        [shape(coarse_fields.shape, F32)] + patches,
        [vmem] * (5 + len(got)),
        [
            pltpu.VMEM((6 * full * 16, LANES), F32),
            pltpu.VMEM((6 * full * 16, LANES), F32),
            pltpu.VMEM((5 * (full - 1) * 16, LANES), F32),
            pltpu.VMEM((6 * deep * 16, LANES), F32),
            pltpu.VMEM((PAR, ROWS_PATCH, LANES), F32),
        ],
    )(kept, beside, rate, notes, early, *got)
    regions = exchange(sends)

    box, *smalls = call(
        functools.partial(fine_kernel, ranks),
        [shape((groups, 6, ROWS_BOX, WIDE), F32)] + [shape((24, LANES), F32)] * ranks,
        [vmem] * (ranks + 4),
        [
            pltpu.VMEM((groups * 6 * ROWS_BOX, LANES), F32),
            pltpu.VMEM((2, groups * 6 * ROWS_BOX, LANES), F32),
            pltpu.VMEM((6, ROWS_BOX, WIDE), F32),
            pltpu.VMEM((96, 2 * WIDE), F32),
            pltpu.VMEM((groups * 96, LANES), F32),
        ],
    )(*regions, box, fine_rate, jnp.asarray(ghost_table(), BF16), jnp.asarray(mean_table(), BF16))
    means = exchange(smalls)

    fine = call(
        store_kernel,
        shape(fine.shape, F32),
        [vmem] * 4,
        [pltpu.VMEM(fine.shape, F32), pltpu.SemaphoreType.DMA((6,))],
        size=4_000_000,
        out_specs=whole(pltpu.HBM),
    )(box, fine, notes, jnp.asarray(grow.T, BF16))
    new = call(fix_kernel, shape(coarse_fields.shape, F32), [vmem] * (1 + ranks))(new, rate, *regions[1:])
    coarse = call(
        functools.partial(place_kernel, ranks),
        shape(coarse_fields.shape, F32),
        [vmem] * (2 + ranks),
        [
            pltpu.VMEM((PAR, 4 * 96, LANES), F32),
            pltpu.VMEM(coarse_fields.shape, F32),
            pltpu.VMEM((ranks, 24, LANES), F32),
            pltpu.SemaphoreType.DMA((6,)),
        ],
        out_specs=whole(pltpu.HBM),
    )(new, notes, *means)
    return coarse, fine.transpose(0, 1, 3, 2, 4)


def solution(mesh):
    in_specs = (
        P(None, ("groups", "gx"), "gy", "gz"),
        P(("groups", "gx"), "gy", "gz"),
        P(("groups", "gx"), "gy", "gz", None, None),
        P(("groups", "gx"), "gy", "gz", None),
        P(("groups", "gx"), "gy", "gz", None),
        P(("groups", "gx"), None, None),
    )
    out_specs = (P(None, ("groups", "gx"), "gy", "gz"), P(("groups", "gx"), "gy", "gz", None, None))
    return jax.shard_map(local, mesh=mesh, in_specs=in_specs, out_specs=out_specs, check_vma=False)
```
